32 devices in a mesh: lat: 4 (over y, x), lon: 8 (over z, core).
Axes of the slice: x: 2, y: 2, z: 4, core: 2. Of those that a mesh axis runs over, the one named last changes fastest.
Arguments:
- background: bfloat16 [64, 256, 512], P('lat', 'lon'), may hold values from -6 to 6
- observations: bfloat16 [32768, 256], P(('lat', 'lon')), may hold values from -6 to 6
- destination: int32 [32768, 1], P(('lat', 'lon')), may hold values from 0 to 31; in each aligned block of 1024 rows (0 to 1023, 1024 to 2047, ...) at most 64 rows name the same one
- footprint: int32 [32768, 4], P(('lat', 'lon')), may hold values from 0 to 511, as said below
- weights: bfloat16 [32768, 4], P(('lat', 'lon')), may hold values from 0.099609375 to 1
- obs_proj: bfloat16 [256, 512], replicated, may hold values from -0.375 to 0.375
- depth_w: float32 [4, 7, 7, 512], replicated, may hold values from -1.5 to 1.5
- point_w: bfloat16 [4, 512, 512], replicated, may hold values from -0.25 to 0.25
- gains: float32 [4, 512], replicated, may hold values from 0.5 to 2
Outputs:
- encoded: bfloat16 [64, 256, 512], P('lat', 'lon')
The draws below stay inside these ranges and needn't reach their ends.
Inputs may be any that keep to these rules, and one draw needn't show every extreme that they name: `destination`: each device's 1024 rows name one tile at most 64 times. footprint[i, k] = (s_i + k * 33) mod 512 for a start cell s_i, so the 4 cells of one observation are distinct.
All inputs are finite; a program needn't handle non-finite values.
Results may differ from the reference program's by a relative error of at most 0.0085.
Values may be sent and summed in bfloat16 or wider, within the bound.
No kernel may reach another device: no remote copies, remote signals or barrier semaphores. Data moves between devices by JAX's collectives and lax.ppermute only.
A program may use at most 64 MiB of HBM per device.

```python
import math
import jax
import jax.numpy as jnp
import numpy as np
from jax import lax

CHAN = 512
FEAT = 256
FOOT = 4
LAYERS = 4
LAT_DEV = 16
LON_DEV = 32
OBS_DEV = 1024
CAP = 64
OBS_TOTAL = 32768
NLAT = 64
NLON = 256
DEVICES = 32


def draw_footprint(key, part):
    key = jax.random.fold_in(key, 7)
    starts = jax.random.randint(key, (OBS_TOTAL,), 0, LAT_DEV * LON_DEV)
    starts = starts.at[0].set(LAT_DEV * LON_DEV - 1).at[1].set(0)
    offsets = jnp.arange(FOOT) * (LON_DEV + 1)
    return ((starts[:, None] + offsets[None, :]) % (LAT_DEV * LON_DEV)).astype(jnp.int32)


def levels(key, extent, cuts, low, top_value):
    def one(dim, shards_of):
        draws = jax.random.uniform(jax.random.fold_in(jax.random.fold_in(key, 6), dim), (shards_of,), jnp.float32, low / len(cuts), top_value / len(cuts))
        return jnp.repeat(jnp.exp(draws), extent[dim] // shards_of).reshape((-1,) + (1,) * (len(extent) - dim - 1))

    gain = one(*cuts[0])
    for cut in cuts[1:]:
        gain = gain * one(*cut)
    return gain


def assign_block(rng, own, number, rows, number_of, top, reach, lean):
    sequence = jax.random.permutation(rng, number_of)
    packed, ordinary = shares(number_of, rows * top, reach, lean, True), shares(number_of, rows * top, reach, lean, False)
    places = jnp.arange(number_of)

    def named(lengths, offset_by):
        used = int((lengths > 0).sum())
        fixed = max(1, used // 4)
        moved = fixed + (places - fixed + offset_by * (used - fixed)) % max(1, number_of - fixed)
        return jnp.zeros((number_of,), jnp.int32).at[sequence[jnp.where(places < fixed, places, moved)]].set(jnp.asarray(lengths, jnp.int32))

    lengths = jnp.where(number % 4 == 0, named(packed, number // 4), named(ordinary, number - number // 4 - 1))
    mixed = jax.random.permutation(jax.random.fold_in(own, 3), number_of)
    source_of, taker = mixed[0:number_of // 2 * 2:2], mixed[1:number_of // 2 * 2:2]
    margin = jnp.minimum(lengths[source_of] - 1, reach - lengths[taker]) // 2
    margin = jnp.where((source_of == sequence[0]) | (taker == sequence[0]) | (lengths[taker] == 0), 0, jnp.maximum(margin, 0))
    moved = jax.random.randint(jax.random.fold_in(own, 4), (number_of // 2,), 0, 1 << 20) % (margin + 1)
    lengths = lengths.at[source_of].add(-moved).at[taker].add(moved)
    items = jnp.searchsorted(jnp.cumsum(lengths), jnp.arange(rows * top), side="right").astype(jnp.int32)
    table = items.reshape(top, rows).T
    table = table[jax.random.permutation(jax.random.fold_in(own, 1), rows)]
    offset_by = jax.random.randint(jax.random.fold_in(own, 2), (rows, 1), 0, top)
    return jnp.take_along_axis(table, (jnp.arange(top)[None, :] + offset_by) % top, axis=1)


def shares(number_of, total, reach, slope, full):
    weights = [(1 << 20) // math.isqrt(grade ** slope) + 1 for grade in range(1, number_of + 1)]
    largest = reach if full else min(reach, max(-(-total // number_of), total * weights[0] // sum(weights)))
    least = 1 if total - largest >= number_of - 1 else 0
    holding, rest = [largest] + [least] * (number_of - 1), total - largest - least * (number_of - 1)
    while rest > 0:
        candidates = [i for i in range(1, number_of) if holding[i] < largest] or [i for i in range(1, number_of) if holding[i] < reach]
        pool, remaining = sum([weights[i] for i in candidates]), rest
        for i in candidates:
            extra = min(reach - holding[i], max(1, remaining * weights[i] // pool), rest)
            holding[i] = holding[i] + extra
            rest = rest - extra
    return np.array(holding)


def bell_draw(stream_key, shape, scale, bound, pieces=(), held_as=jnp.bfloat16):
    array = scale * jax.random.normal(stream_key, shape, jnp.float32)
    if pieces:
        array = array * levels(stream_key, shape, pieces, -0.22, 0.18)
    return jnp.clip(array, -bound, bound).astype(held_as)


def setup_inputs(seed: int = 0) -> dict:
    streams_of = jax.random.split(jax.random.key(seed), 10)
    background = bell_draw(streams_of[0], (NLAT, NLON, CHAN), 1.0, 6.0, ((0, 4), (1, 8)))
    observations = bell_draw(streams_of[1], (OBS_TOTAL, FEAT), 1.0, 6.0, ((0, 32),))
    destination_keys = jax.random.split(jax.random.fold_in(streams_of[2], 1), OBS_TOTAL // OBS_DEV)
    destination_turns = jax.random.permutation(jax.random.fold_in(streams_of[2], 3), OBS_TOTAL // OBS_DEV)
    destination = jax.vmap(lambda own, number: assign_block(jax.random.fold_in(streams_of[2], 2), own, number, OBS_DEV, DEVICES, 1, CAP, 2))(destination_keys, destination_turns).reshape((OBS_TOTAL, 1))
    footprint = draw_footprint(jax.random.fold_in(streams_of[9], 71), 0)
    weights = jnp.clip(jnp.exp(math.log(1.0) - 2.306499 * jax.random.uniform(streams_of[4], (OBS_TOTAL, FOOT), jnp.float32) ** levels(streams_of[4], (OBS_TOTAL, FOOT), ((0, 32),), -0.2, 0.2)), 0.099609375, 1.0).astype(jnp.bfloat16)
    obs_proj = bell_draw(streams_of[5], (FEAT, CHAN), FEAT ** -0.5, 0.375)
    depth_w = bell_draw(streams_of[6], (LAYERS, 7, 7, CHAN), 0.25, 1.5, (), jnp.float32)
    point_w = bell_draw(streams_of[7], (LAYERS, CHAN, CHAN), CHAN ** -0.5, 0.25)
    gains = jnp.clip(jnp.exp(jax.random.uniform(streams_of[8], (LAYERS, CHAN), jnp.float32, math.log(0.5), math.log(2.0))), 0.5, 2.0)
    return {"background": background, "observations": observations, "destination": destination, "footprint": footprint, "weights": weights, "obs_proj": obs_proj, "depth_w": depth_w, "point_w": point_w, "gains": gains}


def depthwise(padded, kernel, rows, cols):
    total = jnp.zeros((rows, cols, padded.shape[2]), jnp.float32)
    for tap_a in range(7):
        for tap_b in range(7):
            total = total + padded[tap_a:tap_a + rows, tap_b:tap_b + cols] * kernel[tap_a, tap_b]
    return total

def reference(background, observations, destination, footprint, weights, obs_proj, depth_w, point_w, gains):
    coded = jnp.dot(observations, obs_proj, preferred_element_type=jnp.float32).astype(jnp.bfloat16)
    coded_wide = coded.astype(jnp.float32)
    tiles_lon = NLON // LON_DEV
    target = destination[:, 0]
    tile_row = target // tiles_lon
    tile_col = target % tiles_lon
    field = jnp.zeros((NLAT * NLON, CHAN), jnp.float32)
    for entry in range(FOOT):
        local = footprint[:, entry]
        grid_row = tile_row * LAT_DEV + local // LON_DEV
        grid_col = tile_col * LON_DEV + local % LON_DEV
        flat = (grid_row * NLON + grid_col).astype(jnp.int32)
        field = field.at[flat].add(weights[:, entry].astype(jnp.float32)[:, None] * coded_wide)
    state = (background.astype(jnp.float32).reshape(NLAT * NLON, CHAN) + field).reshape(NLAT, NLON, CHAN).astype(jnp.bfloat16)
    for layer in range(LAYERS):
        wide = state.astype(jnp.float32)
        padded = jnp.pad(wide, ((3, 3), (0, 0), (0, 0)))
        padded = jnp.concatenate([padded[:, -3:], padded, padded[:, :3]], axis=1)
        spread = depthwise(padded, depth_w[layer], NLAT, NLON)
        scale = lax.rsqrt(lax.optimization_barrier(jnp.mean(spread * spread, axis=-1, keepdims=True)) + 1e-05)
        normed = (spread * scale * gains[layer]).astype(jnp.bfloat16)
        mixed = jnp.dot(normed.reshape(NLAT * NLON, CHAN), point_w[layer], preferred_element_type=jnp.float32)
        state = (wide + jax.nn.gelu(mixed).reshape(NLAT, NLON, CHAN)).astype(jnp.bfloat16)
    return state
```

```python
import functools

import jax
import jax.numpy as jnp
from jax import lax
from jax.experimental import pallas as pl
from jax.experimental.pallas import tpu as pltpu
from jax.sharding import PartitionSpec as P

LANES = 128
META = 8
TAPS = 7
HALO = 3
SHIFT = 2 * HALO
EDGE = 8
ROWS = 8
VMEM_LIMIT = 24 * 1024 * 1024
BF16 = jnp.bfloat16
F32 = jnp.float32


def pack_kernel(cap, dest_ref, meta_ref, obs_ref, send_ref):
    devices = send_ref.shape[0]
    obs_rows = obs_ref.shape[0]
    per = LANES // cap
    dest = dest_ref[...]
    ids = lax.broadcasted_iota(jnp.int32, (devices, obs_rows), 0)
    member = jnp.where(ids == dest, 1.0, 0.0)
    upper = lax.broadcasted_iota(jnp.int32, (LANES, LANES), 0) <= lax.broadcasted_iota(
        jnp.int32, (LANES, LANES), 1
    )
    upper = jnp.where(upper, 1.0, 0.0).astype(BF16)
    seen = jnp.zeros((devices, 1), F32)
    ranks = []
    for first in range(0, obs_rows, LANES):
        part = member[:, first : first + LANES]
        count = jnp.dot(part.astype(BF16), upper, preferred_element_type=F32) + seen
        ranks.append(jnp.sum((count - 1.0) * part, axis=0, keepdims=True))
        seen = count[:, LANES - 1 :]
    rank = jnp.concatenate(ranks, axis=1).astype(jnp.int32)
    position = dest * cap + rank
    lane = lax.broadcasted_iota(jnp.int32, (META, LANES), 1)
    block = min(512, devices * cap)
    for first in range(0, devices * cap, block):
        slot = lax.broadcasted_iota(jnp.int32, (block, obs_rows), 0) + first
        chosen = jnp.where(slot == position, 1.0, 0.0).astype(BF16)
        feats = jnp.dot(chosen, obs_ref[...], preferred_element_type=F32).astype(BF16)
        meta = lax.dot_general(
            meta_ref[...], chosen, (((1,), (1,)), ((), ())), preferred_element_type=F32
        )
        start = first // cap
        count = block // cap
        for half in range(feats.shape[1] // LANES):
            piece = feats[:, half * LANES : (half + 1) * LANES].reshape(count, cap, LANES)
            send_ref[start : start + count, half * cap : (half + 1) * cap, :] = piece
        base = send_ref.shape[1] - META
        for chunk in range(block // LANES):
            values = meta[:, chunk * LANES : (chunk + 1) * LANES]
            turned = [values] + [pltpu.roll(values, k * cap, 1) for k in range(1, per)]
            for own in range(per):
                wide = turned[0]
                for group in range(per):
                    wide = jnp.where(lane // cap == group, turned[(group - own) % per], wide)
                send_ref[start + chunk * per + own, base:, :] = wide.astype(BF16)


def assim_kernel(cap, step, got_ref, proj_ref, back_ref, state_ref, lat_ref, lon_ref, corner_ref):
    devices, depth, _ = got_ref.shape
    rows, cols, chans = back_ref.shape
    cells = rows * cols
    feats = proj_ref.shape[0]
    per = LANES // cap
    halves = feats // LANES
    lane = lax.broadcasted_iota(jnp.int32, (META, LANES), 1)
    cell = lax.broadcasted_iota(jnp.int32, (cells, LANES), 0)
    total = jnp.zeros((cells, feats), F32)
    for pair in range(0, devices // per, 2):
        maps = []
        blocks = []
        for chunk in (pair, pair + 1):
            meta = got_ref[chunk * per, depth - META :, :].astype(F32)
            for group in range(1, per):
                other = got_ref[chunk * per + group, depth - META :, :].astype(F32)
                meta = jnp.where(lane // cap == group, other, meta)
            start = (meta[0:1] * cols + meta[1:2]).astype(jnp.int32)
            away = cell - start
            away = jnp.where(away < 0, away + cells, away)
            amount = jnp.zeros((cells, LANES), F32)
            for entry in range(4):
                amount = jnp.where(away == entry * step, meta[2 + entry : 3 + entry], amount)
            maps.append(amount.astype(BF16))
            block = got_ref[chunk * per : (chunk + 1) * per]
            blocks.append(
                jnp.concatenate(
                    [
                        block[:, half * cap : (half + 1) * cap, :].reshape(LANES, LANES)
                        for half in range(halves)
                    ],
                    axis=1,
                )
            )
        total = total + jnp.dot(
            jnp.concatenate(maps, axis=1),
            jnp.concatenate(blocks, axis=0),
            preferred_element_type=F32,
        )
    assim = jnp.dot(total.astype(BF16), proj_ref[...], preferred_element_type=F32)
    state = back_ref[...].astype(F32) + assim.reshape(rows, cols, chans)
    state = state.astype(BF16)
    state_ref[...] = state
    lat_ref[...] = state[rows - SHIFT :]
    lon_ref[...] = state[:, cols - EDGE :, :]
    corner_ref[...] = state[rows - SHIFT :, cols - EDGE :, :]


def gelu(x):
    inner = x * (0.7978845608028654 + 0.035677408136300125 * (x * x))
    half = 0.5 * x
    return half + half * jnp.tanh(inner)


def layer_kernel(
    shrink,
    own_ref,
    lat_in,
    lon_in,
    corner_in,
    taps_ref,
    mix_ref,
    state_ref,
    lat_ref,
    lon_ref,
    corner_ref,
    wide_ref,
    taps_in,
    spread_ref,
    out_ref,
):
    chans = mix_ref.shape[0]
    groups = chans // LANES
    cols = own_ref.shape[1]
    half = cols // 2
    place = lax.axis_index("lat")
    last = place == lax.axis_size("lat") - 1
    first = place == 0
    rows = state_ref.shape[0] if shrink else own_ref.shape[0]

    def put(row, start, value):
        for g in range(groups):
            wide_ref[g, row, start : start + value.shape[0], :] = value[
                :, g * LANES : (g + 1) * LANES
            ]

    if shrink:
        base = 0

        @pl.loop(0, rows)
        def _(y):
            put(y, 0, own_ref[y].astype(F32))
            put(y, cols, lon_in[y].astype(F32))

        for k in range(SHIFT):
            main = lat_in[k].astype(F32)
            side = corner_in[k].astype(F32)
            if k < HALO:
                main = jnp.where(last, own_ref[rows + k].astype(F32), main)
                side = jnp.where(last, lon_in[rows + k].astype(F32), side)
            put(rows + k, 0, main)
            put(rows + k, cols, side)
    else:
        base = EDGE - SHIFT

        @pl.loop(0, SHIFT)
        def _(y):
            put(y, 0, corner_in[y].astype(F32))
            put(y, EDGE, lat_in[y].astype(F32))

        @pl.loop(0, rows)
        def _(y):
            put(y + SHIFT, 0, lon_in[y].astype(F32))
            put(y + SHIFT, EDGE, own_ref[y].astype(F32))

    @pl.loop(0, rows + SHIFT)
    def _(y):
        for g in range(groups):
            for r in range(TAPS + 1):
                taps_in[g, r, y] = wide_ref[g, y, pl.ds(base + r, half, stride=2), :].astype(BF16)

    def depthwise(y0, count):
        for p in range(2):
            for g in range(groups):
                lanes = slice(g * LANES, (g + 1) * LANES)
                total = None
                for b in range(TAPS):
                    seen = taps_in[g, p + b, pl.ds(y0, count + TAPS - 1)]
                    part = None
                    for a in range(TAPS):
                        term = seen[a : a + count] * taps_ref[a * TAPS + b, :, lanes]
                        part = term if part is None else part + term
                    part = part.astype(F32)
                    total = part if total is None else total + part
                spread_ref[p, pl.ds(y0, count), :, lanes] = total.astype(BF16)

    ones = jnp.ones((chans, LANES), BF16)

    def finish(y0, count):
        for p in range(2):
            spread = spread_ref[p, y0 : y0 + count].reshape(count * half, chans)
            power = jnp.dot(spread * spread, ones, preferred_element_type=F32)
            scale = lax.rsqrt(power * (1.0 / chans) + 1e-05)
            mixed = jnp.dot(spread, mix_ref[...], preferred_element_type=F32)
            for g in range(groups):
                moved = gelu(mixed[:, g * LANES : (g + 1) * LANES] * scale)
                moved = moved.reshape(count, half, LANES)
                center = taps_in[g, p + HALO, y0 + HALO : y0 + HALO + count].astype(F32)
                fresh = center + moved
                for k in range(count):
                    out_ref[g, y0 + k, pl.ds(p, half, stride=2), :] = fresh[k]

    @pl.loop(0, rows // ROWS)
    def _(block):
        depthwise(block * ROWS, ROWS)

    for y0 in range(0, rows, ROWS):
        finish(y0, ROWS)

    def row_of(y):
        return jnp.concatenate([out_ref[g, y] for g in range(groups)], axis=1)

    if shrink:
        edge = slice(cols - EDGE, cols)

        @pl.loop(0, rows)
        def _(y):
            value = row_of(y)
            state_ref[y] = value.astype(BF16)
            lon_ref[y] = value[edge].astype(BF16)

        for k in range(SHIFT):
            value = row_of(rows - SHIFT + k)
            lat_ref[k] = value.astype(BF16)
            corner_ref[k] = value[edge].astype(BF16)
    else:

        @pl.when(last)
        def _():
            taps_in[:, :, rows + SHIFT :] = jnp.zeros(
                (groups, TAPS + 1, HALO, half, LANES), BF16
            )
            depthwise(rows, HALO)
            finish(rows, HALO)

        @pl.loop(0, rows + HALO)
        def _(y):
            value = row_of(y)
            value = jnp.where(jnp.logical_and(first, y < HALO), 0.0, value)
            state_ref[y] = value.astype(BF16)
            lon_ref[y] = value[:EDGE].astype(BF16)

        for k in range(SHIFT):
            value = row_of(k)
            if k < HALO:
                value = jnp.where(first, 0.0, value)
            lat_ref[k] = value.astype(BF16)
            corner_ref[k] = value[:EDGE].astype(BF16)


def edges(rows, cols, chans):
    return (
        jax.ShapeDtypeStruct((rows, cols, chans), BF16),
        jax.ShapeDtypeStruct((SHIFT, cols, chans), BF16),
        jax.ShapeDtypeStruct((rows, EDGE, chans), BF16),
        jax.ShapeDtypeStruct((SHIFT, EDGE, chans), BF16),
    )


def call(kernel, out_shape, inputs, scratch=()):
    whole = pl.BlockSpec(memory_space=pltpu.VMEM)
    single = isinstance(out_shape, jax.ShapeDtypeStruct)
    return pl.pallas_call(
        kernel,
        out_shape=out_shape,
        in_specs=[whole] * len(inputs),
        out_specs=whole if single else [whole] * len(out_shape),
        scratch_shapes=list(scratch),
        compiler_params=pltpu.CompilerParams(vmem_limit_bytes=VMEM_LIMIT),
    )(*inputs)


def layer(state, halo, taps, mix, shrink):
    extended, cols, chans = state.shape
    rows = extended - HALO if shrink else extended
    groups = chans // LANES
    window = rows + 2 * HALO if shrink else rows + 3 * HALO
    height = rows if shrink else rows + HALO
    scratch = (
        pltpu.VMEM((groups, rows + SHIFT, cols + EDGE, LANES), F32),
        pltpu.VMEM((groups, TAPS + 1, window, cols // 2, LANES), BF16),
        pltpu.VMEM((2, height, cols // 2, chans), BF16),
        pltpu.VMEM((groups, height, cols, LANES), F32),
    )
    return call(
        functools.partial(layer_kernel, shrink),
        edges(height, cols, chans),
        (state, *halo, taps, mix),
        scratch,
    )


def exchange(pieces, forward):
    lat, lon, corner = pieces
    count_lat = lax.axis_size("lat")
    count_lon = lax.axis_size("lon")
    along = [(i, i + 1) for i in range(count_lat - 1)]
    around = [(j, (j + 1) % count_lon) for j in range(count_lon)]
    across = [
        (i * count_lon + j, ni * count_lon + nj) for i, ni in along for j, nj in around
    ]
    if not forward:
        along, around, across = ([(t, s) for s, t in p] for p in (along, around, across))
    return (
        lax.ppermute(lat, "lat", along),
        lax.ppermute(lon, "lon", around),
        lax.ppermute(corner, ("lat", "lon"), across),
    )


def body(
    background, observations, destination, footprint, weights, obs_proj, depth_w, point_w, gains
):
    rows, cols, chans = background.shape
    devices = lax.axis_size("lat") * lax.axis_size("lon")
    obs_rows, feats = observations.shape
    cap = 2 * obs_rows // devices
    start = footprint[:, 0]
    meta = jnp.concatenate(
        [
            (start // cols).astype(BF16)[None],
            (start % cols).astype(BF16)[None],
            weights.T,
            jnp.zeros((META - 2 - weights.shape[1], obs_rows), BF16),
        ],
        axis=0,
    )
    depth = cap * (feats // LANES) + META
    send = call(
        functools.partial(pack_kernel, cap),
        jax.ShapeDtypeStruct((devices, depth, LANES), BF16),
        (destination.reshape(1, obs_rows), meta, observations),
    )
    got = lax.all_to_all(send, ("lat", "lon"), split_axis=0, concat_axis=0, tiled=True)
    layers = depth_w.shape[0]
    taps = [
        jnp.broadcast_to(
            depth_w[n].astype(BF16).reshape(TAPS * TAPS, 1, chans), (TAPS * TAPS, cols // 2, chans)
        )
        for n in range(layers)
    ]
    mix = [(gains[n][:, None] * point_w[n].astype(F32)).astype(BF16) for n in range(layers)]
    state, *pieces = call(
        functools.partial(assim_kernel, cap, cols + 1),
        edges(rows, cols, chans),
        (got, obs_proj, background),
    )
    for n in range(layers):
        shrink = n % 2 == 1
        halo = exchange(pieces, not shrink)
        state, *pieces = layer(state, halo, taps[n], mix[n], shrink)
    return state


def solution(mesh):
    placed = (
        P("lat", "lon", None),
        P(("lat", "lon"), None),
        P(("lat", "lon"), None),
        P(("lat", "lon"), None),
        P(("lat", "lon"), None),
        P(),
        P(),
        P(),
        P(),
    )
    return jax.shard_map(
        body, mesh=mesh, in_specs=placed, out_specs=P("lat", "lon", None), check_vma=False
    )
```

```python
import functools

import jax
import jax.numpy as jnp
from jax import lax
from jax.experimental import pallas as pl
from jax.experimental.pallas import tpu as pltpu
from jax.sharding import PartitionSpec as P

LANES = 128
META = 8
TAPS = 7
HALO = 3
SHIFT = 2 * HALO
EDGE = 8
SUBLANES = 8
TILE = 16
SPARE = 4
VMEM_LIMIT = 24 * 1024 * 1024
BF16 = jnp.bfloat16
F32 = jnp.float32


def pack_kernel(cap, cols, dest_hbm, foot_hbm, weights_hbm, obs_hbm, send_ref, dest_ref, foot_ref, weights_ref, obs_ref, sems):
    copies = [
        pltpu.make_async_copy(source, target, sems.at[k])
        for k, (source, target) in enumerate(
            (
                (dest_hbm, dest_ref),
                (obs_hbm, obs_ref),
                (foot_hbm, foot_ref),
                (weights_hbm, weights_ref),
            )
        )
    ]
    for copy in copies:
        copy.start()
    devices = send_ref.shape[0]
    obs_rows = obs_ref.shape[0]
    per = LANES // cap
    upper = lax.broadcasted_iota(jnp.int32, (LANES, LANES), 0) <= lax.broadcasted_iota(
        jnp.int32, (LANES, LANES), 1
    )
    upper = jnp.where(upper, 1.0, 0.0).astype(BF16)
    ids = lax.broadcasted_iota(jnp.int32, (devices, obs_rows), 0)
    copies[0].wait()
    member = jnp.where(ids == dest_ref[...], 1.0, 0.0)
    seen = jnp.zeros((devices, 1), F32)
    ranks = []
    for first in range(0, obs_rows, LANES):
        part = member[:, first : first + LANES]
        count = jnp.dot(part.astype(BF16), upper, preferred_element_type=F32) + seen
        ranks.append(jnp.sum((count - 1.0) * part, axis=0, keepdims=True))
        seen = count[:, LANES - 1 :]
    rank = jnp.concatenate(ranks, axis=1).astype(jnp.int32)
    slot = lax.broadcasted_iota(jnp.int32, (cap, obs_rows), 0)
    ranked = jnp.where(slot == rank, 1.0, 0.0).astype(BF16).reshape(cap // TILE, TILE, obs_rows)
    for copy in copies[1:]:
        copy.wait()
    start = foot_ref[0:1, :]
    meta = jnp.concatenate(
        [
            lax.div(start, cols).astype(F32),
            lax.rem(start, cols).astype(F32),
            weights_ref[...].astype(F32),
            jnp.zeros((META - 2 - weights_ref.shape[0], obs_rows), F32),
        ],
        axis=0,
    ).astype(BF16)
    obs = obs_ref[...]
    lane = lax.broadcasted_iota(jnp.int32, (META, LANES), 1)
    count = min(512, devices * cap) // cap
    for first in range(0, devices, count):
        parts = []
        for d in range(first, first + count):
            mine = jnp.broadcast_to(member[d : d + 1], (TILE, obs_rows)).astype(BF16)
            parts.append((ranked * mine[None]).reshape(cap, obs_rows))
        chosen = jnp.concatenate(parts, axis=0)
        feats = jnp.dot(chosen, obs, preferred_element_type=F32).astype(BF16)
        placed = lax.dot_general(
            meta, chosen, (((1,), (1,)), ((), ())), preferred_element_type=F32
        )
        for half in range(feats.shape[1] // LANES):
            piece = feats[:, half * LANES : (half + 1) * LANES].reshape(count, cap, LANES)
            send_ref[first : first + count, half * cap : (half + 1) * cap, :] = piece
        base = send_ref.shape[1] - META
        for chunk in range(count // per):
            values = placed[:, chunk * LANES : (chunk + 1) * LANES]
            turned = [values] + [pltpu.roll(values, k * cap, 1) for k in range(1, per)]
            for own in range(per):
                wide = turned[0]
                for group in range(per):
                    wide = jnp.where(lane // cap == group, turned[(group - own) % per], wide)
                send_ref[first + chunk * per + own, base:, :] = wide.astype(BF16)


def assim_kernel(cap, step, got_ref, proj_ref, back_ref, state_ref, lat_ref, lon_ref, corner_ref):
    devices, depth, _ = got_ref.shape
    rows, cols, chans = back_ref.shape
    cells = rows * cols
    feats = proj_ref.shape[0]
    per = LANES // cap
    halves = feats // LANES
    lane = lax.broadcasted_iota(jnp.int32, (META, LANES), 1)
    cell = lax.broadcasted_iota(jnp.int32, (cells, LANES), 0)
    total = jnp.zeros((cells, feats), F32)
    for pair in range(0, devices // per, 2):
        maps = []
        blocks = []
        for chunk in (pair, pair + 1):
            meta = got_ref[chunk * per, depth - META :, :].astype(F32)
            for group in range(1, per):
                other = got_ref[chunk * per + group, depth - META :, :].astype(F32)
                meta = jnp.where(lane // cap == group, other, meta)
            start = (meta[0:1] * cols + meta[1:2]).astype(jnp.int32)
            away = cell - start
            away = jnp.where(away < 0, away + cells, away)
            amount = jnp.zeros((cells, LANES), F32)
            for entry in range(4):
                amount = jnp.where(away == entry * step, meta[2 + entry : 3 + entry], amount)
            maps.append(amount.astype(BF16))
            block = got_ref[chunk * per : (chunk + 1) * per]
            blocks.append(
                jnp.concatenate(
                    [
                        block[:, half * cap : (half + 1) * cap, :].reshape(LANES, LANES)
                        for half in range(halves)
                    ],
                    axis=1,
                )
            )
        total = total + jnp.dot(
            jnp.concatenate(maps, axis=1),
            jnp.concatenate(blocks, axis=0),
            preferred_element_type=F32,
        )
    assim = jnp.dot(total.astype(BF16), proj_ref[...], preferred_element_type=F32)
    state = back_ref[...].astype(F32) + assim.reshape(rows, cols, chans)
    state = state.astype(BF16)
    state_ref[...] = state
    lat_ref[...] = state[rows - SHIFT :]
    lon_ref[...] = state[:, cols - EDGE :, :]
    corner_ref[...] = state[rows - SHIFT :, cols - EDGE :, :]


def gelu(x):
    inner = x * (0.7978845608028654 + 0.035677408136300125 * (x * x))
    half = 0.5 * x
    return half + half * jnp.tanh(inner)


def layer_kernel(
    shrink,
    own_ref,
    lat_in,
    lon_in,
    corner_in,
    taps_ref,
    mix_ref,
    state_ref,
    lat_ref,
    lon_ref,
    corner_ref,
    wide_ref,
    taps_in,
    spread_ref,
    out_ref,
):
    chans = mix_ref.shape[0]
    groups = chans // LANES
    cols = own_ref.shape[1]
    phases = cols // SUBLANES
    place = lax.axis_index("lat")
    last = place == lax.axis_size("lat") - 1
    first = place == 0
    rows = state_ref.shape[0] if shrink else own_ref.shape[0]

    def put(row, start, value):
        for g in range(groups):
            wide_ref[g, row, start : start + value.shape[0], :] = value[
                :, g * LANES : (g + 1) * LANES
            ]

    if shrink:
        base = 0

        @pl.loop(0, rows, unroll=2)
        def _(y):
            put(y, 0, own_ref[y].astype(F32))
            put(y, cols, lon_in[y].astype(F32))

        for k in range(SHIFT):
            main = lat_in[k].astype(F32)
            side = corner_in[k].astype(F32)
            if k < HALO:
                main = jnp.where(last, own_ref[rows + k].astype(F32), main)
                side = jnp.where(last, lon_in[rows + k].astype(F32), side)
            else:
                main = jnp.where(last, 0.0, main)
                side = jnp.where(last, 0.0, side)
            put(rows + k, 0, main)
            put(rows + k, cols, side)
    else:
        base = EDGE - SHIFT

        @pl.loop(0, SHIFT, unroll=2)
        def _(y):
            put(y, 0, jnp.where(first, 0.0, corner_in[y].astype(F32)))
            put(y, EDGE, jnp.where(first, 0.0, lat_in[y].astype(F32)))

        @pl.loop(0, rows, unroll=2)
        def _(y):
            put(y + SHIFT, 0, lon_in[y].astype(F32))
            put(y + SHIFT, EDGE, own_ref[y].astype(F32))

    ones = jnp.ones((chans, LANES), BF16)

    def stage(top, high):
        @pl.loop(0, high + TAPS - 1, unroll=2)
        def _(y):
            for g in range(groups):
                for r in range(phases + TAPS - 1):
                    both = [
                        wide_ref[g, top + y + h, pl.ds(base + r, SUBLANES, stride=phases), :]
                        for h in (0, high)
                    ]
                    taps_in[g, r, y] = jnp.concatenate(both, axis=0).astype(BF16)

        def depthwise(p):
            for g in range(groups):
                total = None
                for b in range(TAPS):
                    seen = taps_in[g, p + b, 0 : high + TAPS - 1]
                    part = None
                    for a in range(TAPS):
                        term = seen[a : a + high] * taps_ref[g, a * TAPS + b]
                        part = term if part is None else part + term
                    part = part.astype(F32)
                    total = part if total is None else total + part
                spread_ref[p % 2, 0:high, :, g * LANES : (g + 1) * LANES] = total.astype(BF16)

        def finish(p):
            spread = spread_ref[p % 2, 0:high].reshape(high * TILE, chans)
            power = jnp.dot(spread * spread, ones, preferred_element_type=F32)
            scale = lax.rsqrt(power * (1.0 / chans) + 1e-05)
            mixed = jnp.dot(spread, mix_ref[...], preferred_element_type=F32)
            for g in range(groups):
                moved = gelu(mixed[:, g * LANES : (g + 1) * LANES] * scale)
                moved = moved.reshape(high, TILE, LANES)
                center = taps_in[g, p + HALO, HALO : HALO + high].astype(F32)
                fresh = center + moved
                for k in range(high):
                    for h in range(2):
                        out_ref[g, top + h * high + k, pl.ds(p, SUBLANES, stride=phases), :] = (
                            fresh[k, h * SUBLANES : (h + 1) * SUBLANES]
                        )

        depthwise(0)

        @pl.loop(1, phases)
        def _(p):
            finish(p - 1)
            depthwise(p)

        finish(phases - 1)

    stage(0, rows // 2)

    def row_of(y):
        return jnp.concatenate([out_ref[g, y] for g in range(groups)], axis=1)

    if shrink:
        edge = slice(cols - EDGE, cols)

        @pl.loop(0, rows, unroll=2)
        def _(y):
            value = row_of(y)
            state_ref[y] = value.astype(BF16)
            lon_ref[y] = value[edge].astype(BF16)

        for k in range(SHIFT):
            value = row_of(rows - SHIFT + k)
            lat_ref[k] = value.astype(BF16)
            corner_ref[k] = value[edge].astype(BF16)
    else:

        @pl.when(last)
        def _():
            wide_ref[:, rows + SHIFT :] = jnp.zeros(
                (groups, SPARE, wide_ref.shape[2], LANES), F32
            )
            stage(rows, SPARE // 2)

        def masked(y):
            return jnp.where(jnp.logical_and(first, y < HALO), 0.0, row_of(y))

        @pl.loop(0, rows, unroll=2)
        def _(y):
            value = masked(y)
            state_ref[y] = value.astype(BF16)
            lon_ref[y] = value[:EDGE].astype(BF16)

        for k in range(HALO):
            value = row_of(rows + k)
            state_ref[rows + k] = value.astype(BF16)
            lon_ref[rows + k] = value[:EDGE].astype(BF16)

        for k in range(SHIFT):
            value = masked(k)
            lat_ref[k] = value.astype(BF16)
            corner_ref[k] = value[:EDGE].astype(BF16)


def edges(rows, cols, chans):
    return (
        jax.ShapeDtypeStruct((rows, cols, chans), BF16),
        jax.ShapeDtypeStruct((SHIFT, cols, chans), BF16),
        jax.ShapeDtypeStruct((rows, EDGE, chans), BF16),
        jax.ShapeDtypeStruct((SHIFT, EDGE, chans), BF16),
    )


def call(kernel, out_shape, inputs, scratch=(), space=pltpu.VMEM):
    whole = pl.BlockSpec(memory_space=pltpu.VMEM)
    single = isinstance(out_shape, jax.ShapeDtypeStruct)
    return pl.pallas_call(
        kernel,
        out_shape=out_shape,
        in_specs=[pl.BlockSpec(memory_space=space)] * len(inputs),
        out_specs=whole if single else [whole] * len(out_shape),
        scratch_shapes=list(scratch),
        compiler_params=pltpu.CompilerParams(vmem_limit_bytes=VMEM_LIMIT),
    )(*inputs)


def layer(state, halo, taps, mix, shrink):
    extended, cols, chans = state.shape
    rows = extended - HALO if shrink else extended
    groups = chans // LANES
    phases = cols // SUBLANES
    height = rows if shrink else rows + HALO
    spare = 0 if shrink else SPARE
    scratch = (
        pltpu.VMEM((groups, rows + SHIFT + spare, cols + EDGE, LANES), F32),
        pltpu.VMEM((groups, phases + TAPS - 1, rows // 2 + TAPS - 1, TILE, LANES), BF16),
        pltpu.VMEM((2, rows // 2, TILE, chans), BF16),
        pltpu.VMEM((groups, rows + spare, cols, LANES), F32),
    )
    return call(
        functools.partial(layer_kernel, shrink),
        edges(height, cols, chans),
        (state, *halo, taps, mix),
        scratch,
    )


def exchange(pieces, forward):
    lat, lon, corner = pieces
    count_lat = lax.axis_size("lat")
    count_lon = lax.axis_size("lon")
    along = [(i, (i + 1) % count_lat) for i in range(count_lat)]
    around = [(j, (j + 1) % count_lon) for j in range(count_lon)]
    across = [
        (i * count_lon + j, ni * count_lon + nj) for i, ni in along for j, nj in around
    ]
    if not forward:
        along, around, across = ([(t, s) for s, t in p] for p in (along, around, across))
    return (
        lax.ppermute(lat, "lat", along),
        lax.ppermute(lon, "lon", around),
        lax.ppermute(corner, ("lat", "lon"), across),
    )


def body(
    background, observations, destination, footprint, weights, obs_proj, depth_w, point_w, gains
):
    rows, cols, chans = background.shape
    devices = lax.axis_size("lat") * lax.axis_size("lon")
    obs_rows, feats = observations.shape
    cap = 2 * obs_rows // devices
    depth = cap * (feats // LANES) + META
    foot_count = footprint.shape[1]
    send = call(
        functools.partial(pack_kernel, cap, cols),
        jax.ShapeDtypeStruct((devices, depth, LANES), BF16),
        (destination.T, footprint.T, weights.T, observations),
        (
            pltpu.VMEM((1, obs_rows), jnp.int32),
            pltpu.VMEM((foot_count, obs_rows), jnp.int32),
            pltpu.VMEM((foot_count, obs_rows), BF16),
            pltpu.VMEM((obs_rows, feats), BF16),
            pltpu.SemaphoreType.DMA((4,)),
        ),
        pltpu.HBM,
    )
    got = lax.all_to_all(send, ("lat", "lon"), split_axis=0, concat_axis=0, tiled=True)
    layers = depth_w.shape[0]
    groups = chans // LANES
    taps = depth_w.astype(BF16).reshape(layers, TAPS * TAPS, groups, LANES).transpose(0, 2, 1, 3)
    taps = [
        jnp.broadcast_to(taps[n][:, :, None], (groups, TAPS * TAPS, TILE, LANES))
        for n in range(layers)
    ]
    mix = [(gains[n][:, None] * point_w[n].astype(F32)).astype(BF16) for n in range(layers)]
    got, taps, mix = lax.optimization_barrier((got, taps, mix))
    state, *pieces = call(
        functools.partial(assim_kernel, cap, cols + 1),
        edges(rows, cols, chans),
        (got, obs_proj, background),
    )
    for n in range(layers):
        shrink = n % 2 == 1
        halo = exchange(pieces, not shrink)
        state, *pieces = layer(state, halo, taps[n], mix[n], shrink)
    return state


def solution(mesh):
    placed = (
        P("lat", "lon", None),
        P(("lat", "lon"), None),
        P(("lat", "lon"), None),
        P(("lat", "lon"), None),
        P(("lat", "lon"), None),
        P(),
        P(),
        P(),
        P(),
    )
    return jax.shard_map(
        body, mesh=mesh, in_specs=placed, out_specs=P("lat", "lon", None), check_vma=False
    )
```

```python
import functools

import jax
import jax.numpy as jnp
from jax import lax
from jax.experimental import pallas as pl
from jax.experimental.pallas import tpu as pltpu
from jax.sharding import PartitionSpec as P

LANES = 128
META = 8
TAPS = 7
HALO = 3
SHIFT = 2 * HALO
EDGE = 8
TILE = 16
VMEM_LIMIT = 24 * 1024 * 1024
PACK_LIMIT = 58 * 1024 * 1024
BF16 = jnp.bfloat16
F32 = jnp.float32


def pack_kernel(cap, cols, dest_hbm, foot_hbm, weights_hbm, obs_hbm, send_ref, dest_ref, foot_ref, weights_ref, obs_ref, sems):
    copies = [
        pltpu.make_async_copy(source, target, sems.at[k])
        for k, (source, target) in enumerate(
            (
                (dest_hbm, dest_ref),
                (obs_hbm, obs_ref),
                (foot_hbm, foot_ref),
                (weights_hbm, weights_ref),
            )
        )
    ]
    for copy in copies:
        copy.start()
    devices = send_ref.shape[0]
    obs_rows = obs_ref.shape[0]
    per = LANES // cap
    upper = lax.broadcasted_iota(jnp.int32, (LANES, LANES), 0) <= lax.broadcasted_iota(
        jnp.int32, (LANES, LANES), 1
    )
    upper = jnp.where(upper, 1.0, 0.0).astype(BF16)
    ids = lax.broadcasted_iota(jnp.int32, (devices, obs_rows), 0)
    copies[0].wait()
    member = jnp.where(ids == dest_ref[...], 1.0, 0.0)
    seen = jnp.zeros((devices, 1), F32)
    ranks = []
    for first in range(0, obs_rows, LANES):
        part = member[:, first : first + LANES]
        count = jnp.dot(part.astype(BF16), upper, preferred_element_type=F32) + seen
        ranks.append(jnp.sum((count - 1.0) * part, axis=0, keepdims=True))
        seen = count[:, LANES - 1 :]
    rank = jnp.concatenate(ranks, axis=1).astype(jnp.int32)
    slot = lax.broadcasted_iota(jnp.int32, (cap, obs_rows), 0)
    ranked = jnp.where(slot == rank, 1.0, 0.0).astype(BF16).reshape(cap // TILE, TILE, obs_rows)
    for copy in copies[1:]:
        copy.wait()
    start = foot_ref[0:1, :]
    meta = jnp.concatenate(
        [
            lax.div(start, cols).astype(F32),
            lax.rem(start, cols).astype(F32),
            weights_ref[...].astype(F32),
            jnp.zeros((META - 2 - weights_ref.shape[0], obs_rows), F32),
        ],
        axis=0,
    ).astype(BF16)
    obs = obs_ref[...]
    lane = lax.broadcasted_iota(jnp.int32, (META, LANES), 1)
    count = min(512, devices * cap) // cap
    for first in range(0, devices, count):
        parts = []
        for d in range(first, first + count):
            mine = jnp.broadcast_to(member[d : d + 1], (TILE, obs_rows)).astype(BF16)
            parts.append((ranked * mine[None]).reshape(cap, obs_rows))
        chosen = jnp.concatenate(parts, axis=0)
        feats = jnp.dot(chosen, obs, preferred_element_type=F32).astype(BF16)
        placed = lax.dot_general(
            meta, chosen, (((1,), (1,)), ((), ())), preferred_element_type=F32
        )
        for half in range(feats.shape[1] // LANES):
            piece = feats[:, half * LANES : (half + 1) * LANES].reshape(count, cap, LANES)
            send_ref[first : first + count, half * cap : (half + 1) * cap, :] = piece
        base = send_ref.shape[1] - META
        for chunk in range(count // per):
            values = placed[:, chunk * LANES : (chunk + 1) * LANES]
            turned = [values] + [pltpu.roll(values, k * cap, 1) for k in range(1, per)]
            for own in range(per):
                wide = turned[0]
                for group in range(per):
                    wide = jnp.where(lane // cap == group, turned[(group - own) % per], wide)
                send_ref[first + chunk * per + own, base:, :] = wide.astype(BF16)


def assim_kernel(
    cap, step, got_ref, proj_ref, back_ref, edge_ref, inner_ref, lon_ref, corner_ref
):
    devices, depth, _ = got_ref.shape
    rows, cols, chans = back_ref.shape
    cells = rows * cols
    feats = proj_ref.shape[0]
    per = LANES // cap
    halves = feats // LANES
    lane = lax.broadcasted_iota(jnp.int32, (META, LANES), 1)
    cell = lax.broadcasted_iota(jnp.int32, (cells, LANES), 0)
    total = jnp.zeros((cells, feats), F32)
    for pair in range(0, devices // per, 2):
        maps = []
        blocks = []
        for chunk in (pair, pair + 1):
            meta = got_ref[chunk * per, depth - META :, :].astype(F32)
            for group in range(1, per):
                other = got_ref[chunk * per + group, depth - META :, :].astype(F32)
                meta = jnp.where(lane // cap == group, other, meta)
            start = (meta[0:1] * cols + meta[1:2]).astype(jnp.int32)
            away = cell - start
            away = jnp.where(away < 0, away + cells, away)
            amount = jnp.zeros((cells, LANES), F32)
            for entry in range(4):
                amount = jnp.where(away == entry * step, meta[2 + entry : 3 + entry], amount)
            maps.append(amount.astype(BF16))
            block = got_ref[chunk * per : (chunk + 1) * per]
            blocks.append(
                jnp.concatenate(
                    [
                        block[:, half * cap : (half + 1) * cap, :].reshape(LANES, LANES)
                        for half in range(halves)
                    ],
                    axis=1,
                )
            )
        total = total + jnp.dot(
            jnp.concatenate(maps, axis=1),
            jnp.concatenate(blocks, axis=0),
            preferred_element_type=F32,
        )
    assim = jnp.dot(total.astype(BF16), proj_ref[...], preferred_element_type=F32)
    state = back_ref[...].astype(F32) + assim.reshape(rows, cols, chans)
    state = state.astype(BF16)
    edge_ref[...] = state[rows - SHIFT :]
    inner_ref[...] = state[: rows - SHIFT]
    lon_ref[...] = state[:, cols - EDGE :, :]
    corner_ref[...] = state[rows - SHIFT :, cols - EDGE :, :]


def gelu(x):
    inner = x * (0.7978845608028654 + 0.035677408136300125 * (x * x))
    half = 0.5 * x
    return half + half * jnp.tanh(inner)


def taps_kernel(source_ref, *target_refs):
    @pl.loop(0, source_ref.shape[0])
    def _(k):
        rows = source_ref[k]
        for n, target in enumerate(target_refs):
            for g in range(target.shape[0]):
                row = rows[n : n + 1, g * LANES : (g + 1) * LANES]
                target[g, k] = jnp.broadcast_to(row, (TILE, LANES)).astype(BF16)


def put(wide_ref, row, start, value):
    for g in range(wide_ref.shape[0]):
        wide_ref[g, row, start : start + value.shape[0], :] = value[:, g * LANES : (g + 1) * LANES]


def shifted(wide_ref, taps_in, base, row, target):
    for g in range(wide_ref.shape[0]):
        for r in range(TAPS + 1):
            columns = pl.ds(base + r, TILE, stride=2)
            taps_in[g, r, target] = wide_ref[g, row, columns, :].astype(BF16)


def convolve(taps_in, taps_ref, spread_ref, g, first, count):
    for p in range(2):
        total = None
        for b in range(TAPS):
            seen = taps_in[g, p + b, first : first + count + TAPS - 1]
            part = None
            for a in range(TAPS):
                term = seen[a : a + count] * taps_ref[g, a * TAPS + b]
                part = term if part is None else part + term
            part = part.astype(F32)
            total = part if total is None else total + part
        lanes = pl.ds(pl.multiple_of(g * LANES, LANES), LANES)
        spread_ref[p, first : first + count, :, lanes] = total.astype(BF16)


def finish(taps_in, spread_ref, mix_ref, out_ref, first, count):
    chans = mix_ref.shape[0]
    ones = jnp.ones((chans, LANES), BF16)
    for p in range(2):
        spread = spread_ref[p, first : first + count].reshape(count * TILE, chans)
        power = jnp.dot(spread * spread, ones, preferred_element_type=F32)
        scale = lax.rsqrt(power * (1.0 / chans) + 1e-05)
        mixed = jnp.dot(spread, mix_ref[...], preferred_element_type=F32)
        for g in range(chans // LANES):
            moved = gelu(mixed[:, g * LANES : (g + 1) * LANES] * scale)
            center = taps_in[g, p + HALO, first + HALO : first + HALO + count].astype(F32)
            fresh = center + moved.reshape(count, TILE, LANES)
            for k in range(count):
                out_ref[g, first + k, pl.ds(p, TILE, stride=2), :] = fresh[k]


def row_of(out_ref, y):
    return jnp.concatenate([out_ref[g, y] for g in range(out_ref.shape[0])], axis=1)


def at_last():
    return lax.axis_index("lat") == lax.axis_size("lat") - 1


def inner_kernel(
    shrink,
    edge_in,
    inner_in,
    lon_in,
    taps_ref,
    mix_ref,
    inner_ref,
    lon_ref,
    near_ref,
    wide_ref,
    taps_in,
    spread_ref,
    out_ref,
):
    cols = edge_in.shape[1]
    groups = wide_ref.shape[0]
    own = inner_in.shape[0] - (HALO if shrink else 0)
    rows = own + SHIFT
    count = rows - SHIFT
    side = cols if shrink else 0
    main = 0 if shrink else EDGE
    base = 0 if shrink else EDGE - SHIFT

    def load(ref, place, y):
        put(wide_ref, place, main, ref[y].astype(F32))
        put(wide_ref, place, side, lon_in[place].astype(F32))
        shifted(wide_ref, taps_in, base, place, place)

    @pl.loop(0, SHIFT, unroll=2)
    def _(y):
        load(edge_in, y if shrink else own + y, y)

    @pl.loop(0, own, unroll=2)
    def _(y):
        load(inner_in, y + SHIFT if shrink else y, y)

    near = rows - SHIFT if shrink else 0
    near_ref[...] = taps_in[:, :, near : near + SHIFT]

    @pl.loop(0, groups)
    def _(g):
        convolve(taps_in, taps_ref, spread_ref, g, 0, count)

    finish(taps_in, spread_ref, mix_ref, out_ref, 0, count)
    edge = slice(cols - EDGE, cols) if shrink else slice(0, EDGE)

    @pl.loop(0, count, unroll=2)
    def _(y):
        value = row_of(out_ref, y)
        inner_ref[y] = value.astype(BF16)
        lon_ref[y] = value[edge].astype(BF16)

    if not shrink:

        @pl.when(at_last())
        def _():
            taps_in[:, :, rows:] = jnp.zeros((groups, TAPS + 1, HALO, TILE, LANES), BF16)

            @pl.loop(0, groups)
            def _(g):
                convolve(taps_in, taps_ref, spread_ref, g, count, HALO)

            finish(taps_in, spread_ref, mix_ref, out_ref, count, HALO)

        for k in range(HALO):
            value = row_of(out_ref, count + k)
            inner_ref[count + k] = value.astype(BF16)
            lon_ref[count + k] = value[edge].astype(BF16)


def edge_kernel(
    shrink,
    final,
    inner_in,
    lon_in,
    lat_in,
    corner_in,
    near_ref,
    inner_new,
    lon_new,
    taps_ref,
    mix_ref,
    *refs,
):
    if final:
        state_ref, wide_ref, taps_in, spread_ref, out_ref = refs
    else:
        edge_ref, lon_ref, corner_ref, wide_ref, taps_in, spread_ref, out_ref = refs
    cols = lat_in.shape[1]
    groups = wide_ref.shape[0]
    side = cols if shrink else 0
    main = 0 if shrink else EDGE
    base = 0 if shrink else EDGE - SHIFT
    last = at_last()
    top = lax.axis_index("lat") == 0
    own = SHIFT if not shrink else 0
    for k in range(SHIFT):
        value, beside = lat_in[k].astype(F32), corner_in[k].astype(F32)
        if not shrink:
            value, beside = jnp.where(top, 0.0, value), jnp.where(top, 0.0, beside)
        elif k < HALO:
            rows = lon_in.shape[0] - HALO
            kept = inner_in.shape[0] - HALO
            value = jnp.where(last, inner_in[kept + k].astype(F32), value)
            beside = jnp.where(last, lon_in[rows + k].astype(F32), beside)
        else:
            value, beside = jnp.where(last, 0.0, value), jnp.where(last, 0.0, beside)
        put(wide_ref, k, main, value)
        put(wide_ref, k, side, beside)
        shifted(wide_ref, taps_in, base, k, k if not shrink else k + SHIFT)
    taps_in[:, :, own : own + SHIFT] = near_ref[...]

    @pl.loop(0, groups)
    def _(g):
        convolve(taps_in, taps_ref, spread_ref, g, 0, SHIFT)

    finish(taps_in, spread_ref, mix_ref, out_ref, 0, SHIFT)
    kept = inner_new.shape[0]
    for k in range(SHIFT):
        value = row_of(out_ref, k)
        if final:
            state_ref[kept + k] = value.astype(BF16)
            continue
        if not shrink and k < HALO:
            value = jnp.where(top, 0.0, value)
        value = value.astype(F32)
        edge = value[cols - EDGE :] if shrink else value[:EDGE]
        edge_ref[k] = value.astype(BF16)
        corner_ref[k] = edge.astype(BF16)
        lon_ref[kept + k if shrink else k] = edge.astype(BF16)
    if final:
        state_ref[0:kept] = inner_new[...]
    elif shrink:
        lon_ref[0:kept] = lon_new[...]
    else:
        lon_ref[SHIFT : SHIFT + kept] = lon_new[...]


def call(kernel, out_shape, inputs, scratch=(), limit=VMEM_LIMIT, space=pltpu.VMEM):
    whole = pl.BlockSpec(memory_space=pltpu.VMEM)
    single = isinstance(out_shape, jax.ShapeDtypeStruct)
    return pl.pallas_call(
        kernel,
        out_shape=out_shape,
        in_specs=[pl.BlockSpec(memory_space=space)] * len(inputs),
        out_specs=whole if single else [whole] * len(out_shape),
        scratch_shapes=list(scratch),
        compiler_params=pltpu.CompilerParams(vmem_limit_bytes=limit),
    )(*inputs)


def held(*shape):
    return jax.ShapeDtypeStruct(shape, BF16)


def scratch_of(groups, seen, made, cols, chans):
    return (
        pltpu.VMEM((groups, seen, cols + EDGE, LANES), F32),
        pltpu.VMEM((groups, TAPS + 1, seen, TILE, LANES), BF16),
        pltpu.VMEM((2, made, TILE, chans), BF16),
        pltpu.VMEM((groups, made, cols, LANES), F32),
    )


def layer(state, lon_out, corner_out, taps, mix, shrink, final):
    edge, inner = state
    lat_in, lon_in, corner_in = exchange((edge, lon_out, corner_out), not shrink)
    cols, chans = edge.shape[1:]
    groups = chans // LANES
    rows = inner.shape[0] + SHIFT - (HALO if shrink else 0)
    spare = 0 if shrink else HALO
    made = rows - SHIFT + spare
    inner_new, lon_new, near = call(
        functools.partial(inner_kernel, shrink),
        (
            held(made, cols, chans),
            held(made, EDGE, chans),
            held(groups, TAPS + 1, SHIFT, TILE, LANES),
        ),
        (edge, inner, lon_in, taps, mix),
        scratch_of(groups, rows + spare, made, cols, chans),
    )
    if final:
        outs = held(made + SHIFT, cols, chans)
    else:
        outs = (
            held(SHIFT, cols, chans),
            held(made + SHIFT, EDGE, chans),
            held(SHIFT, EDGE, chans),
        )
    outs = call(
        functools.partial(edge_kernel, shrink, final),
        outs,
        (inner, lon_in, lat_in, corner_in, near, inner_new, lon_new, taps, mix),
        scratch_of(groups, 2 * SHIFT, SHIFT, cols, chans),
    )
    if final:
        return outs
    edge, lon_out, corner_out = outs
    return (edge, inner_new), lon_out, corner_out


def exchange(pieces, forward):
    lat, lon, corner = pieces
    count_lat = lax.axis_size("lat")
    count_lon = lax.axis_size("lon")
    along = [(i, (i + 1) % count_lat) for i in range(count_lat)]
    around = [(j, (j + 1) % count_lon) for j in range(count_lon)]
    across = [
        (i * count_lon + j, ni * count_lon + nj) for i, ni in along for j, nj in around
    ]
    if not forward:
        along, around, across = ([(t, s) for s, t in p] for p in (along, around, across))
    return (
        lax.ppermute(lat, "lat", along),
        lax.ppermute(lon, "lon", around),
        lax.ppermute(corner, ("lat", "lon"), across),
    )


def body(
    background, observations, destination, footprint, weights, obs_proj, depth_w, point_w, gains
):
    rows, cols, chans = background.shape
    devices = lax.axis_size("lat") * lax.axis_size("lon")
    obs_rows, feats = observations.shape
    cap = 2 * obs_rows // devices
    depth = cap * (feats // LANES) + META
    foot_count = footprint.shape[1]
    send = call(
        functools.partial(pack_kernel, cap, cols),
        jax.ShapeDtypeStruct((devices, depth, LANES), BF16),
        (destination.T, footprint.T, weights.T, observations),
        (
            pltpu.VMEM((1, obs_rows), jnp.int32),
            pltpu.VMEM((foot_count, obs_rows), jnp.int32),
            pltpu.VMEM((foot_count, obs_rows), BF16),
            pltpu.VMEM((obs_rows, feats), BF16),
            pltpu.SemaphoreType.DMA((4,)),
        ),
        PACK_LIMIT,
        pltpu.HBM,
    )
    got = lax.all_to_all(send, ("lat", "lon"), split_axis=0, concat_axis=0, tiled=True)
    layers = depth_w.shape[0]
    groups = chans // LANES
    taps = call(
        taps_kernel,
        [held(groups, TAPS * TAPS, TILE, LANES)] * layers,
        (depth_w.transpose(1, 2, 0, 3).reshape(TAPS * TAPS, layers, chans),),
    )
    mix = [(gains[n][:, None] * point_w[n].astype(F32)).astype(BF16) for n in range(layers)]
    got, taps, mix = lax.optimization_barrier((got, taps, mix))
    edge, inner, lon_out, corner_out = call(
        functools.partial(assim_kernel, cap, cols + 1),
        (
            held(SHIFT, cols, chans),
            held(rows - SHIFT, cols, chans),
            held(rows, EDGE, chans),
            held(SHIFT, EDGE, chans),
        ),
        (got, obs_proj, background),
    )
    state = (edge, inner)
    for n in range(layers - 1):
        state, lon_out, corner_out = layer(
            state, lon_out, corner_out, taps[n], mix[n], n % 2 == 1, False
        )
    n = layers - 1
    return layer(state, lon_out, corner_out, taps[n], mix[n], n % 2 == 1, True)


def solution(mesh):
    placed = (
        P("lat", "lon", None),
        P(("lat", "lon"), None),
        P(("lat", "lon"), None),
        P(("lat", "lon"), None),
        P(("lat", "lon"), None),
        P(),
        P(),
        P(),
        P(),
    )
    return jax.shard_map(
        body, mesh=mesh, in_specs=placed, out_specs=P("lat", "lon", None), check_vma=False
    )
```

```python
import functools

import jax
import jax.numpy as jnp
from jax import lax
from jax.experimental import pallas as pl
from jax.experimental.pallas import tpu as pltpu
from jax.sharding import PartitionSpec as P

LANES = 128
META = 8
TAPS = 7
HALO = 3
SHIFT = 2 * HALO
EDGE = 8
TILE = 16
WORK = 40000
VMEM_LIMIT = 24 * 1024 * 1024
PACK_LIMIT = 58 * 1024 * 1024
BF16 = jnp.bfloat16
F32 = jnp.float32


def pack_kernel(cap, cols, dest_hbm, foot_hbm, weights_hbm, obs_hbm, send_ref, dest_ref, foot_ref, weights_ref, obs_ref, sems):
    copies = [
        pltpu.make_async_copy(source, target, sems.at[k])
        for k, (source, target) in enumerate(
            (
                (dest_hbm, dest_ref),
                (obs_hbm, obs_ref),
                (foot_hbm, foot_ref),
                (weights_hbm, weights_ref),
            )
        )
    ]
    for copy in copies:
        copy.start()
    devices = send_ref.shape[0]
    obs_rows = obs_ref.shape[0]
    per = LANES // cap
    upper = lax.broadcasted_iota(jnp.int32, (LANES, LANES), 0) <= lax.broadcasted_iota(
        jnp.int32, (LANES, LANES), 1
    )
    upper = jnp.where(upper, 1.0, 0.0).astype(BF16)
    ids = lax.broadcasted_iota(jnp.int32, (devices, obs_rows), 0)
    copies[0].wait()
    member = jnp.where(ids == dest_ref[...], 1.0, 0.0)
    seen = jnp.zeros((devices, 1), F32)
    ranks = []
    for first in range(0, obs_rows, LANES):
        part = member[:, first : first + LANES]
        count = jnp.dot(part.astype(BF16), upper, preferred_element_type=F32) + seen
        ranks.append(jnp.sum((count - 1.0) * part, axis=0, keepdims=True))
        seen = count[:, LANES - 1 :]
    rank = jnp.concatenate(ranks, axis=1).astype(jnp.int32)
    slot = lax.broadcasted_iota(jnp.int32, (cap, obs_rows), 0)
    ranked = jnp.where(slot == rank, 1.0, 0.0).astype(BF16).reshape(cap // TILE, TILE, obs_rows)
    for copy in copies[1:]:
        copy.wait()
    start = foot_ref[0:1, :]
    meta = jnp.concatenate(
        [
            lax.div(start, cols).astype(F32),
            lax.rem(start, cols).astype(F32),
            weights_ref[...].astype(F32),
            jnp.zeros((META - 2 - weights_ref.shape[0], obs_rows), F32),
        ],
        axis=0,
    ).astype(BF16)
    obs = obs_ref[...]
    lane = lax.broadcasted_iota(jnp.int32, (META, LANES), 1)
    count = min(512, devices * cap) // cap
    for first in range(0, devices, count):
        parts = []
        for d in range(first, first + count):
            mine = jnp.broadcast_to(member[d : d + 1], (TILE, obs_rows)).astype(BF16)
            parts.append((ranked * mine[None]).reshape(cap, obs_rows))
        chosen = jnp.concatenate(parts, axis=0)
        feats = jnp.dot(chosen, obs, preferred_element_type=F32).astype(BF16)
        placed = lax.dot_general(
            meta, chosen, (((1,), (1,)), ((), ())), preferred_element_type=F32
        )
        for half in range(feats.shape[1] // LANES):
            piece = feats[:, half * LANES : (half + 1) * LANES].reshape(count, cap, LANES)
            send_ref[first : first + count, half * cap : (half + 1) * cap, :] = piece
        base = send_ref.shape[1] - META
        for chunk in range(count // per):
            values = placed[:, chunk * LANES : (chunk + 1) * LANES]
            turned = [values] + [pltpu.roll(values, k * cap, 1) for k in range(1, per)]
            for own in range(per):
                wide = turned[0]
                for group in range(per):
                    wide = jnp.where(lane // cap == group, turned[(group - own) % per], wide)
                send_ref[first + chunk * per + own, base:, :] = wide.astype(BF16)


def assim_kernel(
    cap,
    step,
    got_ref,
    proj_hbm,
    back_hbm,
    edge_ref,
    inner_ref,
    lon_ref,
    corner_ref,
    proj_ref,
    back_ref,
    sems,
):
    copies = (
        pltpu.make_async_copy(proj_hbm, proj_ref, sems.at[0]),
        pltpu.make_async_copy(back_hbm, back_ref, sems.at[1]),
    )
    for copy in copies:
        copy.start()
    devices, depth, _ = got_ref.shape
    rows, cols, chans = back_ref.shape
    cells = rows * cols
    feats = proj_ref.shape[0]
    per = LANES // cap
    halves = feats // LANES
    lane = lax.broadcasted_iota(jnp.int32, (META, LANES), 1)
    cell = lax.broadcasted_iota(jnp.int32, (cells, LANES), 0)
    total = jnp.zeros((cells, feats), F32)
    for pair in range(0, devices // per, 2):
        maps = []
        blocks = []
        for chunk in (pair, pair + 1):
            meta = got_ref[chunk * per, depth - META :, :].astype(F32)
            for group in range(1, per):
                other = got_ref[chunk * per + group, depth - META :, :].astype(F32)
                meta = jnp.where(lane // cap == group, other, meta)
            start = (meta[0:1] * cols + meta[1:2]).astype(jnp.int32)
            away = cell - start
            away = jnp.where(away < 0, away + cells, away)
            amount = jnp.zeros((cells, LANES), F32)
            for entry in range(4):
                amount = jnp.where(away == entry * step, meta[2 + entry : 3 + entry], amount)
            maps.append(amount.astype(BF16))
            block = got_ref[chunk * per : (chunk + 1) * per]
            blocks.append(
                jnp.concatenate(
                    [
                        block[:, half * cap : (half + 1) * cap, :].reshape(LANES, LANES)
                        for half in range(halves)
                    ],
                    axis=1,
                )
            )
        total = total + jnp.dot(
            jnp.concatenate(maps, axis=1),
            jnp.concatenate(blocks, axis=0),
            preferred_element_type=F32,
        )
    for copy in copies:
        copy.wait()
    assim = jnp.dot(total.astype(BF16), proj_ref[...], preferred_element_type=F32)
    state = back_ref[...].astype(F32) + assim.reshape(rows, cols, chans)
    state = state.astype(BF16)
    edge_ref[...] = state[rows - SHIFT :]
    inner_ref[...] = state[: rows - SHIFT]
    lon_ref[...] = state[:, cols - EDGE :, :]
    corner_ref[...] = state[rows - SHIFT :, cols - EDGE :, :]


def gelu(x):
    inner = x * (0.7978845608028654 + 0.035677408136300125 * (x * x))
    half = 0.5 * x
    return half + half * jnp.tanh(inner)


def taps_kernel(source_ref, *target_refs):
    @pl.loop(0, source_ref.shape[0])
    def _(k):
        rows = source_ref[k]
        for n, target in enumerate(target_refs):
            for g in range(target.shape[0]):
                row = rows[n : n + 1, g * LANES : (g + 1) * LANES]
                target[g, k] = jnp.broadcast_to(row, (TILE, LANES)).astype(BF16)


def put(wide_ref, row, start, value):
    for g in range(wide_ref.shape[0]):
        wide_ref[g, row, start : start + value.shape[0], :] = value[:, g * LANES : (g + 1) * LANES]


def shifted(wide_ref, taps_in, base, row, target):
    for g in range(wide_ref.shape[0]):
        for r in range(TAPS + 1):
            columns = pl.ds(base + r, TILE, stride=2)
            taps_in[g, r, target] = wide_ref[g, row, columns, :].astype(BF16)


def convolve(taps_in, taps_ref, spread_ref, g, first, count):
    for p in range(2):
        total = None
        for b in range(TAPS):
            seen = taps_in[g, p + b, first : first + count + TAPS - 1]
            part = None
            for a in range(TAPS):
                term = seen[a : a + count] * taps_ref[g, a * TAPS + b]
                part = term if part is None else part + term
            part = part.astype(F32)
            total = part if total is None else total + part
        lanes = pl.ds(pl.multiple_of(g * LANES, LANES), LANES)
        spread_ref[p, first : first + count, :, lanes] = total.astype(BF16)


def finish(taps_in, spread_ref, mix_ref, out_ref, first, count):
    chans = mix_ref.shape[0]
    ones = jnp.ones((chans, LANES), BF16)
    for p in range(2):
        spread = spread_ref[p, first : first + count].reshape(count * TILE, chans)
        power = jnp.dot(spread * spread, ones, preferred_element_type=F32)
        scale = lax.rsqrt(power * (1.0 / chans) + 1e-05)
        mixed = jnp.dot(spread, mix_ref[...], preferred_element_type=F32)
        for g in range(chans // LANES):
            moved = gelu(mixed[:, g * LANES : (g + 1) * LANES] * scale)
            center = taps_in[g, p + HALO, first + HALO : first + HALO + count].astype(F32)
            fresh = center + moved.reshape(count, TILE, LANES)
            for k in range(count):
                out_ref[g, first + k, pl.ds(p, TILE, stride=2), :] = fresh[k]


def row_of(out_ref, y):
    return jnp.concatenate([out_ref[g, y] for g in range(out_ref.shape[0])], axis=1)


def at_last():
    return lax.axis_index("lat") == lax.axis_size("lat") - 1


def inner_kernel(
    shrink,
    edge_in,
    inner_in,
    lon_in,
    taps_ref,
    mix_ref,
    inner_ref,
    lon_ref,
    near_ref,
    wide_ref,
    taps_in,
    spread_ref,
    out_ref,
):
    cols = edge_in.shape[1]
    groups = wide_ref.shape[0]
    own = inner_in.shape[0] - (HALO if shrink else 0)
    rows = own + SHIFT
    count = rows - SHIFT
    side = cols if shrink else 0
    main = 0 if shrink else EDGE
    base = 0 if shrink else EDGE - SHIFT

    def load(ref, place, y):
        put(wide_ref, place, main, ref[y].astype(F32))
        put(wide_ref, place, side, lon_in[place].astype(F32))
        shifted(wide_ref, taps_in, base, place, place)

    @pl.loop(0, SHIFT, unroll=2)
    def _(y):
        load(edge_in, y if shrink else own + y, y)

    @pl.loop(0, own, unroll=2)
    def _(y):
        load(inner_in, y + SHIFT if shrink else y, y)

    near = rows - SHIFT if shrink else 0
    near_ref[...] = taps_in[:, :, near : near + SHIFT]

    @pl.loop(0, groups)
    def _(g):
        convolve(taps_in, taps_ref, spread_ref, g, 0, count)

    finish(taps_in, spread_ref, mix_ref, out_ref, 0, count)
    edge = slice(cols - EDGE, cols) if shrink else slice(0, EDGE)

    @pl.loop(0, count, unroll=2)
    def _(y):
        value = row_of(out_ref, y)
        inner_ref[y] = value.astype(BF16)
        lon_ref[y] = value[edge].astype(BF16)

    if not shrink:

        @pl.when(at_last())
        def _():
            taps_in[:, :, rows:] = jnp.zeros((groups, TAPS + 1, HALO, TILE, LANES), BF16)

            @pl.loop(0, groups)
            def _(g):
                convolve(taps_in, taps_ref, spread_ref, g, count, HALO)

            finish(taps_in, spread_ref, mix_ref, out_ref, count, HALO)

        for k in range(HALO):
            value = row_of(out_ref, count + k)
            inner_ref[count + k] = value.astype(BF16)
            lon_ref[count + k] = value[edge].astype(BF16)


def edge_kernel(
    shrink,
    final,
    inner_in,
    lon_in,
    lat_in,
    corner_in,
    near_ref,
    inner_new,
    lon_new,
    taps_ref,
    mix_ref,
    *refs,
):
    if final:
        state_ref, wide_ref, taps_in, spread_ref, out_ref = refs
    else:
        edge_ref, lon_ref, corner_ref, wide_ref, taps_in, spread_ref, out_ref = refs
    cols = lat_in.shape[1]
    groups = wide_ref.shape[0]
    side = cols if shrink else 0
    main = 0 if shrink else EDGE
    base = 0 if shrink else EDGE - SHIFT
    last = at_last()
    top = lax.axis_index("lat") == 0
    own = SHIFT if not shrink else 0
    for k in range(SHIFT):
        value, beside = lat_in[k].astype(F32), corner_in[k].astype(F32)
        if not shrink:
            value, beside = jnp.where(top, 0.0, value), jnp.where(top, 0.0, beside)
        elif k < HALO:
            rows = lon_in.shape[0] - HALO
            kept = inner_in.shape[0] - HALO
            value = jnp.where(last, inner_in[kept + k].astype(F32), value)
            beside = jnp.where(last, lon_in[rows + k].astype(F32), beside)
        else:
            value, beside = jnp.where(last, 0.0, value), jnp.where(last, 0.0, beside)
        put(wide_ref, k, main, value)
        put(wide_ref, k, side, beside)
        shifted(wide_ref, taps_in, base, k, k if not shrink else k + SHIFT)
    taps_in[:, :, own : own + SHIFT] = near_ref[...]

    @pl.loop(0, groups)
    def _(g):
        convolve(taps_in, taps_ref, spread_ref, g, 0, SHIFT)

    finish(taps_in, spread_ref, mix_ref, out_ref, 0, SHIFT)
    kept = inner_new.shape[0]
    for k in range(SHIFT):
        value = row_of(out_ref, k)
        if final:
            state_ref[kept + k] = value.astype(BF16)
            continue
        if not shrink and k < HALO:
            value = jnp.where(top, 0.0, value)
        value = value.astype(F32)
        edge = value[cols - EDGE :] if shrink else value[:EDGE]
        edge_ref[k] = value.astype(BF16)
        corner_ref[k] = edge.astype(BF16)
        lon_ref[kept + k if shrink else k] = edge.astype(BF16)
    if final:
        state_ref[0:kept] = inner_new[...]
    elif shrink:
        lon_ref[0:kept] = lon_new[...]
    else:
        lon_ref[SHIFT : SHIFT + kept] = lon_new[...]


def call(kernel, out_shape, inputs, scratch=(), limit=VMEM_LIMIT, space=None, work=0):
    whole = pl.BlockSpec(memory_space=pltpu.VMEM)
    single = isinstance(out_shape, jax.ShapeDtypeStruct)
    spaces = space or (pltpu.VMEM,) * len(inputs)
    return pl.pallas_call(
        kernel,
        out_shape=out_shape,
        in_specs=[pl.BlockSpec(memory_space=s) for s in spaces],
        out_specs=whole if single else [whole] * len(out_shape),
        scratch_shapes=list(scratch),
        compiler_params=pltpu.CompilerParams(vmem_limit_bytes=limit),
        cost_estimate=pl.CostEstimate(flops=work, bytes_accessed=0, transcendentals=0),
    )(*inputs)


def held(*shape):
    return jax.ShapeDtypeStruct(shape, BF16)


def scratch_of(groups, seen, made, cols, chans):
    return (
        pltpu.VMEM((groups, seen, cols + EDGE, LANES), F32),
        pltpu.VMEM((groups, TAPS + 1, seen, TILE, LANES), BF16),
        pltpu.VMEM((2, made, TILE, chans), BF16),
        pltpu.VMEM((groups, made, cols, LANES), F32),
    )


def layer(state, lon_out, corner_out, taps, mix, shrink, final):
    edge, inner = state
    lat_in, lon_in, corner_in = exchange((edge, lon_out, corner_out), not shrink)
    cols, chans = edge.shape[1:]
    groups = chans // LANES
    rows = inner.shape[0] + SHIFT - (HALO if shrink else 0)
    spare = 0 if shrink else HALO
    made = rows - SHIFT + spare
    inner_new, lon_new, near = call(
        functools.partial(inner_kernel, shrink),
        (
            held(made, cols, chans),
            held(made, EDGE, chans),
            held(groups, TAPS + 1, SHIFT, TILE, LANES),
        ),
        (edge, inner, lon_in, taps, mix),
        scratch_of(groups, rows + spare, made, cols, chans),
        work=made * cols * chans * WORK,
    )
    if final:
        outs = held(made + SHIFT, cols, chans)
    else:
        outs = (
            held(SHIFT, cols, chans),
            held(made + SHIFT, EDGE, chans),
            held(SHIFT, EDGE, chans),
        )
    outs = call(
        functools.partial(edge_kernel, shrink, final),
        outs,
        (inner, lon_in, lat_in, corner_in, near, inner_new, lon_new, taps, mix),
        scratch_of(groups, 2 * SHIFT, SHIFT, cols, chans),
        work=SHIFT * cols * chans * WORK,
    )
    if final:
        return outs
    edge, lon_out, corner_out = outs
    return (edge, inner_new), lon_out, corner_out


def exchange(pieces, forward):
    lat, lon, corner = pieces
    count_lat = lax.axis_size("lat")
    count_lon = lax.axis_size("lon")
    along = [(i, (i + 1) % count_lat) for i in range(count_lat)]
    around = [(j, (j + 1) % count_lon) for j in range(count_lon)]
    across = [
        (i * count_lon + j, ni * count_lon + nj) for i, ni in along for j, nj in around
    ]
    if not forward:
        along, around, across = ([(t, s) for s, t in p] for p in (along, around, across))
    lon = lax.ppermute(lon, "lon", around)
    lat = lax.ppermute(lat, "lat", along)
    corner = lax.ppermute(corner, ("lat", "lon"), across)
    return lat, lon, corner


def body(
    background, observations, destination, footprint, weights, obs_proj, depth_w, point_w, gains
):
    rows, cols, chans = background.shape
    devices = lax.axis_size("lat") * lax.axis_size("lon")
    obs_rows, feats = observations.shape
    cap = 2 * obs_rows // devices
    depth = cap * (feats // LANES) + META
    foot_count = footprint.shape[1]
    send = call(
        functools.partial(pack_kernel, cap, cols),
        jax.ShapeDtypeStruct((devices, depth, LANES), BF16),
        (destination.T, footprint.T, weights.T, observations),
        (
            pltpu.VMEM((1, obs_rows), jnp.int32),
            pltpu.VMEM((foot_count, obs_rows), jnp.int32),
            pltpu.VMEM((foot_count, obs_rows), BF16),
            pltpu.VMEM((obs_rows, feats), BF16),
            pltpu.SemaphoreType.DMA((4,)),
        ),
        PACK_LIMIT,
        (pltpu.HBM,) * 4,
    )
    got = lax.all_to_all(send, ("lat", "lon"), split_axis=0, concat_axis=0, tiled=True)
    layers = depth_w.shape[0]
    groups = chans // LANES
    taps = call(
        taps_kernel,
        [held(groups, TAPS * TAPS, TILE, LANES)] * layers,
        (depth_w.transpose(1, 2, 0, 3).reshape(TAPS * TAPS, layers, chans),),
    )
    mix = [(gains[n][:, None] * point_w[n].astype(F32)).astype(BF16) for n in range(layers)]
    got, taps, mix = lax.optimization_barrier((got, taps, mix))
    edge, inner, lon_out, corner_out = call(
        functools.partial(assim_kernel, cap, cols + 1),
        (
            held(SHIFT, cols, chans),
            held(rows - SHIFT, cols, chans),
            held(rows, EDGE, chans),
            held(SHIFT, EDGE, chans),
        ),
        (got, obs_proj, background),
        (
            pltpu.VMEM(obs_proj.shape, BF16),
            pltpu.VMEM(background.shape, BF16),
            pltpu.SemaphoreType.DMA((2,)),
        ),
        space=(pltpu.VMEM, pltpu.HBM, pltpu.HBM),
    )
    state = (edge, inner)
    for n in range(layers - 1):
        state, lon_out, corner_out = layer(
            state, lon_out, corner_out, taps[n], mix[n], n % 2 == 1, False
        )
    n = layers - 1
    return layer(state, lon_out, corner_out, taps[n], mix[n], n % 2 == 1, True)


def solution(mesh):
    placed = (
        P("lat", "lon", None),
        P(("lat", "lon"), None),
        P(("lat", "lon"), None),
        P(("lat", "lon"), None),
        P(("lat", "lon"), None),
        P(),
        P(),
        P(),
        P(),
    )
    return jax.shard_map(
        body, mesh=mesh, in_specs=placed, out_specs=P("lat", "lon", None), check_vma=False
    )
```

```python
import functools

import jax
import jax.numpy as jnp
from jax import lax
from jax.experimental import pallas as pl
from jax.experimental.pallas import tpu as pltpu
from jax.sharding import PartitionSpec as P

LANES = 128
META = 8
TAPS = 7
SPLIT = 3
HALO = 3
SHIFT = 2 * HALO
EDGE = 8
TILE = 16
WORK = 40000
VMEM_LIMIT = 24 * 1024 * 1024
PACK_LIMIT = 58 * 1024 * 1024
BF16 = jnp.bfloat16
F32 = jnp.float32


def pack_kernel(cap, cols, dest_hbm, foot_hbm, weights_hbm, obs_hbm, send_ref, dest_ref, foot_ref, weights_ref, obs_ref, sems):
    copies = [
        pltpu.make_async_copy(source, target, sems.at[k])
        for k, (source, target) in enumerate(
            (
                (dest_hbm, dest_ref),
                (obs_hbm, obs_ref),
                (foot_hbm, foot_ref),
                (weights_hbm, weights_ref),
            )
        )
    ]
    for copy in copies:
        copy.start()
    devices = send_ref.shape[0]
    obs_rows = obs_ref.shape[0]
    per = LANES // cap
    upper = lax.broadcasted_iota(jnp.int32, (LANES, LANES), 0) <= lax.broadcasted_iota(
        jnp.int32, (LANES, LANES), 1
    )
    upper = jnp.where(upper, 1.0, 0.0).astype(BF16)
    ids = lax.broadcasted_iota(jnp.int32, (devices, obs_rows), 0)
    copies[0].wait()
    member = jnp.where(ids == dest_ref[...], 1.0, 0.0)
    seen = jnp.zeros((devices, 1), F32)
    ranks = []
    for first in range(0, obs_rows, LANES):
        part = member[:, first : first + LANES]
        count = jnp.dot(part.astype(BF16), upper, preferred_element_type=F32) + seen
        ranks.append(jnp.sum((count - 1.0) * part, axis=0, keepdims=True))
        seen = count[:, LANES - 1 :]
    rank = jnp.concatenate(ranks, axis=1).astype(jnp.int32)
    slot = lax.broadcasted_iota(jnp.int32, (cap, obs_rows), 0)
    ranked = jnp.where(slot == rank, 1.0, 0.0).astype(BF16).reshape(cap // TILE, TILE, obs_rows)
    for copy in copies[1:]:
        copy.wait()
    start = foot_ref[0:1, :]
    meta = jnp.concatenate(
        [
            lax.div(start, cols).astype(F32),
            lax.rem(start, cols).astype(F32),
            weights_ref[...].astype(F32),
            jnp.zeros((META - 2 - weights_ref.shape[0], obs_rows), F32),
        ],
        axis=0,
    ).astype(BF16)
    obs = obs_ref[...]
    lane = lax.broadcasted_iota(jnp.int32, (META, LANES), 1)
    count = min(512, devices * cap) // cap
    for first in range(0, devices, count):
        parts = []
        for d in range(first, first + count):
            mine = jnp.broadcast_to(member[d : d + 1], (TILE, obs_rows)).astype(BF16)
            parts.append((ranked * mine[None]).reshape(cap, obs_rows))
        chosen = jnp.concatenate(parts, axis=0)
        feats = jnp.dot(chosen, obs, preferred_element_type=F32).astype(BF16)
        placed = lax.dot_general(
            meta, chosen, (((1,), (1,)), ((), ())), preferred_element_type=F32
        )
        for half in range(feats.shape[1] // LANES):
            piece = feats[:, half * LANES : (half + 1) * LANES].reshape(count, cap, LANES)
            send_ref[first : first + count, half * cap : (half + 1) * cap, :] = piece
        base = send_ref.shape[1] - META
        for chunk in range(count // per):
            values = placed[:, chunk * LANES : (chunk + 1) * LANES]
            turned = [values] + [pltpu.roll(values, k * cap, 1) for k in range(1, per)]
            for own in range(per):
                wide = turned[0]
                for group in range(per):
                    wide = jnp.where(lane // cap == group, turned[(group - own) % per], wide)
                send_ref[first + chunk * per + own, base:, :] = wide.astype(BF16)


def assim_kernel(
    cap,
    step,
    got_ref,
    proj_hbm,
    back_hbm,
    edge_ref,
    inner_ref,
    lon_ref,
    corner_ref,
    proj_ref,
    back_ref,
    sems,
):
    copies = (
        pltpu.make_async_copy(proj_hbm, proj_ref, sems.at[0]),
        pltpu.make_async_copy(back_hbm, back_ref, sems.at[1]),
    )
    for copy in copies:
        copy.start()
    devices, depth, _ = got_ref.shape
    rows, cols, chans = back_ref.shape
    cells = rows * cols
    feats = proj_ref.shape[0]
    per = LANES // cap
    halves = feats // LANES
    lane = lax.broadcasted_iota(jnp.int32, (META, LANES), 1)
    cell = lax.broadcasted_iota(jnp.int32, (cells, LANES), 0)
    total = jnp.zeros((cells, feats), F32)
    for pair in range(0, devices // per, 2):
        maps = []
        blocks = []
        for chunk in (pair, pair + 1):
            meta = got_ref[chunk * per, depth - META :, :].astype(F32)
            for group in range(1, per):
                other = got_ref[chunk * per + group, depth - META :, :].astype(F32)
                meta = jnp.where(lane // cap == group, other, meta)
            start = (meta[0:1] * cols + meta[1:2]).astype(jnp.int32)
            away = cell - start
            away = jnp.where(away < 0, away + cells, away)
            amount = jnp.zeros((cells, LANES), F32)
            for entry in range(4):
                amount = jnp.where(away == entry * step, meta[2 + entry : 3 + entry], amount)
            maps.append(amount.astype(BF16))
            block = got_ref[chunk * per : (chunk + 1) * per]
            blocks.append(
                jnp.concatenate(
                    [
                        block[:, half * cap : (half + 1) * cap, :].reshape(LANES, LANES)
                        for half in range(halves)
                    ],
                    axis=1,
                )
            )
        total = total + jnp.dot(
            jnp.concatenate(maps, axis=1),
            jnp.concatenate(blocks, axis=0),
            preferred_element_type=F32,
        )
    for copy in copies:
        copy.wait()
    assim = jnp.dot(total.astype(BF16), proj_ref[...], preferred_element_type=F32)
    state = back_ref[...].astype(F32) + assim.reshape(rows, cols, chans)
    state = state.astype(BF16)
    edge_ref[...] = state[rows - SHIFT :]
    inner_ref[...] = state[: rows - SHIFT]
    lon_ref[...] = state[:, cols - EDGE :, :]
    corner_ref[...] = state[rows - SHIFT :, cols - EDGE :, :]


def gelu(x):
    inner = x * (0.7978845608028654 + 0.035677408136300125 * (x * x))
    half = 0.5 * x
    return half + half * jnp.tanh(inner)


def put(wide_ref, row, start, value):
    for g in range(wide_ref.shape[0]):
        wide_ref[g, row, start : start + value.shape[0], :] = value[:, g * LANES : (g + 1) * LANES]


def shifted(wide_ref, taps_in, base, row, target):
    for g in range(wide_ref.shape[0]):
        for r in range(TAPS + 1):
            columns = pl.ds(base + r, TILE, stride=2)
            taps_in[g, r, target] = wide_ref[g, row, columns, :].astype(BF16)


def convolve(taps_in, taps_ref, tap_ref, spread_ref, layer, g, first, count):
    lanes = pl.ds(pl.multiple_of(g * LANES, LANES), LANES)
    for k in range(TAPS * TAPS):
        row = taps_ref[k, layer : layer + 1, lanes]
        tap_ref[k] = jnp.broadcast_to(row, (TILE, LANES)).astype(BF16)
    diagonal = lax.broadcasted_iota(jnp.int32, (LANES, LANES), 0) == lax.broadcasted_iota(
        jnp.int32, (LANES, LANES), 1
    )
    diagonal = jnp.where(diagonal, 1.0, 0.0).astype(BF16).reshape(LANES // TILE, TILE, LANES)
    nothing = jnp.zeros((LANES, LANES), BF16)
    total = None
    for a in range(SPLIT, TAPS):
        blocks = [
            (diagonal * tap_ref[a * TAPS + b][None]).reshape(LANES, LANES) for b in range(TAPS)
        ]
        blocks = [nothing] + blocks + [nothing]
        weights = jnp.concatenate(
            [jnp.concatenate([blocks[r + 1], blocks[r]], axis=1) for r in range(TAPS + 1)], axis=0
        )
        rows = [
            taps_in[g, r, first + a : first + a + count].reshape(count * TILE, LANES)
            for r in range(TAPS + 1)
        ]
        part = jnp.dot(jnp.concatenate(rows, axis=1), weights, preferred_element_type=F32)
        total = part if total is None else total + part
    for p in range(2):
        light = None
        for a in range(SPLIT):
            part = None
            for b in range(TAPS):
                term = taps_in[g, p + b, first + a : first + a + count] * tap_ref[a * TAPS + b]
                part = term if part is None else part + term
            light = part if light is None else light + part
        both = total[:, p * LANES : (p + 1) * LANES].reshape(count, TILE, LANES)
        if light is not None:
            both = both + light.astype(F32)
        spread_ref[p, first : first + count, :, lanes] = both.astype(BF16)


def finish(taps_in, spread_ref, mix_ref, out_ref, layer, first, count):
    chans = mix_ref.shape[1]
    ones = jnp.ones((chans, LANES), BF16)
    for p in range(2):
        spread = spread_ref[p, first : first + count].reshape(count * TILE, chans)
        power = jnp.dot(spread * spread, ones, preferred_element_type=F32)
        scale = lax.rsqrt(power * (1.0 / chans) + 1e-05)
        mixed = jnp.dot(spread, mix_ref[layer], preferred_element_type=F32)
        for g in range(chans // LANES):
            moved = gelu(mixed[:, g * LANES : (g + 1) * LANES] * scale)
            center = taps_in[g, p + HALO, first + HALO : first + HALO + count].astype(F32)
            fresh = center + moved.reshape(count, TILE, LANES)
            for k in range(count):
                out_ref[g, first + k, pl.ds(p, TILE, stride=2), :] = fresh[k]


def row_of(out_ref, y):
    return jnp.concatenate([out_ref[g, y] for g in range(out_ref.shape[0])], axis=1)


def at_last():
    return lax.axis_index("lat") == lax.axis_size("lat") - 1


def inner_kernel(
    shrink,
    layer,
    edge_in,
    inner_in,
    lon_in,
    taps_ref,
    mix_ref,
    inner_ref,
    lon_ref,
    near_ref,
    wide_ref,
    taps_in,
    tap_ref,
    spread_ref,
    out_ref,
):
    cols = edge_in.shape[1]
    groups = wide_ref.shape[0]
    own = inner_in.shape[0] - (HALO if shrink else 0)
    rows = own + SHIFT
    count = rows - SHIFT
    side = cols if shrink else 0
    main = 0 if shrink else EDGE
    base = 0 if shrink else EDGE - SHIFT

    def load(ref, place, y):
        put(wide_ref, place, main, ref[y].astype(F32))
        put(wide_ref, place, side, lon_in[place].astype(F32))
        shifted(wide_ref, taps_in, base, place, place)

    @pl.loop(0, SHIFT, unroll=2)
    def _(y):
        load(edge_in, y if shrink else own + y, y)

    @pl.loop(0, own, unroll=2)
    def _(y):
        load(inner_in, y + SHIFT if shrink else y, y)

    near = rows - SHIFT if shrink else 0
    near_ref[...] = taps_in[:, :, near : near + SHIFT]

    @pl.loop(0, groups)
    def _(g):
        convolve(taps_in, taps_ref, tap_ref, spread_ref, layer, g, 0, count)

    finish(taps_in, spread_ref, mix_ref, out_ref, layer, 0, count)
    edge = slice(cols - EDGE, cols) if shrink else slice(0, EDGE)

    @pl.loop(0, count, unroll=2)
    def _(y):
        value = row_of(out_ref, y)
        inner_ref[y] = value.astype(BF16)
        lon_ref[y] = value[edge].astype(BF16)

    if not shrink:

        @pl.when(at_last())
        def _():
            taps_in[:, :, rows:] = jnp.zeros((groups, TAPS + 1, HALO, TILE, LANES), BF16)

            @pl.loop(0, groups)
            def _(g):
                convolve(taps_in, taps_ref, tap_ref, spread_ref, layer, g, count, HALO)

            finish(taps_in, spread_ref, mix_ref, out_ref, layer, count, HALO)

        for k in range(HALO):
            value = row_of(out_ref, count + k)
            inner_ref[count + k] = value.astype(BF16)
            lon_ref[count + k] = value[edge].astype(BF16)


def edge_kernel(
    shrink,
    final,
    layer,
    inner_in,
    lon_in,
    lat_in,
    corner_in,
    near_ref,
    inner_new,
    lon_new,
    taps_ref,
    mix_ref,
    *refs,
):
    if final:
        state_ref, wide_ref, taps_in, tap_ref, spread_ref, out_ref = refs
    else:
        edge_ref, lon_ref, corner_ref, wide_ref, taps_in, tap_ref, spread_ref, out_ref = refs
    cols = lat_in.shape[1]
    groups = wide_ref.shape[0]
    side = cols if shrink else 0
    main = 0 if shrink else EDGE
    base = 0 if shrink else EDGE - SHIFT
    last = at_last()
    top = lax.axis_index("lat") == 0
    own = SHIFT if not shrink else 0
    for k in range(SHIFT):
        value, beside = lat_in[k].astype(F32), corner_in[k].astype(F32)
        if not shrink:
            value, beside = jnp.where(top, 0.0, value), jnp.where(top, 0.0, beside)
        elif k < HALO:
            rows = lon_in.shape[0] - HALO
            kept = inner_in.shape[0] - HALO
            value = jnp.where(last, inner_in[kept + k].astype(F32), value)
            beside = jnp.where(last, lon_in[rows + k].astype(F32), beside)
        else:
            value, beside = jnp.where(last, 0.0, value), jnp.where(last, 0.0, beside)
        put(wide_ref, k, main, value)
        put(wide_ref, k, side, beside)
        shifted(wide_ref, taps_in, base, k, k if not shrink else k + SHIFT)
    taps_in[:, :, own : own + SHIFT] = near_ref[...]

    @pl.loop(0, groups)
    def _(g):
        convolve(taps_in, taps_ref, tap_ref, spread_ref, layer, g, 0, SHIFT)

    finish(taps_in, spread_ref, mix_ref, out_ref, layer, 0, SHIFT)
    kept = inner_new.shape[0]
    for k in range(SHIFT):
        value = row_of(out_ref, k)
        if final:
            state_ref[kept + k] = value.astype(BF16)
            continue
        if not shrink and k < HALO:
            value = jnp.where(top, 0.0, value)
        value = value.astype(F32)
        edge = value[cols - EDGE :] if shrink else value[:EDGE]
        edge_ref[k] = value.astype(BF16)
        corner_ref[k] = edge.astype(BF16)
        lon_ref[kept + k if shrink else k] = edge.astype(BF16)
    if final:
        state_ref[0:kept] = inner_new[...]
    elif shrink:
        lon_ref[0:kept] = lon_new[...]
    else:
        lon_ref[SHIFT : SHIFT + kept] = lon_new[...]


def call(kernel, out_shape, inputs, scratch=(), limit=VMEM_LIMIT, space=None, work=0):
    whole = pl.BlockSpec(memory_space=pltpu.VMEM)
    single = isinstance(out_shape, jax.ShapeDtypeStruct)
    spaces = space or (pltpu.VMEM,) * len(inputs)
    return pl.pallas_call(
        kernel,
        out_shape=out_shape,
        in_specs=[pl.BlockSpec(memory_space=s) for s in spaces],
        out_specs=whole if single else [whole] * len(out_shape),
        scratch_shapes=list(scratch),
        compiler_params=pltpu.CompilerParams(vmem_limit_bytes=limit),
        cost_estimate=pl.CostEstimate(flops=work, bytes_accessed=0, transcendentals=0),
    )(*inputs)


def held(*shape):
    return jax.ShapeDtypeStruct(shape, BF16)


def scratch_of(groups, seen, made, cols, chans):
    return (
        pltpu.VMEM((groups, seen, cols + EDGE, LANES), F32),
        pltpu.VMEM((groups, TAPS + 1, seen, TILE, LANES), BF16),
        pltpu.VMEM((TAPS * TAPS, TILE, LANES), BF16),
        pltpu.VMEM((2, made, TILE, chans), BF16),
        pltpu.VMEM((groups, made, cols, LANES), F32),
    )


def layer(state, lon_out, corner_out, taps, mix, number, shrink, final):
    edge, inner = state
    lat_in, lon_in, corner_in = exchange((edge, lon_out, corner_out), not shrink)
    cols, chans = edge.shape[1:]
    groups = chans // LANES
    rows = inner.shape[0] + SHIFT - (HALO if shrink else 0)
    spare = 0 if shrink else HALO
    made = rows - SHIFT + spare
    inner_new, lon_new, near = call(
        functools.partial(inner_kernel, shrink, number),
        (
            held(made, cols, chans),
            held(made, EDGE, chans),
            held(groups, TAPS + 1, SHIFT, TILE, LANES),
        ),
        (edge, inner, lon_in, taps, mix),
        scratch_of(groups, rows + spare, made, cols, chans),
        work=made * cols * chans * WORK,
    )
    if final:
        outs = held(made + SHIFT, cols, chans)
    else:
        outs = (
            held(SHIFT, cols, chans),
            held(made + SHIFT, EDGE, chans),
            held(SHIFT, EDGE, chans),
        )
    outs = call(
        functools.partial(edge_kernel, shrink, final, number),
        outs,
        (inner, lon_in, lat_in, corner_in, near, inner_new, lon_new, taps, mix),
        scratch_of(groups, 2 * SHIFT, SHIFT, cols, chans),
        work=SHIFT * cols * chans * WORK,
    )
    if final:
        return outs
    edge, lon_out, corner_out = outs
    return (edge, inner_new), lon_out, corner_out


def exchange(pieces, forward):
    lat, lon, corner = pieces
    count_lat = lax.axis_size("lat")
    count_lon = lax.axis_size("lon")
    along = [(i, (i + 1) % count_lat) for i in range(count_lat)]
    around = [(j, (j + 1) % count_lon) for j in range(count_lon)]
    across = [
        (i * count_lon + j, ni * count_lon + nj) for i, ni in along for j, nj in around
    ]
    if not forward:
        along, around, across = ([(t, s) for s, t in p] for p in (along, around, across))
    lon = lax.ppermute(lon, "lon", around)
    lat = lax.ppermute(lat, "lat", along)
    corner = lax.ppermute(corner, ("lat", "lon"), across)
    return lat, lon, corner


def body(
    background, observations, destination, footprint, weights, obs_proj, depth_w, point_w, gains
):
    rows, cols, chans = background.shape
    devices = lax.axis_size("lat") * lax.axis_size("lon")
    obs_rows, feats = observations.shape
    cap = 2 * obs_rows // devices
    depth = cap * (feats // LANES) + META
    foot_count = footprint.shape[1]
    send = call(
        functools.partial(pack_kernel, cap, cols),
        jax.ShapeDtypeStruct((devices, depth, LANES), BF16),
        (destination.T, footprint.T, weights.T, observations),
        (
            pltpu.VMEM((1, obs_rows), jnp.int32),
            pltpu.VMEM((foot_count, obs_rows), jnp.int32),
            pltpu.VMEM((foot_count, obs_rows), BF16),
            pltpu.VMEM((obs_rows, feats), BF16),
            pltpu.SemaphoreType.DMA((4,)),
        ),
        PACK_LIMIT,
        (pltpu.HBM,) * 4,
    )
    got = lax.all_to_all(send, ("lat", "lon"), split_axis=0, concat_axis=0, tiled=True)
    layers = depth_w.shape[0]
    taps = depth_w.transpose(1, 2, 0, 3).reshape(TAPS * TAPS, layers, chans)
    mix = (gains[:, :, None] * point_w.astype(F32)).astype(BF16)
    got, mix = lax.optimization_barrier((got, mix))
    edge, inner, lon_out, corner_out = call(
        functools.partial(assim_kernel, cap, cols + 1),
        (
            held(SHIFT, cols, chans),
            held(rows - SHIFT, cols, chans),
            held(rows, EDGE, chans),
            held(SHIFT, EDGE, chans),
        ),
        (got, obs_proj, background),
        (
            pltpu.VMEM(obs_proj.shape, BF16),
            pltpu.VMEM(background.shape, BF16),
            pltpu.SemaphoreType.DMA((2,)),
        ),
        space=(pltpu.VMEM, pltpu.HBM, pltpu.HBM),
    )
    state = (edge, inner)
    for n in range(layers - 1):
        state, lon_out, corner_out = layer(
            state, lon_out, corner_out, taps, mix, n, n % 2 == 1, False
        )
    n = layers - 1
    return layer(state, lon_out, corner_out, taps, mix, n, n % 2 == 1, True)


def solution(mesh):
    placed = (
        P("lat", "lon", None),
        P(("lat", "lon"), None),
        P(("lat", "lon"), None),
        P(("lat", "lon"), None),
        P(("lat", "lon"), None),
        P(),
        P(),
        P(),
        P(),
    )
    return jax.shard_map(
        body, mesh=mesh, in_specs=placed, out_specs=P("lat", "lon", None), check_vma=False
    )
```

```python
import functools

import jax
import jax.numpy as jnp
from jax import lax
from jax.experimental import pallas as pl
from jax.experimental.pallas import tpu as pltpu
from jax.sharding import PartitionSpec as P

LANES = 128
META = 8
TAPS = 7
HALO = 3
SHIFT = 2 * HALO
EDGE = 8
TILE = 16
MICROSECOND = 1150000000
WORK = 40000
VMEM_LIMIT = 24 * 1024 * 1024
PACK_LIMIT = 58 * 1024 * 1024
BF16 = jnp.bfloat16
F32 = jnp.float32


def place(cap, first, dest, rank, meta, obs, send_ref):
    members, depth, _ = send_ref.shape
    obs_rows = obs.shape[0]
    per = LANES // cap
    slot = lax.broadcasted_iota(jnp.int32, (cap, obs_rows), 0)
    ranked = jnp.where(slot == rank, 1.0, 0.0).astype(BF16).reshape(cap // TILE, TILE, obs_rows)
    lane = lax.broadcasted_iota(jnp.int32, (META, LANES), 1)
    count = min(512, members * cap) // cap
    for start in range(0, members, count):
        parts = []
        for d in range(start, start + count):
            mine = jnp.where(dest == first + d, 1.0, 0.0)
            mine = jnp.broadcast_to(mine, (TILE, obs_rows)).astype(BF16)
            parts.append((ranked * mine[None]).reshape(cap, obs_rows))
        chosen = jnp.concatenate(parts, axis=0)
        feats = jnp.dot(chosen, obs, preferred_element_type=F32).astype(BF16)
        placed = lax.dot_general(
            meta, chosen, (((1,), (1,)), ((), ())), preferred_element_type=F32
        )
        for half in range(feats.shape[1] // LANES):
            piece = feats[:, half * LANES : (half + 1) * LANES].reshape(count, cap, LANES)
            send_ref[start : start + count, half * cap : (half + 1) * cap, :] = piece
        for chunk in range(count // per):
            values = placed[:, chunk * LANES : (chunk + 1) * LANES]
            turned = [values] + [pltpu.roll(values, k * cap, 1) for k in range(1, per)]
            for own in range(per):
                wide = turned[0]
                for group in range(per):
                    wide = jnp.where(lane // cap == group, turned[(group - own) % per], wide)
                send_ref[start + chunk * per + own, depth - META :, :] = wide.astype(BF16)


def far_kernel(
    cap,
    cols,
    lon,
    dest_hbm,
    foot_hbm,
    weights_hbm,
    obs_hbm,
    send_ref,
    order_ref,
    meta_ref,
    dest_ref,
    foot_ref,
    weights_ref,
    obs_ref,
    sems,
):
    copies = [
        pltpu.make_async_copy(source, target, sems.at[k])
        for k, (source, target) in enumerate(
            (
                (dest_hbm, dest_ref),
                (obs_hbm, obs_ref),
                (foot_hbm, foot_ref),
                (weights_hbm, weights_ref),
            )
        )
    ]
    for copy in copies:
        copy.start()
    members = send_ref.shape[0]
    obs_rows = obs_ref.shape[0]
    half = lon // 2
    upper = lax.broadcasted_iota(jnp.int32, (LANES, LANES), 0) <= lax.broadcasted_iota(
        jnp.int32, (LANES, LANES), 1
    )
    upper = jnp.where(upper, 1.0, 0.0).astype(BF16)
    ids = lax.broadcasted_iota(jnp.int32, (2 * members, obs_rows), 0)
    skip = lax.div(lax.axis_index("lon"), half) * half
    copies[0].wait()
    target = dest_ref[...]
    across = lax.rem(target, lon) - skip
    across = jnp.where(across < 0, across + lon, across)
    dest = lax.div(target, lon) * half + across
    dest = jnp.where(across >= half, dest + (members - half), dest)
    member = jnp.where(ids == dest, 1.0, 0.0)
    seen = jnp.zeros((2 * members, 1), F32)
    ranks = []
    for first in range(0, obs_rows, LANES):
        part = member[:, first : first + LANES]
        count = jnp.dot(part.astype(BF16), upper, preferred_element_type=F32) + seen
        ranks.append(jnp.sum((count - 1.0) * part, axis=0, keepdims=True))
        seen = count[:, LANES - 1 :]
    rank = jnp.concatenate(ranks, axis=1).astype(jnp.int32)
    order_ref[0:1] = dest
    order_ref[1:2] = rank
    for copy in copies[1:]:
        copy.wait()
    start = foot_ref[0:1, :]
    meta = jnp.concatenate(
        [
            lax.div(start, cols).astype(F32),
            lax.rem(start, cols).astype(F32),
            weights_ref[...].astype(F32),
            jnp.zeros((META - 2 - weights_ref.shape[0], obs_rows), F32),
        ],
        axis=0,
    ).astype(BF16)
    meta_ref[...] = meta
    place(cap, members, dest, rank, meta, obs_ref[...], send_ref)


def near_kernel(cap, order_ref, meta_ref, obs_ref, send_ref):
    place(cap, 0, order_ref[0:1], order_ref[1:2], meta_ref[...], obs_ref[...], send_ref)


def gather_kernel(cap, cols, got_ref, field_ref):
    members, depth, _ = got_ref.shape
    cells, feats = field_ref.shape
    step = cols + 1
    per = LANES // cap
    halves = feats // LANES
    lane = lax.broadcasted_iota(jnp.int32, (META, LANES), 1)
    cell = lax.broadcasted_iota(jnp.int32, (cells, LANES), 0)
    total = jnp.zeros((cells, feats), F32)
    for pair in range(0, members // per, 2):
        maps = []
        blocks = []
        for chunk in (pair, pair + 1):
            meta = got_ref[chunk * per, depth - META :, :].astype(F32)
            for group in range(1, per):
                other = got_ref[chunk * per + group, depth - META :, :].astype(F32)
                meta = jnp.where(lane // cap == group, other, meta)
            start = (meta[0:1] * cols + meta[1:2]).astype(jnp.int32)
            away = cell - start
            away = jnp.where(away < 0, away + cells, away)
            amount = jnp.zeros((cells, LANES), F32)
            for entry in range(4):
                amount = jnp.where(away == entry * step, meta[2 + entry : 3 + entry], amount)
            maps.append(amount.astype(BF16))
            block = got_ref[chunk * per : (chunk + 1) * per]
            blocks.append(
                jnp.concatenate(
                    [
                        block[:, half * cap : (half + 1) * cap, :].reshape(LANES, LANES)
                        for half in range(halves)
                    ],
                    axis=1,
                )
            )
        total = total + jnp.dot(
            jnp.concatenate(maps, axis=1),
            jnp.concatenate(blocks, axis=0),
            preferred_element_type=F32,
        )
    field_ref[...] = total.astype(field_ref.dtype)


def state_kernel(near_ref, far_ref, proj_ref, back_ref, edge_ref, inner_ref, lon_ref, corner_ref):
    rows, cols, chans = back_ref.shape
    field = (near_ref[...] + far_ref[...].astype(F32)).astype(BF16)
    assim = jnp.dot(field, proj_ref[...], preferred_element_type=F32)
    state = back_ref[...].astype(F32) + assim.reshape(rows, cols, chans)
    state = state.astype(BF16)
    edge_ref[...] = state[rows - SHIFT :]
    inner_ref[...] = state[: rows - SHIFT]
    lon_ref[...] = state[:, cols - EDGE :, :]
    corner_ref[...] = state[rows - SHIFT :, cols - EDGE :, :]


def gelu(half):
    inner = half * (1.5957691216057308 + 0.285419265090401 * (half * half))
    return half + half * jnp.tanh(inner)


def put(wide_ref, row, start, value):
    for g in range(wide_ref.shape[0]):
        wide_ref[g, row, start : start + value.shape[0], :] = value[:, g * LANES : (g + 1) * LANES]


def shifted(wide_ref, taps_in, base, row, target):
    for g in range(wide_ref.shape[0]):
        for r in range(TAPS + 1):
            columns = pl.ds(base + r, TILE, stride=2)
            taps_in[g, r, target] = wide_ref[g, row, columns, :].astype(BF16)


def convolve(taps_in, taps_ref, tap_ref, spread_ref, layer, g, first, count):
    lanes = pl.ds(pl.multiple_of(g * LANES, LANES), LANES)
    for k in range(TAPS * TAPS):
        row = taps_ref[k, layer : layer + 1, lanes]
        tap_ref[k] = jnp.broadcast_to(row, (TILE, LANES)).astype(BF16)
    for p in range(2):
        total = None
        for b in range(TAPS):
            seen = taps_in[g, p + b, first : first + count + TAPS - 1]
            part = None
            for a in range(TAPS):
                term = seen[a : a + count] * tap_ref[a * TAPS + b]
                part = term if part is None else part + term
            total = part if total is None else total + part
        spread_ref[p, first : first + count, :, lanes] = total


def finish(taps_in, spread_ref, mix_ref, out_ref, layer, first, count):
    chans = mix_ref.shape[1]
    ones = jnp.ones((chans, LANES), BF16)
    for p in range(2):
        spread = spread_ref[p, first : first + count].reshape(count * TILE, chans)
        power = jnp.dot(spread * spread, ones, preferred_element_type=F32)
        scale = 0.5 * lax.rsqrt(power * (1.0 / chans) + 1e-05)
        mixed = jnp.dot(spread, mix_ref[layer], preferred_element_type=F32)
        for g in range(chans // LANES):
            moved = gelu(mixed[:, g * LANES : (g + 1) * LANES] * scale)
            center = taps_in[g, p + HALO, first + HALO : first + HALO + count].astype(F32)
            fresh = center + moved.reshape(count, TILE, LANES)
            for k in range(count):
                out_ref[g, first + k, pl.ds(p, TILE, stride=2), :] = fresh[k]


def row_of(out_ref, y):
    return jnp.concatenate([out_ref[g, y] for g in range(out_ref.shape[0])], axis=1)


def at_last():
    return lax.axis_index("lat") == lax.axis_size("lat") - 1


def inner_kernel(
    shrink,
    layer,
    edge_in,
    inner_in,
    lon_in,
    taps_ref,
    mix_ref,
    inner_ref,
    lon_ref,
    near_ref,
    wide_ref,
    taps_in,
    tap_ref,
    spread_ref,
    out_ref,
):
    cols = edge_in.shape[1]
    groups = wide_ref.shape[0]
    own = inner_in.shape[0] - (HALO if shrink else 0)
    rows = own + SHIFT
    count = rows - SHIFT
    side = cols if shrink else 0
    main = 0 if shrink else EDGE
    base = 0 if shrink else EDGE - SHIFT

    def load(ref, place, y):
        put(wide_ref, place, main, ref[y].astype(F32))
        put(wide_ref, place, side, lon_in[place].astype(F32))
        shifted(wide_ref, taps_in, base, place, place)

    @pl.loop(0, SHIFT, unroll=2)
    def _(y):
        load(edge_in, y if shrink else own + y, y)

    @pl.loop(0, own, unroll=2)
    def _(y):
        load(inner_in, y + SHIFT if shrink else y, y)

    near = rows - SHIFT if shrink else 0
    near_ref[...] = taps_in[:, :, near : near + SHIFT]

    @pl.loop(0, groups)
    def _(g):
        convolve(taps_in, taps_ref, tap_ref, spread_ref, layer, g, 0, count)

    finish(taps_in, spread_ref, mix_ref, out_ref, layer, 0, count)
    edge = slice(cols - EDGE, cols) if shrink else slice(0, EDGE)

    @pl.loop(0, count, unroll=2)
    def _(y):
        value = row_of(out_ref, y)
        inner_ref[y] = value.astype(BF16)
        lon_ref[y] = value[edge].astype(BF16)

    if not shrink:

        @pl.when(at_last())
        def _():
            taps_in[:, :, rows:] = jnp.zeros((groups, TAPS + 1, HALO, TILE, LANES), BF16)

            @pl.loop(0, groups)
            def _(g):
                convolve(taps_in, taps_ref, tap_ref, spread_ref, layer, g, count, HALO)

            finish(taps_in, spread_ref, mix_ref, out_ref, layer, count, HALO)

        for k in range(HALO):
            value = row_of(out_ref, count + k)
            inner_ref[count + k] = value.astype(BF16)
            lon_ref[count + k] = value[edge].astype(BF16)


def edge_kernel(
    shrink,
    final,
    layer,
    inner_in,
    lon_in,
    lat_in,
    corner_in,
    near_ref,
    inner_new,
    lon_new,
    taps_ref,
    mix_ref,
    *refs,
):
    if final:
        state_ref, wide_ref, taps_in, tap_ref, spread_ref, out_ref = refs
    else:
        edge_ref, lon_ref, corner_ref, wide_ref, taps_in, tap_ref, spread_ref, out_ref = refs
    cols = lat_in.shape[1]
    groups = wide_ref.shape[0]
    side = cols if shrink else 0
    main = 0 if shrink else EDGE
    base = 0 if shrink else EDGE - SHIFT
    last = at_last()
    top = lax.axis_index("lat") == 0
    own = SHIFT if not shrink else 0
    for k in range(SHIFT):
        value, beside = lat_in[k].astype(F32), corner_in[k].astype(F32)
        if not shrink:
            value, beside = jnp.where(top, 0.0, value), jnp.where(top, 0.0, beside)
        elif k < HALO:
            rows = lon_in.shape[0] - HALO
            kept = inner_in.shape[0] - HALO
            value = jnp.where(last, inner_in[kept + k].astype(F32), value)
            beside = jnp.where(last, lon_in[rows + k].astype(F32), beside)
        else:
            value, beside = jnp.where(last, 0.0, value), jnp.where(last, 0.0, beside)
        put(wide_ref, k, main, value)
        put(wide_ref, k, side, beside)
        shifted(wide_ref, taps_in, base, k, k if not shrink else k + SHIFT)
    taps_in[:, :, own : own + SHIFT] = near_ref[...]

    @pl.loop(0, groups)
    def _(g):
        convolve(taps_in, taps_ref, tap_ref, spread_ref, layer, g, 0, SHIFT)

    finish(taps_in, spread_ref, mix_ref, out_ref, layer, 0, SHIFT)
    kept = inner_new.shape[0]
    for k in range(SHIFT):
        value = row_of(out_ref, k)
        if final:
            state_ref[kept + k] = value.astype(BF16)
            continue
        if not shrink and k < HALO:
            value = jnp.where(top, 0.0, value)
        value = value.astype(F32)
        edge = value[cols - EDGE :] if shrink else value[:EDGE]
        edge_ref[k] = value.astype(BF16)
        corner_ref[k] = edge.astype(BF16)
        lon_ref[kept + k if shrink else k] = edge.astype(BF16)
    if final:
        state_ref[0:kept] = inner_new[...]
    elif shrink:
        lon_ref[0:kept] = lon_new[...]
    else:
        lon_ref[SHIFT : SHIFT + kept] = lon_new[...]


def call(kernel, out_shape, inputs, scratch=(), limit=VMEM_LIMIT, space=None, work=0):
    whole = pl.BlockSpec(memory_space=pltpu.VMEM)
    single = isinstance(out_shape, jax.ShapeDtypeStruct)
    spaces = space or (pltpu.VMEM,) * len(inputs)
    return pl.pallas_call(
        kernel,
        out_shape=out_shape,
        in_specs=[pl.BlockSpec(memory_space=s) for s in spaces],
        out_specs=whole if single else [whole] * len(out_shape),
        scratch_shapes=list(scratch),
        compiler_params=pltpu.CompilerParams(vmem_limit_bytes=limit),
        cost_estimate=pl.CostEstimate(flops=work, bytes_accessed=0, transcendentals=0),
    )(*inputs)


def held(*shape):
    return jax.ShapeDtypeStruct(shape, BF16)


def scratch_of(groups, seen, made, cols, chans):
    return (
        pltpu.VMEM((groups, seen, cols + EDGE, LANES), F32),
        pltpu.VMEM((groups, TAPS + 1, seen, TILE, LANES), BF16),
        pltpu.VMEM((TAPS * TAPS, TILE, LANES), BF16),
        pltpu.VMEM((2, made, TILE, chans), BF16),
        pltpu.VMEM((groups, made, cols, LANES), F32),
    )


def layer(state, lon_out, corner_out, taps, mix, number, shrink, final):
    edge, inner = state
    lat_in, lon_in, corner_in = exchange((edge, lon_out, corner_out), not shrink)
    cols, chans = edge.shape[1:]
    groups = chans // LANES
    rows = inner.shape[0] + SHIFT - (HALO if shrink else 0)
    spare = 0 if shrink else HALO
    made = rows - SHIFT + spare
    inner_new, lon_new, near = call(
        functools.partial(inner_kernel, shrink, number),
        (
            held(made, cols, chans),
            held(made, EDGE, chans),
            held(groups, TAPS + 1, SHIFT, TILE, LANES),
        ),
        (edge, inner, lon_in, taps, mix),
        scratch_of(groups, rows + spare, made, cols, chans),
        work=made * cols * chans * WORK,
    )
    if final:
        outs = held(made + SHIFT, cols, chans)
    else:
        outs = (
            held(SHIFT, cols, chans),
            held(made + SHIFT, EDGE, chans),
            held(SHIFT, EDGE, chans),
        )
    outs = call(
        functools.partial(edge_kernel, shrink, final, number),
        outs,
        (inner, lon_in, lat_in, corner_in, near, inner_new, lon_new, taps, mix),
        scratch_of(groups, 2 * SHIFT, SHIFT, cols, chans),
        work=SHIFT * cols * chans * WORK,
    )
    if final:
        return outs
    edge, lon_out, corner_out = outs
    return (edge, inner_new), lon_out, corner_out


def exchange(pieces, forward):
    lat, lon, corner = pieces
    count_lat = lax.axis_size("lat")
    count_lon = lax.axis_size("lon")
    along = [(i, (i + 1) % count_lat) for i in range(count_lat)]
    around = [(j, (j + 1) % count_lon) for j in range(count_lon)]
    across = [
        (i * count_lon + j, ni * count_lon + nj) for i, ni in along for j, nj in around
    ]
    if not forward:
        along, around, across = ([(t, s) for s, t in p] for p in (along, around, across))
    lon = lax.ppermute(lon, "lon", around)
    lat = lax.ppermute(lat, "lat", along)
    corner = lax.ppermute(corner, ("lat", "lon"), across)
    return lat, lon, corner


def body(
    background, observations, destination, footprint, weights, obs_proj, depth_w, point_w, gains
):
    rows, cols, chans = background.shape
    lat_count, lon_count = lax.axis_size("lat"), lax.axis_size("lon")
    obs_rows, feats = observations.shape
    cap = 2 * obs_rows // (lat_count * lon_count)
    depth = cap * (feats // LANES) + META
    foot_count = footprint.shape[1]
    half = lon_count // 2
    members = lat_count * half
    block = held(members, depth, LANES)
    send_far, order, meta = call(
        functools.partial(far_kernel, cap, cols, lon_count),
        (
            block,
            jax.ShapeDtypeStruct((2, obs_rows), jnp.int32),
            held(META, obs_rows),
        ),
        (destination.T, footprint.T, weights.T, observations),
        (
            pltpu.VMEM((1, obs_rows), jnp.int32),
            pltpu.VMEM((foot_count, obs_rows), jnp.int32),
            pltpu.VMEM((foot_count, obs_rows), BF16),
            pltpu.VMEM((obs_rows, feats), BF16),
            pltpu.SemaphoreType.DMA((4,)),
        ),
        PACK_LIMIT,
        (pltpu.HBM,) * 4,
        work=3 * MICROSECOND,
    )
    send_near = call(
        functools.partial(near_kernel, cap),
        block,
        (order, meta, observations),
        work=2 * MICROSECOND,
    )
    groups = [
        [i * lon_count + j for i in range(lat_count) for j in range(start, start + half)]
        for start in (0, half)
    ]
    got_far, got_near = (
        lax.all_to_all(
            send,
            ("lat", "lon"),
            split_axis=0,
            concat_axis=0,
            axis_index_groups=groups,
            tiled=True,
        )
        for send in (send_far, send_near)
    )
    cells = rows * cols
    far = call(
        functools.partial(gather_kernel, cap, cols),
        held(cells, feats),
        (got_far,),
        work=MICROSECOND,
    )
    far = lax.ppermute(far, "lon", [(j, (j + half) % lon_count) for j in range(lon_count)])
    near = call(
        functools.partial(gather_kernel, cap, cols),
        jax.ShapeDtypeStruct((cells, feats), F32),
        (got_near,),
        work=MICROSECOND,
    )
    layers = depth_w.shape[0]
    taps = depth_w.transpose(1, 2, 0, 3).reshape(TAPS * TAPS, layers, chans)
    mix = (gains[:, :, None] * point_w.astype(F32)).astype(BF16)
    near, mix = lax.optimization_barrier((near, mix))
    edge, inner, lon_out, corner_out = call(
        state_kernel,
        (
            held(SHIFT, cols, chans),
            held(rows - SHIFT, cols, chans),
            held(rows, EDGE, chans),
            held(SHIFT, EDGE, chans),
        ),
        (near, far, obs_proj, background),
        work=MICROSECOND,
    )
    state = (edge, inner)
    for n in range(layers - 1):
        state, lon_out, corner_out = layer(
            state, lon_out, corner_out, taps, mix, n, n % 2 == 1, False
        )
    n = layers - 1
    return layer(state, lon_out, corner_out, taps, mix, n, n % 2 == 1, True)


def solution(mesh):
    placed = (
        P("lat", "lon", None),
        P(("lat", "lon"), None),
        P(("lat", "lon"), None),
        P(("lat", "lon"), None),
        P(("lat", "lon"), None),
        P(),
        P(),
        P(),
        P(),
    )
    return jax.shard_map(
        body, mesh=mesh, in_specs=placed, out_specs=P("lat", "lon", None), check_vma=False
    )
```

```python
import functools

import jax
import jax.numpy as jnp
from jax import lax
from jax.experimental import pallas as pl
from jax.experimental.pallas import tpu as pltpu
from jax.sharding import PartitionSpec as P

LANES = 128
META = 8
TAPS = 7
HALO = 3
SHIFT = 2 * HALO
EDGE = 8
TILE = 16
MICROSECOND = 1150000000
WORK = 5000
VMEM_LIMIT = 24 * 1024 * 1024
PACK_LIMIT = 58 * 1024 * 1024
BF16 = jnp.bfloat16
F32 = jnp.float32


def place(cap, first, dest, rank, meta, obs, send_ref):
    members, depth, _ = send_ref.shape
    obs_rows = obs.shape[0]
    per = LANES // cap
    slot = lax.broadcasted_iota(jnp.int32, (cap, obs_rows), 0)
    ranked = jnp.where(slot == rank, 1.0, 0.0).astype(BF16).reshape(cap // TILE, TILE, obs_rows)
    lane = lax.broadcasted_iota(jnp.int32, (META, LANES), 1)
    count = min(512, members * cap) // cap
    for start in range(0, members, count):
        parts = []
        for d in range(start, start + count):
            mine = jnp.where(dest == first + d, 1.0, 0.0)
            mine = jnp.broadcast_to(mine, (TILE, obs_rows)).astype(BF16)
            parts.append((ranked * mine[None]).reshape(cap, obs_rows))
        chosen = jnp.concatenate(parts, axis=0)
        feats = jnp.dot(chosen, obs, preferred_element_type=F32).astype(BF16)
        placed = lax.dot_general(
            meta, chosen, (((1,), (1,)), ((), ())), preferred_element_type=F32
        )
        for half in range(feats.shape[1] // LANES):
            piece = feats[:, half * LANES : (half + 1) * LANES].reshape(count, cap, LANES)
            send_ref[start : start + count, half * cap : (half + 1) * cap, :] = piece
        for chunk in range(count // per):
            values = placed[:, chunk * LANES : (chunk + 1) * LANES]
            turned = [values] + [pltpu.roll(values, k * cap, 1) for k in range(1, per)]
            for own in range(per):
                wide = turned[0]
                for group in range(per):
                    wide = jnp.where(lane // cap == group, turned[(group - own) % per], wide)
                send_ref[start + chunk * per + own, depth - META :, :] = wide.astype(BF16)


def far_kernel(
    cap,
    cols,
    lon,
    dest_hbm,
    foot_hbm,
    weights_hbm,
    obs_hbm,
    send_ref,
    order_ref,
    meta_ref,
    dest_ref,
    foot_ref,
    weights_ref,
    obs_ref,
    sems,
):
    copies = [
        pltpu.make_async_copy(source, target, sems.at[k])
        for k, (source, target) in enumerate(
            (
                (dest_hbm, dest_ref),
                (obs_hbm, obs_ref),
                (foot_hbm, foot_ref),
                (weights_hbm, weights_ref),
            )
        )
    ]
    for copy in copies:
        copy.start()
    members = send_ref.shape[0]
    obs_rows = obs_ref.shape[0]
    half = lon // 2
    upper = lax.broadcasted_iota(jnp.int32, (LANES, LANES), 0) <= lax.broadcasted_iota(
        jnp.int32, (LANES, LANES), 1
    )
    upper = jnp.where(upper, 1.0, 0.0).astype(BF16)
    ids = lax.broadcasted_iota(jnp.int32, (2 * members, obs_rows), 0)
    skip = lax.div(lax.axis_index("lon"), half) * half
    copies[0].wait()
    target = dest_ref[...]
    across = lax.rem(target, lon) - skip
    across = jnp.where(across < 0, across + lon, across)
    dest = lax.div(target, lon) * half + across
    dest = jnp.where(across >= half, dest + (members - half), dest)
    member = jnp.where(ids == dest, 1.0, 0.0)
    seen = jnp.zeros((2 * members, 1), F32)
    ranks = []
    for first in range(0, obs_rows, LANES):
        part = member[:, first : first + LANES]
        count = jnp.dot(part.astype(BF16), upper, preferred_element_type=F32) + seen
        ranks.append(jnp.sum((count - 1.0) * part, axis=0, keepdims=True))
        seen = count[:, LANES - 1 :]
    rank = jnp.concatenate(ranks, axis=1).astype(jnp.int32)
    order_ref[0:1] = dest
    order_ref[1:2] = rank
    for copy in copies[1:]:
        copy.wait()
    start = foot_ref[0:1, :]
    meta = jnp.concatenate(
        [
            lax.div(start, cols).astype(F32),
            lax.rem(start, cols).astype(F32),
            weights_ref[...].astype(F32),
            jnp.zeros((META - 2 - weights_ref.shape[0], obs_rows), F32),
        ],
        axis=0,
    ).astype(BF16)
    meta_ref[...] = meta
    place(cap, members, dest, rank, meta, obs_ref[...], send_ref)


def near_kernel(cap, order_ref, meta_ref, obs_ref, after_ref, send_ref):
    del after_ref
    place(cap, 0, order_ref[0:1], order_ref[1:2], meta_ref[...], obs_ref[...], send_ref)


def gather_kernel(cap, cols, got_ref, field_ref):
    members, depth, _ = got_ref.shape
    cells, feats = field_ref.shape
    step = cols + 1
    per = LANES // cap
    halves = feats // LANES
    lane = lax.broadcasted_iota(jnp.int32, (META, LANES), 1)
    cell = lax.broadcasted_iota(jnp.int32, (cells, LANES), 0)
    total = jnp.zeros((cells, feats), F32)
    for pair in range(0, members // per, 2):
        maps = []
        blocks = []
        for chunk in (pair, pair + 1):
            meta = got_ref[chunk * per, depth - META :, :].astype(F32)
            for group in range(1, per):
                other = got_ref[chunk * per + group, depth - META :, :].astype(F32)
                meta = jnp.where(lane // cap == group, other, meta)
            start = (meta[0:1] * cols + meta[1:2]).astype(jnp.int32)
            away = cell - start
            away = jnp.where(away < 0, away + cells, away)
            amount = jnp.zeros((cells, LANES), F32)
            for entry in range(4):
                amount = jnp.where(away == entry * step, meta[2 + entry : 3 + entry], amount)
            maps.append(amount.astype(BF16))
            block = got_ref[chunk * per : (chunk + 1) * per]
            blocks.append(
                jnp.concatenate(
                    [
                        block[:, half * cap : (half + 1) * cap, :].reshape(LANES, LANES)
                        for half in range(halves)
                    ],
                    axis=1,
                )
            )
        total = total + jnp.dot(
            jnp.concatenate(maps, axis=1),
            jnp.concatenate(blocks, axis=0),
            preferred_element_type=F32,
        )
    field_ref[...] = total.astype(field_ref.dtype)


def state_kernel(near_ref, far_ref, proj_ref, back_ref, edge_ref, inner_ref, lon_ref, corner_ref):
    rows, cols, chans = back_ref.shape
    field = (near_ref[...] + far_ref[...].astype(F32)).astype(BF16)
    assim = jnp.dot(field, proj_ref[...], preferred_element_type=F32)
    state = back_ref[...].astype(F32) + assim.reshape(rows, cols, chans)
    state = state.astype(BF16)
    edge_ref[...] = state[rows - SHIFT :]
    inner_ref[...] = state[: rows - SHIFT]
    lon_ref[...] = state[:, cols - EDGE :, :]
    corner_ref[...] = state[rows - SHIFT :, cols - EDGE :, :]


def gelu(half):
    inner = half * (1.5957691216057308 + 0.285419265090401 * (half * half))
    return half + half * jnp.tanh(inner)


def put(wide_ref, row, start, value):
    for g in range(wide_ref.shape[0]):
        wide_ref[g, row, start : start + value.shape[0], :] = value[:, g * LANES : (g + 1) * LANES]


def shifted(wide_ref, taps_in, base, row, target):
    for g in range(wide_ref.shape[0]):
        for r in range(TAPS + 1):
            columns = pl.ds(base + r, TILE, stride=2)
            taps_in[g, r, target] = wide_ref[g, row, columns, :].astype(BF16)


def convolve(taps_in, taps_ref, tap_ref, spread_ref, layer, g, first, count):
    lanes = pl.ds(pl.multiple_of(g * LANES, LANES), LANES)
    for k in range(TAPS * TAPS):
        row = taps_ref[k, layer : layer + 1, lanes]
        tap_ref[k] = jnp.broadcast_to(row, (TILE, LANES)).astype(BF16)
    for p in range(2):
        total = None
        for b in range(TAPS):
            seen = taps_in[g, p + b, first : first + count + TAPS - 1]
            part = None
            for a in range(TAPS):
                term = seen[a : a + count] * tap_ref[a * TAPS + b]
                part = term if part is None else part + term
            total = part if total is None else total + part
        spread_ref[p, first : first + count, :, lanes] = total


def finish(taps_in, spread_ref, mix_ref, out_ref, layer, first, count):
    chans = mix_ref.shape[1]
    ones = jnp.ones((chans, LANES), BF16)
    for p in range(2):
        spread = spread_ref[p, first : first + count].reshape(count * TILE, chans)
        power = jnp.dot(spread * spread, ones, preferred_element_type=F32)
        scale = 0.5 * lax.rsqrt(power * (1.0 / chans) + 1e-05)
        mixed = jnp.dot(spread, mix_ref[layer], preferred_element_type=F32)
        for g in range(chans // LANES):
            moved = gelu(mixed[:, g * LANES : (g + 1) * LANES] * scale)
            center = taps_in[g, p + HALO, first + HALO : first + HALO + count].astype(F32)
            fresh = center + moved.reshape(count, TILE, LANES)
            for k in range(count):
                out_ref[g, first + k, pl.ds(p, TILE, stride=2), :] = fresh[k]


def row_of(out_ref, y):
    return jnp.concatenate([out_ref[g, y] for g in range(out_ref.shape[0])], axis=1)


def at_last():
    return lax.axis_index("lat") == lax.axis_size("lat") - 1


def inner_kernel(
    shrink,
    layer,
    edge_in,
    inner_in,
    lon_in,
    taps_ref,
    mix_ref,
    inner_ref,
    lon_ref,
    near_ref,
    wide_ref,
    taps_in,
    tap_ref,
    spread_ref,
    out_ref,
):
    cols = edge_in.shape[1]
    groups = wide_ref.shape[0]
    own = inner_in.shape[0] - (HALO if shrink else 0)
    rows = own + SHIFT
    count = rows - SHIFT
    side = cols if shrink else 0
    main = 0 if shrink else EDGE
    base = 0 if shrink else EDGE - SHIFT

    def load(ref, place, y):
        put(wide_ref, place, main, ref[y].astype(F32))
        put(wide_ref, place, side, lon_in[place].astype(F32))
        shifted(wide_ref, taps_in, base, place, place)

    @pl.loop(0, SHIFT, unroll=2)
    def _(y):
        load(edge_in, y if shrink else own + y, y)

    @pl.loop(0, own, unroll=2)
    def _(y):
        load(inner_in, y + SHIFT if shrink else y, y)

    near = rows - SHIFT if shrink else 0
    near_ref[...] = taps_in[:, :, near : near + SHIFT]

    @pl.loop(0, groups)
    def _(g):
        convolve(taps_in, taps_ref, tap_ref, spread_ref, layer, g, 0, count)

    finish(taps_in, spread_ref, mix_ref, out_ref, layer, 0, count)
    edge = slice(cols - EDGE, cols) if shrink else slice(0, EDGE)

    @pl.loop(0, count, unroll=2)
    def _(y):
        value = row_of(out_ref, y)
        inner_ref[y] = value.astype(BF16)
        lon_ref[y] = value[edge].astype(BF16)

    if not shrink:

        @pl.when(at_last())
        def _():
            taps_in[:, :, rows:] = jnp.zeros((groups, TAPS + 1, HALO, TILE, LANES), BF16)

            @pl.loop(0, groups)
            def _(g):
                convolve(taps_in, taps_ref, tap_ref, spread_ref, layer, g, count, HALO)

            finish(taps_in, spread_ref, mix_ref, out_ref, layer, count, HALO)

        for k in range(HALO):
            value = row_of(out_ref, count + k)
            inner_ref[count + k] = value.astype(BF16)
            lon_ref[count + k] = value[edge].astype(BF16)


def edge_kernel(
    shrink,
    final,
    layer,
    inner_in,
    lon_in,
    lat_in,
    corner_in,
    near_ref,
    inner_new,
    lon_new,
    taps_ref,
    mix_ref,
    *refs,
):
    if final:
        state_ref, wide_ref, taps_in, tap_ref, spread_ref, out_ref = refs
    else:
        edge_ref, lon_ref, corner_ref, wide_ref, taps_in, tap_ref, spread_ref, out_ref = refs
    cols = lat_in.shape[1]
    groups = wide_ref.shape[0]
    side = cols if shrink else 0
    main = 0 if shrink else EDGE
    base = 0 if shrink else EDGE - SHIFT
    last = at_last()
    top = lax.axis_index("lat") == 0
    own = SHIFT if not shrink else 0
    for k in range(SHIFT):
        value, beside = lat_in[k].astype(F32), corner_in[k].astype(F32)
        if not shrink:
            value, beside = jnp.where(top, 0.0, value), jnp.where(top, 0.0, beside)
        elif k < HALO:
            rows = lon_in.shape[0] - HALO
            kept = inner_in.shape[0] - HALO
            value = jnp.where(last, inner_in[kept + k].astype(F32), value)
            beside = jnp.where(last, lon_in[rows + k].astype(F32), beside)
        else:
            value, beside = jnp.where(last, 0.0, value), jnp.where(last, 0.0, beside)
        put(wide_ref, k, main, value)
        put(wide_ref, k, side, beside)
        shifted(wide_ref, taps_in, base, k, k if not shrink else k + SHIFT)
    taps_in[:, :, own : own + SHIFT] = near_ref[...]

    @pl.loop(0, groups)
    def _(g):
        convolve(taps_in, taps_ref, tap_ref, spread_ref, layer, g, 0, SHIFT)

    finish(taps_in, spread_ref, mix_ref, out_ref, layer, 0, SHIFT)
    kept = inner_new.shape[0]
    for k in range(SHIFT):
        value = row_of(out_ref, k)
        if final:
            state_ref[kept + k] = value.astype(BF16)
            continue
        if not shrink and k < HALO:
            value = jnp.where(top, 0.0, value)
        value = value.astype(F32)
        edge = value[cols - EDGE :] if shrink else value[:EDGE]
        edge_ref[k] = value.astype(BF16)
        corner_ref[k] = edge.astype(BF16)
        lon_ref[kept + k if shrink else k] = edge.astype(BF16)
    if final:
        state_ref[0:kept] = inner_new[...]
    elif shrink:
        lon_ref[0:kept] = lon_new[...]
    else:
        lon_ref[SHIFT : SHIFT + kept] = lon_new[...]


def call(kernel, out_shape, inputs, scratch=(), limit=VMEM_LIMIT, space=None, work=0):
    whole = pl.BlockSpec(memory_space=pltpu.VMEM)
    single = isinstance(out_shape, jax.ShapeDtypeStruct)
    spaces = space or (pltpu.VMEM,) * len(inputs)
    return pl.pallas_call(
        kernel,
        out_shape=out_shape,
        in_specs=[pl.BlockSpec(memory_space=s) for s in spaces],
        out_specs=whole if single else [whole] * len(out_shape),
        scratch_shapes=list(scratch),
        compiler_params=pltpu.CompilerParams(vmem_limit_bytes=limit),
        cost_estimate=pl.CostEstimate(flops=work, bytes_accessed=0, transcendentals=0),
    )(*inputs)


def held(*shape):
    return jax.ShapeDtypeStruct(shape, BF16)


def scratch_of(groups, seen, made, cols, chans):
    return (
        pltpu.VMEM((groups, seen, cols + EDGE, LANES), F32),
        pltpu.VMEM((groups, TAPS + 1, seen, TILE, LANES), BF16),
        pltpu.VMEM((TAPS * TAPS, TILE, LANES), BF16),
        pltpu.VMEM((2, made, TILE, chans), BF16),
        pltpu.VMEM((groups, made, cols, LANES), F32),
    )


def layer(state, lon_out, corner_out, taps, mix, number, shrink, final):
    edge, inner = state
    lat_in, lon_in, corner_in = exchange((edge, lon_out, corner_out), not shrink)
    cols, chans = edge.shape[1:]
    groups = chans // LANES
    rows = inner.shape[0] + SHIFT - (HALO if shrink else 0)
    spare = 0 if shrink else HALO
    made = rows - SHIFT + spare
    inner_new, lon_new, near = call(
        functools.partial(inner_kernel, shrink, number),
        (
            held(made, cols, chans),
            held(made, EDGE, chans),
            held(groups, TAPS + 1, SHIFT, TILE, LANES),
        ),
        (edge, inner, lon_in, taps, mix),
        scratch_of(groups, rows + spare, made, cols, chans),
        work=made * cols * chans * WORK,
    )
    if final:
        outs = held(made + SHIFT, cols, chans)
    else:
        outs = (
            held(SHIFT, cols, chans),
            held(made + SHIFT, EDGE, chans),
            held(SHIFT, EDGE, chans),
        )
    outs = call(
        functools.partial(edge_kernel, shrink, final, number),
        outs,
        (inner, lon_in, lat_in, corner_in, near, inner_new, lon_new, taps, mix),
        scratch_of(groups, 2 * SHIFT, SHIFT, cols, chans),
        work=SHIFT * cols * chans * WORK,
    )
    if final:
        return outs
    edge, lon_out, corner_out = outs
    return (edge, inner_new), lon_out, corner_out


def exchange(pieces, forward):
    lat, lon, corner = pieces
    count_lat = lax.axis_size("lat")
    count_lon = lax.axis_size("lon")
    along = [(i, (i + 1) % count_lat) for i in range(count_lat)]
    around = [(j, (j + 1) % count_lon) for j in range(count_lon)]
    across = [
        (i * count_lon + j, ni * count_lon + nj) for i, ni in along for j, nj in around
    ]
    if not forward:
        along, around, across = ([(t, s) for s, t in p] for p in (along, around, across))
    lon = lax.ppermute(lon, "lon", around)
    lat = lax.ppermute(lat, "lat", along)
    corner = lax.ppermute(corner, ("lat", "lon"), across)
    return lat, lon, corner


def body(
    background, observations, destination, footprint, weights, obs_proj, depth_w, point_w, gains
):
    rows, cols, chans = background.shape
    lat_count, lon_count = lax.axis_size("lat"), lax.axis_size("lon")
    obs_rows, feats = observations.shape
    cap = 2 * obs_rows // (lat_count * lon_count)
    depth = cap * (feats // LANES) + META
    foot_count = footprint.shape[1]
    half = lon_count // 2
    members = lat_count * half
    block = held(members, depth, LANES)
    send_far, order, meta = call(
        functools.partial(far_kernel, cap, cols, lon_count),
        (
            block,
            jax.ShapeDtypeStruct((2, obs_rows), jnp.int32),
            held(META, obs_rows),
        ),
        (destination.T, footprint.T, weights.T, observations),
        (
            pltpu.VMEM((1, obs_rows), jnp.int32),
            pltpu.VMEM((foot_count, obs_rows), jnp.int32),
            pltpu.VMEM((foot_count, obs_rows), BF16),
            pltpu.VMEM((obs_rows, feats), BF16),
            pltpu.SemaphoreType.DMA((4,)),
        ),
        PACK_LIMIT,
        (pltpu.HBM,) * 4,
        work=3 * MICROSECOND,
    )
    groups = [
        [i * lon_count + j for i in range(lat_count) for j in range(start, start + half)]
        for start in (0, half)
    ]
    exchanged = functools.partial(
        lax.all_to_all,
        axis_name=("lat", "lon"),
        split_axis=0,
        concat_axis=0,
        axis_index_groups=groups,
        tiled=True,
    )
    got_far = exchanged(send_far)
    cells = rows * cols
    field = call(
        functools.partial(gather_kernel, cap, cols),
        held(cells, feats),
        (got_far,),
        work=MICROSECOND,
    )
    far = lax.ppermute(field, "lon", [(j, (j + half) % lon_count) for j in range(lon_count)])
    send_near = call(
        functools.partial(near_kernel, cap),
        block,
        (order, meta, observations, field),
        space=(pltpu.VMEM, pltpu.VMEM, pltpu.VMEM, pl.ANY),
        work=2 * MICROSECOND,
    )
    got_near = exchanged(send_near)
    near = call(
        functools.partial(gather_kernel, cap, cols),
        jax.ShapeDtypeStruct((cells, feats), F32),
        (got_near,),
        work=MICROSECOND,
    )
    layers = depth_w.shape[0]
    taps = depth_w.transpose(1, 2, 0, 3).reshape(TAPS * TAPS, layers, chans)
    mix = (gains[:, :, None] * point_w.astype(F32)).astype(BF16)
    near, mix = lax.optimization_barrier((near, mix))
    edge, inner, lon_out, corner_out = call(
        state_kernel,
        (
            held(SHIFT, cols, chans),
            held(rows - SHIFT, cols, chans),
            held(rows, EDGE, chans),
            held(SHIFT, EDGE, chans),
        ),
        (near, far, obs_proj, background),
        work=MICROSECOND,
    )
    state = (edge, inner)
    for n in range(layers - 1):
        state, lon_out, corner_out = layer(
            state, lon_out, corner_out, taps, mix, n, n % 2 == 1, False
        )
    n = layers - 1
    return layer(state, lon_out, corner_out, taps, mix, n, n % 2 == 1, True)


def solution(mesh):
    placed = (
        P("lat", "lon", None),
        P(("lat", "lon"), None),
        P(("lat", "lon"), None),
        P(("lat", "lon"), None),
        P(("lat", "lon"), None),
        P(),
        P(),
        P(),
        P(),
    )
    return jax.shard_map(
        body, mesh=mesh, in_specs=placed, out_specs=P("lat", "lon", None), check_vma=False
    )
```

```python
import functools

import jax
import jax.numpy as jnp
from jax import lax
from jax.experimental import pallas as pl
from jax.experimental.pallas import tpu as pltpu
from jax.sharding import PartitionSpec as P

LANES = 128
META = 8
TAPS = 7
HALO = 3
SHIFT = 2 * HALO
EDGE = 8
TILE = 16
SUBLANES = 8
WORK = 5000
VMEM_LIMIT = 24 * 1024 * 1024
PACK_LIMIT = 58 * 1024 * 1024
BF16 = jnp.bfloat16
F32 = jnp.float32


def pack_kernel(cap, cols, dest_hbm, foot_hbm, weights_hbm, obs_hbm, send_ref, dest_ref, foot_ref, weights_ref, obs_ref, sems):
    copies = [
        pltpu.make_async_copy(source, target, sems.at[k])
        for k, (source, target) in enumerate(
            (
                (dest_hbm, dest_ref),
                (obs_hbm, obs_ref),
                (foot_hbm, foot_ref),
                (weights_hbm, weights_ref),
            )
        )
    ]
    for copy in copies:
        copy.start()
    devices = send_ref.shape[0]
    obs_rows = obs_ref.shape[0]
    per = LANES // cap
    upper = lax.broadcasted_iota(jnp.int32, (LANES, LANES), 0) <= lax.broadcasted_iota(
        jnp.int32, (LANES, LANES), 1
    )
    upper = jnp.where(upper, 1.0, 0.0).astype(BF16)
    ids = lax.broadcasted_iota(jnp.int32, (devices, obs_rows), 0)
    copies[0].wait()
    member = jnp.where(ids == dest_ref[...], 1.0, 0.0)
    seen = jnp.zeros((devices, 1), F32)
    ranks = []
    for first in range(0, obs_rows, LANES):
        part = member[:, first : first + LANES]
        count = jnp.dot(part.astype(BF16), upper, preferred_element_type=F32) + seen
        ranks.append(jnp.sum((count - 1.0) * part, axis=0, keepdims=True))
        seen = count[:, LANES - 1 :]
    rank = jnp.concatenate(ranks, axis=1).astype(jnp.int32)
    slot = lax.broadcasted_iota(jnp.int32, (cap, obs_rows), 0)
    ranked = jnp.where(slot == rank, 1.0, 0.0).astype(BF16).reshape(cap // TILE, TILE, obs_rows)
    for copy in copies[1:]:
        copy.wait()
    start = foot_ref[0:1, :]
    meta = jnp.concatenate(
        [
            lax.div(start, cols).astype(F32),
            lax.rem(start, cols).astype(F32),
            weights_ref[...].astype(F32),
            jnp.zeros((META - 2 - weights_ref.shape[0], obs_rows), F32),
        ],
        axis=0,
    ).astype(BF16)
    obs = obs_ref[...]
    lane = lax.broadcasted_iota(jnp.int32, (META, LANES), 1)
    count = min(512, devices * cap) // cap
    for first in range(0, devices, count):
        parts = []
        for d in range(first, first + count):
            mine = jnp.broadcast_to(member[d : d + 1], (TILE, obs_rows)).astype(BF16)
            parts.append((ranked * mine[None]).reshape(cap, obs_rows))
        chosen = jnp.concatenate(parts, axis=0)
        feats = jnp.dot(chosen, obs, preferred_element_type=F32).astype(BF16)
        placed = lax.dot_general(
            meta, chosen, (((1,), (1,)), ((), ())), preferred_element_type=F32
        )
        for half in range(feats.shape[1] // LANES):
            piece = feats[:, half * LANES : (half + 1) * LANES].reshape(count, cap, LANES)
            send_ref[first : first + count, half * cap : (half + 1) * cap, :] = piece
        base = send_ref.shape[1] - META
        for chunk in range(count // per):
            values = placed[:, chunk * LANES : (chunk + 1) * LANES]
            turned = [values] + [pltpu.roll(values, k * cap, 1) for k in range(1, per)]
            for own in range(per):
                wide = turned[0]
                for group in range(per):
                    wide = jnp.where(lane // cap == group, turned[(group - own) % per], wide)
                send_ref[first + chunk * per + own, base:, :] = wide.astype(BF16)


def assim_kernel(
    cap,
    step,
    got_ref,
    proj_hbm,
    back_hbm,
    edge_ref,
    inner_ref,
    lon_ref,
    corner_ref,
    proj_ref,
    back_ref,
    sems,
):
    copies = (
        pltpu.make_async_copy(proj_hbm, proj_ref, sems.at[0]),
        pltpu.make_async_copy(back_hbm, back_ref, sems.at[1]),
    )
    for copy in copies:
        copy.start()
    devices, depth, _ = got_ref.shape
    rows, cols, chans = back_ref.shape
    cells = rows * cols
    feats = proj_ref.shape[0]
    per = LANES // cap
    halves = feats // LANES
    lane = lax.broadcasted_iota(jnp.int32, (META, LANES), 1)
    cell = lax.broadcasted_iota(jnp.int32, (cells, LANES), 0)
    total = jnp.zeros((cells, feats), F32)
    for pair in range(0, devices // per, 2):
        maps = []
        blocks = []
        for chunk in (pair, pair + 1):
            meta = got_ref[chunk * per, depth - META :, :].astype(F32)
            for group in range(1, per):
                other = got_ref[chunk * per + group, depth - META :, :].astype(F32)
                meta = jnp.where(lane // cap == group, other, meta)
            start = (meta[0:1] * cols + meta[1:2]).astype(jnp.int32)
            away = cell - start
            away = jnp.where(away < 0, away + cells, away)
            amount = jnp.zeros((cells, LANES), F32)
            for entry in range(4):
                amount = jnp.where(away == entry * step, meta[2 + entry : 3 + entry], amount)
            maps.append(amount.astype(BF16))
            block = got_ref[chunk * per : (chunk + 1) * per]
            blocks.append(
                jnp.concatenate(
                    [
                        block[:, half * cap : (half + 1) * cap, :].reshape(LANES, LANES)
                        for half in range(halves)
                    ],
                    axis=1,
                )
            )
        total = total + jnp.dot(
            jnp.concatenate(maps, axis=1),
            jnp.concatenate(blocks, axis=0),
            preferred_element_type=F32,
        )
    for copy in copies:
        copy.wait()
    assim = jnp.dot(total.astype(BF16), proj_ref[...], preferred_element_type=F32)
    state = back_ref[...].astype(F32) + assim.reshape(rows, cols, chans)
    state = state.astype(BF16)
    edge_ref[...] = state[rows - SHIFT :]
    inner_ref[...] = state[: rows - SHIFT]
    lon_ref[...] = state[:, cols - EDGE :, :]
    corner_ref[...] = state[rows - SHIFT :, cols - EDGE :, :]


def gelu(half):
    inner = half * (1.5957691216057308 + 0.285419265090401 * (half * half))
    return half + half * jnp.tanh(inner)


def put(wide_ref, row, start, value):
    for g in range(wide_ref.shape[0]):
        wide_ref[g, row, start : start + value.shape[0], :] = value[:, g * LANES : (g + 1) * LANES]


def shifted(wide_ref, taps_in, base, row, target):
    for g in range(wide_ref.shape[0]):
        for r in range(TAPS + 1):
            columns = pl.ds(base + r, TILE, stride=2)
            taps_in[g, r, target] = wide_ref[g, row, columns, :]


def convolve(taps_in, taps_ref, tap_ref, spread_ref, layer, g, first, count):
    lanes = pl.ds(pl.multiple_of(g * LANES, LANES), LANES)
    for k in range(TAPS * TAPS):
        tap_ref[k] = jnp.broadcast_to(taps_ref[k, layer : layer + 1, lanes], (SUBLANES, LANES))
    for p in range(2):
        halves = []
        for h in range(0, TILE, SUBLANES):
            total = None
            for b in range(TAPS):
                seen = taps_in[g, p + b, first : first + count + TAPS - 1, h : h + SUBLANES, :]
                for a in range(TAPS):
                    term = seen[a : a + count] * tap_ref[a * TAPS + b]
                    total = term if total is None else total + term
            halves.append(total)
        total = jnp.concatenate(halves, axis=1)
        spread_ref[p, first : first + count, :, lanes] = total.astype(BF16)


def finish(taps_in, spread_ref, mix_ref, out_ref, layer, first, count):
    chans = mix_ref.shape[1]
    ones = jnp.ones((chans, LANES), BF16)
    for p in range(2):
        spread = spread_ref[p, first : first + count].reshape(count * TILE, chans)
        power = jnp.dot(spread * spread, ones, preferred_element_type=F32)
        scale = 0.5 * lax.rsqrt(power * (1.0 / chans) + 1e-05)
        mixed = jnp.dot(spread, mix_ref[layer], preferred_element_type=F32)
        for g in range(chans // LANES):
            moved = gelu(mixed[:, g * LANES : (g + 1) * LANES] * scale)
            center = taps_in[g, p + HALO, first + HALO : first + HALO + count]
            fresh = center + moved.reshape(count, TILE, LANES)
            for k in range(count):
                out_ref[g, first + k, pl.ds(p, TILE, stride=2), :] = fresh[k]


def row_of(out_ref, y):
    return jnp.concatenate([out_ref[g, y] for g in range(out_ref.shape[0])], axis=1)


def at_last():
    return lax.axis_index("lat") == lax.axis_size("lat") - 1


def inner_kernel(
    shrink,
    layer,
    edge_in,
    inner_in,
    lon_in,
    taps_ref,
    mix_ref,
    inner_ref,
    lon_ref,
    near_ref,
    wide_ref,
    taps_in,
    tap_ref,
    spread_ref,
    out_ref,
):
    cols = edge_in.shape[1]
    groups = wide_ref.shape[0]
    own = inner_in.shape[0] - (HALO if shrink else 0)
    rows = own + SHIFT
    count = rows - SHIFT
    side = cols if shrink else 0
    main = 0 if shrink else EDGE
    base = 0 if shrink else EDGE - SHIFT

    def load(ref, place, y):
        put(wide_ref, place, main, ref[y].astype(F32))
        put(wide_ref, place, side, lon_in[place].astype(F32))
        shifted(wide_ref, taps_in, base, place, place)

    @pl.loop(0, SHIFT, unroll=2)
    def _(y):
        load(edge_in, y if shrink else own + y, y)

    @pl.loop(0, own, unroll=2)
    def _(y):
        load(inner_in, y + SHIFT if shrink else y, y)

    near = rows - SHIFT if shrink else 0
    near_ref[...] = taps_in[:, :, near : near + SHIFT]

    @pl.loop(0, groups)
    def _(g):
        convolve(taps_in, taps_ref, tap_ref, spread_ref, layer, g, 0, count)

    finish(taps_in, spread_ref, mix_ref, out_ref, layer, 0, count)
    edge = slice(cols - EDGE, cols) if shrink else slice(0, EDGE)

    @pl.loop(0, count, unroll=2)
    def _(y):
        value = row_of(out_ref, y)
        inner_ref[y] = value.astype(BF16)
        lon_ref[y] = value[edge].astype(BF16)

    if not shrink:

        @pl.when(at_last())
        def _():
            taps_in[:, :, rows:] = jnp.zeros((groups, TAPS + 1, HALO, TILE, LANES), F32)

            @pl.loop(0, groups)
            def _(g):
                convolve(taps_in, taps_ref, tap_ref, spread_ref, layer, g, count, HALO)

            finish(taps_in, spread_ref, mix_ref, out_ref, layer, count, HALO)

        for k in range(HALO):
            value = row_of(out_ref, count + k)
            inner_ref[count + k] = value.astype(BF16)
            lon_ref[count + k] = value[edge].astype(BF16)


def edge_kernel(
    shrink,
    final,
    layer,
    inner_in,
    lon_in,
    lat_in,
    corner_in,
    near_ref,
    inner_new,
    lon_new,
    taps_ref,
    mix_ref,
    *refs,
):
    if final:
        state_ref, wide_ref, taps_in, tap_ref, spread_ref, out_ref = refs
    else:
        edge_ref, lon_ref, corner_ref, wide_ref, taps_in, tap_ref, spread_ref, out_ref = refs
    cols = lat_in.shape[1]
    groups = wide_ref.shape[0]
    side = cols if shrink else 0
    main = 0 if shrink else EDGE
    base = 0 if shrink else EDGE - SHIFT
    last = at_last()
    top = lax.axis_index("lat") == 0
    own = SHIFT if not shrink else 0
    for k in range(SHIFT):
        value, beside = lat_in[k].astype(F32), corner_in[k].astype(F32)
        if not shrink:
            value, beside = jnp.where(top, 0.0, value), jnp.where(top, 0.0, beside)
        elif k < HALO:
            rows = lon_in.shape[0] - HALO
            kept = inner_in.shape[0] - HALO
            value = jnp.where(last, inner_in[kept + k].astype(F32), value)
            beside = jnp.where(last, lon_in[rows + k].astype(F32), beside)
        else:
            value, beside = jnp.where(last, 0.0, value), jnp.where(last, 0.0, beside)
        put(wide_ref, k, main, value)
        put(wide_ref, k, side, beside)
        shifted(wide_ref, taps_in, base, k, k if not shrink else k + SHIFT)
    taps_in[:, :, own : own + SHIFT] = near_ref[...]

    @pl.loop(0, groups)
    def _(g):
        convolve(taps_in, taps_ref, tap_ref, spread_ref, layer, g, 0, SHIFT)

    finish(taps_in, spread_ref, mix_ref, out_ref, layer, 0, SHIFT)
    kept = inner_new.shape[0]
    for k in range(SHIFT):
        value = row_of(out_ref, k)
        if final:
            state_ref[kept + k] = value.astype(BF16)
            continue
        if not shrink and k < HALO:
            value = jnp.where(top, 0.0, value)
        value = value.astype(F32)
        edge = value[cols - EDGE :] if shrink else value[:EDGE]
        edge_ref[k] = value.astype(BF16)
        corner_ref[k] = edge.astype(BF16)
        lon_ref[kept + k if shrink else k] = edge.astype(BF16)
    if final:
        state_ref[0:kept] = inner_new[...]
    elif shrink:
        lon_ref[0:kept] = lon_new[...]
    else:
        lon_ref[SHIFT : SHIFT + kept] = lon_new[...]


def call(kernel, out_shape, inputs, scratch=(), limit=VMEM_LIMIT, space=None, work=0):
    whole = pl.BlockSpec(memory_space=pltpu.VMEM)
    single = isinstance(out_shape, jax.ShapeDtypeStruct)
    spaces = space or (pltpu.VMEM,) * len(inputs)
    return pl.pallas_call(
        kernel,
        out_shape=out_shape,
        in_specs=[pl.BlockSpec(memory_space=s) for s in spaces],
        out_specs=whole if single else [whole] * len(out_shape),
        scratch_shapes=list(scratch),
        compiler_params=pltpu.CompilerParams(vmem_limit_bytes=limit),
        cost_estimate=pl.CostEstimate(flops=work, bytes_accessed=0, transcendentals=0),
    )(*inputs)


def held(*shape):
    return jax.ShapeDtypeStruct(shape, BF16)


def scratch_of(groups, seen, made, cols, chans):
    return (
        pltpu.VMEM((groups, seen, cols + EDGE, LANES), F32),
        pltpu.VMEM((groups, TAPS + 1, seen, TILE, LANES), F32),
        pltpu.VMEM((TAPS * TAPS, SUBLANES, LANES), F32),
        pltpu.VMEM((2, made, TILE, chans), BF16),
        pltpu.VMEM((groups, made, cols, LANES), F32),
    )


def layer(state, lon_out, corner_out, taps, mix, number, shrink, final):
    edge, inner = state
    lat_in, lon_in, corner_in = exchange((edge, lon_out, corner_out), not shrink)
    cols, chans = edge.shape[1:]
    groups = chans // LANES
    rows = inner.shape[0] + SHIFT - (HALO if shrink else 0)
    spare = 0 if shrink else HALO
    made = rows - SHIFT + spare
    inner_new, lon_new, near = call(
        functools.partial(inner_kernel, shrink, number),
        (
            held(made, cols, chans),
            held(made, EDGE, chans),
            jax.ShapeDtypeStruct((groups, TAPS + 1, SHIFT, TILE, LANES), F32),
        ),
        (edge, inner, lon_in, taps, mix),
        scratch_of(groups, rows + spare, made, cols, chans),
        work=made * cols * chans * WORK,
    )
    if final:
        outs = held(made + SHIFT, cols, chans)
    else:
        outs = (
            held(SHIFT, cols, chans),
            held(made + SHIFT, EDGE, chans),
            held(SHIFT, EDGE, chans),
        )
    outs = call(
        functools.partial(edge_kernel, shrink, final, number),
        outs,
        (inner, lon_in, lat_in, corner_in, near, inner_new, lon_new, taps, mix),
        scratch_of(groups, 2 * SHIFT, SHIFT, cols, chans),
        work=SHIFT * cols * chans * WORK,
    )
    if final:
        return outs
    edge, lon_out, corner_out = outs
    return (edge, inner_new), lon_out, corner_out


def exchange(pieces, forward):
    lat, lon, corner = pieces
    count_lat = lax.axis_size("lat")
    count_lon = lax.axis_size("lon")
    along = [(i, (i + 1) % count_lat) for i in range(count_lat)]
    around = [(j, (j + 1) % count_lon) for j in range(count_lon)]
    across = [
        (i * count_lon + j, ni * count_lon + nj) for i, ni in along for j, nj in around
    ]
    if not forward:
        along, around, across = ([(t, s) for s, t in p] for p in (along, around, across))
    lon = lax.ppermute(lon, "lon", around)
    lat = lax.ppermute(lat, "lat", along)
    corner = lax.ppermute(corner, ("lat", "lon"), across)
    return lat, lon, corner


def body(
    background, observations, destination, footprint, weights, obs_proj, depth_w, point_w, gains
):
    rows, cols, chans = background.shape
    devices = lax.axis_size("lat") * lax.axis_size("lon")
    obs_rows, feats = observations.shape
    cap = 2 * obs_rows // devices
    depth = cap * (feats // LANES) + META
    foot_count = footprint.shape[1]
    send = call(
        functools.partial(pack_kernel, cap, cols),
        jax.ShapeDtypeStruct((devices, depth, LANES), BF16),
        (destination.T, footprint.T, weights.T, observations),
        (
            pltpu.VMEM((1, obs_rows), jnp.int32),
            pltpu.VMEM((foot_count, obs_rows), jnp.int32),
            pltpu.VMEM((foot_count, obs_rows), BF16),
            pltpu.VMEM((obs_rows, feats), BF16),
            pltpu.SemaphoreType.DMA((4,)),
        ),
        PACK_LIMIT,
        (pltpu.HBM,) * 4,
    )
    got = lax.all_to_all(send, ("lat", "lon"), split_axis=0, concat_axis=0, tiled=True)
    layers = depth_w.shape[0]
    taps = depth_w.transpose(1, 2, 0, 3).reshape(TAPS * TAPS, layers, chans)
    mix = (gains[:, :, None] * point_w.astype(F32)).astype(BF16)
    got, mix = lax.optimization_barrier((got, mix))
    edge, inner, lon_out, corner_out = call(
        functools.partial(assim_kernel, cap, cols + 1),
        (
            held(SHIFT, cols, chans),
            held(rows - SHIFT, cols, chans),
            held(rows, EDGE, chans),
            held(SHIFT, EDGE, chans),
        ),
        (got, obs_proj, background),
        (
            pltpu.VMEM(obs_proj.shape, BF16),
            pltpu.VMEM(background.shape, BF16),
            pltpu.SemaphoreType.DMA((2,)),
        ),
        PACK_LIMIT,
        (pltpu.VMEM, pltpu.HBM, pltpu.HBM),
    )
    state = (edge, inner)
    for n in range(layers - 1):
        state, lon_out, corner_out = layer(
            state, lon_out, corner_out, taps, mix, n, n % 2 == 1, False
        )
    n = layers - 1
    return layer(state, lon_out, corner_out, taps, mix, n, n % 2 == 1, True)


def solution(mesh):
    placed = (
        P("lat", "lon", None),
        P(("lat", "lon"), None),
        P(("lat", "lon"), None),
        P(("lat", "lon"), None),
        P(("lat", "lon"), None),
        P(),
        P(),
        P(),
        P(),
    )
    return jax.shard_map(
        body, mesh=mesh, in_specs=placed, out_specs=P("lat", "lon", None), check_vma=False
    )
```

```python
import functools

import jax
import jax.numpy as jnp
from jax import lax
from jax.experimental import pallas as pl
from jax.experimental.pallas import tpu as pltpu
from jax.sharding import PartitionSpec as P

LANES = 128
META = 8
TAPS = 7
HALO = 3
SHIFT = 2 * HALO
EDGE = 8
TILE = 16
WORK = 5000
VMEM_LIMIT = 24 * 1024 * 1024
PACK_LIMIT = 58 * 1024 * 1024
BF16 = jnp.bfloat16
F32 = jnp.float32


def pack_kernel(cap, cols, dest_hbm, foot_hbm, weights_hbm, obs_hbm, send_ref, dest_ref, foot_ref, weights_ref, obs_ref, sems):
    copies = [
        pltpu.make_async_copy(source, target, sems.at[k])
        for k, (source, target) in enumerate(
            (
                (dest_hbm, dest_ref),
                (obs_hbm, obs_ref),
                (foot_hbm, foot_ref),
                (weights_hbm, weights_ref),
            )
        )
    ]
    for copy in copies:
        copy.start()
    devices = send_ref.shape[0]
    obs_rows = obs_ref.shape[0]
    per = LANES // cap
    upper = lax.broadcasted_iota(jnp.int32, (LANES, LANES), 0) <= lax.broadcasted_iota(
        jnp.int32, (LANES, LANES), 1
    )
    upper = jnp.where(upper, 1.0, 0.0).astype(BF16)
    ids = lax.broadcasted_iota(jnp.int32, (devices, obs_rows), 0)
    copies[0].wait()
    member = jnp.where(ids == dest_ref[...], 1.0, 0.0)
    seen = jnp.zeros((devices, 1), F32)
    ranks = []
    for first in range(0, obs_rows, LANES):
        part = member[:, first : first + LANES]
        count = jnp.dot(part.astype(BF16), upper, preferred_element_type=F32) + seen
        ranks.append(jnp.sum((count - 1.0) * part, axis=0, keepdims=True))
        seen = count[:, LANES - 1 :]
    rank = jnp.concatenate(ranks, axis=1).astype(jnp.int32)
    slot = lax.broadcasted_iota(jnp.int32, (cap, obs_rows), 0)
    ranked = jnp.where(slot == rank, 1.0, 0.0).astype(BF16).reshape(cap // TILE, TILE, obs_rows)
    for copy in copies[1:]:
        copy.wait()
    start = foot_ref[0:1, :]
    meta = jnp.concatenate(
        [
            lax.div(start, cols).astype(F32),
            lax.rem(start, cols).astype(F32),
            weights_ref[...].astype(F32),
            jnp.zeros((META - 2 - weights_ref.shape[0], obs_rows), F32),
        ],
        axis=0,
    ).astype(BF16)
    obs = obs_ref[...]
    lane = lax.broadcasted_iota(jnp.int32, (META, LANES), 1)
    count = min(512, devices * cap) // cap
    for first in range(0, devices, count):
        parts = []
        for d in range(first, first + count):
            mine = jnp.broadcast_to(member[d : d + 1], (TILE, obs_rows)).astype(BF16)
            parts.append((ranked * mine[None]).reshape(cap, obs_rows))
        chosen = jnp.concatenate(parts, axis=0)
        feats = jnp.dot(chosen, obs, preferred_element_type=F32).astype(BF16)
        placed = lax.dot_general(
            meta, chosen, (((1,), (1,)), ((), ())), preferred_element_type=F32
        )
        for half in range(feats.shape[1] // LANES):
            piece = feats[:, half * LANES : (half + 1) * LANES].reshape(count, cap, LANES)
            send_ref[first : first + count, half * cap : (half + 1) * cap, :] = piece
        base = send_ref.shape[1] - META
        for chunk in range(count // per):
            values = placed[:, chunk * LANES : (chunk + 1) * LANES]
            turned = [values] + [pltpu.roll(values, k * cap, 1) for k in range(1, per)]
            for own in range(per):
                wide = turned[0]
                for group in range(per):
                    wide = jnp.where(lane // cap == group, turned[(group - own) % per], wide)
                send_ref[first + chunk * per + own, base:, :] = wide.astype(BF16)


def fetch_kernel(proj_hbm, back_hbm, proj_ref, back_ref, sems):
    copies = (
        pltpu.make_async_copy(proj_hbm, proj_ref, sems.at[0]),
        pltpu.make_async_copy(back_hbm, back_ref, sems.at[1]),
    )
    for copy in copies:
        copy.start()
    for copy in copies:
        copy.wait()


def assim_kernel(
    cap, step, got_ref, proj_ref, back_ref, edge_ref, inner_ref, lon_ref, corner_ref, wide_ref
):
    devices, depth, _ = got_ref.shape
    rows, cols, chans = back_ref.shape
    cells = rows * cols
    feats = proj_ref.shape[0]
    per = LANES // cap
    halves = feats // LANES
    lane = lax.broadcasted_iota(jnp.int32, (META, LANES), 1)
    cell = lax.broadcasted_iota(jnp.int32, (cells, LANES), 0)
    total = jnp.zeros((cells, feats), F32)
    for pair in range(0, devices // per, 2):
        maps = []
        blocks = []
        for chunk in (pair, pair + 1):
            meta = got_ref[chunk * per, depth - META :, :].astype(F32)
            for group in range(1, per):
                other = got_ref[chunk * per + group, depth - META :, :].astype(F32)
                meta = jnp.where(lane // cap == group, other, meta)
            start = (meta[0:1] * cols + meta[1:2]).astype(jnp.int32)
            away = cell - start
            away = jnp.where(away < 0, away + cells, away)
            amount = jnp.zeros((cells, LANES), F32)
            for entry in range(4):
                amount = jnp.where(away == entry * step, meta[2 + entry : 3 + entry], amount)
            maps.append(amount.astype(BF16))
            block = got_ref[chunk * per : (chunk + 1) * per]
            blocks.append(
                jnp.concatenate(
                    [
                        block[:, half * cap : (half + 1) * cap, :].reshape(LANES, LANES)
                        for half in range(halves)
                    ],
                    axis=1,
                )
            )
        total = total + jnp.dot(
            jnp.concatenate(maps, axis=1),
            jnp.concatenate(blocks, axis=0),
            preferred_element_type=F32,
        )
    assim = jnp.dot(total.astype(BF16), proj_ref[...], preferred_element_type=F32)
    state = back_ref[...].astype(F32) + assim.reshape(rows, cols, chans)
    for g in range(chans // LANES):
        wide_ref[g] = state[:, cols - EDGE :, lanes_of(g)].reshape(rows * EDGE, LANES)
    state = state.astype(BF16)
    edge_ref[...] = state[rows - SHIFT :]
    inner_ref[...] = state[: rows - SHIFT]
    for x in range(SHIFT):
        for g in range(chans // LANES):
            column = wide_ref[g, pl.ds(EDGE - SHIFT + x, rows, stride=EDGE), :]
            lon_ref[x, :, lanes_of(g)] = column.astype(BF16)
    corner_ref[...] = state[rows - SHIFT :, cols - EDGE :, :]


def gelu(half):
    inner = half * (1.5957691216057308 + 0.285419265090401 * (half * half))
    return half + half * jnp.tanh(inner)


def put(wide_ref, row, start, value):
    for g in range(wide_ref.shape[0]):
        wide_ref[g, row, start : start + value.shape[0], :] = value[:, g * LANES : (g + 1) * LANES]


def shifted(wide_ref, taps_in, base, row, target):
    for g in range(wide_ref.shape[0]):
        for r in range(TAPS + 1):
            columns = pl.ds(base + r, TILE, stride=2)
            taps_in[g, r, target] = wide_ref[g, row, columns, :].astype(BF16)


def convolve(taps_in, taps_ref, tap_ref, spread_ref, layer, g, first, count):
    lanes = pl.ds(pl.multiple_of(g * LANES, LANES), LANES)
    for k in range(TAPS * TAPS):
        row = taps_ref[k, layer : layer + 1, lanes]
        tap_ref[k] = jnp.broadcast_to(row, (TILE, LANES)).astype(BF16)
    for p in range(2):
        total = None
        for b in range(TAPS):
            seen = taps_in[g, p + b, first : first + count + TAPS - 1]
            part = None
            for a in range(TAPS):
                term = seen[a : a + count] * tap_ref[a * TAPS + b]
                part = term if part is None else part + term
            total = part if total is None else total + part
        spread_ref[p, first : first + count, :, lanes] = total


def finish(taps_in, spread_ref, mix_ref, out_ref, layer, first, count):
    chans = mix_ref.shape[1]
    ones = jnp.ones((chans, LANES), BF16)
    for p in range(2):
        spread = spread_ref[p, first : first + count].reshape(count * TILE, chans)
        power = jnp.dot(spread * spread, ones, preferred_element_type=F32)
        scale = 0.5 * lax.rsqrt(power * (1.0 / chans) + 1e-05)
        mixed = jnp.dot(spread, mix_ref[layer], preferred_element_type=F32)
        for g in range(chans // LANES):
            moved = gelu(mixed[:, g * LANES : (g + 1) * LANES] * scale)
            center = taps_in[g, p + HALO, first + HALO : first + HALO + count].astype(F32)
            fresh = center + moved.reshape(count, TILE, LANES)
            for k in range(count):
                out_ref[g, first + k, pl.ds(p, TILE, stride=2), :] = fresh[k]


def row_of(out_ref, y):
    return jnp.concatenate([out_ref[g, y] for g in range(out_ref.shape[0])], axis=1)


def flat(ref):
    groups, rows, width, lanes = ref.shape
    return ref.reshape(groups, rows * width, lanes)


def lanes_of(g):
    return slice(g * LANES, (g + 1) * LANES)


def at_last():
    return lax.axis_index("lat") == lax.axis_size("lat") - 1


def inner_kernel(
    shrink,
    layer,
    edge_in,
    inner_in,
    lon_in,
    taps_ref,
    mix_ref,
    inner_ref,
    lon_ref,
    near_ref,
    wide_ref,
    taps_in,
    tap_ref,
    spread_ref,
    out_ref,
):
    cols = edge_in.shape[1]
    groups = wide_ref.shape[0]
    width = wide_ref.shape[2]
    own = inner_in.shape[0] - (HALO if shrink else 0)
    rows = own + SHIFT
    count = rows - SHIFT
    main = 0 if shrink else EDGE
    base = 0 if shrink else EDGE - SHIFT
    side = cols if shrink else base

    for g in range(groups):
        for x in range(SHIFT):
            column = lon_in[x, 0:rows, lanes_of(g)].astype(F32)
            flat(wide_ref)[g, pl.ds(side + x, rows, stride=width), :] = column

    def load(ref, place, y):
        put(wide_ref, place, main, ref[y].astype(F32))
        shifted(wide_ref, taps_in, base, place, place)

    @pl.loop(0, SHIFT, unroll=2)
    def _(y):
        load(edge_in, y if shrink else own + y, y)

    @pl.loop(0, own, unroll=2)
    def _(y):
        load(inner_in, y + SHIFT if shrink else y, y)

    near = rows - SHIFT if shrink else 0
    near_ref[...] = taps_in[:, :, near : near + SHIFT]

    @pl.loop(0, groups)
    def _(g):
        convolve(taps_in, taps_ref, tap_ref, spread_ref, layer, g, 0, count)

    finish(taps_in, spread_ref, mix_ref, out_ref, layer, 0, count)
    edge = cols - SHIFT if shrink else 0
    above = 0 if shrink else SHIFT
    for g in range(groups):
        for x in range(SHIFT):
            column = flat(out_ref)[g, pl.ds(edge + x, count, stride=cols), :]
            lon_ref[g, x, above : above + count, :] = column

    @pl.loop(0, count, unroll=2)
    def _(y):
        inner_ref[y] = row_of(out_ref, y).astype(BF16)

    if not shrink:

        @pl.when(at_last())
        def _():
            taps_in[:, :, rows:] = jnp.zeros((groups, TAPS + 1, HALO, TILE, LANES), BF16)

            @pl.loop(0, groups)
            def _(g):
                convolve(taps_in, taps_ref, tap_ref, spread_ref, layer, g, count, HALO)

            finish(taps_in, spread_ref, mix_ref, out_ref, layer, count, HALO)

        for k in range(HALO):
            inner_ref[count + k] = row_of(out_ref, count + k).astype(BF16)


def edge_kernel(
    shrink,
    final,
    layer,
    inner_in,
    lon_in,
    lat_in,
    corner_in,
    near_ref,
    inner_new,
    lon_new,
    taps_ref,
    mix_ref,
    *refs,
):
    if final:
        state_ref, wide_ref, taps_in, tap_ref, spread_ref, out_ref, spare_ref, mix_lon = refs
    else:
        edge_ref, lon_ref, corner_ref = refs[:3]
        wide_ref, taps_in, tap_ref, spread_ref, out_ref, spare_ref, mix_lon = refs[3:]
    cols = lat_in.shape[1]
    groups = wide_ref.shape[0]
    main = 0 if shrink else EDGE
    side = cols if shrink else 0
    base = 0 if shrink else EDGE - SHIFT
    last = at_last()
    top = lax.axis_index("lat") == 0
    own = SHIFT if not shrink else 0
    if shrink:
        for g in range(groups):
            for k in range(2):
                spare = lon_in[SHIFT + k, :, lanes_of(g)].astype(F32)
                spare_ref[g, k * TILE : (k + 1) * TILE, :] = spare
    for k in range(SHIFT):
        value, beside = lat_in[k].astype(F32), corner_in[k].astype(F32)
        if not shrink:
            value, beside = jnp.where(top, 0.0, value), jnp.where(top, 0.0, beside)
        elif k < HALO:
            kept = inner_in.shape[0] - HALO
            value = jnp.where(last, inner_in[kept + k].astype(F32), value)
            beside = beside[:SHIFT]
            extra = [spare_ref[g, pl.ds(k, SHIFT, stride=HALO), :] for g in range(groups)]
            beside = jnp.where(last, jnp.concatenate(extra, axis=1), beside)
        else:
            value, beside = jnp.where(last, 0.0, value), jnp.where(last, 0.0, beside)
        put(wide_ref, k, main, value)
        put(wide_ref, k, side, beside)
        shifted(wide_ref, taps_in, base, k, k if not shrink else k + SHIFT)
    taps_in[:, :, own : own + SHIFT] = near_ref[...]

    @pl.loop(0, groups)
    def _(g):
        convolve(taps_in, taps_ref, tap_ref, spread_ref, layer, g, 0, SHIFT)

    finish(taps_in, spread_ref, mix_ref, out_ref, layer, 0, SHIFT)
    kept = inner_new.shape[0]
    if final:
        for k in range(SHIFT):
            state_ref[kept + k] = row_of(out_ref, k).astype(BF16)
        state_ref[0:kept] = inner_new[...]
        return

    for k in range(SHIFT):
        value = row_of(out_ref, k)
        if not shrink and k < HALO:
            value = jnp.where(top, 0.0, value)
        edge_ref[k] = value.astype(BF16)
        corner_ref[k] = (value[cols - EDGE :] if shrink else value[:EDGE]).astype(BF16)
    edge = cols - SHIFT if shrink else 0
    place = TILE - SHIFT if shrink else 0
    for g in range(groups):
        for x in range(SHIFT):
            column = flat(out_ref)[g, pl.ds(edge + x, SHIFT, stride=cols), :]
            if not shrink:
                outside = lax.broadcasted_iota(jnp.int32, (SHIFT, LANES), 0) < HALO
                column = jnp.where(jnp.logical_and(top, outside), 0.0, column)
            mix_lon[g, x] = lon_new[g, x]
            mix_lon[g, x, place : place + SHIFT, :] = column
            lon_ref[x, :, lanes_of(g)] = mix_lon[g, x].astype(BF16)
    if not shrink:
        for k in range(HALO):
            value = inner_new[kept - HALO + k, 0:TILE, :].astype(F32)
            for g in range(groups):
                spare_ref[g, pl.ds(k, SHIFT, stride=HALO), :] = value[:SHIFT, lanes_of(g)]
        for g in range(groups):
            for k in range(2):
                spare = spare_ref[g, k * TILE : (k + 1) * TILE, :]
                lon_ref[SHIFT + k, :, lanes_of(g)] = spare.astype(BF16)


def call(kernel, out_shape, inputs, scratch=(), limit=VMEM_LIMIT, space=None, work=0):
    whole = pl.BlockSpec(memory_space=pltpu.VMEM)
    single = isinstance(out_shape, jax.ShapeDtypeStruct)
    spaces = space or (pltpu.VMEM,) * len(inputs)
    return pl.pallas_call(
        kernel,
        out_shape=out_shape,
        in_specs=[pl.BlockSpec(memory_space=s) for s in spaces],
        out_specs=whole if single else [whole] * len(out_shape),
        scratch_shapes=list(scratch),
        compiler_params=pltpu.CompilerParams(vmem_limit_bytes=limit),
        cost_estimate=pl.CostEstimate(flops=work, bytes_accessed=0, transcendentals=0),
    )(*inputs)


def held(*shape):
    return jax.ShapeDtypeStruct(shape, BF16)


def scratch_of(groups, seen, made, cols, chans):
    return (
        pltpu.VMEM((groups, seen, cols + EDGE, LANES), F32),
        pltpu.VMEM((groups, TAPS + 1, seen, TILE, LANES), BF16),
        pltpu.VMEM((TAPS * TAPS, TILE, LANES), BF16),
        pltpu.VMEM((2, made, TILE, chans), BF16),
        pltpu.VMEM((groups, made, cols, LANES), F32),
    )


def layer(state, lon_out, corner_out, taps, mix, number, shrink, final):
    edge, inner = state
    lat_in, lon_in, corner_in = exchange((edge, lon_out, corner_out), not shrink)
    cols, chans = edge.shape[1:]
    groups = chans // LANES
    rows = inner.shape[0] + SHIFT - (HALO if shrink else 0)
    spare = 0 if shrink else HALO
    made = rows - SHIFT + spare
    inner_new, lon_new, near = call(
        functools.partial(inner_kernel, shrink, number),
        (
            held(made, cols, chans),
            jax.ShapeDtypeStruct((groups, SHIFT, rows, LANES), F32),
            held(groups, TAPS + 1, SHIFT, TILE, LANES),
        ),
        (edge, inner, lon_in, taps, mix),
        scratch_of(groups, rows + spare, made, cols, chans),
        work=made * cols * chans * WORK,
    )
    if final:
        outs = held(made + SHIFT, cols, chans)
    else:
        outs = (
            held(SHIFT, cols, chans),
            held(SHIFT if shrink else EDGE, rows, chans),
            held(SHIFT, EDGE, chans),
        )
    outs = call(
        functools.partial(edge_kernel, shrink, final, number),
        outs,
        (inner, lon_in, lat_in, corner_in, near, inner_new, lon_new, taps, mix),
        scratch_of(groups, 2 * SHIFT, SHIFT, cols, chans)
        + (
            pltpu.VMEM((groups, 2 * TILE, LANES), F32),
            pltpu.VMEM((groups, SHIFT, rows, LANES), F32),
        ),
        work=SHIFT * cols * chans * WORK,
    )
    if final:
        return outs
    edge, lon_out, corner_out = outs
    return (edge, inner_new), lon_out, corner_out


def exchange(pieces, forward):
    lat, lon, corner = pieces
    count_lat = lax.axis_size("lat")
    count_lon = lax.axis_size("lon")
    along = [(i, (i + 1) % count_lat) for i in range(count_lat)]
    around = [(j, (j + 1) % count_lon) for j in range(count_lon)]
    across = [
        (i * count_lon + j, ni * count_lon + nj) for i, ni in along for j, nj in around
    ]
    if not forward:
        along, around, across = ([(t, s) for s, t in p] for p in (along, around, across))
    lon = lax.ppermute(lon, "lon", around)
    lat = lax.ppermute(lat, "lat", along)
    corner = lax.ppermute(corner, ("lat", "lon"), across)
    return lat, lon, corner


def body(
    background, observations, destination, footprint, weights, obs_proj, depth_w, point_w, gains
):
    rows, cols, chans = background.shape
    devices = lax.axis_size("lat") * lax.axis_size("lon")
    obs_rows, feats = observations.shape
    cap = 2 * obs_rows // devices
    depth = cap * (feats // LANES) + META
    foot_count = footprint.shape[1]
    send = call(
        functools.partial(pack_kernel, cap, cols),
        jax.ShapeDtypeStruct((devices, depth, LANES), BF16),
        (destination.T, footprint.T, weights.T, observations),
        (
            pltpu.VMEM((1, obs_rows), jnp.int32),
            pltpu.VMEM((foot_count, obs_rows), jnp.int32),
            pltpu.VMEM((foot_count, obs_rows), BF16),
            pltpu.VMEM((obs_rows, feats), BF16),
            pltpu.SemaphoreType.DMA((4,)),
        ),
        PACK_LIMIT,
        (pltpu.HBM,) * 4,
    )
    got = lax.all_to_all(send, ("lat", "lon"), split_axis=0, concat_axis=0, tiled=True)
    layers = depth_w.shape[0]
    taps = depth_w.transpose(1, 2, 0, 3).reshape(TAPS * TAPS, layers, chans)
    mix = (gains[:, :, None] * point_w.astype(F32)).astype(BF16)
    proj, back = call(
        fetch_kernel,
        (held(*obs_proj.shape), held(*background.shape)),
        (obs_proj, background),
        (pltpu.SemaphoreType.DMA((2,)),),
        space=(pltpu.HBM, pltpu.HBM),
    )
    got, mix, proj, back = lax.optimization_barrier((got, mix, proj, back))
    edge, inner, lon_out, corner_out = call(
        functools.partial(assim_kernel, cap, cols + 1),
        (
            held(SHIFT, cols, chans),
            held(rows - SHIFT, cols, chans),
            held(SHIFT, rows, chans),
            held(SHIFT, EDGE, chans),
        ),
        (got, proj, back),
        (pltpu.VMEM((chans // LANES, rows * EDGE, LANES), F32),),
    )
    state = (edge, inner)
    for n in range(layers - 1):
        state, lon_out, corner_out = layer(
            state, lon_out, corner_out, taps, mix, n, n % 2 == 1, False
        )
    n = layers - 1
    return layer(state, lon_out, corner_out, taps, mix, n, n % 2 == 1, True)


def solution(mesh):
    placed = (
        P("lat", "lon", None),
        P(("lat", "lon"), None),
        P(("lat", "lon"), None),
        P(("lat", "lon"), None),
        P(("lat", "lon"), None),
        P(),
        P(),
        P(),
        P(),
    )
    return jax.shard_map(
        body, mesh=mesh, in_specs=placed, out_specs=P("lat", "lon", None), check_vma=False
    )
```

```python
import functools

import jax
import jax.numpy as jnp
from jax import lax
from jax.experimental import pallas as pl
from jax.experimental.pallas import tpu as pltpu
from jax.sharding import PartitionSpec as P

LANES = 128
META = 8
TAPS = 7
HALO = 3
SHIFT = 2 * HALO
EDGE = 8
TILE = 16
CHUNK = 4
WORK = 5000
VMEM_LIMIT = 24 * 1024 * 1024
PACK_LIMIT = 58 * 1024 * 1024
BF16 = jnp.bfloat16
F32 = jnp.float32


def pack_kernel(cap, cols, dest_hbm, foot_hbm, weights_hbm, obs_hbm, send_ref, dest_ref, foot_ref, weights_ref, obs_ref, sems):
    copies = [
        pltpu.make_async_copy(source, target, sems.at[k])
        for k, (source, target) in enumerate(
            (
                (dest_hbm, dest_ref),
                (obs_hbm, obs_ref),
                (foot_hbm, foot_ref),
                (weights_hbm, weights_ref),
            )
        )
    ]
    for copy in copies:
        copy.start()
    devices = send_ref.shape[0]
    obs_rows = obs_ref.shape[0]
    per = LANES // cap
    upper = lax.broadcasted_iota(jnp.int32, (LANES, LANES), 0) <= lax.broadcasted_iota(
        jnp.int32, (LANES, LANES), 1
    )
    upper = jnp.where(upper, 1.0, 0.0).astype(BF16)
    ids = lax.broadcasted_iota(jnp.int32, (devices, obs_rows), 0)
    copies[0].wait()
    member = jnp.where(ids == dest_ref[...], 1.0, 0.0)
    seen = jnp.zeros((devices, 1), F32)
    ranks = []
    for first in range(0, obs_rows, LANES):
        part = member[:, first : first + LANES]
        count = jnp.dot(part.astype(BF16), upper, preferred_element_type=F32) + seen
        ranks.append(jnp.sum((count - 1.0) * part, axis=0, keepdims=True))
        seen = count[:, LANES - 1 :]
    rank = jnp.concatenate(ranks, axis=1).astype(jnp.int32)
    slot = lax.broadcasted_iota(jnp.int32, (cap, obs_rows), 0)
    ranked = jnp.where(slot == rank, 1.0, 0.0).astype(BF16).reshape(cap // TILE, TILE, obs_rows)
    for copy in copies[1:]:
        copy.wait()
    start = foot_ref[0:1, :]
    meta = jnp.concatenate(
        [
            lax.div(start, cols).astype(F32),
            lax.rem(start, cols).astype(F32),
            weights_ref[...].astype(F32),
            jnp.zeros((META - 2 - weights_ref.shape[0], obs_rows), F32),
        ],
        axis=0,
    ).astype(BF16)
    obs = obs_ref[...]
    lane = lax.broadcasted_iota(jnp.int32, (META, LANES), 1)
    count = min(512, devices * cap) // cap
    for first in range(0, devices, count):
        parts = []
        for d in range(first, first + count):
            mine = jnp.broadcast_to(member[d : d + 1], (TILE, obs_rows)).astype(BF16)
            parts.append((ranked * mine[None]).reshape(cap, obs_rows))
        chosen = jnp.concatenate(parts, axis=0)
        feats = jnp.dot(chosen, obs, preferred_element_type=F32).astype(BF16)
        placed = lax.dot_general(
            meta, chosen, (((1,), (1,)), ((), ())), preferred_element_type=F32
        )
        for half in range(feats.shape[1] // LANES):
            piece = feats[:, half * LANES : (half + 1) * LANES].reshape(count, cap, LANES)
            send_ref[first : first + count, half * cap : (half + 1) * cap, :] = piece
        base = send_ref.shape[1] - META
        for chunk in range(count // per):
            values = placed[:, chunk * LANES : (chunk + 1) * LANES]
            turned = [values] + [pltpu.roll(values, k * cap, 1) for k in range(1, per)]
            for own in range(per):
                wide = turned[0]
                for group in range(per):
                    wide = jnp.where(lane // cap == group, turned[(group - own) % per], wide)
                send_ref[first + chunk * per + own, base:, :] = wide.astype(BF16)


def fetch_kernel(proj_hbm, back_hbm, proj_ref, back_ref, sems):
    copies = (
        pltpu.make_async_copy(proj_hbm, proj_ref, sems.at[0]),
        pltpu.make_async_copy(back_hbm, back_ref, sems.at[1]),
    )
    for copy in copies:
        copy.start()
    for copy in copies:
        copy.wait()


def assim_kernel(
    cap, step, got_ref, proj_ref, back_ref, edge_ref, inner_ref, lon_ref, corner_ref, wide_ref
):
    devices, depth, _ = got_ref.shape
    rows, cols, chans = back_ref.shape
    cells = rows * cols
    feats = proj_ref.shape[0]
    per = LANES // cap
    halves = feats // LANES
    lane = lax.broadcasted_iota(jnp.int32, (META, LANES), 1)
    cell = lax.broadcasted_iota(jnp.int32, (cells, LANES), 0)
    total = jnp.zeros((cells, feats), F32)
    for pair in range(0, devices // per, 2):
        maps = []
        blocks = []
        for chunk in (pair, pair + 1):
            meta = got_ref[chunk * per, depth - META :, :].astype(F32)
            for group in range(1, per):
                other = got_ref[chunk * per + group, depth - META :, :].astype(F32)
                meta = jnp.where(lane // cap == group, other, meta)
            start = (meta[0:1] * cols + meta[1:2]).astype(jnp.int32)
            away = cell - start
            away = jnp.where(away < 0, away + cells, away)
            amount = jnp.zeros((cells, LANES), F32)
            for entry in range(4):
                amount = jnp.where(away == entry * step, meta[2 + entry : 3 + entry], amount)
            maps.append(amount.astype(BF16))
            block = got_ref[chunk * per : (chunk + 1) * per]
            blocks.append(
                jnp.concatenate(
                    [
                        block[:, half * cap : (half + 1) * cap, :].reshape(LANES, LANES)
                        for half in range(halves)
                    ],
                    axis=1,
                )
            )
        total = total + jnp.dot(
            jnp.concatenate(maps, axis=1),
            jnp.concatenate(blocks, axis=0),
            preferred_element_type=F32,
        )
    field = total.astype(BF16)
    for y0 in range(0, rows, CHUNK):
        assim = jnp.dot(
            field[y0 * cols : (y0 + CHUNK) * cols], proj_ref[...], preferred_element_type=F32
        )
        state = back_ref[y0 : y0 + CHUNK].astype(F32) + assim.reshape(CHUNK, cols, chans)
        side = state[:, cols - EDGE :, :]
        for g in range(chans // LANES):
            wide_ref[g, y0 * EDGE : (y0 + CHUNK) * EDGE] = side[:, :, lanes_of(g)].reshape(
                CHUNK * EDGE, LANES
            )
        state = state.astype(BF16)
        for k in range(CHUNK):
            y = y0 + k
            if y < rows - SHIFT:
                inner_ref[y] = state[k]
            else:
                edge_ref[y - (rows - SHIFT)] = state[k]
                corner_ref[y - (rows - SHIFT)] = state[k, cols - EDGE :, :]
    for x in range(SHIFT):
        for g in range(chans // LANES):
            column = wide_ref[g, pl.ds(EDGE - SHIFT + x, rows, stride=EDGE), :]
            lon_ref[x, :, lanes_of(g)] = column.astype(BF16)


def gelu(half):
    inner = half * (1.5957691216057308 + 0.285419265090401 * (half * half))
    return half + half * jnp.tanh(inner)


def put(wide_ref, row, start, value):
    for g in range(wide_ref.shape[0]):
        wide_ref[g, row, start : start + value.shape[0], :] = value[:, g * LANES : (g + 1) * LANES]


def shifted(wide_ref, taps_in, base, row, target):
    for g in range(wide_ref.shape[0]):
        for r in range(TAPS + 1):
            columns = pl.ds(base + r, TILE, stride=2)
            taps_in[g, r, target] = wide_ref[g, row, columns, :].astype(BF16)


def convolve(taps_in, taps_ref, tap_ref, spread_ref, layer, g, first, count):
    lanes = load_taps(taps_ref, tap_ref, layer, g)
    for p in range(2):
        total = None
        for b in range(TAPS):
            seen = taps_in[g, p + b, first : first + count + TAPS - 1]
            part = None
            for a in range(TAPS):
                term = seen[a : a + count] * tap_ref[a * TAPS + b]
                part = term if part is None else part + term
            total = part if total is None else total + part
        spread_ref[p, first : first + count, :, lanes] = total


def own_row(shrink, row):
    if shrink:
        return row if row < SHIFT else None
    return row - SHIFT if row >= SHIFT else None


def partial_sums(taps_in, tap_ref, g, p, k, rows):
    total = None
    for b in range(TAPS):
        for a in range(TAPS):
            row = rows(k + a)
            if row is not None:
                term = taps_in[g, p + b, row] * tap_ref[a * TAPS + b]
                total = term if total is None else total + term
    return total


def load_taps(taps_ref, tap_ref, layer, g):
    lanes = pl.ds(pl.multiple_of(g * LANES, LANES), LANES)
    for k in range(TAPS * TAPS):
        row = taps_ref[k, layer : layer + 1, lanes]
        tap_ref[k] = jnp.broadcast_to(row, (TILE, LANES)).astype(BF16)
    return lanes


def finish(taps_in, spread_ref, mix_ref, out_ref, layer, first, count):
    chans = mix_ref.shape[1]
    ones = jnp.ones((chans, LANES), BF16)
    for p in range(2):
        spread = spread_ref[p, first : first + count].reshape(count * TILE, chans)
        power = jnp.dot(spread * spread, ones, preferred_element_type=F32)
        scale = 0.5 * lax.rsqrt(power * (1.0 / chans) + 1e-05)
        mixed = jnp.dot(spread, mix_ref[layer], preferred_element_type=F32)
        for g in range(chans // LANES):
            moved = gelu(mixed[:, g * LANES : (g + 1) * LANES] * scale)
            center = taps_in[g, p + HALO, first + HALO : first + HALO + count].astype(F32)
            fresh = center + moved.reshape(count, TILE, LANES)
            for k in range(count):
                out_ref[g, first + k, pl.ds(p, TILE, stride=2), :] = fresh[k]


def row_of(out_ref, y):
    return jnp.concatenate([out_ref[g, y] for g in range(out_ref.shape[0])], axis=1)


def flat(ref):
    groups, rows, width, lanes = ref.shape
    return ref.reshape(groups, rows * width, lanes)


def lanes_of(g):
    return slice(g * LANES, (g + 1) * LANES)


def at_last():
    return lax.axis_index("lat") == lax.axis_size("lat") - 1


def inner_kernel(
    shrink,
    layer,
    edge_in,
    inner_in,
    lon_in,
    taps_ref,
    mix_ref,
    inner_ref,
    lon_ref,
    near_ref,
    part_ref,
    wide_ref,
    taps_in,
    tap_ref,
    spread_ref,
    out_ref,
):
    cols = edge_in.shape[1]
    groups = wide_ref.shape[0]
    width = wide_ref.shape[2]
    own = inner_in.shape[0] - (HALO if shrink else 0)
    rows = own + SHIFT
    count = rows - SHIFT
    main = 0 if shrink else EDGE
    base = 0 if shrink else EDGE - SHIFT
    side = cols if shrink else base

    for g in range(groups):
        for x in range(SHIFT):
            column = lon_in[x, 0:rows, lanes_of(g)].astype(F32)
            flat(wide_ref)[g, pl.ds(side + x, rows, stride=width), :] = column

    def load(ref, place, y):
        put(wide_ref, place, main, ref[y].astype(F32))
        shifted(wide_ref, taps_in, base, place, place)

    @pl.loop(0, SHIFT, unroll=2)
    def _(y):
        load(edge_in, y if shrink else own + y, y)

    @pl.loop(0, own, unroll=2)
    def _(y):
        load(inner_in, y + SHIFT if shrink else y, y)

    near = rows - SHIFT if shrink else 0
    centers = near + (HALO if shrink else 0)
    near_ref[...] = taps_in[:, HALO : HALO + 2, centers : centers + HALO]

    def near_row(row):
        own_one = own_row(shrink, row)
        return None if own_one is None else near + own_one

    @pl.loop(0, groups)
    def _(g):
        convolve(taps_in, taps_ref, tap_ref, spread_ref, layer, g, 0, count)
        lanes = pl.ds(pl.multiple_of(g * LANES, LANES), LANES)
        for p in range(2):
            for k in range(SHIFT):
                part_ref[p, k, :, lanes] = partial_sums(taps_in, tap_ref, g, p, k, near_row)

    finish(taps_in, spread_ref, mix_ref, out_ref, layer, 0, count)
    edge = cols - SHIFT if shrink else 0
    above = 0 if shrink else SHIFT
    for g in range(groups):
        for x in range(SHIFT):
            column = flat(out_ref)[g, pl.ds(edge + x, count, stride=cols), :]
            lon_ref[g, x, above : above + count, :] = column

    @pl.loop(0, count, unroll=2)
    def _(y):
        inner_ref[y] = row_of(out_ref, y).astype(BF16)

    if not shrink:

        @pl.when(at_last())
        def _():
            taps_in[:, :, rows:] = jnp.zeros((groups, TAPS + 1, HALO, TILE, LANES), BF16)

            @pl.loop(0, groups)
            def _(g):
                convolve(taps_in, taps_ref, tap_ref, spread_ref, layer, g, count, HALO)

            finish(taps_in, spread_ref, mix_ref, out_ref, layer, count, HALO)

        for k in range(HALO):
            inner_ref[count + k] = row_of(out_ref, count + k).astype(BF16)


def edge_kernel(
    shrink,
    final,
    layer,
    inner_in,
    lon_in,
    lat_in,
    corner_in,
    near_ref,
    part_ref,
    inner_new,
    lon_new,
    taps_ref,
    mix_ref,
    *refs,
):
    if final:
        state_ref, wide_ref, taps_in, tap_ref, spread_ref, out_ref, spare_ref, mix_lon = refs
    else:
        edge_ref, lon_ref, corner_ref = refs[:3]
        wide_ref, taps_in, tap_ref, spread_ref, out_ref, spare_ref, mix_lon = refs[3:]
    cols = lat_in.shape[1]
    groups = wide_ref.shape[0]
    main = 0 if shrink else EDGE
    side = cols if shrink else 0
    base = 0 if shrink else EDGE - SHIFT
    last = at_last()
    top = lax.axis_index("lat") == 0
    own = SHIFT if not shrink else 0
    if shrink:
        for g in range(groups):
            for k in range(2):
                spare = lon_in[SHIFT + k, :, lanes_of(g)].astype(F32)
                spare_ref[g, k * TILE : (k + 1) * TILE, :] = spare
    for k in range(SHIFT):
        value, beside = lat_in[k].astype(F32), corner_in[k].astype(F32)
        if not shrink:
            value, beside = jnp.where(top, 0.0, value), jnp.where(top, 0.0, beside)
        elif k < HALO:
            kept = inner_in.shape[0] - HALO
            value = jnp.where(last, inner_in[kept + k].astype(F32), value)
            beside = beside[:SHIFT]
            extra = [spare_ref[g, pl.ds(k, SHIFT, stride=HALO), :] for g in range(groups)]
            beside = jnp.where(last, jnp.concatenate(extra, axis=1), beside)
        else:
            value, beside = jnp.where(last, 0.0, value), jnp.where(last, 0.0, beside)
        put(wide_ref, k, main, value)
        put(wide_ref, k, side, beside)
        shifted(wide_ref, taps_in, base, k, k if not shrink else k + SHIFT)
    centers = own + (HALO if shrink else 0)
    taps_in[:, HALO : HALO + 2, centers : centers + HALO] = near_ref[...]

    def halo_row(row):
        return row if own_row(shrink, row) is None else None

    @pl.loop(0, groups)
    def _(g):
        lanes = load_taps(taps_ref, tap_ref, layer, g)
        for p in range(2):
            for k in range(SHIFT):
                total = partial_sums(taps_in, tap_ref, g, p, k, halo_row)
                spread_ref[p, k, :, lanes] = total + part_ref[p, k, :, lanes]

    finish(taps_in, spread_ref, mix_ref, out_ref, layer, 0, SHIFT)
    kept = inner_new.shape[0]
    if final:
        for k in range(SHIFT):
            state_ref[kept + k] = row_of(out_ref, k).astype(BF16)
        state_ref[0:kept] = inner_new[...]
        return

    for k in range(SHIFT):
        value = row_of(out_ref, k)
        if not shrink and k < HALO:
            value = jnp.where(top, 0.0, value)
        edge_ref[k] = value.astype(BF16)
        corner_ref[k] = (value[cols - EDGE :] if shrink else value[:EDGE]).astype(BF16)
    edge = cols - SHIFT if shrink else 0
    place = TILE - SHIFT if shrink else 0
    for g in range(groups):
        for x in range(SHIFT):
            column = flat(out_ref)[g, pl.ds(edge + x, SHIFT, stride=cols), :]
            if not shrink:
                outside = lax.broadcasted_iota(jnp.int32, (SHIFT, LANES), 0) < HALO
                column = jnp.where(jnp.logical_and(top, outside), 0.0, column)
            mix_lon[g, x] = lon_new[g, x]
            mix_lon[g, x, place : place + SHIFT, :] = column
            lon_ref[x, :, lanes_of(g)] = mix_lon[g, x].astype(BF16)
    if not shrink:
        for k in range(HALO):
            value = inner_new[kept - HALO + k, 0:TILE, :].astype(F32)
            for g in range(groups):
                spare_ref[g, pl.ds(k, SHIFT, stride=HALO), :] = value[:SHIFT, lanes_of(g)]
        for g in range(groups):
            for k in range(2):
                spare = spare_ref[g, k * TILE : (k + 1) * TILE, :]
                lon_ref[SHIFT + k, :, lanes_of(g)] = spare.astype(BF16)


def call(kernel, out_shape, inputs, scratch=(), limit=VMEM_LIMIT, space=None, work=0):
    whole = pl.BlockSpec(memory_space=pltpu.VMEM)
    single = isinstance(out_shape, jax.ShapeDtypeStruct)
    spaces = space or (pltpu.VMEM,) * len(inputs)
    return pl.pallas_call(
        kernel,
        out_shape=out_shape,
        in_specs=[pl.BlockSpec(memory_space=s) for s in spaces],
        out_specs=whole if single else [whole] * len(out_shape),
        scratch_shapes=list(scratch),
        compiler_params=pltpu.CompilerParams(vmem_limit_bytes=limit),
        cost_estimate=pl.CostEstimate(flops=work, bytes_accessed=0, transcendentals=0),
    )(*inputs)


def held(*shape):
    return jax.ShapeDtypeStruct(shape, BF16)


def scratch_of(groups, seen, made, cols, chans):
    return (
        pltpu.VMEM((groups, seen, cols + EDGE, LANES), F32),
        pltpu.VMEM((groups, TAPS + 1, seen, TILE, LANES), BF16),
        pltpu.VMEM((TAPS * TAPS, TILE, LANES), BF16),
        pltpu.VMEM((2, made, TILE, chans), BF16),
        pltpu.VMEM((groups, made, cols, LANES), F32),
    )


def layer(state, lon_out, corner_out, taps, mix, number, shrink, final):
    edge, inner = state
    lat_in, lon_in, corner_in = exchange((edge, lon_out, corner_out), not shrink)
    cols, chans = edge.shape[1:]
    groups = chans // LANES
    rows = inner.shape[0] + SHIFT - (HALO if shrink else 0)
    spare = 0 if shrink else HALO
    made = rows - SHIFT + spare
    inner_new, lon_new, near, part = call(
        functools.partial(inner_kernel, shrink, number),
        (
            held(made, cols, chans),
            jax.ShapeDtypeStruct((groups, SHIFT, rows, LANES), F32),
            held(groups, 2, HALO, TILE, LANES),
            held(2, SHIFT, TILE, chans),
        ),
        (edge, inner, lon_in, taps, mix),
        scratch_of(groups, rows + spare, made, cols, chans),
        work=made * cols * chans * WORK,
    )
    if final:
        outs = held(made + SHIFT, cols, chans)
    else:
        outs = (
            held(SHIFT, cols, chans),
            held(SHIFT if shrink else EDGE, rows, chans),
            held(SHIFT, EDGE, chans),
        )
    outs = call(
        functools.partial(edge_kernel, shrink, final, number),
        outs,
        (inner, lon_in, lat_in, corner_in, near, part, inner_new, lon_new, taps, mix),
        scratch_of(groups, 2 * SHIFT, SHIFT, cols, chans)
        + (
            pltpu.VMEM((groups, 2 * TILE, LANES), F32),
            pltpu.VMEM((groups, SHIFT, rows, LANES), F32),
        ),
        work=SHIFT * cols * chans * WORK,
    )
    if final:
        return outs
    edge, lon_out, corner_out = outs
    return (edge, inner_new), lon_out, corner_out


def exchange(pieces, forward):
    lat, lon, corner = pieces
    count_lat = lax.axis_size("lat")
    count_lon = lax.axis_size("lon")
    along = [(i, (i + 1) % count_lat) for i in range(count_lat)]
    around = [(j, (j + 1) % count_lon) for j in range(count_lon)]
    across = [
        (i * count_lon + j, ni * count_lon + nj) for i, ni in along for j, nj in around
    ]
    if not forward:
        along, around, across = ([(t, s) for s, t in p] for p in (along, around, across))
    lon = lax.ppermute(lon, "lon", around)
    lat = lax.ppermute(lat, "lat", along)
    corner = lax.ppermute(corner, ("lat", "lon"), across)
    return lat, lon, corner


def body(
    background, observations, destination, footprint, weights, obs_proj, depth_w, point_w, gains
):
    rows, cols, chans = background.shape
    devices = lax.axis_size("lat") * lax.axis_size("lon")
    obs_rows, feats = observations.shape
    cap = 2 * obs_rows // devices
    depth = cap * (feats // LANES) + META
    foot_count = footprint.shape[1]
    send = call(
        functools.partial(pack_kernel, cap, cols),
        jax.ShapeDtypeStruct((devices, depth, LANES), BF16),
        (destination.T, footprint.T, weights.T, observations),
        (
            pltpu.VMEM((1, obs_rows), jnp.int32),
            pltpu.VMEM((foot_count, obs_rows), jnp.int32),
            pltpu.VMEM((foot_count, obs_rows), BF16),
            pltpu.VMEM((obs_rows, feats), BF16),
            pltpu.SemaphoreType.DMA((4,)),
        ),
        PACK_LIMIT,
        (pltpu.HBM,) * 4,
    )
    got = lax.all_to_all(send, ("lat", "lon"), split_axis=0, concat_axis=0, tiled=True)
    layers = depth_w.shape[0]
    taps = depth_w.transpose(1, 2, 0, 3).reshape(TAPS * TAPS, layers, chans)
    mix = (gains[:, :, None] * point_w.astype(F32)).astype(BF16)
    proj, back = call(
        fetch_kernel,
        (held(*obs_proj.shape), held(*background.shape)),
        (obs_proj, background),
        (pltpu.SemaphoreType.DMA((2,)),),
        space=(pltpu.HBM, pltpu.HBM),
    )
    got, mix, proj, back = lax.optimization_barrier((got, mix, proj, back))
    edge, inner, lon_out, corner_out = call(
        functools.partial(assim_kernel, cap, cols + 1),
        (
            held(SHIFT, cols, chans),
            held(rows - SHIFT, cols, chans),
            held(SHIFT, rows, chans),
            held(SHIFT, EDGE, chans),
        ),
        (got, proj, back),
        (pltpu.VMEM((chans // LANES, rows * EDGE, LANES), F32),),
    )
    state = (edge, inner)
    for n in range(layers - 1):
        state, lon_out, corner_out = layer(
            state, lon_out, corner_out, taps, mix, n, n % 2 == 1, False
        )
    n = layers - 1
    return layer(state, lon_out, corner_out, taps, mix, n, n % 2 == 1, True)


def solution(mesh):
    placed = (
        P("lat", "lon", None),
        P(("lat", "lon"), None),
        P(("lat", "lon"), None),
        P(("lat", "lon"), None),
        P(("lat", "lon"), None),
        P(),
        P(),
        P(),
        P(),
    )
    return jax.shard_map(
        body, mesh=mesh, in_specs=placed, out_specs=P("lat", "lon", None), check_vma=False
    )
```

```python
import functools

import jax
import jax.numpy as jnp
from jax import lax
from jax.experimental import pallas as pl
from jax.experimental.pallas import tpu as pltpu
from jax.sharding import PartitionSpec as P

LANES = 128
META = 8
TAPS = 7
HALO = 3
SHIFT = 2 * HALO
EDGE = 8
TILE = 16
WORK = 5000
VMEM_LIMIT = 24 * 1024 * 1024
PACK_LIMIT = 58 * 1024 * 1024
BF16 = jnp.bfloat16
F32 = jnp.float32


def pack_kernel(cap, cols, dest_hbm, foot_hbm, weights_hbm, obs_hbm, send_ref, dest_ref, foot_ref, weights_ref, obs_ref, sems):
    copies = [
        pltpu.make_async_copy(source, target, sems.at[k])
        for k, (source, target) in enumerate(
            (
                (dest_hbm, dest_ref),
                (obs_hbm, obs_ref),
                (foot_hbm, foot_ref),
                (weights_hbm, weights_ref),
            )
        )
    ]
    for copy in copies:
        copy.start()
    devices = send_ref.shape[0]
    obs_rows = obs_ref.shape[0]
    per = LANES // cap
    upper = lax.broadcasted_iota(jnp.int32, (LANES, LANES), 0) <= lax.broadcasted_iota(
        jnp.int32, (LANES, LANES), 1
    )
    upper = jnp.where(upper, 1.0, 0.0).astype(BF16)
    ids = lax.broadcasted_iota(jnp.int32, (devices, obs_rows), 0)
    copies[0].wait()
    member = jnp.where(ids == dest_ref[...], 1.0, 0.0)
    seen = jnp.zeros((devices, 1), F32)
    ranks = []
    for first in range(0, obs_rows, LANES):
        part = member[:, first : first + LANES]
        count = jnp.dot(part.astype(BF16), upper, preferred_element_type=F32) + seen
        ranks.append(jnp.sum((count - 1.0) * part, axis=0, keepdims=True))
        seen = count[:, LANES - 1 :]
    rank = jnp.concatenate(ranks, axis=1).astype(jnp.int32)
    slot = lax.broadcasted_iota(jnp.int32, (cap, obs_rows), 0)
    ranked = jnp.where(slot == rank, 1.0, 0.0).astype(BF16).reshape(cap // TILE, TILE, obs_rows)
    for copy in copies[1:]:
        copy.wait()
    start = foot_ref[0:1, :]
    meta = jnp.concatenate(
        [
            lax.div(start, cols).astype(F32),
            lax.rem(start, cols).astype(F32),
            weights_ref[...].astype(F32),
            jnp.zeros((META - 2 - weights_ref.shape[0], obs_rows), F32),
        ],
        axis=0,
    ).astype(BF16)
    obs = obs_ref[...]
    lane = lax.broadcasted_iota(jnp.int32, (META, LANES), 1)
    count = min(512, devices * cap) // cap
    for first in range(0, devices, count):
        parts = []
        for d in range(first, first + count):
            mine = jnp.broadcast_to(member[d : d + 1], (TILE, obs_rows)).astype(BF16)
            parts.append((ranked * mine[None]).reshape(cap, obs_rows))
        chosen = jnp.concatenate(parts, axis=0)
        feats = jnp.dot(chosen, obs, preferred_element_type=F32).astype(BF16)
        placed = lax.dot_general(
            meta, chosen, (((1,), (1,)), ((), ())), preferred_element_type=F32
        )
        for half in range(feats.shape[1] // LANES):
            piece = feats[:, half * LANES : (half + 1) * LANES].reshape(count, cap, LANES)
            send_ref[first : first + count, half * cap : (half + 1) * cap, :] = piece
        base = send_ref.shape[1] - META
        for chunk in range(count // per):
            values = placed[:, chunk * LANES : (chunk + 1) * LANES]
            turned = [values] + [pltpu.roll(values, k * cap, 1) for k in range(1, per)]
            for own in range(per):
                wide = turned[0]
                for group in range(per):
                    wide = jnp.where(lane // cap == group, turned[(group - own) % per], wide)
                send_ref[first + chunk * per + own, base:, :] = wide.astype(BF16)


def fetch_kernel(proj_hbm, back_hbm, proj_ref, back_ref, sems):
    copies = (
        pltpu.make_async_copy(proj_hbm, proj_ref, sems.at[0]),
        pltpu.make_async_copy(back_hbm, back_ref, sems.at[1]),
    )
    for copy in copies:
        copy.start()
    for copy in copies:
        copy.wait()


def assim_kernel(
    cap, step, got_ref, proj_ref, back_ref, edge_ref, inner_ref, lon_ref, corner_ref, wide_ref
):
    devices, depth, _ = got_ref.shape
    rows, cols, chans = back_ref.shape
    cells = rows * cols
    feats = proj_ref.shape[0]
    per = LANES // cap
    halves = feats // LANES
    lane = lax.broadcasted_iota(jnp.int32, (META, LANES), 1)
    cell = lax.broadcasted_iota(jnp.int32, (cells, LANES), 0)
    total = jnp.zeros((cells, feats), F32)
    for pair in range(0, devices // per, 2):
        maps = []
        blocks = []
        for chunk in (pair, pair + 1):
            meta = got_ref[chunk * per, depth - META :, :].astype(F32)
            for group in range(1, per):
                other = got_ref[chunk * per + group, depth - META :, :].astype(F32)
                meta = jnp.where(lane // cap == group, other, meta)
            start = (meta[0:1] * cols + meta[1:2]).astype(jnp.int32)
            away = cell - start
            away = jnp.where(away < 0, away + cells, away)
            amount = jnp.zeros((cells, LANES), F32)
            for entry in range(4):
                amount = jnp.where(away == entry * step, meta[2 + entry : 3 + entry], amount)
            maps.append(amount.astype(BF16))
            block = got_ref[chunk * per : (chunk + 1) * per]
            blocks.append(
                jnp.concatenate(
                    [
                        block[:, half * cap : (half + 1) * cap, :].reshape(LANES, LANES)
                        for half in range(halves)
                    ],
                    axis=1,
                )
            )
        total = total + jnp.dot(
            jnp.concatenate(maps, axis=1),
            jnp.concatenate(blocks, axis=0),
            preferred_element_type=F32,
        )
    assim = jnp.dot(total.astype(BF16), proj_ref[...], preferred_element_type=F32)
    state = back_ref[...].astype(F32) + assim.reshape(rows, cols, chans)
    for g in range(chans // LANES):
        wide_ref[g] = state[:, cols - EDGE :, lanes_of(g)].reshape(rows * EDGE, LANES)
    state = state.astype(BF16)
    edge_ref[...] = state[rows - SHIFT :]
    inner_ref[...] = state[: rows - SHIFT]
    for x in range(SHIFT):
        for g in range(chans // LANES):
            column = wide_ref[g, pl.ds(EDGE - SHIFT + x, rows, stride=EDGE), :]
            lon_ref[x, :, lanes_of(g)] = column.astype(BF16)
    corner_ref[...] = state[rows - SHIFT :, cols - EDGE :, :]


def gelu(half):
    inner = half * (1.5957691216057308 + 0.285419265090401 * (half * half))
    return half + half * jnp.tanh(inner)


def put(wide_ref, row, start, value):
    for g in range(wide_ref.shape[0]):
        wide_ref[g, row, start : start + value.shape[0], :] = value[:, g * LANES : (g + 1) * LANES]


def shifted(wide_ref, taps_in, base, row, target):
    for g in range(wide_ref.shape[0]):
        for r in range(TAPS + 1):
            columns = pl.ds(base + r, TILE, stride=2)
            taps_in[g, r, target] = wide_ref[g, row, columns, :].astype(BF16)


def convolve(taps_in, taps_ref, gains_ref, tap_ref, spread_ref, layer, g, first, count):
    lanes = pl.ds(pl.multiple_of(g * LANES, LANES), LANES)
    gain = gains_ref[layer : layer + 1, lanes]
    for k in range(TAPS * TAPS):
        row = taps_ref[k, layer : layer + 1, lanes] * gain
        tap_ref[k] = jnp.broadcast_to(row, (TILE, LANES)).astype(BF16)
    for p in range(2):
        total = None
        for b in range(TAPS):
            seen = taps_in[g, p + b, first : first + count + TAPS - 1]
            part = None
            for a in range(TAPS):
                term = seen[a : a + count] * tap_ref[a * TAPS + b]
                part = term if part is None else part + term
            total = part if total is None else total + part
        spread_ref[p, first : first + count, :, lanes] = total


def finish(taps_in, gains_ref, spread_ref, mix_ref, out_ref, layer, first, count):
    chans = mix_ref.shape[1]
    ones = jnp.ones((chans, LANES), BF16)
    gain = gains_ref[layer : layer + 1, :]
    inverse = jnp.broadcast_to(1.0 / (gain * gain), (TILE, chans)).astype(BF16)
    for p in range(2):
        spread = spread_ref[p, first : first + count].reshape(count * TILE, chans)
        square = spread * spread
        square = (square.reshape(count, TILE, chans) * inverse[None]).reshape(count * TILE, chans)
        power = jnp.dot(square, ones, preferred_element_type=F32)
        scale = 0.5 * lax.rsqrt(power * (1.0 / chans) + 1e-05)
        mixed = jnp.dot(spread, mix_ref[layer], preferred_element_type=F32)
        for g in range(chans // LANES):
            moved = gelu(mixed[:, g * LANES : (g + 1) * LANES] * scale)
            center = taps_in[g, p + HALO, first + HALO : first + HALO + count].astype(F32)
            fresh = center + moved.reshape(count, TILE, LANES)
            for k in range(count):
                out_ref[g, first + k, pl.ds(p, TILE, stride=2), :] = fresh[k]


def row_of(out_ref, y):
    return jnp.concatenate([out_ref[g, y] for g in range(out_ref.shape[0])], axis=1)


def flat(ref):
    groups, rows, width, lanes = ref.shape
    return ref.reshape(groups, rows * width, lanes)


def lanes_of(g):
    return slice(g * LANES, (g + 1) * LANES)


def at_last():
    return lax.axis_index("lat") == lax.axis_size("lat") - 1


def inner_kernel(
    shrink,
    layer,
    edge_in,
    inner_in,
    lon_in,
    taps_ref,
    gains_ref,
    mix_ref,
    inner_ref,
    lon_ref,
    near_ref,
    wide_ref,
    taps_in,
    tap_ref,
    spread_ref,
    out_ref,
):
    cols = edge_in.shape[1]
    groups = wide_ref.shape[0]
    width = wide_ref.shape[2]
    own = inner_in.shape[0] - (HALO if shrink else 0)
    rows = own + SHIFT
    count = rows - SHIFT
    main = 0 if shrink else EDGE
    base = 0 if shrink else EDGE - SHIFT
    side = cols if shrink else base

    for g in range(groups):
        for x in range(SHIFT):
            column = lon_in[x, 0:rows, lanes_of(g)].astype(F32)
            flat(wide_ref)[g, pl.ds(side + x, rows, stride=width), :] = column

    def load(ref, place, y):
        put(wide_ref, place, main, ref[y].astype(F32))
        shifted(wide_ref, taps_in, base, place, place)

    @pl.loop(0, SHIFT, unroll=2)
    def _(y):
        load(edge_in, y if shrink else own + y, y)

    @pl.loop(0, own, unroll=2)
    def _(y):
        load(inner_in, y + SHIFT if shrink else y, y)

    near = rows - SHIFT if shrink else 0
    near_ref[...] = taps_in[:, :, near : near + SHIFT]

    @pl.loop(0, groups)
    def _(g):
        convolve(taps_in, taps_ref, gains_ref, tap_ref, spread_ref, layer, g, 0, count)

    finish(taps_in, gains_ref, spread_ref, mix_ref, out_ref, layer, 0, count)
    edge = cols - SHIFT if shrink else 0
    above = 0 if shrink else SHIFT
    for g in range(groups):
        for x in range(SHIFT):
            column = flat(out_ref)[g, pl.ds(edge + x, count, stride=cols), :]
            lon_ref[g, x, above : above + count, :] = column

    @pl.loop(0, count, unroll=2)
    def _(y):
        inner_ref[y] = row_of(out_ref, y).astype(BF16)

    if not shrink:

        @pl.when(at_last())
        def _():
            taps_in[:, :, rows:] = jnp.zeros((groups, TAPS + 1, HALO, TILE, LANES), BF16)

            @pl.loop(0, groups)
            def _(g):
                convolve(taps_in, taps_ref, gains_ref, tap_ref, spread_ref, layer, g, count, HALO)

            finish(taps_in, gains_ref, spread_ref, mix_ref, out_ref, layer, count, HALO)

        for k in range(HALO):
            inner_ref[count + k] = row_of(out_ref, count + k).astype(BF16)


def edge_kernel(
    shrink,
    final,
    layer,
    inner_in,
    lon_in,
    lat_in,
    corner_in,
    near_ref,
    inner_new,
    lon_new,
    taps_ref,
    gains_ref,
    mix_ref,
    *refs,
):
    if final:
        state_ref, wide_ref, taps_in, tap_ref, spread_ref, out_ref, spare_ref, mix_lon = refs
    else:
        edge_ref, lon_ref, corner_ref = refs[:3]
        wide_ref, taps_in, tap_ref, spread_ref, out_ref, spare_ref, mix_lon = refs[3:]
    cols = lat_in.shape[1]
    groups = wide_ref.shape[0]
    main = 0 if shrink else EDGE
    side = cols if shrink else 0
    base = 0 if shrink else EDGE - SHIFT
    last = at_last()
    top = lax.axis_index("lat") == 0
    own = SHIFT if not shrink else 0
    if shrink:
        for g in range(groups):
            for k in range(2):
                spare = lon_in[SHIFT + k, :, lanes_of(g)].astype(F32)
                spare_ref[g, k * TILE : (k + 1) * TILE, :] = spare
    for k in range(SHIFT):
        value, beside = lat_in[k].astype(F32), corner_in[k].astype(F32)
        if not shrink:
            value, beside = jnp.where(top, 0.0, value), jnp.where(top, 0.0, beside)
        elif k < HALO:
            kept = inner_in.shape[0] - HALO
            value = jnp.where(last, inner_in[kept + k].astype(F32), value)
            beside = beside[:SHIFT]
            extra = [spare_ref[g, pl.ds(k, SHIFT, stride=HALO), :] for g in range(groups)]
            beside = jnp.where(last, jnp.concatenate(extra, axis=1), beside)
        else:
            value, beside = jnp.where(last, 0.0, value), jnp.where(last, 0.0, beside)
        put(wide_ref, k, main, value)
        put(wide_ref, k, side, beside)
        shifted(wide_ref, taps_in, base, k, k if not shrink else k + SHIFT)
    taps_in[:, :, own : own + SHIFT] = near_ref[...]

    @pl.loop(0, groups)
    def _(g):
        convolve(taps_in, taps_ref, gains_ref, tap_ref, spread_ref, layer, g, 0, SHIFT)

    finish(taps_in, gains_ref, spread_ref, mix_ref, out_ref, layer, 0, SHIFT)
    kept = inner_new.shape[0]
    if final:
        for k in range(SHIFT):
            state_ref[kept + k] = row_of(out_ref, k).astype(BF16)
        state_ref[0:kept] = inner_new[...]
        return

    for k in range(SHIFT):
        value = row_of(out_ref, k)
        if not shrink and k < HALO:
            value = jnp.where(top, 0.0, value)
        edge_ref[k] = value.astype(BF16)
        corner_ref[k] = (value[cols - EDGE :] if shrink else value[:EDGE]).astype(BF16)
    edge = cols - SHIFT if shrink else 0
    place = TILE - SHIFT if shrink else 0
    for g in range(groups):
        for x in range(SHIFT):
            column = flat(out_ref)[g, pl.ds(edge + x, SHIFT, stride=cols), :]
            if not shrink:
                outside = lax.broadcasted_iota(jnp.int32, (SHIFT, LANES), 0) < HALO
                column = jnp.where(jnp.logical_and(top, outside), 0.0, column)
            mix_lon[g, x] = lon_new[g, x]
            mix_lon[g, x, place : place + SHIFT, :] = column
            lon_ref[x, :, lanes_of(g)] = mix_lon[g, x].astype(BF16)
    if not shrink:
        for k in range(HALO):
            value = inner_new[kept - HALO + k, 0:TILE, :].astype(F32)
            for g in range(groups):
                spare_ref[g, pl.ds(k, SHIFT, stride=HALO), :] = value[:SHIFT, lanes_of(g)]
        for g in range(groups):
            for k in range(2):
                spare = spare_ref[g, k * TILE : (k + 1) * TILE, :]
                lon_ref[SHIFT + k, :, lanes_of(g)] = spare.astype(BF16)


def call(kernel, out_shape, inputs, scratch=(), limit=VMEM_LIMIT, space=None, work=0):
    whole = pl.BlockSpec(memory_space=pltpu.VMEM)
    single = isinstance(out_shape, jax.ShapeDtypeStruct)
    spaces = space or (pltpu.VMEM,) * len(inputs)
    return pl.pallas_call(
        kernel,
        out_shape=out_shape,
        in_specs=[pl.BlockSpec(memory_space=s) for s in spaces],
        out_specs=whole if single else [whole] * len(out_shape),
        scratch_shapes=list(scratch),
        compiler_params=pltpu.CompilerParams(vmem_limit_bytes=limit),
        cost_estimate=pl.CostEstimate(flops=work, bytes_accessed=0, transcendentals=0),
    )(*inputs)


def held(*shape):
    return jax.ShapeDtypeStruct(shape, BF16)


def scratch_of(groups, seen, made, cols, chans):
    return (
        pltpu.VMEM((groups, seen, cols + EDGE, LANES), F32),
        pltpu.VMEM((groups, TAPS + 1, seen, TILE, LANES), BF16),
        pltpu.VMEM((TAPS * TAPS, TILE, LANES), BF16),
        pltpu.VMEM((2, made, TILE, chans), BF16),
        pltpu.VMEM((groups, made, cols, LANES), F32),
    )


def layer(state, lon_out, corner_out, taps, gains, mix, number, shrink, final):
    edge, inner = state
    lat_in, lon_in, corner_in = exchange((edge, lon_out, corner_out), not shrink)
    cols, chans = edge.shape[1:]
    groups = chans // LANES
    rows = inner.shape[0] + SHIFT - (HALO if shrink else 0)
    spare = 0 if shrink else HALO
    made = rows - SHIFT + spare
    inner_new, lon_new, near = call(
        functools.partial(inner_kernel, shrink, number),
        (
            held(made, cols, chans),
            jax.ShapeDtypeStruct((groups, SHIFT, rows, LANES), F32),
            held(groups, TAPS + 1, SHIFT, TILE, LANES),
        ),
        (edge, inner, lon_in, taps, gains, mix),
        scratch_of(groups, rows + spare, made, cols, chans),
        work=made * cols * chans * WORK,
    )
    if final:
        outs = held(made + SHIFT, cols, chans)
    else:
        outs = (
            held(SHIFT, cols, chans),
            held(SHIFT if shrink else EDGE, rows, chans),
            held(SHIFT, EDGE, chans),
        )
    outs = call(
        functools.partial(edge_kernel, shrink, final, number),
        outs,
        (inner, lon_in, lat_in, corner_in, near, inner_new, lon_new, taps, gains, mix),
        scratch_of(groups, 2 * SHIFT, SHIFT, cols, chans)
        + (
            pltpu.VMEM((groups, 2 * TILE, LANES), F32),
            pltpu.VMEM((groups, SHIFT, rows, LANES), F32),
        ),
        work=SHIFT * cols * chans * WORK,
    )
    if final:
        return outs
    edge, lon_out, corner_out = outs
    return (edge, inner_new), lon_out, corner_out


def exchange(pieces, forward):
    lat, lon, corner = pieces
    count_lat = lax.axis_size("lat")
    count_lon = lax.axis_size("lon")
    along = [(i, (i + 1) % count_lat) for i in range(count_lat)]
    around = [(j, (j + 1) % count_lon) for j in range(count_lon)]
    across = [
        (i * count_lon + j, ni * count_lon + nj) for i, ni in along for j, nj in around
    ]
    if not forward:
        along, around, across = ([(t, s) for s, t in p] for p in (along, around, across))
    lon = lax.ppermute(lon, "lon", around)
    lat = lax.ppermute(lat, "lat", along)
    corner = lax.ppermute(corner, ("lat", "lon"), across)
    return lat, lon, corner


def body(
    background, observations, destination, footprint, weights, obs_proj, depth_w, point_w, gains
):
    rows, cols, chans = background.shape
    devices = lax.axis_size("lat") * lax.axis_size("lon")
    obs_rows, feats = observations.shape
    cap = 2 * obs_rows // devices
    depth = cap * (feats // LANES) + META
    foot_count = footprint.shape[1]
    send = call(
        functools.partial(pack_kernel, cap, cols),
        jax.ShapeDtypeStruct((devices, depth, LANES), BF16),
        (destination.T, footprint.T, weights.T, observations),
        (
            pltpu.VMEM((1, obs_rows), jnp.int32),
            pltpu.VMEM((foot_count, obs_rows), jnp.int32),
            pltpu.VMEM((foot_count, obs_rows), BF16),
            pltpu.VMEM((obs_rows, feats), BF16),
            pltpu.SemaphoreType.DMA((4,)),
        ),
        PACK_LIMIT,
        (pltpu.HBM,) * 4,
    )
    got = lax.all_to_all(send, ("lat", "lon"), split_axis=0, concat_axis=0, tiled=True)
    layers = depth_w.shape[0]
    taps = depth_w.transpose(1, 2, 0, 3).reshape(TAPS * TAPS, layers, chans)
    proj, back = call(
        fetch_kernel,
        (held(*obs_proj.shape), held(*background.shape)),
        (obs_proj, background),
        (pltpu.SemaphoreType.DMA((2,)),),
        space=(pltpu.HBM, pltpu.HBM),
    )
    got, proj, back = lax.optimization_barrier((got, proj, back))
    edge, inner, lon_out, corner_out = call(
        functools.partial(assim_kernel, cap, cols + 1),
        (
            held(SHIFT, cols, chans),
            held(rows - SHIFT, cols, chans),
            held(SHIFT, rows, chans),
            held(SHIFT, EDGE, chans),
        ),
        (got, proj, back),
        (pltpu.VMEM((chans // LANES, rows * EDGE, LANES), F32),),
    )
    state = (edge, inner)
    for n in range(layers - 1):
        state, lon_out, corner_out = layer(
            state, lon_out, corner_out, taps, gains, point_w, n, n % 2 == 1, False
        )
    n = layers - 1
    return layer(state, lon_out, corner_out, taps, gains, point_w, n, n % 2 == 1, True)


def solution(mesh):
    placed = (
        P("lat", "lon", None),
        P(("lat", "lon"), None),
        P(("lat", "lon"), None),
        P(("lat", "lon"), None),
        P(("lat", "lon"), None),
        P(),
        P(),
        P(),
        P(),
    )
    return jax.shard_map(
        body, mesh=mesh, in_specs=placed, out_specs=P("lat", "lon", None), check_vma=False
    )
```

```python
import functools

import jax
import jax.numpy as jnp
from jax import lax
from jax.experimental import pallas as pl
from jax.experimental.pallas import tpu as pltpu
from jax.sharding import PartitionSpec as P

LANES = 128
META = 8
TAPS = 7
HALO = 3
SHIFT = 2 * HALO
EDGE = 8
TILE = 16
PIECES = 4
SPARE = 4
WORK = 5000
VMEM_LIMIT = 24 * 1024 * 1024
PACK_LIMIT = 58 * 1024 * 1024
BF16 = jnp.bfloat16
F32 = jnp.float32


def pack_kernel(cap, cols, dest_hbm, foot_hbm, weights_hbm, obs_hbm, send_ref, dest_ref, foot_ref, weights_ref, obs_ref, sems):
    copies = [
        pltpu.make_async_copy(source, target, sems.at[k])
        for k, (source, target) in enumerate(
            (
                (dest_hbm, dest_ref),
                (obs_hbm, obs_ref),
                (foot_hbm, foot_ref),
                (weights_hbm, weights_ref),
            )
        )
    ]
    for copy in copies:
        copy.start()
    devices = send_ref.shape[0]
    obs_rows = obs_ref.shape[0]
    per = LANES // cap
    upper = lax.broadcasted_iota(jnp.int32, (LANES, LANES), 0) <= lax.broadcasted_iota(
        jnp.int32, (LANES, LANES), 1
    )
    upper = jnp.where(upper, 1.0, 0.0).astype(BF16)
    ids = lax.broadcasted_iota(jnp.int32, (devices, obs_rows), 0)
    copies[0].wait()
    member = jnp.where(ids == dest_ref[...], 1.0, 0.0)
    seen = jnp.zeros((devices, 1), F32)
    ranks = []
    for first in range(0, obs_rows, LANES):
        part = member[:, first : first + LANES]
        count = jnp.dot(part.astype(BF16), upper, preferred_element_type=F32) + seen
        ranks.append(jnp.sum((count - 1.0) * part, axis=0, keepdims=True))
        seen = count[:, LANES - 1 :]
    rank = jnp.concatenate(ranks, axis=1).astype(jnp.int32)
    slot = lax.broadcasted_iota(jnp.int32, (cap, obs_rows), 0)
    ranked = jnp.where(slot == rank, 1.0, 0.0).astype(BF16).reshape(cap // TILE, TILE, obs_rows)
    for copy in copies[1:]:
        copy.wait()
    start = foot_ref[0:1, :]
    meta = jnp.concatenate(
        [
            lax.div(start, cols).astype(F32),
            lax.rem(start, cols).astype(F32),
            weights_ref[...].astype(F32),
            jnp.zeros((META - 2 - weights_ref.shape[0], obs_rows), F32),
        ],
        axis=0,
    ).astype(BF16)
    obs = obs_ref[...]
    lane = lax.broadcasted_iota(jnp.int32, (META, LANES), 1)
    count = min(512, devices * cap) // cap
    for first in range(0, devices, count):
        parts = []
        for d in range(first, first + count):
            mine = jnp.broadcast_to(member[d : d + 1], (TILE, obs_rows)).astype(BF16)
            parts.append((ranked * mine[None]).reshape(cap, obs_rows))
        chosen = jnp.concatenate(parts, axis=0)
        feats = jnp.dot(chosen, obs, preferred_element_type=F32).astype(BF16)
        placed = lax.dot_general(
            meta, chosen, (((1,), (1,)), ((), ())), preferred_element_type=F32
        )
        for half in range(feats.shape[1] // LANES):
            piece = feats[:, half * LANES : (half + 1) * LANES].reshape(count, cap, LANES)
            send_ref[first : first + count, half * cap : (half + 1) * cap, :] = piece
        base = send_ref.shape[1] - META
        for chunk in range(count // per):
            values = placed[:, chunk * LANES : (chunk + 1) * LANES]
            turned = [values] + [pltpu.roll(values, k * cap, 1) for k in range(1, per)]
            for own in range(per):
                wide = turned[0]
                for group in range(per):
                    wide = jnp.where(lane // cap == group, turned[(group - own) % per], wide)
                send_ref[first + chunk * per + own, base:, :] = wide.astype(BF16)


def fetch_kernel(proj_hbm, back_hbm, proj_ref, back_ref, sems):
    copies = (
        pltpu.make_async_copy(proj_hbm, proj_ref, sems.at[0]),
        pltpu.make_async_copy(back_hbm, back_ref, sems.at[1]),
    )
    for copy in copies:
        copy.start()
    for copy in copies:
        copy.wait()


def assim_kernel(
    cap,
    step,
    got_hbm,
    proj_ref,
    back_ref,
    edge_ref,
    left_ref,
    right_ref,
    lon_ref,
    corner_ref,
    got_ref,
    wide_ref,
    sems,
):
    piece = got_ref.shape[0] // PIECES
    copies = [
        pltpu.make_async_copy(
            got_hbm.at[k * piece : (k + 1) * piece],
            got_ref.at[k * piece : (k + 1) * piece],
            sems.at[k],
        )
        for k in range(PIECES)
    ]
    for copy in copies:
        copy.start()
    devices, depth, _ = got_ref.shape
    rows, cols, chans = back_ref.shape
    cells = rows * cols
    feats = proj_ref.shape[0]
    per = LANES // cap
    halves = feats // LANES
    lane = lax.broadcasted_iota(jnp.int32, (META, LANES), 1)
    cell = lax.broadcasted_iota(jnp.int32, (cells, LANES), 0)
    total = jnp.zeros((cells, feats), F32)
    for pair in range(0, devices // per, 2):
        if pair * per % piece == 0:
            copies[pair * per // piece].wait()
        maps = []
        blocks = []
        for chunk in (pair, pair + 1):
            meta = got_ref[chunk * per, depth - META :, :].astype(F32)
            for group in range(1, per):
                other = got_ref[chunk * per + group, depth - META :, :].astype(F32)
                meta = jnp.where(lane // cap == group, other, meta)
            start = (meta[0:1] * cols + meta[1:2]).astype(jnp.int32)
            away = cell - start
            away = jnp.where(away < 0, away + cells, away)
            amount = jnp.zeros((cells, LANES), F32)
            for entry in range(4):
                amount = jnp.where(away == entry * step, meta[2 + entry : 3 + entry], amount)
            maps.append(amount.astype(BF16))
            block = got_ref[chunk * per : (chunk + 1) * per]
            blocks.append(
                jnp.concatenate(
                    [
                        block[:, half * cap : (half + 1) * cap, :].reshape(LANES, LANES)
                        for half in range(halves)
                    ],
                    axis=1,
                )
            )
        total = total + jnp.dot(
            jnp.concatenate(maps, axis=1),
            jnp.concatenate(blocks, axis=0),
            preferred_element_type=F32,
        )
    assim = jnp.dot(total.astype(BF16), proj_ref[...], preferred_element_type=F32)
    state = back_ref[...].astype(F32) + assim.reshape(rows, cols, chans)
    for g in range(chans // LANES):
        wide_ref[g] = state[:, cols - EDGE :, lanes_of(g)].reshape(rows * EDGE, LANES)
    state = state.astype(BF16)
    edge_ref[...] = state[rows - SHIFT :]
    left_ref[...] = state[: rows - SHIFT, :TILE]
    right_ref[...] = state[: rows - SHIFT, TILE:]
    for x in range(SHIFT):
        for g in range(chans // LANES):
            column = wide_ref[g, pl.ds(EDGE - SHIFT + x, rows, stride=EDGE), :]
            lon_ref[x, :, lanes_of(g)] = column.astype(BF16)
    corner_ref[...] = state[rows - SHIFT :, cols - EDGE :, :]


def gelu(half):
    inner = half * (1.5957691216057308 + 0.285419265090401 * (half * half))
    return half + half * jnp.tanh(inner)


def put(wide_ref, row, start, value):
    for g in range(wide_ref.shape[0]):
        wide_ref[g, row, start : start + value.shape[0], :] = value[:, g * LANES : (g + 1) * LANES]


def shifted(wide_ref, taps_in, base, row, target):
    for g in range(wide_ref.shape[0]):
        for r in range(TAPS + 1):
            columns = pl.ds(base + r, TILE, stride=2)
            taps_in[g, r, target] = wide_ref[g, row, columns, :].astype(BF16)


def convolve(taps_in, taps_ref, tap_ref, spread_ref, layer, g, first, count):
    lanes = pl.ds(pl.multiple_of(g * LANES, LANES), LANES)
    for k in range(TAPS * TAPS):
        row = taps_ref[k, layer : layer + 1, lanes]
        tap_ref[k] = jnp.broadcast_to(row, (TILE, LANES)).astype(BF16)
    for p in range(2):
        total = None
        for b in range(TAPS):
            seen = taps_in[g, p + b, first : first + count + TAPS - 1]
            part = None
            for a in range(TAPS):
                term = seen[a : a + count] * tap_ref[a * TAPS + b]
                part = term if part is None else part + term
            total = part if total is None else total + part
        spread_ref[p, first : first + count, :, lanes] = total


def finish(taps_in, spread_ref, mix_ref, out_ref, layer, first, count, stacked=1):
    chans = mix_ref.shape[1]
    ones = jnp.ones((chans, LANES), BF16)
    step = TILE // stacked
    spread = spread_ref[:, first : first + count].reshape(2 * count * TILE, chans)
    power = jnp.dot(spread * spread, ones, preferred_element_type=F32)
    scale = 0.5 * lax.rsqrt(power * (1.0 / chans) + 1e-05)
    mixed = jnp.dot(spread, mix_ref[layer], preferred_element_type=F32)
    for g in range(chans // LANES):
        moved = gelu(mixed[:, lanes_of(g)] * scale).reshape(2, count, TILE, LANES)
        for p in range(2):
            center = taps_in[g, p + HALO, first + HALO : first + HALO + count].astype(F32)
            fresh = center + moved[p]
            for k in range(count):
                for h in range(stacked):
                    row = first * stacked + h * count + k
                    out_ref[g, row, pl.ds(p, step, stride=2), :] = fresh[
                        k, h * step : (h + 1) * step
                    ]


def row_of(out_ref, y):
    return jnp.concatenate([out_ref[g, y] for g in range(out_ref.shape[0])], axis=1)


def flat(ref):
    groups, rows, width, lanes = ref.shape
    return ref.reshape(groups, rows * width, lanes)


def lanes_of(g):
    return slice(g * LANES, (g + 1) * LANES)


def at_last():
    return lax.axis_index("lat") == lax.axis_size("lat") - 1


def block_kernel(shrink, lead, layer, edge_in, left_in, right_in, *refs):
    if lead:
        taps_ref, mix_ref, block_ref, *scratch = refs
    else:
        lon_in, taps_ref, mix_ref, block_ref, lon_ref, near_ref, *scratch = refs
    wide_ref, taps_in, tap_ref, spread_ref, out_ref = scratch
    cols = edge_in.shape[1]
    groups = wide_ref.shape[0]
    width = wide_ref.shape[2]
    own = left_in.shape[0] - (SPARE if shrink else 0)
    rows = own + SHIFT
    main = 0 if shrink else EDGE
    base = 0 if shrink else EDGE - SHIFT
    start = base + (0 if lead == shrink else TILE)

    if not lead:
        side = cols if shrink else base
        for g in range(groups):
            for x in range(SHIFT):
                column = lon_in[x, 0:rows, lanes_of(g)].astype(F32)
                flat(wide_ref)[g, pl.ds(side + x, rows, stride=width), :] = column

    @pl.loop(0, SHIFT, unroll=2)
    def _(y):
        put(wide_ref, y if shrink else own + y, main, edge_in[y].astype(F32))

    @pl.loop(0, own, unroll=2)
    def _(y):
        place = y + SHIFT if shrink else y
        put(wide_ref, place, main, left_in[y].astype(F32))
        put(wide_ref, place, main + TILE, right_in[y].astype(F32))

    def stage(top, high):
        @pl.loop(0, high + TAPS - 1)
        def _(y):
            for g in range(groups):
                for r in range(TAPS + 1):
                    both = [
                        wide_ref[g, top + y + h, pl.ds(start + r, TILE // 2, stride=2), :]
                        for h in (0, high)
                    ]
                    taps_in[g, r, y] = jnp.concatenate(both, axis=0).astype(BF16)

        @pl.loop(0, groups)
        def _(g):
            convolve(taps_in, taps_ref, tap_ref, spread_ref, layer, g, 0, high)

        finish(taps_in, spread_ref, mix_ref, out_ref, layer, 0, high, 2)

        @pl.loop(0, 2 * high, unroll=2)
        def _(y):
            block_ref[top + y] = row_of(out_ref, y).astype(BF16)

    stage(0, own // 2)
    if not lead:
        edge = TILE - SHIFT if shrink else 0
        above = 0 if shrink else SHIFT
        near = rows - SHIFT if shrink else 0
        for g in range(groups):
            for x in range(SHIFT):
                column = flat(out_ref)[g, pl.ds(edge + x, own, stride=TILE), :]
                lon_ref[g, x, above : above + own, :] = column
            for r in range(TAPS + 1):
                for k in range(SHIFT):
                    columns = pl.ds(base + r, TILE, stride=2)
                    near_ref[g, r, k] = wide_ref[g, near + k, columns, :].astype(BF16)
    if not shrink:

        @pl.when(at_last())
        def _():
            wide_ref[:, rows:] = jnp.zeros((groups, SPARE, width, LANES), F32)
            stage(own, SPARE // 2)


def edge_kernel(
    shrink,
    final,
    layer,
    left_in,
    right_in,
    lon_in,
    lat_in,
    corner_in,
    near_ref,
    left_new,
    right_new,
    lon_new,
    taps_ref,
    mix_ref,
    *refs,
):
    if final:
        state_ref, wide_ref, taps_in, tap_ref, spread_ref, out_ref, spare_ref, mix_lon = refs
    else:
        edge_ref, lon_ref, corner_ref = refs[:3]
        wide_ref, taps_in, tap_ref, spread_ref, out_ref, spare_ref, mix_lon = refs[3:]
    cols = lat_in.shape[1]
    groups = wide_ref.shape[0]
    main = 0 if shrink else EDGE
    side = cols if shrink else 0
    base = 0 if shrink else EDGE - SHIFT
    last = at_last()
    top = lax.axis_index("lat") == 0
    own = SHIFT if not shrink else 0
    if shrink:
        for g in range(groups):
            for k in range(2):
                spare = lon_in[SHIFT + k, :, lanes_of(g)].astype(F32)
                spare_ref[g, k * TILE : (k + 1) * TILE, :] = spare
    for k in range(SHIFT):
        value, beside = lat_in[k].astype(F32), corner_in[k].astype(F32)
        if not shrink:
            value, beside = jnp.where(top, 0.0, value), jnp.where(top, 0.0, beside)
        elif k < HALO:
            kept = left_in.shape[0] - SPARE + k
            inner = jnp.concatenate([left_in[kept], right_in[kept]], axis=0)
            value = jnp.where(last, inner.astype(F32), value)
            beside = beside[:SHIFT]
            extra = [spare_ref[g, pl.ds(k, SHIFT, stride=HALO), :] for g in range(groups)]
            beside = jnp.where(last, jnp.concatenate(extra, axis=1), beside)
        else:
            value, beside = jnp.where(last, 0.0, value), jnp.where(last, 0.0, beside)
        put(wide_ref, k, main, value)
        put(wide_ref, k, side, beside)
        shifted(wide_ref, taps_in, base, k, k if not shrink else k + SHIFT)
    taps_in[:, :, own : own + SHIFT] = near_ref[...]

    @pl.loop(0, groups)
    def _(g):
        convolve(taps_in, taps_ref, tap_ref, spread_ref, layer, g, 0, SHIFT)

    finish(taps_in, spread_ref, mix_ref, out_ref, layer, 0, SHIFT)
    kept = left_new.shape[0]
    if final:
        for k in range(SHIFT):
            state_ref[kept + k] = row_of(out_ref, k).astype(BF16)
        state_ref[0:kept, 0:TILE, :] = left_new[...]
        state_ref[0:kept, TILE:cols, :] = right_new[...]
        return

    for k in range(SHIFT):
        value = row_of(out_ref, k)
        if not shrink and k < HALO:
            value = jnp.where(top, 0.0, value)
        edge_ref[k] = value.astype(BF16)
        corner_ref[k] = (value[cols - EDGE :] if shrink else value[:EDGE]).astype(BF16)
    edge = cols - SHIFT if shrink else 0
    place = TILE - SHIFT if shrink else 0
    for g in range(groups):
        for x in range(SHIFT):
            column = flat(out_ref)[g, pl.ds(edge + x, SHIFT, stride=cols), :]
            if not shrink:
                outside = lax.broadcasted_iota(jnp.int32, (SHIFT, LANES), 0) < HALO
                column = jnp.where(jnp.logical_and(top, outside), 0.0, column)
            mix_lon[g, x] = lon_new[g, x]
            mix_lon[g, x, place : place + SHIFT, :] = column
            lon_ref[x, :, lanes_of(g)] = mix_lon[g, x].astype(BF16)
    if not shrink:
        for k in range(HALO):
            value = left_new[kept - SPARE + k].astype(F32)
            for g in range(groups):
                spare_ref[g, pl.ds(k, SHIFT, stride=HALO), :] = value[:SHIFT, lanes_of(g)]
        for g in range(groups):
            for k in range(2):
                spare = spare_ref[g, k * TILE : (k + 1) * TILE, :]
                lon_ref[SHIFT + k, :, lanes_of(g)] = spare.astype(BF16)


def call(kernel, out_shape, inputs, scratch=(), limit=VMEM_LIMIT, space=None, work=0):
    whole = pl.BlockSpec(memory_space=pltpu.VMEM)
    single = isinstance(out_shape, jax.ShapeDtypeStruct)
    spaces = space or (pltpu.VMEM,) * len(inputs)
    return pl.pallas_call(
        kernel,
        out_shape=out_shape,
        in_specs=[pl.BlockSpec(memory_space=s) for s in spaces],
        out_specs=whole if single else [whole] * len(out_shape),
        scratch_shapes=list(scratch),
        compiler_params=pltpu.CompilerParams(vmem_limit_bytes=limit),
        cost_estimate=pl.CostEstimate(flops=work, bytes_accessed=0, transcendentals=0),
    )(*inputs)


def held(*shape):
    return jax.ShapeDtypeStruct(shape, BF16)


def scratch_of(groups, seen, made, cols, chans):
    return (
        pltpu.VMEM((groups, seen, cols + EDGE, LANES), F32),
        pltpu.VMEM((groups, TAPS + 1, seen, TILE, LANES), BF16),
        pltpu.VMEM((TAPS * TAPS, TILE, LANES), BF16),
        pltpu.VMEM((2, made, TILE, chans), BF16),
        pltpu.VMEM((groups, made, cols, LANES), F32),
    )


def layer(state, lon_out, corner_out, taps, mix, number, shrink, final):
    edge, left, right = state
    lat_in, lon_in, corner_in = exchange((edge, lon_out, corner_out), not shrink)
    cols, chans = edge.shape[1:]
    groups = chans // LANES
    own = left.shape[0] - (SPARE if shrink else 0)
    rows = own + SHIFT
    spare = 0 if shrink else SPARE
    made = own + spare
    block = held(made, TILE, chans)
    scratch = (
        pltpu.VMEM((groups, rows + spare, cols + EDGE, LANES), F32),
        pltpu.VMEM((groups, TAPS + 1, own // 2 + TAPS - 1, TILE, LANES), BF16),
        pltpu.VMEM((TAPS * TAPS, TILE, LANES), BF16),
        pltpu.VMEM((2, own // 2, TILE, chans), BF16),
        pltpu.VMEM((groups, own, TILE, LANES), F32),
    )
    lead = call(
        functools.partial(block_kernel, shrink, True, number),
        block,
        (edge, left, right, taps, mix),
        scratch,
    )
    trail, lon_new, near = call(
        functools.partial(block_kernel, shrink, False, number),
        (
            block,
            jax.ShapeDtypeStruct((groups, SHIFT, rows, LANES), F32),
            held(groups, TAPS + 1, SHIFT, TILE, LANES),
        ),
        (edge, left, right, lon_in, taps, mix),
        scratch,
        work=made * cols * chans * WORK,
    )
    new = (lead, trail) if shrink else (trail, lead)
    if final:
        outs = held(made + SHIFT, cols, chans)
    else:
        outs = (
            held(SHIFT, cols, chans),
            held(SHIFT if shrink else EDGE, rows, chans),
            held(SHIFT, EDGE, chans),
        )
    outs = call(
        functools.partial(edge_kernel, shrink, final, number),
        outs,
        (left, right, lon_in, lat_in, corner_in, near, *new, lon_new, taps, mix),
        scratch_of(groups, 2 * SHIFT, SHIFT, cols, chans)
        + (
            pltpu.VMEM((groups, 2 * TILE, LANES), F32),
            pltpu.VMEM((groups, SHIFT, rows, LANES), F32),
        ),
        work=SHIFT * cols * chans * WORK,
    )
    if final:
        return outs
    edge, lon_out, corner_out = outs
    return (edge, *new), lon_out, corner_out


def exchange(pieces, forward):
    lat, lon, corner = pieces
    count_lat = lax.axis_size("lat")
    count_lon = lax.axis_size("lon")
    along = [(i, (i + 1) % count_lat) for i in range(count_lat)]
    around = [(j, (j + 1) % count_lon) for j in range(count_lon)]
    across = [
        (i * count_lon + j, ni * count_lon + nj) for i, ni in along for j, nj in around
    ]
    if not forward:
        along, around, across = ([(t, s) for s, t in p] for p in (along, around, across))
    lon = lax.ppermute(lon, "lon", around)
    lat = lax.ppermute(lat, "lat", along)
    corner = lax.ppermute(corner, ("lat", "lon"), across)
    return lat, lon, corner


def body(
    background, observations, destination, footprint, weights, obs_proj, depth_w, point_w, gains
):
    rows, cols, chans = background.shape
    devices = lax.axis_size("lat") * lax.axis_size("lon")
    obs_rows, feats = observations.shape
    cap = 2 * obs_rows // devices
    depth = cap * (feats // LANES) + META
    foot_count = footprint.shape[1]
    send = call(
        functools.partial(pack_kernel, cap, cols),
        jax.ShapeDtypeStruct((devices, depth, LANES), BF16),
        (destination.T, footprint.T, weights.T, observations),
        (
            pltpu.VMEM((1, obs_rows), jnp.int32),
            pltpu.VMEM((foot_count, obs_rows), jnp.int32),
            pltpu.VMEM((foot_count, obs_rows), BF16),
            pltpu.VMEM((obs_rows, feats), BF16),
            pltpu.SemaphoreType.DMA((4,)),
        ),
        PACK_LIMIT,
        (pltpu.HBM,) * 4,
    )
    got = lax.all_to_all(send, ("lat", "lon"), split_axis=0, concat_axis=0, tiled=True)
    layers = depth_w.shape[0]
    taps = depth_w.transpose(1, 2, 0, 3).reshape(TAPS * TAPS, layers, chans)
    mix = (gains[:, :, None] * point_w.astype(F32)).astype(BF16)
    proj, back = call(
        fetch_kernel,
        (held(*obs_proj.shape), held(*background.shape)),
        (obs_proj, background),
        (pltpu.SemaphoreType.DMA((2,)),),
        space=(pltpu.HBM, pltpu.HBM),
    )
    got, mix, proj, back = lax.optimization_barrier((got, mix, proj, back))
    edge, left, right, lon_out, corner_out = call(
        functools.partial(assim_kernel, cap, cols + 1),
        (
            held(SHIFT, cols, chans),
            held(rows - SHIFT, TILE, chans),
            held(rows - SHIFT, TILE, chans),
            held(SHIFT, rows, chans),
            held(SHIFT, EDGE, chans),
        ),
        (got, proj, back),
        (
            pltpu.VMEM((devices, depth, LANES), BF16),
            pltpu.VMEM((chans // LANES, rows * EDGE, LANES), F32),
            pltpu.SemaphoreType.DMA((PIECES,)),
        ),
        space=(pltpu.HBM, pltpu.VMEM, pltpu.VMEM),
    )
    state = (edge, left, right)
    for n in range(layers - 1):
        state, lon_out, corner_out = layer(
            state, lon_out, corner_out, taps, mix, n, n % 2 == 1, False
        )
    n = layers - 1
    return layer(state, lon_out, corner_out, taps, mix, n, n % 2 == 1, True)


def solution(mesh):
    placed = (
        P("lat", "lon", None),
        P(("lat", "lon"), None),
        P(("lat", "lon"), None),
        P(("lat", "lon"), None),
        P(("lat", "lon"), None),
        P(),
        P(),
        P(),
        P(),
    )
    return jax.shard_map(
        body, mesh=mesh, in_specs=placed, out_specs=P("lat", "lon", None), check_vma=False
    )
```

```python
import functools

import jax
import jax.numpy as jnp
from jax import lax
from jax.experimental import pallas as pl
from jax.experimental.pallas import tpu as pltpu
from jax.sharding import PartitionSpec as P

LANES = 128
META = 8
TAPS = 7
HALO = 3
SHIFT = 2 * HALO
EDGE = 8
TILE = 16
PIECES = 4
SPARE = 4
WORK = 5000
VMEM_LIMIT = 24 * 1024 * 1024
PACK_LIMIT = 58 * 1024 * 1024
BF16 = jnp.bfloat16
F32 = jnp.float32


def pack_kernel(cap, cols, dest_hbm, foot_hbm, weights_hbm, obs_hbm, send_ref, dest_ref, foot_ref, weights_ref, obs_ref, sems):
    copies = [
        pltpu.make_async_copy(source, target, sems.at[k])
        for k, (source, target) in enumerate(
            (
                (dest_hbm, dest_ref),
                (obs_hbm, obs_ref),
                (foot_hbm, foot_ref),
                (weights_hbm, weights_ref),
            )
        )
    ]
    for copy in copies:
        copy.start()
    devices = send_ref.shape[0]
    obs_rows = obs_ref.shape[0]
    per = LANES // cap
    upper = lax.broadcasted_iota(jnp.int32, (LANES, LANES), 0) <= lax.broadcasted_iota(
        jnp.int32, (LANES, LANES), 1
    )
    upper = jnp.where(upper, 1.0, 0.0).astype(BF16)
    ids = lax.broadcasted_iota(jnp.int32, (devices, obs_rows), 0)
    copies[0].wait()
    member = jnp.where(ids == dest_ref[...], 1.0, 0.0)
    seen = jnp.zeros((devices, 1), F32)
    ranks = []
    for first in range(0, obs_rows, LANES):
        part = member[:, first : first + LANES]
        count = jnp.dot(part.astype(BF16), upper, preferred_element_type=F32) + seen
        ranks.append(jnp.sum((count - 1.0) * part, axis=0, keepdims=True))
        seen = count[:, LANES - 1 :]
    rank = jnp.concatenate(ranks, axis=1).astype(jnp.int32)
    slot = lax.broadcasted_iota(jnp.int32, (cap, obs_rows), 0)
    ranked = jnp.where(slot == rank, 1.0, 0.0).astype(BF16).reshape(cap // TILE, TILE, obs_rows)
    for copy in copies[1:]:
        copy.wait()
    start = foot_ref[0:1, :]
    meta = jnp.concatenate(
        [
            lax.div(start, cols).astype(F32),
            lax.rem(start, cols).astype(F32),
            weights_ref[...].astype(F32),
            jnp.zeros((META - 2 - weights_ref.shape[0], obs_rows), F32),
        ],
        axis=0,
    ).astype(BF16)
    obs = obs_ref[...]
    lane = lax.broadcasted_iota(jnp.int32, (META, LANES), 1)
    count = min(512, devices * cap) // cap
    for first in range(0, devices, count):
        parts = []
        for d in range(first, first + count):
            mine = jnp.broadcast_to(member[d : d + 1], (TILE, obs_rows)).astype(BF16)
            parts.append((ranked * mine[None]).reshape(cap, obs_rows))
        chosen = jnp.concatenate(parts, axis=0)
        feats = jnp.dot(chosen, obs, preferred_element_type=F32).astype(BF16)
        placed = lax.dot_general(
            meta, chosen, (((1,), (1,)), ((), ())), preferred_element_type=F32
        )
        for half in range(feats.shape[1] // LANES):
            piece = feats[:, half * LANES : (half + 1) * LANES].reshape(count, cap, LANES)
            send_ref[first : first + count, half * cap : (half + 1) * cap, :] = piece
        base = send_ref.shape[1] - META
        for chunk in range(count // per):
            values = placed[:, chunk * LANES : (chunk + 1) * LANES]
            turned = [values] + [pltpu.roll(values, k * cap, 1) for k in range(1, per)]
            for own in range(per):
                wide = turned[0]
                for group in range(per):
                    wide = jnp.where(lane // cap == group, turned[(group - own) % per], wide)
                send_ref[first + chunk * per + own, base:, :] = wide.astype(BF16)


def fetch_kernel(proj_hbm, back_hbm, proj_ref, back_ref, sems):
    copies = (
        pltpu.make_async_copy(proj_hbm, proj_ref, sems.at[0]),
        pltpu.make_async_copy(back_hbm, back_ref, sems.at[1]),
    )
    for copy in copies:
        copy.start()
    for copy in copies:
        copy.wait()


def assim_kernel(
    cap,
    step,
    got_hbm,
    proj_ref,
    back_ref,
    edge_ref,
    left_ref,
    right_ref,
    lon_ref,
    corner_ref,
    got_ref,
    wide_ref,
    sems,
):
    piece = got_ref.shape[0] // PIECES
    copies = [
        pltpu.make_async_copy(
            got_hbm.at[k * piece : (k + 1) * piece],
            got_ref.at[k * piece : (k + 1) * piece],
            sems.at[k],
        )
        for k in range(PIECES)
    ]
    for copy in copies:
        copy.start()
    devices, depth, _ = got_ref.shape
    rows, cols, chans = back_ref.shape
    cells = rows * cols
    feats = proj_ref.shape[0]
    per = LANES // cap
    halves = feats // LANES
    lane = lax.broadcasted_iota(jnp.int32, (META, LANES), 1)
    cell = lax.broadcasted_iota(jnp.int32, (cells, LANES), 0)
    total = jnp.zeros((cells, feats), F32)
    for pair in range(0, devices // per, 2):
        if pair * per % piece == 0:
            copies[pair * per // piece].wait()
        maps = []
        blocks = []
        for chunk in (pair, pair + 1):
            meta = got_ref[chunk * per, depth - META :, :].astype(F32)
            for group in range(1, per):
                other = got_ref[chunk * per + group, depth - META :, :].astype(F32)
                meta = jnp.where(lane // cap == group, other, meta)
            start = (meta[0:1] * cols + meta[1:2]).astype(jnp.int32)
            away = cell - start
            away = jnp.where(away < 0, away + cells, away)
            amount = jnp.zeros((cells, LANES), F32)
            for entry in range(4):
                amount = jnp.where(away == entry * step, meta[2 + entry : 3 + entry], amount)
            maps.append(amount.astype(BF16))
            block = got_ref[chunk * per : (chunk + 1) * per]
            blocks.append(
                jnp.concatenate(
                    [
                        block[:, half * cap : (half + 1) * cap, :].reshape(LANES, LANES)
                        for half in range(halves)
                    ],
                    axis=1,
                )
            )
        total = total + jnp.dot(
            jnp.concatenate(maps, axis=1),
            jnp.concatenate(blocks, axis=0),
            preferred_element_type=F32,
        )
    assim = jnp.dot(total.astype(BF16), proj_ref[...], preferred_element_type=F32)
    state = back_ref[...].astype(F32) + assim.reshape(rows, cols, chans)
    for g in range(chans // LANES):
        wide_ref[g] = state[:, cols - EDGE :, lanes_of(g)].reshape(rows * EDGE, LANES)
    state = state.astype(BF16)
    edge_ref[...] = state[rows - SHIFT :]
    left_ref[...] = state[: rows - SHIFT, :TILE]
    right_ref[...] = state[: rows - SHIFT, TILE:]
    for x in range(SHIFT):
        for g in range(chans // LANES):
            column = wide_ref[g, pl.ds(EDGE - SHIFT + x, rows, stride=EDGE), :]
            lon_ref[x, :, lanes_of(g)] = column.astype(BF16)
    corner_ref[...] = state[rows - SHIFT :, cols - EDGE :, :]


def gelu(half):
    inner = half * (1.5957691216057308 + 0.285419265090401 * (half * half))
    return half + half * jnp.tanh(inner)


def put(wide_ref, row, start, value):
    for g in range(wide_ref.shape[0]):
        wide_ref[g, row, start : start + value.shape[0], :] = value[:, g * LANES : (g + 1) * LANES]


def shifted(wide_ref, taps_in, base, row, target):
    for g in range(wide_ref.shape[0]):
        for r in range(TAPS + 1):
            columns = pl.ds(base + r, TILE, stride=2)
            taps_in[g, r, target] = wide_ref[g, row, columns, :].astype(BF16)


def convolve(taps_in, taps_ref, tap_ref, spread_ref, layer, g, first, count):
    lanes = pl.ds(pl.multiple_of(g * LANES, LANES), LANES)
    for k in range(TAPS * TAPS):
        row = taps_ref[k, layer : layer + 1, lanes]
        tap_ref[k] = jnp.broadcast_to(row, (TILE, LANES)).astype(BF16)
    for p in range(2):
        total = None
        for b in range(TAPS):
            seen = taps_in[g, p + b, first : first + count + TAPS - 1]
            part = None
            for a in range(TAPS):
                term = seen[a : a + count] * tap_ref[a * TAPS + b]
                part = term if part is None else part + term
            total = part if total is None else total + part
        spread_ref[p, first : first + count, :, lanes] = total


def finish(taps_in, spread_ref, mix_ref, out_ref, layer, first, count, stacked=1):
    chans = mix_ref.shape[1]
    ones = jnp.ones((chans, LANES), BF16)
    step = TILE // stacked
    spread = spread_ref[:, first : first + count].reshape(2 * count * TILE, chans)
    power = jnp.dot(spread * spread, ones, preferred_element_type=F32)
    scale = 0.5 * lax.rsqrt(power * (1.0 / chans) + 1e-05)
    mixed = jnp.dot(spread, mix_ref[layer], preferred_element_type=F32)
    for g in range(chans // LANES):
        moved = gelu(mixed[:, lanes_of(g)] * scale).reshape(2, count, TILE, LANES)
        for p in range(2):
            center = taps_in[g, p + HALO, first + HALO : first + HALO + count].astype(F32)
            fresh = center + moved[p]
            for k in range(count):
                for h in range(stacked):
                    row = first * stacked + h * count + k
                    out_ref[g, row, pl.ds(p, step, stride=2), :] = fresh[
                        k, h * step : (h + 1) * step
                    ]


def row_of(out_ref, y):
    return jnp.concatenate([out_ref[g, y] for g in range(out_ref.shape[0])], axis=1)


def flat(ref):
    groups, rows, width, lanes = ref.shape
    return ref.reshape(groups, rows * width, lanes)


def lanes_of(g):
    return slice(g * LANES, (g + 1) * LANES)


def at_last():
    return lax.axis_index("lat") == lax.axis_size("lat") - 1


def block_kernel(shrink, lead, layer, edge_in, left_in, right_in, *refs):
    if lead:
        taps_ref, mix_ref, block_ref, *scratch = refs
    else:
        lon_in, taps_ref, mix_ref, block_ref, lon_ref, near_ref, *scratch = refs
    wide_ref, taps_in, tap_ref, spread_ref, out_ref = scratch
    cols = edge_in.shape[1]
    groups = wide_ref.shape[0]
    width = wide_ref.shape[2]
    own = left_in.shape[0] - (SPARE if shrink else 0)
    rows = own + SHIFT
    main = 0 if shrink else EDGE
    base = 0 if shrink else EDGE - SHIFT
    start = base + (0 if lead == shrink else TILE)

    if not lead:
        side = cols if shrink else base
        for g in range(groups):
            for x in range(SHIFT):
                column = lon_in[x, 0:rows, lanes_of(g)].astype(F32)
                flat(wide_ref)[g, pl.ds(side + x, rows, stride=width), :] = column

    @pl.loop(0, SHIFT, unroll=2)
    def _(y):
        put(wide_ref, y if shrink else own + y, main, edge_in[y].astype(F32))

    @pl.loop(0, own, unroll=2)
    def _(y):
        place = y + SHIFT if shrink else y
        put(wide_ref, place, main, left_in[y].astype(F32))
        put(wide_ref, place, main + TILE, right_in[y].astype(F32))

    def stage(top, high):
        @pl.loop(0, high + TAPS - 1)
        def _(y):
            for g in range(groups):
                for r in range(TAPS + 1):
                    both = [
                        wide_ref[g, top + y + h, pl.ds(start + r, TILE // 2, stride=2), :]
                        for h in (0, high)
                    ]
                    taps_in[g, r, y] = jnp.concatenate(both, axis=0).astype(BF16)

        @pl.loop(0, groups)
        def _(g):
            convolve(taps_in, taps_ref, tap_ref, spread_ref, layer, g, 0, high)

        finish(taps_in, spread_ref, mix_ref, out_ref, layer, 0, high, 2)

        @pl.loop(0, 2 * high, unroll=2)
        def _(y):
            block_ref[top + y] = row_of(out_ref, y).astype(BF16)

    stage(0, own // 2)
    if not lead:
        edge = TILE - SHIFT if shrink else 0
        above = 0 if shrink else SHIFT
        near = rows - SHIFT if shrink else 0
        for g in range(groups):
            for x in range(SHIFT):
                column = flat(out_ref)[g, pl.ds(edge + x, own, stride=TILE), :]
                lon_ref[g, x, above : above + own, :] = column
            for r in range(TAPS + 1):
                for k in range(SHIFT):
                    columns = pl.ds(base + r, TILE, stride=2)
                    near_ref[g, r, k] = wide_ref[g, near + k, columns, :].astype(BF16)
    if not shrink:

        @pl.when(at_last())
        def _():
            wide_ref[:, rows:] = jnp.zeros((groups, SPARE, width, LANES), F32)
            stage(own, SPARE // 2)


def edge_kernel(
    shrink,
    final,
    layer,
    left_in,
    right_in,
    lon_in,
    lat_in,
    corner_in,
    near_ref,
    left_new,
    right_new,
    lon_new,
    taps_ref,
    mix_ref,
    *refs,
):
    if final:
        state_ref, wide_ref, taps_in, tap_ref, spread_ref, out_ref, spare_ref, mix_lon = refs
    else:
        edge_ref, lon_ref, corner_ref = refs[:3]
        wide_ref, taps_in, tap_ref, spread_ref, out_ref, spare_ref, mix_lon = refs[3:]
    cols = lat_in.shape[1]
    groups = wide_ref.shape[0]
    main = 0 if shrink else EDGE
    side = cols if shrink else 0
    base = 0 if shrink else EDGE - SHIFT
    last = at_last()
    top = lax.axis_index("lat") == 0
    own = SHIFT if not shrink else 0
    if shrink:
        for g in range(groups):
            for k in range(2):
                spare = lon_in[SHIFT + k, :, lanes_of(g)].astype(F32)
                spare_ref[g, k * TILE : (k + 1) * TILE, :] = spare
    for k in range(SHIFT):
        value, beside = lat_in[k].astype(F32), corner_in[k].astype(F32)
        if not shrink:
            value, beside = jnp.where(top, 0.0, value), jnp.where(top, 0.0, beside)
        elif k < HALO:
            kept = left_in.shape[0] - SPARE + k
            inner = jnp.concatenate([left_in[kept], right_in[kept]], axis=0)
            value = jnp.where(last, inner.astype(F32), value)
            beside = beside[:SHIFT]
            extra = [spare_ref[g, pl.ds(k, SHIFT, stride=HALO), :] for g in range(groups)]
            beside = jnp.where(last, jnp.concatenate(extra, axis=1), beside)
        else:
            value, beside = jnp.where(last, 0.0, value), jnp.where(last, 0.0, beside)
        put(wide_ref, k, main, value)
        put(wide_ref, k, side, beside)
        shifted(wide_ref, taps_in, base, k, k if not shrink else k + SHIFT)
    taps_in[:, :, own : own + SHIFT] = near_ref[...]

    @pl.loop(0, groups)
    def _(g):
        convolve(taps_in, taps_ref, tap_ref, spread_ref, layer, g, 0, SHIFT)

    finish(taps_in, spread_ref, mix_ref, out_ref, layer, 0, SHIFT)
    kept = left_new.shape[0]
    if final:
        for k in range(SHIFT):
            state_ref[kept + k] = row_of(out_ref, k).astype(BF16)
        state_ref[0:kept, 0:TILE, :] = left_new[...]
        state_ref[0:kept, TILE:cols, :] = right_new[...]
        return

    for k in range(SHIFT):
        value = row_of(out_ref, k)
        if not shrink and k < HALO:
            value = jnp.where(top, 0.0, value)
        edge_ref[k] = value.astype(BF16)
        corner_ref[k] = (value[cols - EDGE :] if shrink else value[:EDGE]).astype(BF16)
    edge = cols - SHIFT if shrink else 0
    place = TILE - SHIFT if shrink else 0
    for g in range(groups):
        for x in range(SHIFT):
            column = flat(out_ref)[g, pl.ds(edge + x, SHIFT, stride=cols), :]
            if not shrink:
                outside = lax.broadcasted_iota(jnp.int32, (SHIFT, LANES), 0) < HALO
                column = jnp.where(jnp.logical_and(top, outside), 0.0, column)
            mix_lon[g, x] = lon_new[g, x]
            mix_lon[g, x, place : place + SHIFT, :] = column
            lon_ref[x, :, lanes_of(g)] = mix_lon[g, x].astype(BF16)
    if not shrink:
        for k in range(HALO):
            value = left_new[kept - SPARE + k].astype(F32)
            for g in range(groups):
                spare_ref[g, pl.ds(k, SHIFT, stride=HALO), :] = value[:SHIFT, lanes_of(g)]
        for g in range(groups):
            for k in range(2):
                spare = spare_ref[g, k * TILE : (k + 1) * TILE, :]
                lon_ref[SHIFT + k, :, lanes_of(g)] = spare.astype(BF16)


def call(kernel, out_shape, inputs, scratch=(), limit=VMEM_LIMIT, space=None, work=0):
    whole = pl.BlockSpec(memory_space=pltpu.VMEM)
    single = isinstance(out_shape, jax.ShapeDtypeStruct)
    spaces = space or (pltpu.VMEM,) * len(inputs)
    return pl.pallas_call(
        kernel,
        out_shape=out_shape,
        in_specs=[pl.BlockSpec(memory_space=s) for s in spaces],
        out_specs=whole if single else [whole] * len(out_shape),
        scratch_shapes=list(scratch),
        compiler_params=pltpu.CompilerParams(vmem_limit_bytes=limit),
        cost_estimate=pl.CostEstimate(flops=work, bytes_accessed=0, transcendentals=0),
    )(*inputs)


def held(*shape):
    return jax.ShapeDtypeStruct(shape, BF16)


def scratch_of(groups, seen, made, cols, chans):
    return (
        pltpu.VMEM((groups, seen, cols + EDGE, LANES), F32),
        pltpu.VMEM((groups, TAPS + 1, seen, TILE, LANES), BF16),
        pltpu.VMEM((TAPS * TAPS, TILE, LANES), BF16),
        pltpu.VMEM((2, made, TILE, chans), BF16),
        pltpu.VMEM((groups, made, cols, LANES), F32),
    )


def layer(state, lon_out, corner_out, taps, mix, number, shrink, final):
    edge, left, right = state
    lat_in, lon_in, corner_in = exchange((edge, lon_out, corner_out), not shrink)
    cols, chans = edge.shape[1:]
    groups = chans // LANES
    own = left.shape[0] - (SPARE if shrink else 0)
    rows = own + SHIFT
    spare = 0 if shrink else SPARE
    made = own + spare
    block = held(made, TILE, chans)
    scratch = (
        pltpu.VMEM((groups, rows + spare, cols + EDGE, LANES), F32),
        pltpu.VMEM((groups, TAPS + 1, own // 2 + TAPS - 1, TILE, LANES), BF16),
        pltpu.VMEM((TAPS * TAPS, TILE, LANES), BF16),
        pltpu.VMEM((2, own // 2, TILE, chans), BF16),
        pltpu.VMEM((groups, own, TILE, LANES), F32),
    )
    lead = call(
        functools.partial(block_kernel, shrink, True, number),
        block,
        (edge, left, right, taps, mix),
        scratch,
        work=made * TILE * chans * WORK,
    )
    trail, lon_new, near = call(
        functools.partial(block_kernel, shrink, False, number),
        (
            block,
            jax.ShapeDtypeStruct((groups, SHIFT, rows, LANES), F32),
            held(groups, TAPS + 1, SHIFT, TILE, LANES),
        ),
        (edge, left, right, lon_in, taps, mix),
        scratch,
        work=made * TILE * chans * WORK * 7 // 5,
    )
    new = (lead, trail) if shrink else (trail, lead)
    if final:
        outs = held(made + SHIFT, cols, chans)
    else:
        outs = (
            held(SHIFT, cols, chans),
            held(SHIFT if shrink else EDGE, rows, chans),
            held(SHIFT, EDGE, chans),
        )
    outs = call(
        functools.partial(edge_kernel, shrink, final, number),
        outs,
        (left, right, lon_in, lat_in, corner_in, near, *new, lon_new, taps, mix),
        scratch_of(groups, 2 * SHIFT, SHIFT, cols, chans)
        + (
            pltpu.VMEM((groups, 2 * TILE, LANES), F32),
            pltpu.VMEM((groups, SHIFT, rows, LANES), F32),
        ),
        work=SHIFT * cols * chans * WORK,
    )
    if final:
        return outs
    edge, lon_out, corner_out = outs
    return (edge, *new), lon_out, corner_out


def exchange(pieces, forward):
    lat, lon, corner = pieces
    count_lat = lax.axis_size("lat")
    count_lon = lax.axis_size("lon")
    along = [(i, (i + 1) % count_lat) for i in range(count_lat)]
    around = [(j, (j + 1) % count_lon) for j in range(count_lon)]
    across = [
        (i * count_lon + j, ni * count_lon + nj) for i, ni in along for j, nj in around
    ]
    if not forward:
        along, around, across = ([(t, s) for s, t in p] for p in (along, around, across))
    lon = lax.ppermute(lon, "lon", around)
    lat = lax.ppermute(lat, "lat", along)
    corner = lax.ppermute(corner, ("lat", "lon"), across)
    return lat, lon, corner


def body(
    background, observations, destination, footprint, weights, obs_proj, depth_w, point_w, gains
):
    rows, cols, chans = background.shape
    devices = lax.axis_size("lat") * lax.axis_size("lon")
    obs_rows, feats = observations.shape
    cap = 2 * obs_rows // devices
    depth = cap * (feats // LANES) + META
    foot_count = footprint.shape[1]
    send = call(
        functools.partial(pack_kernel, cap, cols),
        jax.ShapeDtypeStruct((devices, depth, LANES), BF16),
        (destination.T, footprint.T, weights.T, observations),
        (
            pltpu.VMEM((1, obs_rows), jnp.int32),
            pltpu.VMEM((foot_count, obs_rows), jnp.int32),
            pltpu.VMEM((foot_count, obs_rows), BF16),
            pltpu.VMEM((obs_rows, feats), BF16),
            pltpu.SemaphoreType.DMA((4,)),
        ),
        PACK_LIMIT,
        (pltpu.HBM,) * 4,
    )
    got = lax.all_to_all(send, ("lat", "lon"), split_axis=0, concat_axis=0, tiled=True)
    layers = depth_w.shape[0]
    taps = depth_w.transpose(1, 2, 0, 3).reshape(TAPS * TAPS, layers, chans)
    mix = (gains[:, :, None] * point_w.astype(F32)).astype(BF16)
    proj, back = call(
        fetch_kernel,
        (held(*obs_proj.shape), held(*background.shape)),
        (obs_proj, background),
        (pltpu.SemaphoreType.DMA((2,)),),
        space=(pltpu.HBM, pltpu.HBM),
    )
    got, mix, proj, back = lax.optimization_barrier((got, mix, proj, back))
    edge, left, right, lon_out, corner_out = call(
        functools.partial(assim_kernel, cap, cols + 1),
        (
            held(SHIFT, cols, chans),
            held(rows - SHIFT, TILE, chans),
            held(rows - SHIFT, TILE, chans),
            held(SHIFT, rows, chans),
            held(SHIFT, EDGE, chans),
        ),
        (got, proj, back),
        (
            pltpu.VMEM((devices, depth, LANES), BF16),
            pltpu.VMEM((chans // LANES, rows * EDGE, LANES), F32),
            pltpu.SemaphoreType.DMA((PIECES,)),
        ),
        space=(pltpu.HBM, pltpu.VMEM, pltpu.VMEM),
    )
    state = (edge, left, right)
    for n in range(layers - 1):
        state, lon_out, corner_out = layer(
            state, lon_out, corner_out, taps, mix, n, n % 2 == 1, False
        )
    n = layers - 1
    return layer(state, lon_out, corner_out, taps, mix, n, n % 2 == 1, True)


def solution(mesh):
    placed = (
        P("lat", "lon", None),
        P(("lat", "lon"), None),
        P(("lat", "lon"), None),
        P(("lat", "lon"), None),
        P(("lat", "lon"), None),
        P(),
        P(),
        P(),
        P(),
    )
    return jax.shard_map(
        body, mesh=mesh, in_specs=placed, out_specs=P("lat", "lon", None), check_vma=False
    )
```

```python
import functools

import jax
import jax.numpy as jnp
from jax import lax
from jax.experimental import pallas as pl
from jax.experimental.pallas import tpu as pltpu
from jax.sharding import PartitionSpec as P

LANES = 128
META = 8
TAPS = 7
HALO = 3
SHIFT = 2 * HALO
EDGE = 8
TILE = 16
PIECES = 4
SPARE = 4
WORK = 5000
VMEM_LIMIT = 24 * 1024 * 1024
PACK_LIMIT = 58 * 1024 * 1024
BF16 = jnp.bfloat16
F32 = jnp.float32


def pack_kernel(cap, cols, dest_hbm, foot_hbm, weights_hbm, obs_hbm, send_ref, dest_ref, foot_ref, weights_ref, obs_ref, sems):
    copies = [
        pltpu.make_async_copy(source, target, sems.at[k])
        for k, (source, target) in enumerate(
            (
                (dest_hbm, dest_ref),
                (obs_hbm, obs_ref),
                (foot_hbm, foot_ref),
                (weights_hbm, weights_ref),
            )
        )
    ]
    for copy in copies:
        copy.start()
    devices = send_ref.shape[0]
    obs_rows = obs_ref.shape[0]
    per = LANES // cap
    upper = lax.broadcasted_iota(jnp.int32, (LANES, LANES), 0) <= lax.broadcasted_iota(
        jnp.int32, (LANES, LANES), 1
    )
    upper = jnp.where(upper, 1.0, 0.0).astype(BF16)
    ids = lax.broadcasted_iota(jnp.int32, (devices, obs_rows), 0)
    copies[0].wait()
    member = jnp.where(ids == dest_ref[...], 1.0, 0.0)
    seen = jnp.zeros((devices, 1), F32)
    ranks = []
    for first in range(0, obs_rows, LANES):
        part = member[:, first : first + LANES]
        count = jnp.dot(part.astype(BF16), upper, preferred_element_type=F32) + seen
        ranks.append(jnp.sum((count - 1.0) * part, axis=0, keepdims=True))
        seen = count[:, LANES - 1 :]
    rank = jnp.concatenate(ranks, axis=1).astype(jnp.int32)
    slot = lax.broadcasted_iota(jnp.int32, (cap, obs_rows), 0)
    ranked = jnp.where(slot == rank, 1.0, 0.0).astype(BF16).reshape(cap // TILE, TILE, obs_rows)
    for copy in copies[1:]:
        copy.wait()
    start = foot_ref[0:1, :]
    meta = jnp.concatenate(
        [
            lax.div(start, cols).astype(F32),
            lax.rem(start, cols).astype(F32),
            weights_ref[...].astype(F32),
            jnp.zeros((META - 2 - weights_ref.shape[0], obs_rows), F32),
        ],
        axis=0,
    ).astype(BF16)
    obs = obs_ref[...]
    lane = lax.broadcasted_iota(jnp.int32, (META, LANES), 1)
    count = min(512, devices * cap) // cap
    for first in range(0, devices, count):
        parts = []
        for d in range(first, first + count):
            mine = jnp.broadcast_to(member[d : d + 1], (TILE, obs_rows)).astype(BF16)
            parts.append((ranked * mine[None]).reshape(cap, obs_rows))
        chosen = jnp.concatenate(parts, axis=0)
        feats = jnp.dot(chosen, obs, preferred_element_type=F32).astype(BF16)
        placed = lax.dot_general(
            meta, chosen, (((1,), (1,)), ((), ())), preferred_element_type=F32
        )
        for half in range(feats.shape[1] // LANES):
            piece = feats[:, half * LANES : (half + 1) * LANES].reshape(count, cap, LANES)
            send_ref[first : first + count, half * cap : (half + 1) * cap, :] = piece
        base = send_ref.shape[1] - META
        for chunk in range(count // per):
            values = placed[:, chunk * LANES : (chunk + 1) * LANES]
            turned = [values] + [pltpu.roll(values, k * cap, 1) for k in range(1, per)]
            for own in range(per):
                wide = turned[0]
                for group in range(per):
                    wide = jnp.where(lane // cap == group, turned[(group - own) % per], wide)
                send_ref[first + chunk * per + own, base:, :] = wide.astype(BF16)


def fetch_kernel(proj_hbm, back_hbm, proj_ref, back_ref, sems):
    copies = (
        pltpu.make_async_copy(proj_hbm, proj_ref, sems.at[0]),
        pltpu.make_async_copy(back_hbm, back_ref, sems.at[1]),
    )
    for copy in copies:
        copy.start()
    for copy in copies:
        copy.wait()


def assim_kernel(
    cap,
    got_hbm,
    proj_ref,
    back_ref,
    edge_ref,
    left_ref,
    right_ref,
    lon_ref,
    corner_ref,
    got_ref,
    wide_ref,
    sems,
):
    piece = got_ref.shape[0] // PIECES
    copies = [
        pltpu.make_async_copy(
            got_hbm.at[k * piece : (k + 1) * piece],
            got_ref.at[k * piece : (k + 1) * piece],
            sems.at[k],
        )
        for k in range(PIECES)
    ]
    for copy in copies:
        copy.start()
    devices, depth, _ = got_ref.shape
    rows, cols, chans = back_ref.shape
    cells = rows * cols
    feats = proj_ref.shape[0]
    per = LANES // cap
    halves = feats // LANES
    lane = lax.broadcasted_iota(jnp.int32, (META, LANES), 1)
    every_row = lax.broadcasted_iota(jnp.int32, (rows, LANES), 0).astype(F32)
    every_column = lax.broadcasted_iota(jnp.int32, (cols, LANES), 0).astype(F32)
    total = jnp.zeros((cells, feats), F32)
    for pair in range(0, devices // per, 2):
        if pair * per % piece == 0:
            copies[pair * per // piece].wait()
        maps = []
        blocks = []
        for chunk in (pair, pair + 1):
            meta = got_ref[chunk * per, depth - META :, :].astype(F32)
            for group in range(1, per):
                other = got_ref[chunk * per + group, depth - META :, :].astype(F32)
                meta = jnp.where(lane // cap == group, other, meta)
            row, column = meta[0:1], meta[1:2]
            amount = jnp.zeros((rows, LANES), F32)
            place = jnp.full((rows, LANES), -1.0, F32)
            for entry in range(4):
                at = column + entry
                over = at >= cols
                below = row + entry + jnp.where(over, 1.0, 0.0)
                hit = every_row == jnp.where(below >= rows, below - rows, below)
                place = jnp.where(hit, jnp.where(over, at - cols, at), place)
                amount = jnp.where(hit, meta[2 + entry : 3 + entry], amount)
            amount = jnp.concatenate(
                [
                    jnp.where(every_column == place[y : y + 1], amount[y : y + 1], 0.0)
                    for y in range(rows)
                ],
                axis=0,
            )
            maps.append(amount.astype(BF16))
            block = got_ref[chunk * per : (chunk + 1) * per]
            blocks.append(
                jnp.concatenate(
                    [
                        block[:, half * cap : (half + 1) * cap, :].reshape(LANES, LANES)
                        for half in range(halves)
                    ],
                    axis=1,
                )
            )
        total = total + jnp.dot(
            jnp.concatenate(maps, axis=1),
            jnp.concatenate(blocks, axis=0),
            preferred_element_type=F32,
        )
    assim = jnp.dot(total.astype(BF16), proj_ref[...], preferred_element_type=F32)
    state = back_ref[...].astype(F32) + assim.reshape(rows, cols, chans)
    for g in range(chans // LANES):
        wide_ref[g] = state[:, cols - EDGE :, lanes_of(g)].reshape(rows * EDGE, LANES)
    state = state.astype(BF16)
    edge_ref[...] = state[rows - SHIFT :]
    left_ref[...] = state[: rows - SHIFT, :TILE]
    right_ref[...] = state[: rows - SHIFT, TILE:]
    for x in range(SHIFT):
        for g in range(chans // LANES):
            column = wide_ref[g, pl.ds(EDGE - SHIFT + x, rows, stride=EDGE), :]
            lon_ref[x, :, lanes_of(g)] = column.astype(BF16)
    corner_ref[...] = state[rows - SHIFT :, cols - EDGE :, :]


def gelu(half):
    inner = half * (1.5957691216057308 + 0.285419265090401 * (half * half))
    return half + half * jnp.tanh(inner)


def put(wide_ref, row, start, value):
    for g in range(wide_ref.shape[0]):
        wide_ref[g, row, start : start + value.shape[0], :] = value[:, g * LANES : (g + 1) * LANES]


def shifted(wide_ref, taps_in, base, row, target):
    for g in range(wide_ref.shape[0]):
        for r in range(TAPS + 1):
            columns = pl.ds(base + r, TILE, stride=2)
            taps_in[g, r, target] = wide_ref[g, row, columns, :].astype(BF16)


def convolve(taps_in, taps_ref, tap_ref, spread_ref, layer, g, first, count):
    lanes = pl.ds(pl.multiple_of(g * LANES, LANES), LANES)
    for k in range(TAPS * TAPS):
        row = taps_ref[k, layer : layer + 1, lanes]
        tap_ref[k] = jnp.broadcast_to(row, (TILE, LANES)).astype(BF16)
    for p in range(2):
        total = None
        for b in range(TAPS):
            seen = taps_in[g, p + b, first : first + count + TAPS - 1]
            part = None
            for a in range(TAPS):
                term = seen[a : a + count] * tap_ref[a * TAPS + b]
                part = term if part is None else part + term
            total = part if total is None else total + part
        spread_ref[p, first : first + count, :, lanes] = total


def finish(taps_in, spread_ref, mix_ref, out_ref, layer, first, count, stacked=1):
    chans = mix_ref.shape[1]
    ones = jnp.ones((chans, LANES), BF16)
    step = TILE // stacked
    spread = spread_ref[:, first : first + count].reshape(2 * count * TILE, chans)
    power = jnp.dot(spread * spread, ones, preferred_element_type=F32)
    scale = 0.5 * lax.rsqrt(power * (1.0 / chans) + 1e-05)
    mixed = jnp.dot(spread, mix_ref[layer], preferred_element_type=F32)
    for g in range(chans // LANES):
        moved = gelu(mixed[:, lanes_of(g)] * scale).reshape(2, count, TILE, LANES)
        for p in range(2):
            center = taps_in[g, p + HALO, first + HALO : first + HALO + count].astype(F32)
            fresh = center + moved[p]
            for k in range(count):
                for h in range(stacked):
                    row = first * stacked + h * count + k
                    out_ref[g, row, pl.ds(p, step, stride=2), :] = fresh[
                        k, h * step : (h + 1) * step
                    ]


def row_of(out_ref, y):
    return jnp.concatenate([out_ref[g, y] for g in range(out_ref.shape[0])], axis=1)


def flat(ref):
    groups, rows, width, lanes = ref.shape
    return ref.reshape(groups, rows * width, lanes)


def lanes_of(g):
    return slice(g * LANES, (g + 1) * LANES)


def at_last():
    return lax.axis_index("lat") == lax.axis_size("lat") - 1


def block_kernel(shrink, lead, layer, edge_in, left_in, right_in, *refs):
    if lead:
        taps_ref, mix_ref, block_ref, *scratch = refs
    else:
        lon_in, taps_ref, mix_ref, block_ref, lon_ref, near_ref, *scratch = refs
    wide_ref, taps_in, tap_ref, spread_ref, out_ref = scratch
    cols = edge_in.shape[1]
    groups = wide_ref.shape[0]
    width = wide_ref.shape[2]
    own = left_in.shape[0] - (SPARE if shrink else 0)
    rows = own + SHIFT
    main = 0 if shrink else EDGE
    base = 0 if shrink else EDGE - SHIFT
    start = base + (0 if lead == shrink else TILE)

    if not lead:
        side = cols if shrink else base
        for g in range(groups):
            for x in range(SHIFT):
                column = lon_in[x, 0:rows, lanes_of(g)].astype(F32)
                flat(wide_ref)[g, pl.ds(side + x, rows, stride=width), :] = column

    @pl.loop(0, SHIFT, unroll=2)
    def _(y):
        put(wide_ref, y if shrink else own + y, main, edge_in[y].astype(F32))

    @pl.loop(0, own, unroll=2)
    def _(y):
        place = y + SHIFT if shrink else y
        put(wide_ref, place, main, left_in[y].astype(F32))
        put(wide_ref, place, main + TILE, right_in[y].astype(F32))

    def stage(high):
        @pl.loop(0, high + TAPS - 1)
        def _(y):
            for g in range(groups):
                for r in range(TAPS + 1):
                    both = [
                        wide_ref[g, y + h, pl.ds(start + r, TILE // 2, stride=2), :]
                        for h in (0, high)
                    ]
                    taps_in[g, r, y] = jnp.concatenate(both, axis=0).astype(BF16)

        @pl.loop(0, groups)
        def _(g):
            convolve(taps_in, taps_ref, tap_ref, spread_ref, layer, g, 0, high)

        finish(taps_in, spread_ref, mix_ref, out_ref, layer, 0, high, 2)

        @pl.loop(0, 2 * high, unroll=2)
        def _(y):
            block_ref[y] = row_of(out_ref, y).astype(BF16)

    if shrink:
        stage(own // 2)
    else:

        @pl.when(at_last())
        def _():
            wide_ref[:, rows:] = jnp.zeros((groups, SPARE, width, LANES), F32)
            stage((own + SPARE) // 2)

        @pl.when(jnp.logical_not(at_last()))
        def _():
            stage(own // 2)

    if not lead:
        edge = TILE - SHIFT if shrink else 0
        above = 0 if shrink else SHIFT
        near = rows - SHIFT if shrink else 0
        for g in range(groups):
            for x in range(SHIFT):
                column = flat(out_ref)[g, pl.ds(edge + x, own, stride=TILE), :]
                lon_ref[g, x, above : above + own, :] = column
            for r in range(TAPS + 1):
                for k in range(SHIFT):
                    columns = pl.ds(base + r, TILE, stride=2)
                    near_ref[g, r, k] = wide_ref[g, near + k, columns, :].astype(BF16)

def edge_kernel(
    shrink,
    final,
    layer,
    left_in,
    right_in,
    lon_in,
    lat_in,
    corner_in,
    near_ref,
    left_new,
    right_new,
    lon_new,
    taps_ref,
    mix_ref,
    *refs,
):
    if final:
        state_ref, wide_ref, taps_in, tap_ref, spread_ref, out_ref, spare_ref, mix_lon = refs[:8]
        rows_ref, sems = refs[8:]
        kept, width = left_new.shape[:2]
        copies = [
            pltpu.make_async_copy(left_new, state_ref.at[0:kept, 0:width], sems.at[0]),
            pltpu.make_async_copy(
                right_new, state_ref.at[0:kept, width : 2 * width], sems.at[1]
            ),
            pltpu.make_async_copy(rows_ref, state_ref.at[kept : kept + SHIFT], sems.at[2]),
        ]
        copies[0].start()
        copies[1].start()
    else:
        edge_ref, lon_ref, corner_ref = refs[:3]
        wide_ref, taps_in, tap_ref, spread_ref, out_ref, spare_ref, mix_lon = refs[3:]
    cols = lat_in.shape[1]
    groups = wide_ref.shape[0]
    main = 0 if shrink else EDGE
    side = cols if shrink else 0
    base = 0 if shrink else EDGE - SHIFT
    last = at_last()
    top = lax.axis_index("lat") == 0
    own = SHIFT if not shrink else 0
    if shrink:
        for g in range(groups):
            for k in range(2):
                spare = lon_in[SHIFT + k, :, lanes_of(g)].astype(F32)
                spare_ref[g, k * TILE : (k + 1) * TILE, :] = spare
    for k in range(SHIFT):
        value, beside = lat_in[k].astype(F32), corner_in[k].astype(F32)
        if not shrink:
            value, beside = jnp.where(top, 0.0, value), jnp.where(top, 0.0, beside)
        elif k < HALO:
            kept = left_in.shape[0] - SPARE + k
            inner = jnp.concatenate([left_in[kept], right_in[kept]], axis=0)
            value = jnp.where(last, inner.astype(F32), value)
            beside = beside[:SHIFT]
            extra = [spare_ref[g, pl.ds(k, SHIFT, stride=HALO), :] for g in range(groups)]
            beside = jnp.where(last, jnp.concatenate(extra, axis=1), beside)
        else:
            value, beside = jnp.where(last, 0.0, value), jnp.where(last, 0.0, beside)
        put(wide_ref, k, main, value)
        put(wide_ref, k, side, beside)
        shifted(wide_ref, taps_in, base, k, k if not shrink else k + SHIFT)
    taps_in[:, :, own : own + SHIFT] = near_ref[...]

    @pl.loop(0, groups)
    def _(g):
        convolve(taps_in, taps_ref, tap_ref, spread_ref, layer, g, 0, SHIFT)

    finish(taps_in, spread_ref, mix_ref, out_ref, layer, 0, SHIFT)
    kept = left_new.shape[0]
    if final:
        for k in range(SHIFT):
            rows_ref[k] = row_of(out_ref, k).astype(BF16)
        copies[2].start()
        for copy in copies:
            copy.wait()
        return

    for k in range(SHIFT):
        value = row_of(out_ref, k)
        if not shrink and k < HALO:
            value = jnp.where(top, 0.0, value)
        edge_ref[k] = value.astype(BF16)
        corner_ref[k] = (value[cols - EDGE :] if shrink else value[:EDGE]).astype(BF16)
    edge = cols - SHIFT if shrink else 0
    place = TILE - SHIFT if shrink else 0
    for g in range(groups):
        for x in range(SHIFT):
            column = flat(out_ref)[g, pl.ds(edge + x, SHIFT, stride=cols), :]
            if not shrink:
                outside = lax.broadcasted_iota(jnp.int32, (SHIFT, LANES), 0) < HALO
                column = jnp.where(jnp.logical_and(top, outside), 0.0, column)
            mix_lon[g, x] = lon_new[g, x]
            mix_lon[g, x, place : place + SHIFT, :] = column
            lon_ref[x, :, lanes_of(g)] = mix_lon[g, x].astype(BF16)
    if not shrink:
        for k in range(HALO):
            value = left_new[kept - SPARE + k].astype(F32)
            for g in range(groups):
                spare_ref[g, pl.ds(k, SHIFT, stride=HALO), :] = value[:SHIFT, lanes_of(g)]
        for g in range(groups):
            for k in range(2):
                spare = spare_ref[g, k * TILE : (k + 1) * TILE, :]
                lon_ref[SHIFT + k, :, lanes_of(g)] = spare.astype(BF16)


def call(kernel, out_shape, inputs, scratch=(), limit=VMEM_LIMIT, space=None, work=0, out_space=pltpu.VMEM):
    whole = pl.BlockSpec(memory_space=out_space)
    single = isinstance(out_shape, jax.ShapeDtypeStruct)
    spaces = space or (pltpu.VMEM,) * len(inputs)
    return pl.pallas_call(
        kernel,
        out_shape=out_shape,
        in_specs=[pl.BlockSpec(memory_space=s) for s in spaces],
        out_specs=whole if single else [whole] * len(out_shape),
        scratch_shapes=list(scratch),
        compiler_params=pltpu.CompilerParams(vmem_limit_bytes=limit),
        cost_estimate=pl.CostEstimate(flops=work, bytes_accessed=0, transcendentals=0),
    )(*inputs)


def held(*shape):
    return jax.ShapeDtypeStruct(shape, BF16)


def scratch_of(groups, seen, made, cols, chans):
    return (
        pltpu.VMEM((groups, seen, cols + EDGE, LANES), F32),
        pltpu.VMEM((groups, TAPS + 1, seen, TILE, LANES), BF16),
        pltpu.VMEM((TAPS * TAPS, TILE, LANES), BF16),
        pltpu.VMEM((2, made, TILE, chans), BF16),
        pltpu.VMEM((groups, made, cols, LANES), F32),
    )


def layer(state, lon_out, corner_out, taps, mix, number, shrink, final):
    edge, left, right = state
    lat_in, lon_in, corner_in = exchange((edge, lon_out, corner_out), not shrink)
    cols, chans = edge.shape[1:]
    groups = chans // LANES
    own = left.shape[0] - (SPARE if shrink else 0)
    rows = own + SHIFT
    spare = 0 if shrink else SPARE
    made = own + spare
    block = held(made, TILE, chans)
    scratch = (
        pltpu.VMEM((groups, rows + spare, cols + EDGE, LANES), F32),
        pltpu.VMEM((groups, TAPS + 1, made // 2 + TAPS - 1, TILE, LANES), BF16),
        pltpu.VMEM((TAPS * TAPS, TILE, LANES), BF16),
        pltpu.VMEM((2, made // 2, TILE, chans), BF16),
        pltpu.VMEM((groups, made, TILE, LANES), F32),
    )
    lead = call(
        functools.partial(block_kernel, shrink, True, number),
        block,
        (edge, left, right, taps, mix),
        scratch,
        work=made * TILE * chans * WORK,
    )
    trail, lon_new, near = call(
        functools.partial(block_kernel, shrink, False, number),
        (
            block,
            jax.ShapeDtypeStruct((groups, SHIFT, rows, LANES), F32),
            held(groups, TAPS + 1, SHIFT, TILE, LANES),
        ),
        (edge, left, right, lon_in, taps, mix),
        scratch,
        work=made * TILE * chans * WORK * 7 // 5,
    )
    new = (lead, trail) if shrink else (trail, lead)
    last_scratch = ()
    if final:
        outs = held(made + SHIFT, cols, chans)
        last_scratch = (pltpu.VMEM((SHIFT, cols, chans), BF16), pltpu.SemaphoreType.DMA((3,)))
    else:
        outs = (
            held(SHIFT, cols, chans),
            held(SHIFT if shrink else EDGE, rows, chans),
            held(SHIFT, EDGE, chans),
        )
    outs = call(
        functools.partial(edge_kernel, shrink, final, number),
        outs,
        (left, right, lon_in, lat_in, corner_in, near, *new, lon_new, taps, mix),
        scratch_of(groups, 2 * SHIFT, SHIFT, cols, chans)
        + (
            pltpu.VMEM((groups, 2 * TILE, LANES), F32),
            pltpu.VMEM((groups, SHIFT, rows, LANES), F32),
        )
        + last_scratch,
        out_space=pltpu.HBM if final else pltpu.VMEM,
        work=SHIFT * cols * chans * WORK,
    )
    if final:
        return outs
    edge, lon_out, corner_out = outs
    return (edge, *new), lon_out, corner_out


def exchange(pieces, forward):
    lat, lon, corner = pieces
    count_lat = lax.axis_size("lat")
    count_lon = lax.axis_size("lon")
    along = [(i, (i + 1) % count_lat) for i in range(count_lat)]
    around = [(j, (j + 1) % count_lon) for j in range(count_lon)]
    across = [
        (i * count_lon + j, ni * count_lon + nj) for i, ni in along for j, nj in around
    ]
    if not forward:
        along, around, across = ([(t, s) for s, t in p] for p in (along, around, across))
    lon = lax.ppermute(lon, "lon", around)
    lat = lax.ppermute(lat, "lat", along)
    corner = lax.ppermute(corner, ("lat", "lon"), across)
    return lat, lon, corner


def body(
    background, observations, destination, footprint, weights, obs_proj, depth_w, point_w, gains
):
    rows, cols, chans = background.shape
    devices = lax.axis_size("lat") * lax.axis_size("lon")
    obs_rows, feats = observations.shape
    cap = 2 * obs_rows // devices
    depth = cap * (feats // LANES) + META
    foot_count = footprint.shape[1]
    send = call(
        functools.partial(pack_kernel, cap, cols),
        jax.ShapeDtypeStruct((devices, depth, LANES), BF16),
        (destination.T, footprint.T, weights.T, observations),
        (
            pltpu.VMEM((1, obs_rows), jnp.int32),
            pltpu.VMEM((foot_count, obs_rows), jnp.int32),
            pltpu.VMEM((foot_count, obs_rows), BF16),
            pltpu.VMEM((obs_rows, feats), BF16),
            pltpu.SemaphoreType.DMA((4,)),
        ),
        PACK_LIMIT,
        (pltpu.HBM,) * 4,
    )
    got = lax.all_to_all(send, ("lat", "lon"), split_axis=0, concat_axis=0, tiled=True)
    layers = depth_w.shape[0]
    taps = depth_w.transpose(1, 2, 0, 3).reshape(TAPS * TAPS, layers, chans)
    mix = (gains[:, :, None] * point_w.astype(F32)).astype(BF16)
    proj, back = call(
        fetch_kernel,
        (held(*obs_proj.shape), held(*background.shape)),
        (obs_proj, background),
        (pltpu.SemaphoreType.DMA((2,)),),
        space=(pltpu.HBM, pltpu.HBM),
    )
    got, mix, proj, back = lax.optimization_barrier((got, mix, proj, back))
    edge, left, right, lon_out, corner_out = call(
        functools.partial(assim_kernel, cap),
        (
            held(SHIFT, cols, chans),
            held(rows - SHIFT, TILE, chans),
            held(rows - SHIFT, TILE, chans),
            held(SHIFT, rows, chans),
            held(SHIFT, EDGE, chans),
        ),
        (got, proj, back),
        (
            pltpu.VMEM((devices, depth, LANES), BF16),
            pltpu.VMEM((chans // LANES, rows * EDGE, LANES), F32),
            pltpu.SemaphoreType.DMA((PIECES,)),
        ),
        space=(pltpu.HBM, pltpu.VMEM, pltpu.VMEM),
    )
    state = (edge, left, right)
    for n in range(layers - 1):
        state, lon_out, corner_out = layer(
            state, lon_out, corner_out, taps, mix, n, n % 2 == 1, False
        )
    n = layers - 1
    return layer(state, lon_out, corner_out, taps, mix, n, n % 2 == 1, True)


def solution(mesh):
    placed = (
        P("lat", "lon", None),
        P(("lat", "lon"), None),
        P(("lat", "lon"), None),
        P(("lat", "lon"), None),
        P(("lat", "lon"), None),
        P(),
        P(),
        P(),
        P(),
    )
    return jax.shard_map(
        body, mesh=mesh, in_specs=placed, out_specs=P("lat", "lon", None), check_vma=False
    )
```

```python
import functools

import jax
import jax.numpy as jnp
from jax import lax
from jax.experimental import pallas as pl
from jax.experimental.pallas import tpu as pltpu
from jax.sharding import PartitionSpec as P

LANES = 128
META = 8
TAPS = 7
HALO = 3
SHIFT = 2 * HALO
EDGE = 8
TILE = 16
PIECES = 4
SPARE = 4
WORK = 1000
VMEM_LIMIT = 24 * 1024 * 1024
PACK_LIMIT = 58 * 1024 * 1024
BF16 = jnp.bfloat16
F32 = jnp.float32


def pack_kernel(cap, cols, dest_hbm, foot_hbm, weights_hbm, obs_hbm, send_ref, dest_ref, foot_ref, weights_ref, obs_ref, sems):
    copies = [
        pltpu.make_async_copy(source, target, sems.at[k])
        for k, (source, target) in enumerate(
            (
                (dest_hbm, dest_ref),
                (obs_hbm, obs_ref),
                (foot_hbm, foot_ref),
                (weights_hbm, weights_ref),
            )
        )
    ]
    for copy in copies:
        copy.start()
    devices = send_ref.shape[0]
    obs_rows = obs_ref.shape[0]
    per = LANES // cap
    upper = lax.broadcasted_iota(jnp.int32, (LANES, LANES), 0) <= lax.broadcasted_iota(
        jnp.int32, (LANES, LANES), 1
    )
    upper = jnp.where(upper, 1.0, 0.0).astype(BF16)
    ids = lax.broadcasted_iota(jnp.int32, (devices, obs_rows), 0)
    copies[0].wait()
    member = jnp.where(ids == dest_ref[...], 1.0, 0.0)
    seen = jnp.zeros((devices, 1), F32)
    ranks = []
    for first in range(0, obs_rows, LANES):
        part = member[:, first : first + LANES]
        count = jnp.dot(part.astype(BF16), upper, preferred_element_type=F32) + seen
        ranks.append(jnp.sum((count - 1.0) * part, axis=0, keepdims=True))
        seen = count[:, LANES - 1 :]
    rank = jnp.concatenate(ranks, axis=1).astype(jnp.int32)
    slot = lax.broadcasted_iota(jnp.int32, (cap, obs_rows), 0)
    ranked = jnp.where(slot == rank, 1.0, 0.0).astype(BF16).reshape(cap // TILE, TILE, obs_rows)
    for copy in copies[1:]:
        copy.wait()
    start = foot_ref[0:1, :]
    meta = jnp.concatenate(
        [
            lax.div(start, cols).astype(F32),
            lax.rem(start, cols).astype(F32),
            weights_ref[...].astype(F32),
            jnp.zeros((META - 2 - weights_ref.shape[0], obs_rows), F32),
        ],
        axis=0,
    ).astype(BF16)
    obs = obs_ref[...]
    lane = lax.broadcasted_iota(jnp.int32, (META, LANES), 1)
    count = min(512, devices * cap) // cap
    for first in range(0, devices, count):
        parts = []
        for d in range(first, first + count):
            mine = jnp.broadcast_to(member[d : d + 1], (TILE, obs_rows)).astype(BF16)
            parts.append((ranked * mine[None]).reshape(cap, obs_rows))
        chosen = jnp.concatenate(parts, axis=0)
        feats = jnp.dot(chosen, obs, preferred_element_type=F32).astype(BF16)
        placed = lax.dot_general(
            meta, chosen, (((1,), (1,)), ((), ())), preferred_element_type=F32
        )
        for half in range(feats.shape[1] // LANES):
            piece = feats[:, half * LANES : (half + 1) * LANES].reshape(count, cap, LANES)
            send_ref[first : first + count, half * cap : (half + 1) * cap, :] = piece
        base = send_ref.shape[1] - META
        for chunk in range(count // per):
            values = placed[:, chunk * LANES : (chunk + 1) * LANES]
            turned = [values] + [pltpu.roll(values, k * cap, 1) for k in range(1, per)]
            for own in range(per):
                wide = turned[0]
                for group in range(per):
                    wide = jnp.where(lane // cap == group, turned[(group - own) % per], wide)
                send_ref[first + chunk * per + own, base:, :] = wide.astype(BF16)


def fetch_kernel(proj_hbm, back_hbm, proj_ref, back_ref, sems):
    copies = (
        pltpu.make_async_copy(proj_hbm, proj_ref, sems.at[0]),
        pltpu.make_async_copy(back_hbm, back_ref, sems.at[1]),
    )
    for copy in copies:
        copy.start()
    for copy in copies:
        copy.wait()


def assim_kernel(
    cap,
    got_hbm,
    proj_ref,
    back_ref,
    edge_ref,
    left_ref,
    right_ref,
    lon_ref,
    corner_ref,
    got_ref,
    wide_ref,
    sems,
):
    piece = got_ref.shape[0] // PIECES
    copies = [
        pltpu.make_async_copy(
            got_hbm.at[k * piece : (k + 1) * piece],
            got_ref.at[k * piece : (k + 1) * piece],
            sems.at[k],
        )
        for k in range(PIECES)
    ]
    for copy in copies:
        copy.start()
    devices, depth, _ = got_ref.shape
    rows, cols, chans = back_ref.shape
    cells = rows * cols
    feats = proj_ref.shape[0]
    per = LANES // cap
    halves = feats // LANES
    lane = lax.broadcasted_iota(jnp.int32, (META, LANES), 1)
    every_row = lax.broadcasted_iota(jnp.int32, (rows, LANES), 0).astype(F32)
    every_column = lax.broadcasted_iota(jnp.int32, (cols, LANES), 0).astype(F32)
    total = jnp.zeros((cells, feats), F32)
    for pair in range(0, devices // per, 2):
        if pair * per % piece == 0:
            copies[pair * per // piece].wait()
        maps = []
        blocks = []
        for chunk in (pair, pair + 1):
            meta = got_ref[chunk * per, depth - META :, :].astype(F32)
            for group in range(1, per):
                other = got_ref[chunk * per + group, depth - META :, :].astype(F32)
                meta = jnp.where(lane // cap == group, other, meta)
            row, column = meta[0:1], meta[1:2]
            amount = jnp.zeros((rows, LANES), F32)
            place = jnp.full((rows, LANES), -1.0, F32)
            for entry in range(4):
                at = column + entry
                over = at >= cols
                below = row + entry + jnp.where(over, 1.0, 0.0)
                hit = every_row == jnp.where(below >= rows, below - rows, below)
                place = jnp.where(hit, jnp.where(over, at - cols, at), place)
                amount = jnp.where(hit, meta[2 + entry : 3 + entry], amount)
            amount = jnp.concatenate(
                [
                    jnp.where(every_column == place[y : y + 1], amount[y : y + 1], 0.0)
                    for y in range(rows)
                ],
                axis=0,
            )
            maps.append(amount.astype(BF16))
            block = got_ref[chunk * per : (chunk + 1) * per]
            blocks.append(
                jnp.concatenate(
                    [
                        block[:, half * cap : (half + 1) * cap, :].reshape(LANES, LANES)
                        for half in range(halves)
                    ],
                    axis=1,
                )
            )
        total = total + jnp.dot(
            jnp.concatenate(maps, axis=1),
            jnp.concatenate(blocks, axis=0),
            preferred_element_type=F32,
        )
    assim = jnp.dot(total.astype(BF16), proj_ref[...], preferred_element_type=F32)
    state = back_ref[...].astype(F32) + assim.reshape(rows, cols, chans)
    for g in range(chans // LANES):
        wide_ref[g] = state[:, cols - EDGE :, lanes_of(g)].reshape(rows * EDGE, LANES)
    state = state.astype(BF16)
    edge_ref[...] = state[rows - SHIFT :]
    left_ref[...] = state[: rows - SHIFT, :TILE]
    right_ref[...] = state[: rows - SHIFT, TILE:]
    for x in range(SHIFT):
        for g in range(chans // LANES):
            column = wide_ref[g, pl.ds(EDGE - SHIFT + x, rows, stride=EDGE), :]
            lon_ref[x, :, lanes_of(g)] = column.astype(BF16)
    corner_ref[...] = state[rows - SHIFT :, cols - EDGE :, :]


def gelu(half):
    inner = half * (1.5957691216057308 + 0.285419265090401 * (half * half))
    return half + half * jnp.tanh(inner)


def put(wide_ref, row, start, value):
    for g in range(wide_ref.shape[0]):
        wide_ref[g, row, start : start + value.shape[0], :] = value[:, g * LANES : (g + 1) * LANES]


def shifted(wide_ref, taps_in, base, row, target):
    for g in range(wide_ref.shape[0]):
        for r in range(TAPS + 1):
            columns = pl.ds(base + r, TILE, stride=2)
            taps_in[g, r, target] = wide_ref[g, row, columns, :].astype(BF16)


def convolve(taps_in, taps_ref, tap_ref, spread_ref, layer, g, first, count):
    lanes = pl.ds(pl.multiple_of(g * LANES, LANES), LANES)
    for k in range(TAPS * TAPS):
        row = taps_ref[k, layer : layer + 1, lanes]
        tap_ref[k] = jnp.broadcast_to(row, (TILE, LANES)).astype(BF16)
    for p in range(2):
        total = None
        for b in range(TAPS):
            seen = taps_in[g, p + b, first : first + count + TAPS - 1]
            part = None
            for a in range(TAPS):
                term = seen[a : a + count] * tap_ref[a * TAPS + b]
                part = term if part is None else part + term
            total = part if total is None else total + part
        spread_ref[p, first : first + count, :, lanes] = total


def finish(taps_in, spread_ref, mix_ref, out_ref, layer, first, count, stacked=1):
    chans = mix_ref.shape[1]
    ones = jnp.ones((chans, LANES), BF16)
    step = TILE // stacked
    spread = spread_ref[:, first : first + count].reshape(2 * count * TILE, chans)
    power = jnp.dot(spread * spread, ones, preferred_element_type=F32)
    scale = 0.5 * lax.rsqrt(power * (1.0 / chans) + 1e-05)
    mixed = jnp.dot(spread, mix_ref[layer], preferred_element_type=F32)
    for g in range(chans // LANES):
        moved = gelu(mixed[:, lanes_of(g)] * scale).reshape(2, count, TILE, LANES)
        for p in range(2):
            center = taps_in[g, p + HALO, first + HALO : first + HALO + count].astype(F32)
            fresh = center + moved[p]
            for k in range(count):
                for h in range(stacked):
                    row = first * stacked + h * count + k
                    out_ref[g, row, pl.ds(p, step, stride=2), :] = fresh[
                        k, h * step : (h + 1) * step
                    ]


def row_of(out_ref, y):
    return jnp.concatenate([out_ref[g, y] for g in range(out_ref.shape[0])], axis=1)


def flat(ref):
    groups, rows, width, lanes = ref.shape
    return ref.reshape(groups, rows * width, lanes)


def lanes_of(g):
    return slice(g * LANES, (g + 1) * LANES)


def at_last():
    return lax.axis_index("lat") == lax.axis_size("lat") - 1


def block_kernel(shrink, lead, layer, edge_in, left_in, right_in, *refs):
    if lead:
        taps_ref, mix_ref, block_ref, *scratch = refs
    else:
        lon_in, taps_ref, mix_ref, block_ref, lon_ref, near_ref, *scratch = refs
    wide_ref, taps_in, tap_ref, spread_ref, out_ref = scratch
    cols = edge_in.shape[1]
    groups = wide_ref.shape[0]
    width = wide_ref.shape[2]
    own = left_in.shape[0] - (SPARE if shrink else 0)
    rows = own + SHIFT
    main = 0 if shrink else EDGE
    base = 0 if shrink else EDGE - SHIFT
    start = base + (0 if lead == shrink else TILE)

    if not lead:
        side = cols if shrink else base
        for g in range(groups):
            for x in range(SHIFT):
                column = lon_in[x, 0:rows, lanes_of(g)].astype(F32)
                flat(wide_ref)[g, pl.ds(side + x, rows, stride=width), :] = column

    @pl.loop(0, SHIFT, unroll=2)
    def _(y):
        put(wide_ref, y if shrink else own + y, main, edge_in[y].astype(F32))

    @pl.loop(0, own, unroll=2)
    def _(y):
        place = y + SHIFT if shrink else y
        put(wide_ref, place, main, left_in[y].astype(F32))
        put(wide_ref, place, main + TILE, right_in[y].astype(F32))

    def stage(high):
        @pl.loop(0, high + TAPS - 1)
        def _(y):
            for g in range(groups):
                for r in range(TAPS + 1):
                    both = [
                        wide_ref[g, y + h, pl.ds(start + r, TILE // 2, stride=2), :]
                        for h in (0, high)
                    ]
                    taps_in[g, r, y] = jnp.concatenate(both, axis=0).astype(BF16)

        @pl.loop(0, groups)
        def _(g):
            convolve(taps_in, taps_ref, tap_ref, spread_ref, layer, g, 0, high)

        finish(taps_in, spread_ref, mix_ref, out_ref, layer, 0, high, 2)

        @pl.loop(0, 2 * high, unroll=2)
        def _(y):
            block_ref[y] = row_of(out_ref, y).astype(BF16)

    if shrink:
        stage(own // 2)
    else:

        @pl.when(at_last())
        def _():
            wide_ref[:, rows:] = jnp.zeros((groups, SPARE, width, LANES), F32)
            stage((own + SPARE) // 2)

        @pl.when(jnp.logical_not(at_last()))
        def _():
            stage(own // 2)

    if not lead:
        edge = TILE - SHIFT if shrink else 0
        above = 0 if shrink else SHIFT
        near = rows - SHIFT if shrink else 0
        for g in range(groups):
            for x in range(SHIFT):
                column = flat(out_ref)[g, pl.ds(edge + x, own, stride=TILE), :]
                lon_ref[g, x, above : above + own, :] = column
            for r in range(TAPS + 1):
                for k in range(SHIFT):
                    columns = pl.ds(base + r, TILE, stride=2)
                    near_ref[g, r, k] = wide_ref[g, near + k, columns, :].astype(BF16)

def edge_kernel(
    shrink,
    final,
    layer,
    left_in,
    right_in,
    lon_in,
    lat_in,
    corner_in,
    near_ref,
    left_new,
    right_new,
    lon_new,
    taps_ref,
    mix_ref,
    *refs,
):
    if final:
        state_ref, wide_ref, taps_in, tap_ref, spread_ref, out_ref, spare_ref, mix_lon = refs[:8]
        rows_ref, sems = refs[8:]
        kept, width = left_new.shape[:2]
        copies = [
            pltpu.make_async_copy(left_new, state_ref.at[0:kept, 0:width], sems.at[0]),
            pltpu.make_async_copy(
                right_new, state_ref.at[0:kept, width : 2 * width], sems.at[1]
            ),
            pltpu.make_async_copy(rows_ref, state_ref.at[kept : kept + SHIFT], sems.at[2]),
        ]
        copies[0].start()
        copies[1].start()
    else:
        edge_ref, lon_ref, corner_ref = refs[:3]
        wide_ref, taps_in, tap_ref, spread_ref, out_ref, spare_ref, mix_lon = refs[3:]
    cols = lat_in.shape[1]
    groups = wide_ref.shape[0]
    main = 0 if shrink else EDGE
    side = cols if shrink else 0
    base = 0 if shrink else EDGE - SHIFT
    last = at_last()
    top = lax.axis_index("lat") == 0
    own = SHIFT if not shrink else 0
    if shrink:
        for g in range(groups):
            for k in range(2):
                spare = lon_in[SHIFT + k, :, lanes_of(g)].astype(F32)
                spare_ref[g, k * TILE : (k + 1) * TILE, :] = spare
    for k in range(SHIFT):
        value, beside = lat_in[k].astype(F32), corner_in[k].astype(F32)
        if not shrink:
            value, beside = jnp.where(top, 0.0, value), jnp.where(top, 0.0, beside)
        elif k < HALO:
            kept = left_in.shape[0] - SPARE + k
            inner = jnp.concatenate([left_in[kept], right_in[kept]], axis=0)
            value = jnp.where(last, inner.astype(F32), value)
            beside = beside[:SHIFT]
            extra = [spare_ref[g, pl.ds(k, SHIFT, stride=HALO), :] for g in range(groups)]
            beside = jnp.where(last, jnp.concatenate(extra, axis=1), beside)
        else:
            value, beside = jnp.where(last, 0.0, value), jnp.where(last, 0.0, beside)
        put(wide_ref, k, main, value)
        put(wide_ref, k, side, beside)
        shifted(wide_ref, taps_in, base, k, k if not shrink else k + SHIFT)
    taps_in[:, :, own : own + SHIFT] = near_ref[...]

    @pl.loop(0, groups)
    def _(g):
        convolve(taps_in, taps_ref, tap_ref, spread_ref, layer, g, 0, SHIFT)

    finish(taps_in, spread_ref, mix_ref, out_ref, layer, 0, SHIFT)
    kept = left_new.shape[0]
    if final:
        for k in range(SHIFT):
            rows_ref[k] = row_of(out_ref, k).astype(BF16)
        copies[2].start()
        for copy in copies:
            copy.wait()
        return

    for k in range(SHIFT):
        value = row_of(out_ref, k)
        if not shrink and k < HALO:
            value = jnp.where(top, 0.0, value)
        edge_ref[k] = value.astype(BF16)
        corner_ref[k] = (value[cols - EDGE :] if shrink else value[:EDGE]).astype(BF16)
    edge = cols - SHIFT if shrink else 0
    place = TILE - SHIFT if shrink else 0
    for g in range(groups):
        for x in range(SHIFT):
            column = flat(out_ref)[g, pl.ds(edge + x, SHIFT, stride=cols), :]
            if not shrink:
                outside = lax.broadcasted_iota(jnp.int32, (SHIFT, LANES), 0) < HALO
                column = jnp.where(jnp.logical_and(top, outside), 0.0, column)
            mix_lon[g, x] = lon_new[g, x]
            mix_lon[g, x, place : place + SHIFT, :] = column
            lon_ref[x, :, lanes_of(g)] = mix_lon[g, x].astype(BF16)
    if not shrink:
        for k in range(HALO):
            value = left_new[kept - SPARE + k].astype(F32)
            for g in range(groups):
                spare_ref[g, pl.ds(k, SHIFT, stride=HALO), :] = value[:SHIFT, lanes_of(g)]
        for g in range(groups):
            for k in range(2):
                spare = spare_ref[g, k * TILE : (k + 1) * TILE, :]
                lon_ref[SHIFT + k, :, lanes_of(g)] = spare.astype(BF16)


def call(kernel, out_shape, inputs, scratch=(), limit=VMEM_LIMIT, space=None, work=0, out_space=pltpu.VMEM):
    whole = pl.BlockSpec(memory_space=out_space)
    single = isinstance(out_shape, jax.ShapeDtypeStruct)
    spaces = space or (pltpu.VMEM,) * len(inputs)
    return pl.pallas_call(
        kernel,
        out_shape=out_shape,
        in_specs=[pl.BlockSpec(memory_space=s) for s in spaces],
        out_specs=whole if single else [whole] * len(out_shape),
        scratch_shapes=list(scratch),
        compiler_params=pltpu.CompilerParams(vmem_limit_bytes=limit),
        cost_estimate=pl.CostEstimate(flops=work, bytes_accessed=0, transcendentals=0),
    )(*inputs)


def held(*shape):
    return jax.ShapeDtypeStruct(shape, BF16)


def scratch_of(groups, seen, made, cols, chans):
    return (
        pltpu.VMEM((groups, seen, cols + EDGE, LANES), F32),
        pltpu.VMEM((groups, TAPS + 1, seen, TILE, LANES), BF16),
        pltpu.VMEM((TAPS * TAPS, TILE, LANES), BF16),
        pltpu.VMEM((2, made, TILE, chans), BF16),
        pltpu.VMEM((groups, made, cols, LANES), F32),
    )


def layer(state, lon_out, corner_out, taps, mix, number, shrink, final):
    edge, left, right = state
    lat_in, lon_in, corner_in = exchange((edge, lon_out, corner_out), not shrink)
    cols, chans = edge.shape[1:]
    groups = chans // LANES
    own = left.shape[0] - (SPARE if shrink else 0)
    rows = own + SHIFT
    spare = 0 if shrink else SPARE
    made = own + spare
    block = held(made, TILE, chans)
    scratch = (
        pltpu.VMEM((groups, rows + spare, cols + EDGE, LANES), F32),
        pltpu.VMEM((groups, TAPS + 1, made // 2 + TAPS - 1, TILE, LANES), BF16),
        pltpu.VMEM((TAPS * TAPS, TILE, LANES), BF16),
        pltpu.VMEM((2, made // 2, TILE, chans), BF16),
        pltpu.VMEM((groups, made, TILE, LANES), F32),
    )
    lead = call(
        functools.partial(block_kernel, shrink, True, number),
        block,
        (edge, left, right, taps, mix),
        scratch,
        work=made * TILE * chans * WORK * (5 if shrink else 3),
    )
    trail, lon_new, near = call(
        functools.partial(block_kernel, shrink, False, number),
        (
            block,
            jax.ShapeDtypeStruct((groups, SHIFT, rows, LANES), F32),
            held(groups, TAPS + 1, SHIFT, TILE, LANES),
        ),
        (edge, left, right, lon_in, taps, mix),
        scratch,
        work=made * TILE * chans * WORK * (7 if shrink else 11),
    )
    new = (lead, trail) if shrink else (trail, lead)
    last_scratch = ()
    if final:
        outs = held(made + SHIFT, cols, chans)
        last_scratch = (pltpu.VMEM((SHIFT, cols, chans), BF16), pltpu.SemaphoreType.DMA((3,)))
    else:
        outs = (
            held(SHIFT, cols, chans),
            held(SHIFT if shrink else EDGE, rows, chans),
            held(SHIFT, EDGE, chans),
        )
    outs = call(
        functools.partial(edge_kernel, shrink, final, number),
        outs,
        (left, right, lon_in, lat_in, corner_in, near, *new, lon_new, taps, mix),
        scratch_of(groups, 2 * SHIFT, SHIFT, cols, chans)
        + (
            pltpu.VMEM((groups, 2 * TILE, LANES), F32),
            pltpu.VMEM((groups, SHIFT, rows, LANES), F32),
        )
        + last_scratch,
        out_space=pltpu.HBM if final else pltpu.VMEM,
        work=SHIFT * cols * chans * WORK * 5,
    )
    if final:
        return outs
    edge, lon_out, corner_out = outs
    return (edge, *new), lon_out, corner_out


def exchange(pieces, forward):
    lat, lon, corner = pieces
    count_lat = lax.axis_size("lat")
    count_lon = lax.axis_size("lon")
    along = [(i, (i + 1) % count_lat) for i in range(count_lat)]
    around = [(j, (j + 1) % count_lon) for j in range(count_lon)]
    across = [
        (i * count_lon + j, ni * count_lon + nj) for i, ni in along for j, nj in around
    ]
    if not forward:
        along, around, across = ([(t, s) for s, t in p] for p in (along, around, across))
    lon = lax.ppermute(lon, "lon", around)
    lat = lax.ppermute(lat, "lat", along)
    corner = lax.ppermute(corner, ("lat", "lon"), across)
    return lat, lon, corner


def body(
    background, observations, destination, footprint, weights, obs_proj, depth_w, point_w, gains
):
    rows, cols, chans = background.shape
    devices = lax.axis_size("lat") * lax.axis_size("lon")
    obs_rows, feats = observations.shape
    cap = 2 * obs_rows // devices
    depth = cap * (feats // LANES) + META
    foot_count = footprint.shape[1]
    send = call(
        functools.partial(pack_kernel, cap, cols),
        jax.ShapeDtypeStruct((devices, depth, LANES), BF16),
        (destination.T, footprint.T, weights.T, observations),
        (
            pltpu.VMEM((1, obs_rows), jnp.int32),
            pltpu.VMEM((foot_count, obs_rows), jnp.int32),
            pltpu.VMEM((foot_count, obs_rows), BF16),
            pltpu.VMEM((obs_rows, feats), BF16),
            pltpu.SemaphoreType.DMA((4,)),
        ),
        PACK_LIMIT,
        (pltpu.HBM,) * 4,
    )
    got = lax.all_to_all(send, ("lat", "lon"), split_axis=0, concat_axis=0, tiled=True)
    layers = depth_w.shape[0]
    taps = depth_w.transpose(1, 2, 0, 3).reshape(TAPS * TAPS, layers, chans)
    mix = (gains[:, :, None] * point_w.astype(F32)).astype(BF16)
    proj, back = call(
        fetch_kernel,
        (held(*obs_proj.shape), held(*background.shape)),
        (obs_proj, background),
        (pltpu.SemaphoreType.DMA((2,)),),
        space=(pltpu.HBM, pltpu.HBM),
    )
    got, mix, proj, back = lax.optimization_barrier((got, mix, proj, back))
    edge, left, right, lon_out, corner_out = call(
        functools.partial(assim_kernel, cap),
        (
            held(SHIFT, cols, chans),
            held(rows - SHIFT, TILE, chans),
            held(rows - SHIFT, TILE, chans),
            held(SHIFT, rows, chans),
            held(SHIFT, EDGE, chans),
        ),
        (got, proj, back),
        (
            pltpu.VMEM((devices, depth, LANES), BF16),
            pltpu.VMEM((chans // LANES, rows * EDGE, LANES), F32),
            pltpu.SemaphoreType.DMA((PIECES,)),
        ),
        space=(pltpu.HBM, pltpu.VMEM, pltpu.VMEM),
    )
    state = (edge, left, right)
    for n in range(layers - 1):
        state, lon_out, corner_out = layer(
            state, lon_out, corner_out, taps, mix, n, n % 2 == 1, False
        )
    n = layers - 1
    return layer(state, lon_out, corner_out, taps, mix, n, n % 2 == 1, True)


def solution(mesh):
    placed = (
        P("lat", "lon", None),
        P(("lat", "lon"), None),
        P(("lat", "lon"), None),
        P(("lat", "lon"), None),
        P(("lat", "lon"), None),
        P(),
        P(),
        P(),
        P(),
    )
    return jax.shard_map(
        body, mesh=mesh, in_specs=placed, out_specs=P("lat", "lon", None), check_vma=False
    )
```

```python
import functools

import jax
import jax.numpy as jnp
from jax import lax
from jax.experimental import pallas as pl
from jax.experimental.pallas import tpu as pltpu
from jax.sharding import PartitionSpec as P

LANES = 128
META = 8
TAPS = 7
HALO = 3
SHIFT = 2 * HALO
EDGE = 8
TILE = 16
PIECES = 4
SPARE = 4
WORK = 1000
VMEM_LIMIT = 24 * 1024 * 1024
PACK_LIMIT = 58 * 1024 * 1024
BF16 = jnp.bfloat16
F32 = jnp.float32


def pack_kernel(cap, cols, dest_hbm, foot_hbm, weights_hbm, obs_hbm, send_ref, dest_ref, foot_ref, weights_ref, obs_ref, sems):
    copies = [
        pltpu.make_async_copy(source, target, sems.at[k])
        for k, (source, target) in enumerate(
            (
                (dest_hbm, dest_ref),
                (obs_hbm, obs_ref),
                (foot_hbm, foot_ref),
                (weights_hbm, weights_ref),
            )
        )
    ]
    for copy in copies:
        copy.start()
    devices = send_ref.shape[0]
    obs_rows = obs_ref.shape[0]
    per = LANES // cap
    upper = lax.broadcasted_iota(jnp.int32, (LANES, LANES), 0) <= lax.broadcasted_iota(
        jnp.int32, (LANES, LANES), 1
    )
    upper = jnp.where(upper, 1.0, 0.0).astype(BF16)
    ids = lax.broadcasted_iota(jnp.int32, (devices, obs_rows), 0)
    copies[0].wait()
    member = jnp.where(ids == dest_ref[...], 1.0, 0.0)
    seen = jnp.zeros((devices, 1), F32)
    ranks = []
    for first in range(0, obs_rows, LANES):
        part = member[:, first : first + LANES]
        count = jnp.dot(part.astype(BF16), upper, preferred_element_type=F32) + seen
        ranks.append(jnp.sum((count - 1.0) * part, axis=0, keepdims=True))
        seen = count[:, LANES - 1 :]
    rank = jnp.concatenate(ranks, axis=1).astype(jnp.int32)
    slot = lax.broadcasted_iota(jnp.int32, (cap, obs_rows), 0)
    ranked = jnp.where(slot == rank, 1.0, 0.0).astype(BF16).reshape(cap // TILE, TILE, obs_rows)
    for copy in copies[1:]:
        copy.wait()
    start = foot_ref[0:1, :]
    meta = jnp.concatenate(
        [
            lax.div(start, cols).astype(F32),
            lax.rem(start, cols).astype(F32),
            weights_ref[...].astype(F32),
            jnp.zeros((META - 2 - weights_ref.shape[0], obs_rows), F32),
        ],
        axis=0,
    ).astype(BF16)
    obs = obs_ref[...]
    lane = lax.broadcasted_iota(jnp.int32, (META, LANES), 1)
    count = min(512, devices * cap) // cap
    for first in range(0, devices, count):
        parts = []
        for d in range(first, first + count):
            mine = jnp.broadcast_to(member[d : d + 1], (TILE, obs_rows)).astype(BF16)
            parts.append((ranked * mine[None]).reshape(cap, obs_rows))
        chosen = jnp.concatenate(parts, axis=0)
        feats = jnp.dot(chosen, obs, preferred_element_type=F32).astype(BF16)
        placed = lax.dot_general(
            meta, chosen, (((1,), (1,)), ((), ())), preferred_element_type=F32
        )
        for half in range(feats.shape[1] // LANES):
            piece = feats[:, half * LANES : (half + 1) * LANES].reshape(count, cap, LANES)
            send_ref[first : first + count, half * cap : (half + 1) * cap, :] = piece
        base = send_ref.shape[1] - META
        for chunk in range(count // per):
            values = placed[:, chunk * LANES : (chunk + 1) * LANES]
            turned = [values] + [pltpu.roll(values, k * cap, 1) for k in range(1, per)]
            for own in range(per):
                wide = turned[0]
                for group in range(per):
                    wide = jnp.where(lane // cap == group, turned[(group - own) % per], wide)
                send_ref[first + chunk * per + own, base:, :] = wide.astype(BF16)


def fetch_kernel(proj_hbm, back_hbm, proj_ref, back_ref, sems):
    copies = (
        pltpu.make_async_copy(proj_hbm, proj_ref, sems.at[0]),
        pltpu.make_async_copy(back_hbm, back_ref, sems.at[1]),
    )
    for copy in copies:
        copy.start()
    for copy in copies:
        copy.wait()


def assim_kernel(
    cap,
    got_hbm,
    proj_ref,
    back_ref,
    edge_ref,
    left_ref,
    right_ref,
    lon_ref,
    corner_ref,
    got_ref,
    wide_ref,
    sems,
):
    piece = got_ref.shape[0] // PIECES
    copies = [
        pltpu.make_async_copy(
            got_hbm.at[k * piece : (k + 1) * piece],
            got_ref.at[k * piece : (k + 1) * piece],
            sems.at[k],
        )
        for k in range(PIECES)
    ]
    for copy in copies:
        copy.start()
    devices, depth, _ = got_ref.shape
    rows, cols, chans = back_ref.shape
    cells = rows * cols
    feats = proj_ref.shape[0]
    per = LANES // cap
    halves = feats // LANES
    lane = lax.broadcasted_iota(jnp.int32, (META, LANES), 1)
    every_row = lax.broadcasted_iota(jnp.int32, (rows, LANES), 0).astype(F32)
    every_column = lax.broadcasted_iota(jnp.int32, (cols, LANES), 0).astype(F32)
    total = jnp.zeros((cells, feats), F32)
    for pair in range(0, devices // per, 2):
        if pair * per % piece == 0:
            copies[pair * per // piece].wait()
        maps = []
        blocks = []
        for chunk in (pair, pair + 1):
            meta = got_ref[chunk * per, depth - META :, :].astype(F32)
            for group in range(1, per):
                other = got_ref[chunk * per + group, depth - META :, :].astype(F32)
                meta = jnp.where(lane // cap == group, other, meta)
            row, column = meta[0:1], meta[1:2]
            amount = jnp.zeros((rows, LANES), F32)
            place = jnp.full((rows, LANES), -1.0, F32)
            for entry in range(4):
                at = column + entry
                over = at >= cols
                below = row + entry + jnp.where(over, 1.0, 0.0)
                hit = every_row == jnp.where(below >= rows, below - rows, below)
                place = jnp.where(hit, jnp.where(over, at - cols, at), place)
                amount = jnp.where(hit, meta[2 + entry : 3 + entry], amount)
            amount = jnp.concatenate(
                [
                    jnp.where(every_column == place[y : y + 1], amount[y : y + 1], 0.0)
                    for y in range(rows)
                ],
                axis=0,
            )
            maps.append(amount.astype(BF16))
            block = got_ref[chunk * per : (chunk + 1) * per]
            blocks.append(
                jnp.concatenate(
                    [
                        block[:, half * cap : (half + 1) * cap, :].reshape(LANES, LANES)
                        for half in range(halves)
                    ],
                    axis=1,
                )
            )
        total = total + jnp.dot(
            jnp.concatenate(maps, axis=1),
            jnp.concatenate(blocks, axis=0),
            preferred_element_type=F32,
        )
    assim = jnp.dot(total.astype(BF16), proj_ref[...], preferred_element_type=F32)
    state = back_ref[...].astype(F32) + assim.reshape(rows, cols, chans)
    for g in range(chans // LANES):
        wide_ref[g] = state[:, cols - EDGE :, lanes_of(g)].reshape(rows * EDGE, LANES)
    state = state.astype(BF16)
    edge_ref[...] = state[rows - SHIFT :]
    left_ref[...] = state[: rows - SHIFT, :TILE]
    right_ref[...] = state[: rows - SHIFT, TILE:]
    for x in range(SHIFT):
        for g in range(chans // LANES):
            column = wide_ref[g, pl.ds(EDGE - SHIFT + x, rows, stride=EDGE), :]
            lon_ref[x, :, lanes_of(g)] = column.astype(BF16)
    corner_ref[...] = state[rows - SHIFT :, cols - EDGE :, :]


def gelu(half):
    inner = half * (1.5957691216057308 + 0.285419265090401 * (half * half))
    return half + half * jnp.tanh(inner)


def put(wide_ref, row, start, value):
    for g in range(wide_ref.shape[0]):
        wide_ref[g, row, start : start + value.shape[0], :] = value[:, g * LANES : (g + 1) * LANES]


def shifted(wide_ref, taps_in, base, row, target):
    for g in range(wide_ref.shape[0]):
        for r in range(TAPS + 1):
            columns = pl.ds(base + r, TILE, stride=2)
            taps_in[g, r, target] = wide_ref[g, row, columns, :].astype(BF16)


def spread_taps(taps_ref, tap_ref, layer):
    @pl.loop(0, tap_ref.shape[0])
    def _(g):
        lanes = pl.ds(pl.multiple_of(g * LANES, LANES), LANES)
        for k in range(TAPS * TAPS):
            row = taps_ref[k, layer : layer + 1, lanes]
            tap_ref[g, k] = jnp.broadcast_to(row, (TILE, LANES)).astype(BF16)


def convolve(taps_in, tap_ref, spread_ref, g, count):
    lanes = pl.ds(pl.multiple_of(g * LANES, LANES), LANES)
    for p in range(2):
        total = None
        for b in range(TAPS):
            seen = taps_in[g, p + b, 0 : count + TAPS - 1]
            part = None
            for a in range(TAPS):
                term = seen[a : a + count] * tap_ref[g, a * TAPS + b]
                part = term if part is None else part + term
            total = part if total is None else total + part
        spread_ref[p, 0:count, :, lanes] = total


def finish(taps_in, spread_ref, mix_ref, out_ref, layer, first, count, stacked=1):
    chans = mix_ref.shape[1]
    ones = jnp.ones((chans, LANES), BF16)
    step = TILE // stacked
    spread = spread_ref[:, first : first + count].reshape(2 * count * TILE, chans)
    power = jnp.dot(spread * spread, ones, preferred_element_type=F32)
    scale = 0.5 * lax.rsqrt(power * (1.0 / chans) + 1e-05)
    mixed = jnp.dot(spread, mix_ref[layer], preferred_element_type=F32)
    for g in range(chans // LANES):
        moved = gelu(mixed[:, lanes_of(g)] * scale).reshape(2, count, TILE, LANES)
        for p in range(2):
            center = taps_in[g, p + HALO, first + HALO : first + HALO + count].astype(F32)
            fresh = center + moved[p]
            for k in range(count):
                for h in range(stacked):
                    row = first * stacked + h * count + k
                    out_ref[g, row, pl.ds(p, step, stride=2), :] = fresh[
                        k, h * step : (h + 1) * step
                    ]


def row_of(out_ref, y):
    return jnp.concatenate([out_ref[g, y] for g in range(out_ref.shape[0])], axis=1)


def flat(ref):
    groups, rows, width, lanes = ref.shape
    return ref.reshape(groups, rows * width, lanes)


def lanes_of(g):
    return slice(g * LANES, (g + 1) * LANES)


def at_last():
    return lax.axis_index("lat") == lax.axis_size("lat") - 1


def block_kernel(shrink, lead, layer, edge_in, left_in, right_in, *refs):
    if lead:
        taps_ref, mix_ref, block_ref, tap_ref, *scratch = refs
        spread_taps(taps_ref, tap_ref, layer)
    else:
        lon_in, tap_ref, mix_ref, block_ref, lon_ref, near_ref, *scratch = refs
    wide_ref, taps_in, spread_ref, out_ref = scratch
    cols = edge_in.shape[1]
    groups = wide_ref.shape[0]
    width = wide_ref.shape[2]
    own = left_in.shape[0] - (SPARE if shrink else 0)
    rows = own + SHIFT
    main = 0 if shrink else EDGE
    base = 0 if shrink else EDGE - SHIFT
    start = base + (0 if lead == shrink else TILE)

    if not lead:
        side = cols if shrink else base
        for g in range(groups):
            for x in range(SHIFT):
                column = lon_in[x, 0:rows, lanes_of(g)].astype(F32)
                flat(wide_ref)[g, pl.ds(side + x, rows, stride=width), :] = column

    @pl.loop(0, SHIFT, unroll=2)
    def _(y):
        put(wide_ref, y if shrink else own + y, main, edge_in[y].astype(F32))

    @pl.loop(0, own, unroll=2)
    def _(y):
        place = y + SHIFT if shrink else y
        put(wide_ref, place, main, left_in[y].astype(F32))
        put(wide_ref, place, main + TILE, right_in[y].astype(F32))

    def stage(high):
        @pl.loop(0, high + TAPS - 1)
        def _(y):
            for g in range(groups):
                for r in range(TAPS + 1):
                    both = [
                        wide_ref[g, y + h, pl.ds(start + r, TILE // 2, stride=2), :]
                        for h in (0, high)
                    ]
                    taps_in[g, r, y] = jnp.concatenate(both, axis=0).astype(BF16)

        @pl.loop(0, groups)
        def _(g):
            convolve(taps_in, tap_ref, spread_ref, g, high)

        finish(taps_in, spread_ref, mix_ref, out_ref, layer, 0, high, 2)

        @pl.loop(0, 2 * high, unroll=2)
        def _(y):
            block_ref[y] = row_of(out_ref, y).astype(BF16)

    if shrink:
        stage(own // 2)
    else:

        @pl.when(at_last())
        def _():
            wide_ref[:, rows:] = jnp.zeros((groups, SPARE, width, LANES), F32)
            stage((own + SPARE) // 2)

        @pl.when(jnp.logical_not(at_last()))
        def _():
            stage(own // 2)

    if not lead:
        edge = TILE - SHIFT if shrink else 0
        above = 0 if shrink else SHIFT
        near = rows - SHIFT if shrink else 0
        for g in range(groups):
            for x in range(SHIFT):
                column = flat(out_ref)[g, pl.ds(edge + x, own, stride=TILE), :]
                lon_ref[g, x, above : above + own, :] = column
            for r in range(TAPS + 1):
                for k in range(SHIFT):
                    columns = pl.ds(base + r, TILE, stride=2)
                    near_ref[g, r, k] = wide_ref[g, near + k, columns, :].astype(BF16)

def edge_kernel(
    shrink,
    final,
    layer,
    left_in,
    right_in,
    lon_in,
    lat_in,
    corner_in,
    near_ref,
    left_new,
    right_new,
    lon_new,
    tap_ref,
    mix_ref,
    *refs,
):
    if final:
        state_ref, wide_ref, taps_in, spread_ref, out_ref, spare_ref, mix_lon = refs[:7]
        rows_ref, sems = refs[7:]
        kept, width = left_new.shape[:2]
        copies = [
            pltpu.make_async_copy(left_new, state_ref.at[0:kept, 0:width], sems.at[0]),
            pltpu.make_async_copy(
                right_new, state_ref.at[0:kept, width : 2 * width], sems.at[1]
            ),
            pltpu.make_async_copy(rows_ref, state_ref.at[kept : kept + SHIFT], sems.at[2]),
        ]
        copies[0].start()
        copies[1].start()
    else:
        edge_ref, lon_ref, corner_ref = refs[:3]
        wide_ref, taps_in, spread_ref, out_ref, spare_ref, mix_lon = refs[3:]
    cols = lat_in.shape[1]
    groups = wide_ref.shape[0]
    main = 0 if shrink else EDGE
    side = cols if shrink else 0
    base = 0 if shrink else EDGE - SHIFT
    last = at_last()
    top = lax.axis_index("lat") == 0
    own = SHIFT if not shrink else 0
    if shrink:
        for g in range(groups):
            for k in range(2):
                spare = lon_in[SHIFT + k, :, lanes_of(g)].astype(F32)
                spare_ref[g, k * TILE : (k + 1) * TILE, :] = spare
    for k in range(SHIFT):
        value, beside = lat_in[k].astype(F32), corner_in[k].astype(F32)
        if not shrink:
            value, beside = jnp.where(top, 0.0, value), jnp.where(top, 0.0, beside)
        elif k < HALO:
            kept = left_in.shape[0] - SPARE + k
            inner = jnp.concatenate([left_in[kept], right_in[kept]], axis=0)
            value = jnp.where(last, inner.astype(F32), value)
            beside = beside[:SHIFT]
            extra = [spare_ref[g, pl.ds(k, SHIFT, stride=HALO), :] for g in range(groups)]
            beside = jnp.where(last, jnp.concatenate(extra, axis=1), beside)
        else:
            value, beside = jnp.where(last, 0.0, value), jnp.where(last, 0.0, beside)
        put(wide_ref, k, main, value)
        put(wide_ref, k, side, beside)
        shifted(wide_ref, taps_in, base, k, k if not shrink else k + SHIFT)
    taps_in[:, :, own : own + SHIFT] = near_ref[...]

    @pl.loop(0, groups)
    def _(g):
        convolve(taps_in, tap_ref, spread_ref, g, SHIFT)

    finish(taps_in, spread_ref, mix_ref, out_ref, layer, 0, SHIFT)
    kept = left_new.shape[0]
    if final:
        for k in range(SHIFT):
            rows_ref[k] = row_of(out_ref, k).astype(BF16)
        copies[2].start()
        for copy in copies:
            copy.wait()
        return

    for k in range(SHIFT):
        value = row_of(out_ref, k)
        if not shrink and k < HALO:
            value = jnp.where(top, 0.0, value)
        edge_ref[k] = value.astype(BF16)
        corner_ref[k] = (value[cols - EDGE :] if shrink else value[:EDGE]).astype(BF16)
    edge = cols - SHIFT if shrink else 0
    place = TILE - SHIFT if shrink else 0
    for g in range(groups):
        for x in range(SHIFT):
            column = flat(out_ref)[g, pl.ds(edge + x, SHIFT, stride=cols), :]
            if not shrink:
                outside = lax.broadcasted_iota(jnp.int32, (SHIFT, LANES), 0) < HALO
                column = jnp.where(jnp.logical_and(top, outside), 0.0, column)
            mix_lon[g, x] = lon_new[g, x]
            mix_lon[g, x, place : place + SHIFT, :] = column
            lon_ref[x, :, lanes_of(g)] = mix_lon[g, x].astype(BF16)
    if not shrink:
        for k in range(HALO):
            value = left_new[kept - SPARE + k].astype(F32)
            for g in range(groups):
                spare_ref[g, pl.ds(k, SHIFT, stride=HALO), :] = value[:SHIFT, lanes_of(g)]
        for g in range(groups):
            for k in range(2):
                spare = spare_ref[g, k * TILE : (k + 1) * TILE, :]
                lon_ref[SHIFT + k, :, lanes_of(g)] = spare.astype(BF16)


def call(kernel, out_shape, inputs, scratch=(), limit=VMEM_LIMIT, space=None, work=0, out_space=pltpu.VMEM):
    whole = pl.BlockSpec(memory_space=out_space)
    single = isinstance(out_shape, jax.ShapeDtypeStruct)
    spaces = space or (pltpu.VMEM,) * len(inputs)
    return pl.pallas_call(
        kernel,
        out_shape=out_shape,
        in_specs=[pl.BlockSpec(memory_space=s) for s in spaces],
        out_specs=whole if single else [whole] * len(out_shape),
        scratch_shapes=list(scratch),
        compiler_params=pltpu.CompilerParams(vmem_limit_bytes=limit),
        cost_estimate=pl.CostEstimate(flops=work, bytes_accessed=0, transcendentals=0),
    )(*inputs)


def held(*shape):
    return jax.ShapeDtypeStruct(shape, BF16)


def scratch_of(groups, seen, made, cols, chans):
    return (
        pltpu.VMEM((groups, seen, cols + EDGE, LANES), F32),
        pltpu.VMEM((groups, TAPS + 1, seen, TILE, LANES), BF16),
        pltpu.VMEM((2, made, TILE, chans), BF16),
        pltpu.VMEM((groups, made, cols, LANES), F32),
    )


def layer(state, lon_out, corner_out, taps, mix, number, shrink, final):
    edge, left, right = state
    lat_in, lon_in, corner_in = exchange((edge, lon_out, corner_out), not shrink)
    cols, chans = edge.shape[1:]
    groups = chans // LANES
    own = left.shape[0] - (SPARE if shrink else 0)
    rows = own + SHIFT
    spare = 0 if shrink else SPARE
    made = own + spare
    block = held(made, TILE, chans)
    scratch = (
        pltpu.VMEM((groups, rows + spare, cols + EDGE, LANES), F32),
        pltpu.VMEM((groups, TAPS + 1, made // 2 + TAPS - 1, TILE, LANES), BF16),
        pltpu.VMEM((2, made // 2, TILE, chans), BF16),
        pltpu.VMEM((groups, made, TILE, LANES), F32),
    )
    lead, wide_taps = call(
        functools.partial(block_kernel, shrink, True, number),
        (block, held(groups, TAPS * TAPS, TILE, LANES)),
        (edge, left, right, taps, mix),
        scratch,
        work=made * TILE * chans * WORK * (5 if shrink else 3),
    )
    trail, lon_new, near = call(
        functools.partial(block_kernel, shrink, False, number),
        (
            block,
            jax.ShapeDtypeStruct((groups, SHIFT, rows, LANES), F32),
            held(groups, TAPS + 1, SHIFT, TILE, LANES),
        ),
        (edge, left, right, lon_in, wide_taps, mix),
        scratch,
        work=made * TILE * chans * WORK * (7 if shrink else 11),
    )
    new = (lead, trail) if shrink else (trail, lead)
    last_scratch = ()
    if final:
        outs = held(made + SHIFT, cols, chans)
        last_scratch = (pltpu.VMEM((SHIFT, cols, chans), BF16), pltpu.SemaphoreType.DMA((3,)))
    else:
        outs = (
            held(SHIFT, cols, chans),
            held(SHIFT if shrink else EDGE, rows, chans),
            held(SHIFT, EDGE, chans),
        )
    outs = call(
        functools.partial(edge_kernel, shrink, final, number),
        outs,
        (left, right, lon_in, lat_in, corner_in, near, *new, lon_new, wide_taps, mix),
        scratch_of(groups, 2 * SHIFT, SHIFT, cols, chans)
        + (
            pltpu.VMEM((groups, 2 * TILE, LANES), F32),
            pltpu.VMEM((groups, SHIFT, rows, LANES), F32),
        )
        + last_scratch,
        out_space=pltpu.HBM if final else pltpu.VMEM,
        work=SHIFT * cols * chans * WORK * 5,
    )
    if final:
        return outs
    edge, lon_out, corner_out = outs
    return (edge, *new), lon_out, corner_out


def exchange(pieces, forward):
    lat, lon, corner = pieces
    count_lat = lax.axis_size("lat")
    count_lon = lax.axis_size("lon")
    along = [(i, (i + 1) % count_lat) for i in range(count_lat)]
    around = [(j, (j + 1) % count_lon) for j in range(count_lon)]
    across = [
        (i * count_lon + j, ni * count_lon + nj) for i, ni in along for j, nj in around
    ]
    if not forward:
        along, around, across = ([(t, s) for s, t in p] for p in (along, around, across))
    lon = lax.ppermute(lon, "lon", around)
    lat = lax.ppermute(lat, "lat", along)
    corner = lax.ppermute(corner, ("lat", "lon"), across)
    return lat, lon, corner


def body(
    background, observations, destination, footprint, weights, obs_proj, depth_w, point_w, gains
):
    rows, cols, chans = background.shape
    devices = lax.axis_size("lat") * lax.axis_size("lon")
    obs_rows, feats = observations.shape
    cap = 2 * obs_rows // devices
    depth = cap * (feats // LANES) + META
    foot_count = footprint.shape[1]
    send = call(
        functools.partial(pack_kernel, cap, cols),
        jax.ShapeDtypeStruct((devices, depth, LANES), BF16),
        (destination.T, footprint.T, weights.T, observations),
        (
            pltpu.VMEM((1, obs_rows), jnp.int32),
            pltpu.VMEM((foot_count, obs_rows), jnp.int32),
            pltpu.VMEM((foot_count, obs_rows), BF16),
            pltpu.VMEM((obs_rows, feats), BF16),
            pltpu.SemaphoreType.DMA((4,)),
        ),
        PACK_LIMIT,
        (pltpu.HBM,) * 4,
    )
    got = lax.all_to_all(send, ("lat", "lon"), split_axis=0, concat_axis=0, tiled=True)
    layers = depth_w.shape[0]
    taps = depth_w.transpose(1, 2, 0, 3).reshape(TAPS * TAPS, layers, chans)
    mix = (gains[:, :, None] * point_w.astype(F32)).astype(BF16)
    proj, back = call(
        fetch_kernel,
        (held(*obs_proj.shape), held(*background.shape)),
        (obs_proj, background),
        (pltpu.SemaphoreType.DMA((2,)),),
        space=(pltpu.HBM, pltpu.HBM),
    )
    got, mix, proj, back = lax.optimization_barrier((got, mix, proj, back))
    edge, left, right, lon_out, corner_out = call(
        functools.partial(assim_kernel, cap),
        (
            held(SHIFT, cols, chans),
            held(rows - SHIFT, TILE, chans),
            held(rows - SHIFT, TILE, chans),
            held(SHIFT, rows, chans),
            held(SHIFT, EDGE, chans),
        ),
        (got, proj, back),
        (
            pltpu.VMEM((devices, depth, LANES), BF16),
            pltpu.VMEM((chans // LANES, rows * EDGE, LANES), F32),
            pltpu.SemaphoreType.DMA((PIECES,)),
        ),
        space=(pltpu.HBM, pltpu.VMEM, pltpu.VMEM),
    )
    state = (edge, left, right)
    for n in range(layers - 1):
        state, lon_out, corner_out = layer(
            state, lon_out, corner_out, taps, mix, n, n % 2 == 1, False
        )
    n = layers - 1
    return layer(state, lon_out, corner_out, taps, mix, n, n % 2 == 1, True)


def solution(mesh):
    placed = (
        P("lat", "lon", None),
        P(("lat", "lon"), None),
        P(("lat", "lon"), None),
        P(("lat", "lon"), None),
        P(("lat", "lon"), None),
        P(),
        P(),
        P(),
        P(),
    )
    return jax.shard_map(
        body, mesh=mesh, in_specs=placed, out_specs=P("lat", "lon", None), check_vma=False
    )
```

```python
import functools

import jax
import jax.numpy as jnp
from jax import lax
from jax.experimental import pallas as pl
from jax.experimental.pallas import tpu as pltpu
from jax.sharding import PartitionSpec as P

LANES = 128
META = 8
TAPS = 7
HALO = 3
SHIFT = 2 * HALO
EDGE = 8
TILE = 16
PIECES = 4
SPARE = 4
WORK = 1000
VMEM_LIMIT = 24 * 1024 * 1024
PACK_LIMIT = 58 * 1024 * 1024
BF16 = jnp.bfloat16
F32 = jnp.float32


def pack_kernel(cap, cols, dest_hbm, foot_hbm, weights_hbm, obs_hbm, send_ref, dest_ref, foot_ref, weights_ref, obs_ref, sems):
    copies = [
        pltpu.make_async_copy(source, target, sems.at[k])
        for k, (source, target) in enumerate(
            (
                (dest_hbm, dest_ref),
                (obs_hbm, obs_ref),
                (foot_hbm, foot_ref),
                (weights_hbm, weights_ref),
            )
        )
    ]
    for copy in copies:
        copy.start()
    devices = send_ref.shape[0]
    obs_rows = obs_ref.shape[0]
    per = LANES // cap
    upper = lax.broadcasted_iota(jnp.int32, (LANES, LANES), 0) <= lax.broadcasted_iota(
        jnp.int32, (LANES, LANES), 1
    )
    upper = jnp.where(upper, 1.0, 0.0).astype(BF16)
    ids = lax.broadcasted_iota(jnp.int32, (devices, obs_rows), 0)
    copies[0].wait()
    member = jnp.where(ids == dest_ref[...], 1.0, 0.0)
    seen = jnp.zeros((devices, 1), F32)
    ranks = []
    for first in range(0, obs_rows, LANES):
        part = member[:, first : first + LANES]
        count = jnp.dot(part.astype(BF16), upper, preferred_element_type=F32) + seen
        ranks.append(jnp.sum((count - 1.0) * part, axis=0, keepdims=True))
        seen = count[:, LANES - 1 :]
    rank = jnp.concatenate(ranks, axis=1).astype(jnp.int32)
    slot = lax.broadcasted_iota(jnp.int32, (cap, obs_rows), 0)
    ranked = jnp.where(slot == rank, 1.0, 0.0).astype(BF16).reshape(cap // TILE, TILE, obs_rows)
    for copy in copies[1:]:
        copy.wait()
    start = foot_ref[0:1, :]
    meta = jnp.concatenate(
        [
            lax.div(start, cols).astype(F32),
            lax.rem(start, cols).astype(F32),
            weights_ref[...].astype(F32),
            jnp.zeros((META - 2 - weights_ref.shape[0], obs_rows), F32),
        ],
        axis=0,
    ).astype(BF16)
    obs = obs_ref[...]
    lane = lax.broadcasted_iota(jnp.int32, (META, LANES), 1)
    count = min(512, devices * cap) // cap
    for first in range(0, devices, count):
        parts = []
        for d in range(first, first + count):
            mine = jnp.broadcast_to(member[d : d + 1], (TILE, obs_rows)).astype(BF16)
            parts.append((ranked * mine[None]).reshape(cap, obs_rows))
        chosen = jnp.concatenate(parts, axis=0)
        feats = jnp.dot(chosen, obs, preferred_element_type=F32).astype(BF16)
        placed = lax.dot_general(
            meta, chosen, (((1,), (1,)), ((), ())), preferred_element_type=F32
        )
        for half in range(feats.shape[1] // LANES):
            piece = feats[:, half * LANES : (half + 1) * LANES].reshape(count, cap, LANES)
            send_ref[first : first + count, half * cap : (half + 1) * cap, :] = piece
        base = send_ref.shape[1] - META
        for chunk in range(count // per):
            values = placed[:, chunk * LANES : (chunk + 1) * LANES]
            turned = [values] + [pltpu.roll(values, k * cap, 1) for k in range(1, per)]
            for own in range(per):
                wide = turned[0]
                for group in range(per):
                    wide = jnp.where(lane // cap == group, turned[(group - own) % per], wide)
                send_ref[first + chunk * per + own, base:, :] = wide.astype(BF16)


def fetch_kernel(proj_hbm, back_hbm, proj_ref, back_ref, sems):
    copies = (
        pltpu.make_async_copy(proj_hbm, proj_ref, sems.at[0]),
        pltpu.make_async_copy(back_hbm, back_ref, sems.at[1]),
    )
    for copy in copies:
        copy.start()
    for copy in copies:
        copy.wait()


def assim_kernel(
    cap,
    got_hbm,
    proj_ref,
    back_ref,
    edge_ref,
    left_ref,
    right_ref,
    lon_ref,
    corner_ref,
    got_ref,
    wide_ref,
    sems,
):
    piece = got_ref.shape[0] // PIECES
    copies = [
        pltpu.make_async_copy(
            got_hbm.at[k * piece : (k + 1) * piece],
            got_ref.at[k * piece : (k + 1) * piece],
            sems.at[k],
        )
        for k in range(PIECES)
    ]
    for copy in copies:
        copy.start()
    devices, depth, _ = got_ref.shape
    rows, cols, chans = back_ref.shape
    cells = rows * cols
    feats = proj_ref.shape[0]
    per = LANES // cap
    halves = feats // LANES
    lane = lax.broadcasted_iota(jnp.int32, (META, LANES), 1)
    every_row = lax.broadcasted_iota(jnp.int32, (rows, LANES), 0).astype(F32)
    every_column = lax.broadcasted_iota(jnp.int32, (cols, LANES), 0).astype(F32)
    total = jnp.zeros((cells, feats), F32)
    for pair in range(0, devices // per, 2):
        if pair * per % piece == 0:
            copies[pair * per // piece].wait()
        maps = []
        blocks = []
        for chunk in (pair, pair + 1):
            meta = got_ref[chunk * per, depth - META :, :].astype(F32)
            for group in range(1, per):
                other = got_ref[chunk * per + group, depth - META :, :].astype(F32)
                meta = jnp.where(lane // cap == group, other, meta)
            row, column = meta[0:1], meta[1:2]
            amount = jnp.zeros((rows, LANES), F32)
            place = jnp.full((rows, LANES), -1.0, F32)
            for entry in range(4):
                at = column + entry
                over = at >= cols
                below = row + entry + jnp.where(over, 1.0, 0.0)
                hit = every_row == jnp.where(below >= rows, below - rows, below)
                place = jnp.where(hit, jnp.where(over, at - cols, at), place)
                amount = jnp.where(hit, meta[2 + entry : 3 + entry], amount)
            amount = jnp.concatenate(
                [
                    jnp.where(every_column == place[y : y + 1], amount[y : y + 1], 0.0)
                    for y in range(rows)
                ],
                axis=0,
            )
            maps.append(amount.astype(BF16))
            block = got_ref[chunk * per : (chunk + 1) * per]
            blocks.append(
                jnp.concatenate(
                    [
                        block[:, half * cap : (half + 1) * cap, :].reshape(LANES, LANES)
                        for half in range(halves)
                    ],
                    axis=1,
                )
            )
        total = total + jnp.dot(
            jnp.concatenate(maps, axis=1),
            jnp.concatenate(blocks, axis=0),
            preferred_element_type=F32,
        )
    assim = jnp.dot(total.astype(BF16), proj_ref[...], preferred_element_type=F32)
    state = back_ref[...].astype(F32) + assim.reshape(rows, cols, chans)
    for g in range(chans // LANES):
        wide_ref[g] = state[:, cols - EDGE :, lanes_of(g)].reshape(rows * EDGE, LANES)
    state = state.astype(BF16)
    edge_ref[...] = state[rows - SHIFT :]
    left_ref[...] = state[: rows - SHIFT, :TILE]
    right_ref[...] = state[: rows - SHIFT, TILE:]
    for x in range(SHIFT):
        for g in range(chans // LANES):
            column = wide_ref[g, pl.ds(EDGE - SHIFT + x, rows, stride=EDGE), :]
            lon_ref[x, :, lanes_of(g)] = column.astype(BF16)
    corner_ref[...] = state[rows - SHIFT :, cols - EDGE :, :]


def gelu(half):
    inner = half * (1.5957691216057308 + 0.285419265090401 * (half * half))
    return half + half * jnp.tanh(inner)


def put(wide_ref, row, start, value):
    for g in range(wide_ref.shape[0]):
        wide_ref[g, row, start : start + value.shape[0], :] = value[:, g * LANES : (g + 1) * LANES]


def shifted(wide_ref, taps_in, base, row, target):
    for g in range(wide_ref.shape[0]):
        for r in range(TAPS + 1):
            columns = pl.ds(base + r, TILE, stride=2)
            taps_in[g, r, target] = wide_ref[g, row, columns, :].astype(BF16)


def convolve(taps_in, taps_ref, tap_ref, spread_ref, layer, g, count):
    lanes = pl.ds(pl.multiple_of(g * LANES, LANES), LANES)

    @pl.loop(0, TAPS)
    def _(a):
        for b in range(TAPS):
            row = taps_ref[a * TAPS + b, layer : layer + 1, lanes]
            tap_ref[a * TAPS + b] = jnp.broadcast_to(row, (TILE, LANES)).astype(BF16)

    @pl.loop(0, 2)
    def _(p):
        total = None
        for b in range(TAPS):
            seen = taps_in[g, p + b, 0 : count + TAPS - 1]
            part = None
            for a in range(TAPS):
                term = seen[a : a + count] * tap_ref[a * TAPS + b]
                part = term if part is None else part + term
            total = part if total is None else total + part
        spread_ref[p, 0:count, :, lanes] = total


def finish(taps_in, spread_ref, mix_ref, out_ref, layer, first, count, stacked=1):
    chans = mix_ref.shape[1]
    ones = jnp.ones((chans, LANES), BF16)
    step = TILE // stacked
    spread = spread_ref[:, first : first + count].reshape(2 * count * TILE, chans)
    power = jnp.dot(spread * spread, ones, preferred_element_type=F32)
    scale = 0.5 * lax.rsqrt(power * (1.0 / chans) + 1e-05)
    mixed = jnp.dot(spread, mix_ref[layer], preferred_element_type=F32)
    for g in range(chans // LANES):
        moved = gelu(mixed[:, lanes_of(g)] * scale).reshape(2, count, TILE, LANES)
        for p in range(2):
            center = taps_in[g, p + HALO, first + HALO : first + HALO + count].astype(F32)
            fresh = center + moved[p]
            for k in range(count):
                for h in range(stacked):
                    row = first * stacked + h * count + k
                    out_ref[g, row, pl.ds(p, step, stride=2), :] = fresh[
                        k, h * step : (h + 1) * step
                    ]


def row_of(out_ref, y):
    return jnp.concatenate([out_ref[g, y] for g in range(out_ref.shape[0])], axis=1)


def flat(ref):
    groups, rows, width, lanes = ref.shape
    return ref.reshape(groups, rows * width, lanes)


def lanes_of(g):
    return slice(g * LANES, (g + 1) * LANES)


def at_last():
    return lax.axis_index("lat") == lax.axis_size("lat") - 1


def block_kernel(shrink, lead, layer, edge_in, left_in, right_in, *refs):
    if lead:
        taps_ref, mix_ref, block_ref, *scratch = refs
    else:
        lon_in, taps_ref, mix_ref, block_ref, lon_ref, near_ref, *scratch = refs
    wide_ref, taps_in, tap_ref, spread_ref, out_ref = scratch
    cols = edge_in.shape[1]
    groups = wide_ref.shape[0]
    width = wide_ref.shape[2]
    own = left_in.shape[0] - (SPARE if shrink else 0)
    rows = own + SHIFT
    main = 0 if shrink else EDGE
    base = 0 if shrink else EDGE - SHIFT
    start = base + (0 if lead == shrink else TILE)

    if not lead:
        side = cols if shrink else base
        for g in range(groups):
            for x in range(SHIFT):
                column = lon_in[x, 0:rows, lanes_of(g)].astype(F32)
                flat(wide_ref)[g, pl.ds(side + x, rows, stride=width), :] = column

    @pl.loop(0, SHIFT, unroll=2)
    def _(y):
        put(wide_ref, y if shrink else own + y, main, edge_in[y].astype(F32))

    @pl.loop(0, own, unroll=2)
    def _(y):
        place = y + SHIFT if shrink else y
        put(wide_ref, place, main, left_in[y].astype(F32))
        put(wide_ref, place, main + TILE, right_in[y].astype(F32))

    def stage(high):
        @pl.loop(0, high + TAPS - 1)
        def _(y):
            for g in range(groups):
                for r in range(TAPS + 1):
                    both = [
                        wide_ref[g, y + h, pl.ds(start + r, TILE // 2, stride=2), :]
                        for h in (0, high)
                    ]
                    taps_in[g, r, y] = jnp.concatenate(both, axis=0).astype(BF16)

        @pl.loop(0, groups)
        def _(g):
            convolve(taps_in, taps_ref, tap_ref, spread_ref, layer, g, high)

        finish(taps_in, spread_ref, mix_ref, out_ref, layer, 0, high, 2)

        @pl.loop(0, 2 * high, unroll=2)
        def _(y):
            block_ref[y] = row_of(out_ref, y).astype(BF16)

    if shrink:
        stage(own // 2)
    else:

        @pl.when(at_last())
        def _():
            wide_ref[:, rows:] = jnp.zeros((groups, SPARE, width, LANES), F32)
            stage((own + SPARE) // 2)

        @pl.when(jnp.logical_not(at_last()))
        def _():
            stage(own // 2)

    if not lead:
        edge = TILE - SHIFT if shrink else 0
        above = 0 if shrink else SHIFT
        near = rows - SHIFT if shrink else 0
        for g in range(groups):
            for x in range(SHIFT):
                column = flat(out_ref)[g, pl.ds(edge + x, own, stride=TILE), :]
                lon_ref[g, x, above : above + own, :] = column

        @pl.loop(0, SHIFT)
        def _(k):
            shifted(wide_ref, near_ref, base, near + k, k)


def edge_kernel(
    shrink,
    final,
    layer,
    left_in,
    right_in,
    lon_in,
    lat_in,
    corner_in,
    near_ref,
    left_new,
    right_new,
    lon_new,
    taps_ref,
    mix_ref,
    *refs,
):
    if final:
        state_ref, wide_ref, taps_in, tap_ref, spread_ref, out_ref, spare_ref, mix_lon = refs[:8]
        rows_ref, sems = refs[8:]
        kept, width = left_new.shape[:2]
        copies = [
            pltpu.make_async_copy(left_new, state_ref.at[0:kept, 0:width], sems.at[0]),
            pltpu.make_async_copy(
                right_new, state_ref.at[0:kept, width : 2 * width], sems.at[1]
            ),
            pltpu.make_async_copy(rows_ref, state_ref.at[kept : kept + SHIFT], sems.at[2]),
        ]
        copies[0].start()
        copies[1].start()
    else:
        edge_ref, lon_ref, corner_ref = refs[:3]
        wide_ref, taps_in, tap_ref, spread_ref, out_ref, spare_ref, mix_lon = refs[3:]
    cols = lat_in.shape[1]
    groups = wide_ref.shape[0]
    main = 0 if shrink else EDGE
    side = cols if shrink else 0
    base = 0 if shrink else EDGE - SHIFT
    last = at_last()
    top = lax.axis_index("lat") == 0
    own = SHIFT if not shrink else 0
    if shrink:
        for g in range(groups):
            for k in range(2):
                spare = lon_in[SHIFT + k, :, lanes_of(g)].astype(F32)
                spare_ref[g, k * TILE : (k + 1) * TILE, :] = spare
    def load(k, value, beside):
        put(wide_ref, k, main, value)
        put(wide_ref, k, side, beside)
        shifted(wide_ref, taps_in, base, k, k + SHIFT if shrink else k)

    if shrink:

        @pl.loop(0, HALO)
        def _(k):
            kept = left_in.shape[0] - SPARE + k
            inner = jnp.concatenate([left_in[kept], right_in[kept]], axis=0)
            extra = [spare_ref[g, pl.ds(k, SHIFT, stride=HALO), :] for g in range(groups)]
            load(
                k,
                jnp.where(last, inner.astype(F32), lat_in[k].astype(F32)),
                jnp.where(last, jnp.concatenate(extra, axis=1), corner_in[k].astype(F32)[:SHIFT]),
            )

    outside = last if shrink else top

    @pl.loop(HALO if shrink else 0, SHIFT)
    def _(k):
        load(
            k,
            jnp.where(outside, 0.0, lat_in[k].astype(F32)),
            jnp.where(outside, 0.0, corner_in[k].astype(F32)),
        )

    taps_in[:, :, own : own + SHIFT] = near_ref[...]

    @pl.loop(0, groups)
    def _(g):
        convolve(taps_in, taps_ref, tap_ref, spread_ref, layer, g, SHIFT)

    finish(taps_in, spread_ref, mix_ref, out_ref, layer, 0, SHIFT)
    kept = left_new.shape[0]
    if final:

        @pl.loop(0, SHIFT)
        def _(k):
            rows_ref[k] = row_of(out_ref, k).astype(BF16)

        copies[2].start()
        for copy in copies:
            copy.wait()
        return

    @pl.loop(0, SHIFT)
    def _(k):
        value = row_of(out_ref, k)
        if not shrink:
            value = jnp.where(jnp.logical_and(top, k < HALO), 0.0, value)
        edge_ref[k] = value.astype(BF16)
        corner_ref[k] = (value[cols - EDGE :] if shrink else value[:EDGE]).astype(BF16)

    edge = cols - SHIFT if shrink else 0
    place = TILE - SHIFT if shrink else 0
    for g in range(groups):
        for x in range(SHIFT):
            column = flat(out_ref)[g, pl.ds(edge + x, SHIFT, stride=cols), :]
            if not shrink:
                above = lax.broadcasted_iota(jnp.int32, (SHIFT, LANES), 0) < HALO
                column = jnp.where(jnp.logical_and(top, above), 0.0, column)
            mix_lon[g, x] = lon_new[g, x]
            mix_lon[g, x, place : place + SHIFT, :] = column
            lon_ref[x, :, lanes_of(g)] = mix_lon[g, x].astype(BF16)
    if not shrink:
        for k in range(HALO):
            value = left_new[kept - SPARE + k].astype(F32)
            for g in range(groups):
                spare_ref[g, pl.ds(k, SHIFT, stride=HALO), :] = value[:SHIFT, lanes_of(g)]
        for g in range(groups):
            for k in range(2):
                spare = spare_ref[g, k * TILE : (k + 1) * TILE, :]
                lon_ref[SHIFT + k, :, lanes_of(g)] = spare.astype(BF16)


def call(kernel, out_shape, inputs, scratch=(), limit=VMEM_LIMIT, space=None, work=0, out_space=pltpu.VMEM):
    whole = pl.BlockSpec(memory_space=out_space)
    single = isinstance(out_shape, jax.ShapeDtypeStruct)
    spaces = space or (pltpu.VMEM,) * len(inputs)
    return pl.pallas_call(
        kernel,
        out_shape=out_shape,
        in_specs=[pl.BlockSpec(memory_space=s) for s in spaces],
        out_specs=whole if single else [whole] * len(out_shape),
        scratch_shapes=list(scratch),
        compiler_params=pltpu.CompilerParams(vmem_limit_bytes=limit),
        cost_estimate=pl.CostEstimate(flops=work, bytes_accessed=0, transcendentals=0),
    )(*inputs)


def held(*shape):
    return jax.ShapeDtypeStruct(shape, BF16)


def scratch_of(groups, seen, made, cols, chans):
    return (
        pltpu.VMEM((groups, seen, cols + EDGE, LANES), F32),
        pltpu.VMEM((groups, TAPS + 1, seen, TILE, LANES), BF16),
        pltpu.VMEM((TAPS * TAPS, TILE, LANES), BF16),
        pltpu.VMEM((2, made, TILE, chans), BF16),
        pltpu.VMEM((groups, made, cols, LANES), F32),
    )


def layer(state, lon_out, corner_out, taps, mix, number, shrink, final):
    edge, left, right = state
    lat_in, lon_in, corner_in = exchange((edge, lon_out, corner_out), not shrink)
    cols, chans = edge.shape[1:]
    groups = chans // LANES
    own = left.shape[0] - (SPARE if shrink else 0)
    rows = own + SHIFT
    spare = 0 if shrink else SPARE
    made = own + spare
    block = held(made, TILE, chans)
    scratch = (
        pltpu.VMEM((groups, rows + spare, cols + EDGE, LANES), F32),
        pltpu.VMEM((groups, TAPS + 1, made // 2 + TAPS - 1, TILE, LANES), BF16),
        pltpu.VMEM((TAPS * TAPS, TILE, LANES), BF16),
        pltpu.VMEM((2, made // 2, TILE, chans), BF16),
        pltpu.VMEM((groups, made, TILE, LANES), F32),
    )
    lead = call(
        functools.partial(block_kernel, shrink, True, number),
        block,
        (edge, left, right, taps, mix),
        scratch,
        work=made * TILE * chans * WORK * (5 if shrink else 3),
    )
    trail, lon_new, near = call(
        functools.partial(block_kernel, shrink, False, number),
        (
            block,
            jax.ShapeDtypeStruct((groups, SHIFT, rows, LANES), F32),
            held(groups, TAPS + 1, SHIFT, TILE, LANES),
        ),
        (edge, left, right, lon_in, taps, mix),
        scratch,
        work=made * TILE * chans * WORK * (7 if shrink else 11),
    )
    new = (lead, trail) if shrink else (trail, lead)
    last_scratch = ()
    if final:
        outs = held(made + SHIFT, cols, chans)
        last_scratch = (pltpu.VMEM((SHIFT, cols, chans), BF16), pltpu.SemaphoreType.DMA((3,)))
    else:
        outs = (
            held(SHIFT, cols, chans),
            held(SHIFT if shrink else EDGE, rows, chans),
            held(SHIFT, EDGE, chans),
        )
    outs = call(
        functools.partial(edge_kernel, shrink, final, number),
        outs,
        (left, right, lon_in, lat_in, corner_in, near, *new, lon_new, taps, mix),
        scratch_of(groups, 2 * SHIFT, SHIFT, cols, chans)
        + (
            pltpu.VMEM((groups, 2 * TILE, LANES), F32),
            pltpu.VMEM((groups, SHIFT, rows, LANES), F32),
        )
        + last_scratch,
        out_space=pltpu.HBM if final else pltpu.VMEM,
        work=SHIFT * cols * chans * WORK * 5,
    )
    if final:
        return outs
    edge, lon_out, corner_out = outs
    return (edge, *new), lon_out, corner_out


def exchange(pieces, forward):
    lat, lon, corner = pieces
    count_lat = lax.axis_size("lat")
    count_lon = lax.axis_size("lon")
    along = [(i, (i + 1) % count_lat) for i in range(count_lat)]
    around = [(j, (j + 1) % count_lon) for j in range(count_lon)]
    across = [
        (i * count_lon + j, ni * count_lon + nj) for i, ni in along for j, nj in around
    ]
    if not forward:
        along, around, across = ([(t, s) for s, t in p] for p in (along, around, across))
    lon = lax.ppermute(lon, "lon", around)
    lat = lax.ppermute(lat, "lat", along)
    corner = lax.ppermute(corner, ("lat", "lon"), across)
    return lat, lon, corner


def body(
    background, observations, destination, footprint, weights, obs_proj, depth_w, point_w, gains
):
    rows, cols, chans = background.shape
    devices = lax.axis_size("lat") * lax.axis_size("lon")
    obs_rows, feats = observations.shape
    cap = 2 * obs_rows // devices
    depth = cap * (feats // LANES) + META
    foot_count = footprint.shape[1]
    send = call(
        functools.partial(pack_kernel, cap, cols),
        jax.ShapeDtypeStruct((devices, depth, LANES), BF16),
        (destination.T, footprint.T, weights.T, observations),
        (
            pltpu.VMEM((1, obs_rows), jnp.int32),
            pltpu.VMEM((foot_count, obs_rows), jnp.int32),
            pltpu.VMEM((foot_count, obs_rows), BF16),
            pltpu.VMEM((obs_rows, feats), BF16),
            pltpu.SemaphoreType.DMA((4,)),
        ),
        PACK_LIMIT,
        (pltpu.HBM,) * 4,
    )
    got = lax.all_to_all(send, ("lat", "lon"), split_axis=0, concat_axis=0, tiled=True)
    layers = depth_w.shape[0]
    taps = depth_w.transpose(1, 2, 0, 3).reshape(TAPS * TAPS, layers, chans)
    mix = (gains[:, :, None] * point_w.astype(F32)).astype(BF16)
    proj, back = call(
        fetch_kernel,
        (held(*obs_proj.shape), held(*background.shape)),
        (obs_proj, background),
        (pltpu.SemaphoreType.DMA((2,)),),
        space=(pltpu.HBM, pltpu.HBM),
    )
    got, mix, proj, back = lax.optimization_barrier((got, mix, proj, back))
    edge, left, right, lon_out, corner_out = call(
        functools.partial(assim_kernel, cap),
        (
            held(SHIFT, cols, chans),
            held(rows - SHIFT, TILE, chans),
            held(rows - SHIFT, TILE, chans),
            held(SHIFT, rows, chans),
            held(SHIFT, EDGE, chans),
        ),
        (got, proj, back),
        (
            pltpu.VMEM((devices, depth, LANES), BF16),
            pltpu.VMEM((chans // LANES, rows * EDGE, LANES), F32),
            pltpu.SemaphoreType.DMA((PIECES,)),
        ),
        space=(pltpu.HBM, pltpu.VMEM, pltpu.VMEM),
    )
    state = (edge, left, right)
    for n in range(layers - 1):
        state, lon_out, corner_out = layer(
            state, lon_out, corner_out, taps, mix, n, n % 2 == 1, False
        )
    n = layers - 1
    return layer(state, lon_out, corner_out, taps, mix, n, n % 2 == 1, True)


def solution(mesh):
    placed = (
        P("lat", "lon", None),
        P(("lat", "lon"), None),
        P(("lat", "lon"), None),
        P(("lat", "lon"), None),
        P(("lat", "lon"), None),
        P(),
        P(),
        P(),
        P(),
    )
    return jax.shard_map(
        body, mesh=mesh, in_specs=placed, out_specs=P("lat", "lon", None), check_vma=False
    )
```

```python
import functools

import jax
import jax.numpy as jnp
from jax import lax
from jax.experimental import pallas as pl
from jax.experimental.pallas import tpu as pltpu
from jax.sharding import PartitionSpec as P

LANES = 128
META = 8
TAPS = 7
HALO = 3
SHIFT = 2 * HALO
EDGE = 8
TILE = 16
PIECES = 4
SPARE = 4
WORK = 1000
VMEM_LIMIT = 24 * 1024 * 1024
PACK_LIMIT = 58 * 1024 * 1024
BF16 = jnp.bfloat16
F32 = jnp.float32


def pack_kernel(cap, cols, dest_hbm, foot_hbm, weights_hbm, obs_hbm, send_ref, dest_ref, foot_ref, weights_ref, obs_ref, sems):
    copies = [
        pltpu.make_async_copy(source, target, sems.at[k])
        for k, (source, target) in enumerate(
            (
                (dest_hbm, dest_ref),
                (obs_hbm, obs_ref),
                (foot_hbm, foot_ref),
                (weights_hbm, weights_ref),
            )
        )
    ]
    for copy in copies:
        copy.start()
    devices = send_ref.shape[0]
    obs_rows = obs_ref.shape[0]
    per = LANES // cap
    upper = lax.broadcasted_iota(jnp.int32, (LANES, LANES), 0) <= lax.broadcasted_iota(
        jnp.int32, (LANES, LANES), 1
    )
    upper = jnp.where(upper, 1.0, 0.0).astype(BF16)
    ids = lax.broadcasted_iota(jnp.int32, (devices, obs_rows), 0)
    copies[0].wait()
    member = jnp.where(ids == dest_ref[...], 1.0, 0.0)
    seen = jnp.zeros((devices, 1), F32)
    ranks = []
    for first in range(0, obs_rows, LANES):
        part = member[:, first : first + LANES]
        count = jnp.dot(part.astype(BF16), upper, preferred_element_type=F32) + seen
        ranks.append(jnp.sum((count - 1.0) * part, axis=0, keepdims=True))
        seen = count[:, LANES - 1 :]
    rank = jnp.concatenate(ranks, axis=1).astype(jnp.int32)
    slot = lax.broadcasted_iota(jnp.int32, (cap, obs_rows), 0)
    ranked = jnp.where(slot == rank, 1.0, 0.0).astype(BF16).reshape(cap // TILE, TILE, obs_rows)
    for copy in copies[1:]:
        copy.wait()
    start = foot_ref[0:1, :]
    meta = jnp.concatenate(
        [
            lax.div(start, cols).astype(F32),
            lax.rem(start, cols).astype(F32),
            weights_ref[...].astype(F32),
            jnp.zeros((META - 2 - weights_ref.shape[0], obs_rows), F32),
        ],
        axis=0,
    ).astype(BF16)
    obs = obs_ref[...]
    lane = lax.broadcasted_iota(jnp.int32, (META, LANES), 1)
    count = min(512, devices * cap) // cap
    for first in range(0, devices, count):
        parts = []
        for d in range(first, first + count):
            mine = jnp.broadcast_to(member[d : d + 1], (TILE, obs_rows)).astype(BF16)
            parts.append((ranked * mine[None]).reshape(cap, obs_rows))
        chosen = jnp.concatenate(parts, axis=0)
        feats = jnp.dot(chosen, obs, preferred_element_type=F32).astype(BF16)
        placed = lax.dot_general(
            meta, chosen, (((1,), (1,)), ((), ())), preferred_element_type=F32
        )
        for half in range(feats.shape[1] // LANES):
            piece = feats[:, half * LANES : (half + 1) * LANES].reshape(count, cap, LANES)
            send_ref[first : first + count, half * cap : (half + 1) * cap, :] = piece
        base = send_ref.shape[1] - META
        for chunk in range(count // per):
            values = placed[:, chunk * LANES : (chunk + 1) * LANES]
            turned = [values] + [pltpu.roll(values, k * cap, 1) for k in range(1, per)]
            for own in range(per):
                wide = turned[0]
                for group in range(per):
                    wide = jnp.where(lane // cap == group, turned[(group - own) % per], wide)
                send_ref[first + chunk * per + own, base:, :] = wide.astype(BF16)


def fetch_kernel(proj_hbm, back_hbm, proj_ref, back_ref, sems):
    copies = (
        pltpu.make_async_copy(proj_hbm, proj_ref, sems.at[0]),
        pltpu.make_async_copy(back_hbm, back_ref, sems.at[1]),
    )
    for copy in copies:
        copy.start()
    for copy in copies:
        copy.wait()


def assim_kernel(
    cap,
    got_hbm,
    proj_ref,
    back_ref,
    edge_ref,
    left_ref,
    right_ref,
    lon_ref,
    corner_ref,
    got_ref,
    wide_ref,
    sems,
):
    piece = got_ref.shape[0] // PIECES
    copies = [
        pltpu.make_async_copy(
            got_hbm.at[k * piece : (k + 1) * piece],
            got_ref.at[k * piece : (k + 1) * piece],
            sems.at[k],
        )
        for k in range(PIECES)
    ]
    for copy in copies:
        copy.start()
    devices, depth, _ = got_ref.shape
    rows, cols, chans = back_ref.shape
    cells = rows * cols
    feats = proj_ref.shape[0]
    per = LANES // cap
    halves = feats // LANES
    lane = lax.broadcasted_iota(jnp.int32, (META, LANES), 1)
    every_row = lax.broadcasted_iota(jnp.int32, (rows, LANES), 0).astype(F32)
    every_column = lax.broadcasted_iota(jnp.int32, (cols, LANES), 0).astype(F32)
    total = jnp.zeros((cells, feats), F32)
    for pair in range(0, devices // per, 2):
        if pair * per % piece == 0:
            copies[pair * per // piece].wait()
        maps = []
        blocks = []
        for chunk in (pair, pair + 1):
            meta = got_ref[chunk * per, depth - META :, :].astype(F32)
            for group in range(1, per):
                other = got_ref[chunk * per + group, depth - META :, :].astype(F32)
                meta = jnp.where(lane // cap == group, other, meta)
            row, column = meta[0:1], meta[1:2]
            amount = jnp.zeros((rows, LANES), F32)
            place = jnp.full((rows, LANES), -1.0, F32)
            for entry in range(4):
                at = column + entry
                over = at >= cols
                below = row + entry + jnp.where(over, 1.0, 0.0)
                hit = every_row == jnp.where(below >= rows, below - rows, below)
                place = jnp.where(hit, jnp.where(over, at - cols, at), place)
                amount = jnp.where(hit, meta[2 + entry : 3 + entry], amount)
            amount = jnp.concatenate(
                [
                    jnp.where(every_column == place[y : y + 1], amount[y : y + 1], 0.0)
                    for y in range(rows)
                ],
                axis=0,
            )
            maps.append(amount.astype(BF16))
            block = got_ref[chunk * per : (chunk + 1) * per]
            blocks.append(
                jnp.concatenate(
                    [
                        block[:, half * cap : (half + 1) * cap, :].reshape(LANES, LANES)
                        for half in range(halves)
                    ],
                    axis=1,
                )
            )
        total = total + jnp.dot(
            jnp.concatenate(maps, axis=1),
            jnp.concatenate(blocks, axis=0),
            preferred_element_type=F32,
        )
    assim = jnp.dot(total.astype(BF16), proj_ref[...], preferred_element_type=F32)
    state = back_ref[...].astype(F32) + assim.reshape(rows, cols, chans)
    for g in range(chans // LANES):
        wide_ref[g] = state[:, cols - EDGE :, lanes_of(g)].reshape(rows * EDGE, LANES)
    state = state.astype(BF16)
    edge_ref[...] = state[rows - SHIFT :]
    left_ref[...] = state[: rows - SHIFT, :TILE]
    right_ref[...] = state[: rows - SHIFT, TILE:]
    for x in range(SHIFT):
        for g in range(chans // LANES):
            column = wide_ref[g, pl.ds(EDGE - SHIFT + x, rows, stride=EDGE), :]
            lon_ref[x, :, lanes_of(g)] = column.astype(BF16)
    corner_ref[...] = state[rows - SHIFT :, cols - EDGE :, :]


def gelu(half):
    inner = half * (1.5957691216057308 + 0.285419265090401 * (half * half))
    return half + half * jnp.tanh(inner)


def put(wide_ref, row, start, value):
    for g in range(wide_ref.shape[0]):
        wide_ref[g, row, start : start + value.shape[0], :] = value[:, g * LANES : (g + 1) * LANES]


def shifted(wide_ref, taps_in, base, row, target):
    for g in range(wide_ref.shape[0]):
        for r in range(TAPS + 1):
            columns = pl.ds(base + r, TILE, stride=2)
            taps_in[g, r, target] = wide_ref[g, row, columns, :].astype(BF16)


def convolve(shifts, taps_ref, tap_ref, spread_ref, layer, g, first, count):
    lanes = pl.ds(pl.multiple_of(g * LANES, LANES), LANES)
    for k in range(TAPS * TAPS):
        row = taps_ref[k, layer : layer + 1, lanes]
        tap_ref[k] = jnp.broadcast_to(row, (TILE, LANES)).astype(BF16)
    for p in range(2):
        total = None
        for b in range(TAPS):
            seen = shifts[p + b, first : first + count + TAPS - 1]
            part = None
            for a in range(TAPS):
                term = seen[a : a + count] * tap_ref[a * TAPS + b]
                part = term if part is None else part + term
            total = part if total is None else total + part
        spread_ref[p, first : first + count, :, lanes] = total


def finish(center_ref, spread_ref, mix_ref, out_ref, layer, first, count, stacked=1):
    chans = mix_ref.shape[1]
    ones = jnp.ones((chans, LANES), BF16)
    step = TILE // stacked
    spread = spread_ref[:, first : first + count].reshape(2 * count * TILE, chans)
    power = jnp.dot(spread * spread, ones, preferred_element_type=F32)
    scale = 0.5 * lax.rsqrt(power * (1.0 / chans) + 1e-05)
    mixed = jnp.dot(spread, mix_ref[layer], preferred_element_type=F32)
    for g in range(chans // LANES):
        moved = gelu(mixed[:, lanes_of(g)] * scale).reshape(2, count, TILE, LANES)
        for p in range(2):
            center = center_ref[g, p, first : first + count].astype(F32)
            fresh = center + moved[p]
            for k in range(count):
                for h in range(stacked):
                    row = first * stacked + h * count + k
                    out_ref[g, row, pl.ds(p, step, stride=2), :] = fresh[
                        k, h * step : (h + 1) * step
                    ]


def row_of(out_ref, y):
    return jnp.concatenate([out_ref[g, y] for g in range(out_ref.shape[0])], axis=1)


def flat(ref):
    groups, rows, width, lanes = ref.shape
    return ref.reshape(groups, rows * width, lanes)


def lanes_of(g):
    return slice(g * LANES, (g + 1) * LANES)


def at_last():
    return lax.axis_index("lat") == lax.axis_size("lat") - 1


def block_kernel(shrink, lead, layer, edge_in, left_in, right_in, *refs):
    if lead:
        taps_ref, mix_ref, block_ref, *scratch = refs
    else:
        lon_in, taps_ref, mix_ref, block_ref, lon_ref, near_ref, *scratch = refs
    wide_ref, taps_in, center_ref, tap_ref, spread_ref, out_ref = scratch
    cols = edge_in.shape[1]
    groups = wide_ref.shape[0]
    width = wide_ref.shape[2]
    own = left_in.shape[0] - (SPARE if shrink else 0)
    rows = own + SHIFT
    main = 0 if shrink else EDGE
    base = 0 if shrink else EDGE - SHIFT
    start = base + (0 if lead == shrink else TILE)

    if not lead:
        side = cols if shrink else base
        for g in range(groups):
            for x in range(SHIFT):
                column = lon_in[x, 0:rows, lanes_of(g)].astype(F32)
                flat(wide_ref)[g, pl.ds(side + x, rows, stride=width), :] = column

    @pl.loop(0, SHIFT, unroll=2)
    def _(y):
        put(wide_ref, y if shrink else own + y, main, edge_in[y].astype(F32))

    @pl.loop(0, own, unroll=2)
    def _(y):
        place = y + SHIFT if shrink else y
        put(wide_ref, place, main, left_in[y].astype(F32))
        put(wide_ref, place, main + TILE, right_in[y].astype(F32))

    def stage(high):
        @pl.loop(0, groups)
        def _(g):
            for y in range(high + TAPS - 1):
                for r in range(TAPS + 1):
                    both = [
                        wide_ref[g, y + h, pl.ds(start + r, TILE // 2, stride=2), :]
                        for h in (0, high)
                    ]
                    taps_in[r, y] = jnp.concatenate(both, axis=0).astype(BF16)
            center_ref[g, :, 0:high] = taps_in[HALO : HALO + 2, HALO : HALO + high]
            convolve(taps_in, taps_ref, tap_ref, spread_ref, layer, g, 0, high)

        finish(center_ref, spread_ref, mix_ref, out_ref, layer, 0, high, 2)

        @pl.loop(0, 2 * high, unroll=2)
        def _(y):
            block_ref[y] = row_of(out_ref, y).astype(BF16)

    if shrink:
        stage(own // 2)
    else:

        @pl.when(at_last())
        def _():
            wide_ref[:, rows:] = jnp.zeros((groups, SPARE, width, LANES), F32)
            stage((own + SPARE) // 2)

        @pl.when(jnp.logical_not(at_last()))
        def _():
            stage(own // 2)

    if not lead:
        edge = TILE - SHIFT if shrink else 0
        above = 0 if shrink else SHIFT
        near = rows - SHIFT if shrink else 0
        for g in range(groups):
            for x in range(SHIFT):
                column = flat(out_ref)[g, pl.ds(edge + x, own, stride=TILE), :]
                lon_ref[g, x, above : above + own, :] = column
            for r in range(TAPS + 1):
                for k in range(SHIFT):
                    columns = pl.ds(base + r, TILE, stride=2)
                    near_ref[g, r, k] = wide_ref[g, near + k, columns, :].astype(BF16)

def edge_kernel(
    shrink,
    final,
    layer,
    left_in,
    right_in,
    lon_in,
    lat_in,
    corner_in,
    near_ref,
    left_new,
    right_new,
    lon_new,
    taps_ref,
    mix_ref,
    *refs,
):
    if final:
        state_ref, wide_ref, taps_in, tap_ref, spread_ref, out_ref, spare_ref, mix_lon = refs[:8]
        rows_ref, sems = refs[8:]
        kept, width = left_new.shape[:2]
        copies = [
            pltpu.make_async_copy(left_new, state_ref.at[0:kept, 0:width], sems.at[0]),
            pltpu.make_async_copy(
                right_new, state_ref.at[0:kept, width : 2 * width], sems.at[1]
            ),
            pltpu.make_async_copy(rows_ref, state_ref.at[kept : kept + SHIFT], sems.at[2]),
        ]
        copies[0].start()
        copies[1].start()
    else:
        edge_ref, lon_ref, corner_ref = refs[:3]
        wide_ref, taps_in, tap_ref, spread_ref, out_ref, spare_ref, mix_lon = refs[3:]
    cols = lat_in.shape[1]
    groups = wide_ref.shape[0]
    main = 0 if shrink else EDGE
    side = cols if shrink else 0
    base = 0 if shrink else EDGE - SHIFT
    last = at_last()
    top = lax.axis_index("lat") == 0
    own = SHIFT if not shrink else 0
    if shrink:
        for g in range(groups):
            for k in range(2):
                spare = lon_in[SHIFT + k, :, lanes_of(g)].astype(F32)
                spare_ref[g, k * TILE : (k + 1) * TILE, :] = spare
    for k in range(SHIFT):
        value, beside = lat_in[k].astype(F32), corner_in[k].astype(F32)
        if not shrink:
            value, beside = jnp.where(top, 0.0, value), jnp.where(top, 0.0, beside)
        elif k < HALO:
            kept = left_in.shape[0] - SPARE + k
            inner = jnp.concatenate([left_in[kept], right_in[kept]], axis=0)
            value = jnp.where(last, inner.astype(F32), value)
            beside = beside[:SHIFT]
            extra = [spare_ref[g, pl.ds(k, SHIFT, stride=HALO), :] for g in range(groups)]
            beside = jnp.where(last, jnp.concatenate(extra, axis=1), beside)
        else:
            value, beside = jnp.where(last, 0.0, value), jnp.where(last, 0.0, beside)
        put(wide_ref, k, main, value)
        put(wide_ref, k, side, beside)
        shifted(wide_ref, taps_in, base, k, k if not shrink else k + SHIFT)
    taps_in[:, :, own : own + SHIFT] = near_ref[...]

    @pl.loop(0, groups)
    def _(g):
        convolve(taps_in.at[g], taps_ref, tap_ref, spread_ref, layer, g, 0, SHIFT)

    center_ref = taps_in.at[:, HALO : HALO + 2, HALO : HALO + SHIFT]
    finish(center_ref, spread_ref, mix_ref, out_ref, layer, 0, SHIFT)
    kept = left_new.shape[0]
    if final:
        for k in range(SHIFT):
            rows_ref[k] = row_of(out_ref, k).astype(BF16)
        copies[2].start()
        for copy in copies:
            copy.wait()
        return

    for k in range(SHIFT):
        value = row_of(out_ref, k)
        if not shrink and k < HALO:
            value = jnp.where(top, 0.0, value)
        edge_ref[k] = value.astype(BF16)
        corner_ref[k] = (value[cols - EDGE :] if shrink else value[:EDGE]).astype(BF16)
    edge = cols - SHIFT if shrink else 0
    place = TILE - SHIFT if shrink else 0
    for g in range(groups):
        for x in range(SHIFT):
            column = flat(out_ref)[g, pl.ds(edge + x, SHIFT, stride=cols), :]
            if not shrink:
                outside = lax.broadcasted_iota(jnp.int32, (SHIFT, LANES), 0) < HALO
                column = jnp.where(jnp.logical_and(top, outside), 0.0, column)
            mix_lon[g, x] = lon_new[g, x]
            mix_lon[g, x, place : place + SHIFT, :] = column
            lon_ref[x, :, lanes_of(g)] = mix_lon[g, x].astype(BF16)
    if not shrink:
        for k in range(HALO):
            value = left_new[kept - SPARE + k].astype(F32)
            for g in range(groups):
                spare_ref[g, pl.ds(k, SHIFT, stride=HALO), :] = value[:SHIFT, lanes_of(g)]
        for g in range(groups):
            for k in range(2):
                spare = spare_ref[g, k * TILE : (k + 1) * TILE, :]
                lon_ref[SHIFT + k, :, lanes_of(g)] = spare.astype(BF16)


def call(kernel, out_shape, inputs, scratch=(), limit=VMEM_LIMIT, space=None, work=0, out_space=pltpu.VMEM):
    whole = pl.BlockSpec(memory_space=out_space)
    single = isinstance(out_shape, jax.ShapeDtypeStruct)
    spaces = space or (pltpu.VMEM,) * len(inputs)
    return pl.pallas_call(
        kernel,
        out_shape=out_shape,
        in_specs=[pl.BlockSpec(memory_space=s) for s in spaces],
        out_specs=whole if single else [whole] * len(out_shape),
        scratch_shapes=list(scratch),
        compiler_params=pltpu.CompilerParams(vmem_limit_bytes=limit),
        cost_estimate=pl.CostEstimate(flops=work, bytes_accessed=0, transcendentals=0),
    )(*inputs)


def held(*shape):
    return jax.ShapeDtypeStruct(shape, BF16)


def scratch_of(groups, seen, made, cols, chans):
    return (
        pltpu.VMEM((groups, seen, cols + EDGE, LANES), F32),
        pltpu.VMEM((groups, TAPS + 1, seen, TILE, LANES), BF16),
        pltpu.VMEM((TAPS * TAPS, TILE, LANES), BF16),
        pltpu.VMEM((2, made, TILE, chans), BF16),
        pltpu.VMEM((groups, made, cols, LANES), F32),
    )


def layer(state, lon_out, corner_out, taps, mix, number, shrink, final):
    edge, left, right = state
    lat_in, lon_in, corner_in = exchange((edge, lon_out, corner_out), not shrink)
    cols, chans = edge.shape[1:]
    groups = chans // LANES
    own = left.shape[0] - (SPARE if shrink else 0)
    rows = own + SHIFT
    spare = 0 if shrink else SPARE
    made = own + spare
    block = held(made, TILE, chans)
    scratch = (
        pltpu.VMEM((groups, rows + spare, cols + EDGE, LANES), F32),
        pltpu.VMEM((TAPS + 1, made // 2 + TAPS - 1, TILE, LANES), BF16),
        pltpu.VMEM((groups, 2, made // 2, TILE, LANES), BF16),
        pltpu.VMEM((TAPS * TAPS, TILE, LANES), BF16),
        pltpu.VMEM((2, made // 2, TILE, chans), BF16),
        pltpu.VMEM((groups, made, TILE, LANES), F32),
    )
    lead = call(
        functools.partial(block_kernel, shrink, True, number),
        block,
        (edge, left, right, taps, mix),
        scratch,
        work=made * TILE * chans * WORK * (5 if shrink else 3),
    )
    trail, lon_new, near = call(
        functools.partial(block_kernel, shrink, False, number),
        (
            block,
            jax.ShapeDtypeStruct((groups, SHIFT, rows, LANES), F32),
            held(groups, TAPS + 1, SHIFT, TILE, LANES),
        ),
        (edge, left, right, lon_in, taps, mix),
        scratch,
        work=made * TILE * chans * WORK * (7 if shrink else 11),
    )
    new = (lead, trail) if shrink else (trail, lead)
    last_scratch = ()
    if final:
        outs = held(made + SHIFT, cols, chans)
        last_scratch = (pltpu.VMEM((SHIFT, cols, chans), BF16), pltpu.SemaphoreType.DMA((3,)))
    else:
        outs = (
            held(SHIFT, cols, chans),
            held(SHIFT if shrink else EDGE, rows, chans),
            held(SHIFT, EDGE, chans),
        )
    outs = call(
        functools.partial(edge_kernel, shrink, final, number),
        outs,
        (left, right, lon_in, lat_in, corner_in, near, *new, lon_new, taps, mix),
        scratch_of(groups, 2 * SHIFT, SHIFT, cols, chans)
        + (
            pltpu.VMEM((groups, 2 * TILE, LANES), F32),
            pltpu.VMEM((groups, SHIFT, rows, LANES), F32),
        )
        + last_scratch,
        out_space=pltpu.HBM if final else pltpu.VMEM,
        work=SHIFT * cols * chans * WORK * 5,
    )
    if final:
        return outs
    edge, lon_out, corner_out = outs
    return (edge, *new), lon_out, corner_out


def exchange(pieces, forward):
    lat, lon, corner = pieces
    count_lat = lax.axis_size("lat")
    count_lon = lax.axis_size("lon")
    along = [(i, (i + 1) % count_lat) for i in range(count_lat)]
    around = [(j, (j + 1) % count_lon) for j in range(count_lon)]
    across = [
        (i * count_lon + j, ni * count_lon + nj) for i, ni in along for j, nj in around
    ]
    if not forward:
        along, around, across = ([(t, s) for s, t in p] for p in (along, around, across))
    lon = lax.ppermute(lon, "lon", around)
    lat = lax.ppermute(lat, "lat", along)
    corner = lax.ppermute(corner, ("lat", "lon"), across)
    return lat, lon, corner


def body(
    background, observations, destination, footprint, weights, obs_proj, depth_w, point_w, gains
):
    rows, cols, chans = background.shape
    devices = lax.axis_size("lat") * lax.axis_size("lon")
    obs_rows, feats = observations.shape
    cap = 2 * obs_rows // devices
    depth = cap * (feats // LANES) + META
    foot_count = footprint.shape[1]
    send = call(
        functools.partial(pack_kernel, cap, cols),
        jax.ShapeDtypeStruct((devices, depth, LANES), BF16),
        (destination.T, footprint.T, weights.T, observations),
        (
            pltpu.VMEM((1, obs_rows), jnp.int32),
            pltpu.VMEM((foot_count, obs_rows), jnp.int32),
            pltpu.VMEM((foot_count, obs_rows), BF16),
            pltpu.VMEM((obs_rows, feats), BF16),
            pltpu.SemaphoreType.DMA((4,)),
        ),
        PACK_LIMIT,
        (pltpu.HBM,) * 4,
    )
    got = lax.all_to_all(send, ("lat", "lon"), split_axis=0, concat_axis=0, tiled=True)
    layers = depth_w.shape[0]
    taps = depth_w.transpose(1, 2, 0, 3).reshape(TAPS * TAPS, layers, chans)
    mix = (gains[:, :, None] * point_w.astype(F32)).astype(BF16)
    proj, back = call(
        fetch_kernel,
        (held(*obs_proj.shape), held(*background.shape)),
        (obs_proj, background),
        (pltpu.SemaphoreType.DMA((2,)),),
        space=(pltpu.HBM, pltpu.HBM),
    )
    got, mix, proj, back = lax.optimization_barrier((got, mix, proj, back))
    edge, left, right, lon_out, corner_out = call(
        functools.partial(assim_kernel, cap),
        (
            held(SHIFT, cols, chans),
            held(rows - SHIFT, TILE, chans),
            held(rows - SHIFT, TILE, chans),
            held(SHIFT, rows, chans),
            held(SHIFT, EDGE, chans),
        ),
        (got, proj, back),
        (
            pltpu.VMEM((devices, depth, LANES), BF16),
            pltpu.VMEM((chans // LANES, rows * EDGE, LANES), F32),
            pltpu.SemaphoreType.DMA((PIECES,)),
        ),
        space=(pltpu.HBM, pltpu.VMEM, pltpu.VMEM),
    )
    state = (edge, left, right)
    for n in range(layers - 1):
        state, lon_out, corner_out = layer(
            state, lon_out, corner_out, taps, mix, n, n % 2 == 1, False
        )
    n = layers - 1
    return layer(state, lon_out, corner_out, taps, mix, n, n % 2 == 1, True)


def solution(mesh):
    placed = (
        P("lat", "lon", None),
        P(("lat", "lon"), None),
        P(("lat", "lon"), None),
        P(("lat", "lon"), None),
        P(("lat", "lon"), None),
        P(),
        P(),
        P(),
        P(),
    )
    return jax.shard_map(
        body, mesh=mesh, in_specs=placed, out_specs=P("lat", "lon", None), check_vma=False
    )
```

```python
import functools

import jax
import jax.numpy as jnp
from jax import lax
from jax.experimental import pallas as pl
from jax.experimental.pallas import tpu as pltpu
from jax.sharding import PartitionSpec as P

LANES = 128
META = 8
TAPS = 7
HALO = 3
SHIFT = 2 * HALO
EDGE = 8
TILE = 16
PIECES = 4
SPARE = 4
WORK = 1000
VMEM_LIMIT = 24 * 1024 * 1024
PACK_LIMIT = 58 * 1024 * 1024
BF16 = jnp.bfloat16
F32 = jnp.float32


def pack_kernel(cap, cols, dest_hbm, foot_hbm, weights_hbm, obs_hbm, send_ref, dest_ref, foot_ref, weights_ref, obs_ref, sems):
    copies = [
        pltpu.make_async_copy(source, target, sems.at[k])
        for k, (source, target) in enumerate(
            (
                (dest_hbm, dest_ref),
                (obs_hbm, obs_ref),
                (foot_hbm, foot_ref),
                (weights_hbm, weights_ref),
            )
        )
    ]
    for copy in copies:
        copy.start()
    devices = send_ref.shape[0]
    obs_rows = obs_ref.shape[0]
    per = LANES // cap
    upper = lax.broadcasted_iota(jnp.int32, (LANES, LANES), 0) <= lax.broadcasted_iota(
        jnp.int32, (LANES, LANES), 1
    )
    upper = jnp.where(upper, 1.0, 0.0).astype(BF16)
    ids = lax.broadcasted_iota(jnp.int32, (devices, obs_rows), 0)
    copies[0].wait()
    member = jnp.where(ids == dest_ref[...], 1.0, 0.0)
    seen = jnp.zeros((devices, 1), F32)
    ranks = []
    for first in range(0, obs_rows, LANES):
        part = member[:, first : first + LANES]
        count = jnp.dot(part.astype(BF16), upper, preferred_element_type=F32) + seen
        ranks.append(jnp.sum((count - 1.0) * part, axis=0, keepdims=True))
        seen = count[:, LANES - 1 :]
    rank = jnp.concatenate(ranks, axis=1).astype(jnp.int32)
    slot = lax.broadcasted_iota(jnp.int32, (cap, obs_rows), 0)
    ranked = jnp.where(slot == rank, 1.0, 0.0).astype(BF16).reshape(cap // TILE, TILE, obs_rows)
    for copy in copies[1:]:
        copy.wait()
    start = foot_ref[0:1, :]
    meta = jnp.concatenate(
        [
            lax.div(start, cols).astype(F32),
            lax.rem(start, cols).astype(F32),
            weights_ref[...].astype(F32),
            jnp.zeros((META - 2 - weights_ref.shape[0], obs_rows), F32),
        ],
        axis=0,
    ).astype(BF16)
    obs = obs_ref[...]
    lane = lax.broadcasted_iota(jnp.int32, (META, LANES), 1)
    count = min(512, devices * cap) // cap
    for first in range(0, devices, count):
        parts = []
        for d in range(first, first + count):
            mine = jnp.broadcast_to(member[d : d + 1], (TILE, obs_rows)).astype(BF16)
            parts.append((ranked * mine[None]).reshape(cap, obs_rows))
        chosen = jnp.concatenate(parts, axis=0)
        feats = jnp.dot(chosen, obs, preferred_element_type=F32).astype(BF16)
        placed = lax.dot_general(
            meta, chosen, (((1,), (1,)), ((), ())), preferred_element_type=F32
        )
        for half in range(feats.shape[1] // LANES):
            piece = feats[:, half * LANES : (half + 1) * LANES].reshape(count, cap, LANES)
            send_ref[first : first + count, half * cap : (half + 1) * cap, :] = piece
        base = send_ref.shape[1] - META
        for chunk in range(count // per):
            values = placed[:, chunk * LANES : (chunk + 1) * LANES]
            turned = [values] + [pltpu.roll(values, k * cap, 1) for k in range(1, per)]
            for own in range(per):
                wide = turned[0]
                for group in range(per):
                    wide = jnp.where(lane // cap == group, turned[(group - own) % per], wide)
                send_ref[first + chunk * per + own, base:, :] = wide.astype(BF16)


def fetch_kernel(proj_hbm, back_hbm, proj_ref, back_ref, sems):
    copies = (
        pltpu.make_async_copy(proj_hbm, proj_ref, sems.at[0]),
        pltpu.make_async_copy(back_hbm, back_ref, sems.at[1]),
    )
    for copy in copies:
        copy.start()
    for copy in copies:
        copy.wait()


def assim_kernel(
    cap,
    got_hbm,
    proj_ref,
    back_ref,
    edge_ref,
    left_ref,
    right_ref,
    lon_ref,
    corner_ref,
    got_ref,
    wide_ref,
    sems,
):
    piece = got_ref.shape[0] // PIECES
    copies = [
        pltpu.make_async_copy(
            got_hbm.at[k * piece : (k + 1) * piece],
            got_ref.at[k * piece : (k + 1) * piece],
            sems.at[k],
        )
        for k in range(PIECES)
    ]
    for copy in copies:
        copy.start()
    devices, depth, _ = got_ref.shape
    rows, cols, chans = back_ref.shape
    cells = rows * cols
    feats = proj_ref.shape[0]
    per = LANES // cap
    halves = feats // LANES
    lane = lax.broadcasted_iota(jnp.int32, (META, LANES), 1)
    every_row = lax.broadcasted_iota(jnp.int32, (rows, LANES), 0).astype(F32)
    every_column = lax.broadcasted_iota(jnp.int32, (cols, LANES), 0).astype(F32)
    total = jnp.zeros((cells, feats), F32)
    for pair in range(0, devices // per, 2):
        if pair * per % piece == 0:
            copies[pair * per // piece].wait()
        maps = []
        blocks = []
        for chunk in (pair, pair + 1):
            meta = got_ref[chunk * per, depth - META :, :].astype(F32)
            for group in range(1, per):
                other = got_ref[chunk * per + group, depth - META :, :].astype(F32)
                meta = jnp.where(lane // cap == group, other, meta)
            row, column = meta[0:1], meta[1:2]
            amount = jnp.zeros((rows, LANES), F32)
            place = jnp.full((rows, LANES), -1.0, F32)
            for entry in range(4):
                at = column + entry
                over = at >= cols
                below = row + entry + jnp.where(over, 1.0, 0.0)
                hit = every_row == jnp.where(below >= rows, below - rows, below)
                place = jnp.where(hit, jnp.where(over, at - cols, at), place)
                amount = jnp.where(hit, meta[2 + entry : 3 + entry], amount)
            amount = jnp.concatenate(
                [
                    jnp.where(every_column == place[y : y + 1], amount[y : y + 1], 0.0)
                    for y in range(rows)
                ],
                axis=0,
            )
            maps.append(amount.astype(BF16))
            block = got_ref[chunk * per : (chunk + 1) * per]
            blocks.append(
                jnp.concatenate(
                    [
                        block[:, half * cap : (half + 1) * cap, :].reshape(LANES, LANES)
                        for half in range(halves)
                    ],
                    axis=1,
                )
            )
        total = total + jnp.dot(
            jnp.concatenate(maps, axis=1),
            jnp.concatenate(blocks, axis=0),
            preferred_element_type=F32,
        )
    assim = jnp.dot(total.astype(BF16), proj_ref[...], preferred_element_type=F32)
    state = back_ref[...].astype(F32) + assim.reshape(rows, cols, chans)
    for g in range(chans // LANES):
        wide_ref[g] = state[:, cols - EDGE :, lanes_of(g)].reshape(rows * EDGE, LANES)
    state = state.astype(BF16)
    edge_ref[...] = state[rows - SHIFT :]
    left_ref[...] = state[: rows - SHIFT, :TILE]
    right_ref[...] = state[: rows - SHIFT, TILE:]
    for x in range(SHIFT):
        for g in range(chans // LANES):
            column = wide_ref[g, pl.ds(EDGE - SHIFT + x, rows, stride=EDGE), :]
            lon_ref[x, :, lanes_of(g)] = column.astype(BF16)
    corner_ref[...] = state[rows - SHIFT :, cols - EDGE :, :]


def gelu(half):
    inner = half * (1.5957691216057308 + 0.285419265090401 * (half * half))
    return half + half * jnp.tanh(inner)


def put(wide_ref, row, start, value):
    for g in range(wide_ref.shape[0]):
        wide_ref[g, row, start : start + value.shape[0], :] = value[:, g * LANES : (g + 1) * LANES]


def shifted(wide_ref, taps_in, base, row, target):
    for g in range(wide_ref.shape[0]):
        for r in range(TAPS + 1):
            columns = pl.ds(base + r, TILE, stride=2)
            taps_in[g, r, target] = wide_ref[g, row, columns, :].astype(BF16)


def convolve(shifts, taps_ref, tap_ref, spread_ref, layer, g, first, count):
    lanes = pl.ds(pl.multiple_of(g * LANES, LANES), LANES)
    for k in range(TAPS * TAPS):
        row = taps_ref[k, layer : layer + 1, lanes]
        tap_ref[k] = jnp.broadcast_to(row, (TILE, LANES)).astype(BF16)
    for p in range(2):
        total = None
        for b in range(TAPS):
            seen = shifts[p + b, first : first + count + TAPS - 1]
            part = None
            for a in range(TAPS):
                term = seen[a : a + count] * tap_ref[a * TAPS + b]
                part = term if part is None else part + term
            total = part if total is None else total + part
        spread_ref[p, first : first + count, :, lanes] = total


def finish(center_ref, spread_ref, mix_ref, out_ref, layer, first, count, stacked=1):
    chans = mix_ref.shape[1]
    ones = jnp.ones((chans, LANES), BF16)
    step = TILE // stacked
    spread = spread_ref[:, first : first + count].reshape(2 * count * TILE, chans)
    power = jnp.dot(spread * spread, ones, preferred_element_type=F32)
    scale = 0.5 * lax.rsqrt(power * (1.0 / chans) + 1e-05)
    mixed = jnp.dot(spread, mix_ref[layer], preferred_element_type=F32)
    for g in range(chans // LANES):
        moved = gelu(mixed[:, lanes_of(g)] * scale).reshape(2, count, TILE, LANES)
        for p in range(2):
            center = center_ref[g, p, first : first + count].astype(F32)
            fresh = center + moved[p]
            for k in range(count):
                for h in range(stacked):
                    row = first * stacked + h * count + k
                    out_ref[g, row, pl.ds(p, step, stride=2), :] = fresh[
                        k, h * step : (h + 1) * step
                    ]


def row_of(out_ref, y):
    return jnp.concatenate([out_ref[g, y] for g in range(out_ref.shape[0])], axis=1)


def flat(ref):
    groups, rows, width, lanes = ref.shape
    return ref.reshape(groups, rows * width, lanes)


def lanes_of(g):
    return slice(g * LANES, (g + 1) * LANES)


def at_last():
    return lax.axis_index("lat") == lax.axis_size("lat") - 1


def block_kernel(shrink, lead, layer, edge_in, left_in, right_in, *refs):
    if lead:
        taps_ref, mix_ref, block_ref, *scratch = refs
    else:
        lon_in, taps_ref, mix_ref, block_ref, lon_ref, near_ref, *scratch = refs
    wide_ref, taps_in, center_ref, tap_ref, spread_ref, out_ref = scratch
    cols = edge_in.shape[1]
    groups = wide_ref.shape[0]
    width = wide_ref.shape[2]
    own = left_in.shape[0] - (SPARE if shrink else 0)
    rows = own + SHIFT
    main = 0 if shrink else EDGE
    base = 0 if shrink else EDGE - SHIFT
    start = base + (0 if lead == shrink else TILE)

    if not lead:
        side = cols if shrink else base
        for g in range(groups):
            for x in range(SHIFT):
                column = lon_in[x, 0:rows, lanes_of(g)].astype(F32)
                flat(wide_ref)[g, pl.ds(side + x, rows, stride=width), :] = column

    @pl.loop(0, SHIFT, unroll=2)
    def _(y):
        put(wide_ref, y if shrink else own + y, main, edge_in[y].astype(F32))

    @pl.loop(0, own, unroll=2)
    def _(y):
        place = y + SHIFT if shrink else y
        put(wide_ref, place, main, left_in[y].astype(F32))
        put(wide_ref, place, main + TILE, right_in[y].astype(F32))

    def stage(high):
        @pl.loop(0, groups)
        def _(g):
            for y in range(high + TAPS - 1):
                for r in range(TAPS + 1):
                    both = [
                        wide_ref[g, y + h, pl.ds(start + r, TILE // 2, stride=2), :]
                        for h in (0, high)
                    ]
                    taps_in[r, y] = jnp.concatenate(both, axis=0).astype(BF16)
            center_ref[g, :, 0:high] = taps_in[HALO : HALO + 2, HALO : HALO + high]
            convolve(taps_in, taps_ref, tap_ref, spread_ref, layer, g, 0, high)

        finish(center_ref, spread_ref, mix_ref, out_ref, layer, 0, high, 2)

        @pl.loop(0, 2 * high, unroll=2)
        def _(y):
            block_ref[y] = row_of(out_ref, y).astype(BF16)

    if shrink:
        stage(own // 2)
    else:

        @pl.when(at_last())
        def _():
            wide_ref[:, rows:] = jnp.zeros((groups, SPARE, width, LANES), F32)
            stage((own + SPARE) // 2)

        @pl.when(jnp.logical_not(at_last()))
        def _():
            stage(own // 2)

    if not lead:
        edge = TILE - SHIFT if shrink else 0
        above = 0 if shrink else SHIFT
        near = rows - SHIFT if shrink else 0
        for g in range(groups):
            for x in range(SHIFT):
                column = flat(out_ref)[g, pl.ds(edge + x, own, stride=TILE), :]
                lon_ref[g, x, above : above + own, :] = column
            for r in range(TAPS + 1):
                for k in range(SHIFT):
                    columns = pl.ds(base + r, TILE, stride=2)
                    near_ref[g, r, k] = wide_ref[g, near + k, columns, :].astype(BF16)

def edge_kernel(
    shrink,
    final,
    layer,
    left_in,
    right_in,
    lon_in,
    lat_in,
    corner_in,
    near_ref,
    left_new,
    right_new,
    lon_new,
    taps_ref,
    mix_ref,
    *refs,
):
    if final:
        state_ref, wide_ref, taps_in, center_ref, tap_ref, spread_ref, out_ref = refs[:7]
        spare_ref, mix_lon, rows_ref, sems = refs[7:]
        kept, width = left_new.shape[:2]
        copies = [
            pltpu.make_async_copy(left_new, state_ref.at[0:kept, 0:width], sems.at[0]),
            pltpu.make_async_copy(
                right_new, state_ref.at[0:kept, width : 2 * width], sems.at[1]
            ),
            pltpu.make_async_copy(rows_ref, state_ref.at[kept : kept + SHIFT], sems.at[2]),
        ]
        copies[0].start()
        copies[1].start()
    else:
        edge_ref, lon_ref, corner_ref = refs[:3]
        wide_ref, taps_in, center_ref, tap_ref, spread_ref, out_ref, spare_ref, mix_lon = refs[3:]
    cols = lat_in.shape[1]
    groups = wide_ref.shape[0]
    main = 0 if shrink else EDGE
    side = cols if shrink else 0
    base = 0 if shrink else EDGE - SHIFT
    last = at_last()
    top = lax.axis_index("lat") == 0
    own = SHIFT if not shrink else 0
    if shrink:
        for g in range(groups):
            for k in range(2):
                spare = lon_in[SHIFT + k, :, lanes_of(g)].astype(F32)
                spare_ref[g, k * TILE : (k + 1) * TILE, :] = spare
    for k in range(SHIFT):
        value, beside = lat_in[k].astype(F32), corner_in[k].astype(F32)
        if not shrink:
            value, beside = jnp.where(top, 0.0, value), jnp.where(top, 0.0, beside)
        elif k < HALO:
            kept = left_in.shape[0] - SPARE + k
            inner = jnp.concatenate([left_in[kept], right_in[kept]], axis=0)
            value = jnp.where(last, inner.astype(F32), value)
            beside = beside[:SHIFT]
            extra = [spare_ref[g, pl.ds(k, SHIFT, stride=HALO), :] for g in range(groups)]
            beside = jnp.where(last, jnp.concatenate(extra, axis=1), beside)
        else:
            value, beside = jnp.where(last, 0.0, value), jnp.where(last, 0.0, beside)
        put(wide_ref, k, main, value)
        put(wide_ref, k, side, beside)

    @pl.loop(0, groups)
    def _(g):
        for k in range(SHIFT):
            for r in range(TAPS + 1):
                columns = pl.ds(base + r, TILE, stride=2)
                taps_in[r, SHIFT - own + k] = wide_ref[g, k, columns, :].astype(BF16)
        taps_in[:, own : own + SHIFT] = near_ref[g]
        center_ref[g] = taps_in[HALO : HALO + 2, HALO : HALO + SHIFT]
        convolve(taps_in, taps_ref, tap_ref, spread_ref, layer, g, 0, SHIFT)

    finish(center_ref, spread_ref, mix_ref, out_ref, layer, 0, SHIFT)
    kept = left_new.shape[0]
    if final:
        for k in range(SHIFT):
            rows_ref[k] = row_of(out_ref, k).astype(BF16)
        copies[2].start()
        for copy in copies:
            copy.wait()
        return

    for k in range(SHIFT):
        value = row_of(out_ref, k)
        if not shrink and k < HALO:
            value = jnp.where(top, 0.0, value)
        edge_ref[k] = value.astype(BF16)
        corner_ref[k] = (value[cols - EDGE :] if shrink else value[:EDGE]).astype(BF16)
    edge = cols - SHIFT if shrink else 0
    place = TILE - SHIFT if shrink else 0
    for g in range(groups):
        for x in range(SHIFT):
            column = flat(out_ref)[g, pl.ds(edge + x, SHIFT, stride=cols), :]
            if not shrink:
                outside = lax.broadcasted_iota(jnp.int32, (SHIFT, LANES), 0) < HALO
                column = jnp.where(jnp.logical_and(top, outside), 0.0, column)
            mix_lon[g, x] = lon_new[g, x]
            mix_lon[g, x, place : place + SHIFT, :] = column
            lon_ref[x, :, lanes_of(g)] = mix_lon[g, x].astype(BF16)
    if not shrink:
        for k in range(HALO):
            value = left_new[kept - SPARE + k].astype(F32)
            for g in range(groups):
                spare_ref[g, pl.ds(k, SHIFT, stride=HALO), :] = value[:SHIFT, lanes_of(g)]
        for g in range(groups):
            for k in range(2):
                spare = spare_ref[g, k * TILE : (k + 1) * TILE, :]
                lon_ref[SHIFT + k, :, lanes_of(g)] = spare.astype(BF16)


def call(kernel, out_shape, inputs, scratch=(), limit=VMEM_LIMIT, space=None, work=0, out_space=pltpu.VMEM):
    whole = pl.BlockSpec(memory_space=out_space)
    single = isinstance(out_shape, jax.ShapeDtypeStruct)
    spaces = space or (pltpu.VMEM,) * len(inputs)
    return pl.pallas_call(
        kernel,
        out_shape=out_shape,
        in_specs=[pl.BlockSpec(memory_space=s) for s in spaces],
        out_specs=whole if single else [whole] * len(out_shape),
        scratch_shapes=list(scratch),
        compiler_params=pltpu.CompilerParams(vmem_limit_bytes=limit),
        cost_estimate=pl.CostEstimate(flops=work, bytes_accessed=0, transcendentals=0),
    )(*inputs)


def held(*shape):
    return jax.ShapeDtypeStruct(shape, BF16)


def scratch_of(groups, seen, made, cols, chans):
    return (
        pltpu.VMEM((groups, seen, cols + EDGE, LANES), F32),
        pltpu.VMEM((TAPS + 1, seen, TILE, LANES), BF16),
        pltpu.VMEM((groups, 2, made, TILE, LANES), BF16),
        pltpu.VMEM((TAPS * TAPS, TILE, LANES), BF16),
        pltpu.VMEM((2, made, TILE, chans), BF16),
        pltpu.VMEM((groups, made, cols, LANES), F32),
    )


def layer(state, lon_out, corner_out, taps, mix, number, shrink, final):
    edge, left, right = state
    lat_in, lon_in, corner_in = exchange((edge, lon_out, corner_out), not shrink)
    cols, chans = edge.shape[1:]
    groups = chans // LANES
    own = left.shape[0] - (SPARE if shrink else 0)
    rows = own + SHIFT
    spare = 0 if shrink else SPARE
    made = own + spare
    block = held(made, TILE, chans)
    scratch = (
        pltpu.VMEM((groups, rows + spare, cols + EDGE, LANES), F32),
        pltpu.VMEM((TAPS + 1, made // 2 + TAPS - 1, TILE, LANES), BF16),
        pltpu.VMEM((groups, 2, made // 2, TILE, LANES), BF16),
        pltpu.VMEM((TAPS * TAPS, TILE, LANES), BF16),
        pltpu.VMEM((2, made // 2, TILE, chans), BF16),
        pltpu.VMEM((groups, made, TILE, LANES), F32),
    )
    lead = call(
        functools.partial(block_kernel, shrink, True, number),
        block,
        (edge, left, right, taps, mix),
        scratch,
        work=made * TILE * chans * WORK * (5 if shrink else 3),
    )
    trail, lon_new, near = call(
        functools.partial(block_kernel, shrink, False, number),
        (
            block,
            jax.ShapeDtypeStruct((groups, SHIFT, rows, LANES), F32),
            held(groups, TAPS + 1, SHIFT, TILE, LANES),
        ),
        (edge, left, right, lon_in, taps, mix),
        scratch,
        work=made * TILE * chans * WORK * (7 if shrink else 11),
    )
    new = (lead, trail) if shrink else (trail, lead)
    last_scratch = ()
    if final:
        outs = held(made + SHIFT, cols, chans)
        last_scratch = (pltpu.VMEM((SHIFT, cols, chans), BF16), pltpu.SemaphoreType.DMA((3,)))
    else:
        outs = (
            held(SHIFT, cols, chans),
            held(SHIFT if shrink else EDGE, rows, chans),
            held(SHIFT, EDGE, chans),
        )
    outs = call(
        functools.partial(edge_kernel, shrink, final, number),
        outs,
        (left, right, lon_in, lat_in, corner_in, near, *new, lon_new, taps, mix),
        scratch_of(groups, 2 * SHIFT, SHIFT, cols, chans)
        + (
            pltpu.VMEM((groups, 2 * TILE, LANES), F32),
            pltpu.VMEM((groups, SHIFT, rows, LANES), F32),
        )
        + last_scratch,
        out_space=pltpu.HBM if final else pltpu.VMEM,
        work=SHIFT * cols * chans * WORK * 5,
    )
    if final:
        return outs
    edge, lon_out, corner_out = outs
    return (edge, *new), lon_out, corner_out


def exchange(pieces, forward):
    lat, lon, corner = pieces
    count_lat = lax.axis_size("lat")
    count_lon = lax.axis_size("lon")
    along = [(i, (i + 1) % count_lat) for i in range(count_lat)]
    around = [(j, (j + 1) % count_lon) for j in range(count_lon)]
    across = [
        (i * count_lon + j, ni * count_lon + nj) for i, ni in along for j, nj in around
    ]
    if not forward:
        along, around, across = ([(t, s) for s, t in p] for p in (along, around, across))
    lon = lax.ppermute(lon, "lon", around)
    lat = lax.ppermute(lat, "lat", along)
    corner = lax.ppermute(corner, ("lat", "lon"), across)
    return lat, lon, corner


def body(
    background, observations, destination, footprint, weights, obs_proj, depth_w, point_w, gains
):
    rows, cols, chans = background.shape
    devices = lax.axis_size("lat") * lax.axis_size("lon")
    obs_rows, feats = observations.shape
    cap = 2 * obs_rows // devices
    depth = cap * (feats // LANES) + META
    foot_count = footprint.shape[1]
    send = call(
        functools.partial(pack_kernel, cap, cols),
        jax.ShapeDtypeStruct((devices, depth, LANES), BF16),
        (destination.T, footprint.T, weights.T, observations),
        (
            pltpu.VMEM((1, obs_rows), jnp.int32),
            pltpu.VMEM((foot_count, obs_rows), jnp.int32),
            pltpu.VMEM((foot_count, obs_rows), BF16),
            pltpu.VMEM((obs_rows, feats), BF16),
            pltpu.SemaphoreType.DMA((4,)),
        ),
        PACK_LIMIT,
        (pltpu.HBM,) * 4,
    )
    got = lax.all_to_all(send, ("lat", "lon"), split_axis=0, concat_axis=0, tiled=True)
    layers = depth_w.shape[0]
    taps = depth_w.transpose(1, 2, 0, 3).reshape(TAPS * TAPS, layers, chans)
    mix = (gains[:, :, None] * point_w.astype(F32)).astype(BF16)
    proj, back = call(
        fetch_kernel,
        (held(*obs_proj.shape), held(*background.shape)),
        (obs_proj, background),
        (pltpu.SemaphoreType.DMA((2,)),),
        space=(pltpu.HBM, pltpu.HBM),
    )
    got, mix, proj, back = lax.optimization_barrier((got, mix, proj, back))
    edge, left, right, lon_out, corner_out = call(
        functools.partial(assim_kernel, cap),
        (
            held(SHIFT, cols, chans),
            held(rows - SHIFT, TILE, chans),
            held(rows - SHIFT, TILE, chans),
            held(SHIFT, rows, chans),
            held(SHIFT, EDGE, chans),
        ),
        (got, proj, back),
        (
            pltpu.VMEM((devices, depth, LANES), BF16),
            pltpu.VMEM((chans // LANES, rows * EDGE, LANES), F32),
            pltpu.SemaphoreType.DMA((PIECES,)),
        ),
        space=(pltpu.HBM, pltpu.VMEM, pltpu.VMEM),
    )
    state = (edge, left, right)
    for n in range(layers - 1):
        state, lon_out, corner_out = layer(
            state, lon_out, corner_out, taps, mix, n, n % 2 == 1, False
        )
    n = layers - 1
    return layer(state, lon_out, corner_out, taps, mix, n, n % 2 == 1, True)


def solution(mesh):
    placed = (
        P("lat", "lon", None),
        P(("lat", "lon"), None),
        P(("lat", "lon"), None),
        P(("lat", "lon"), None),
        P(("lat", "lon"), None),
        P(),
        P(),
        P(),
        P(),
    )
    return jax.shard_map(
        body, mesh=mesh, in_specs=placed, out_specs=P("lat", "lon", None), check_vma=False
    )
```
